32 devices in a mesh: groups: 2 (over x), replica: 4 (over z), tensor: 4 (over y, core).
Axes of the slice: x: 2, y: 2, z: 4, core: 2. Of those that a mesh axis runs over, the one named last changes fastest.
Arguments:
- tokens: bfloat16 [3072, 8192], P(('groups', 'replica', 'tensor')), parts along dimension 0, may hold values from -3 to 3
- gain: bfloat16 [8192], replicated, may hold values from 0.099609375 to 1.8984375
- w_query: bfloat16 [8192, 4096], P(None, 'tensor'), may hold values from -0.0625 to 0.0625
- w_keyvalue: bfloat16 [8192, 1024], P(None, 'tensor'), may hold values from -0.0625 to 0.0625
- w_out: bfloat16 [4096, 8192], P('tensor'), may hold values from -0.25 to 0.25
- kv_pool: bfloat16 [128, 4, 64, 256], P(('groups', 'replica', 'tensor')), parts along dimension 0, may hold values from -96 to 96
- suffix_pages: int32 [8, 4], P(('groups', 'replica')), parts along dimension 0, may hold values from 1 to 24, 48 in all within a row
- page_index: int32 [8, 16, 2], P(('groups', 'replica')), parts along dimension 0, may hold values from 0 to 3
- page_request: int32 [8, 16, 2], P(('groups', 'replica')), parts along dimension 0, may hold values from -1 to 3, as said below
- new_slot: int32 [8, 6], P(('groups', 'replica')), parts along dimension 0, may hold values from 0 to 15, as said below
Outputs:
- layer_out: bfloat16 [3072, 8192], P(('groups', 'replica', 'tensor')), parts along dimension 0
- pool_out: bfloat16 [128, 4, 64, 256], P(('groups', 'replica', 'tensor')), parts along dimension 0
The draws below stay inside these ranges and needn't reach their ends.
There are 2 independent parts, one for each index of `groups`. The reference program is written for one: setup_inputs(seed, part) draws one part's arguments, and reference() takes and returns one part's arrays. A program takes and returns all parts, laid end to end along the dimension named above; an argument that names none is the same for every part. Nothing has to cross between parts.
Inputs may be any that keep to these rules, and one draw needn't show every extreme that they name: `page_request`: -1 marks an empty slot. `new_slot`: distinct within a replica's row.
All inputs are finite; a program needn't handle non-finite values.
Results may differ from the reference program's by a relative error of at most 0.012.
The reference program's roundings to bfloat16 on the way count: a program that leaves them out, or rounds other values in their place, can miss the bound.
Values may be sent and summed in bfloat16 or wider, within the bound.
No kernel may reach another device: no remote copies, remote signals or barrier semaphores. Data moves between devices by JAX's collectives and lax.ppermute only.
A program may use at most 192 MiB of HBM per device.

```python
import math
import jax
import jax.numpy as jnp
import numpy as np
from jax import lax

D = 8192
HEADS = 32
KV_HEADS = 4
HEAD_DIM = 128
PAGE = 64
UNIT = 8
REQS = 4
CAP = 2
POOL_DEV = 4
ROWS = 384
TOKENS = 1536
N_REPLICA = 4
N_TENSOR = 4


def draw_kv_pool(key, part):
    key = jax.random.fold_in(key, 53)
    streams = jax.random.split(key, 1)
    shape = (N_REPLICA * N_TENSOR * POOL_DEV, KV_HEADS, PAGE, 2 * HEAD_DIM)
    values = jnp.clip(jax.random.normal(streams[0], shape, jnp.float32), -6.0, 6.0)
    return values.astype(jnp.bfloat16)


def draw_page_index(key, part):
    key = jax.random.fold_in(key, 11)
    owners = N_REPLICA * N_TENSOR
    values = jax.random.randint(key, (N_REPLICA, owners, CAP), 0, POOL_DEV)
    values = values.at[0, 0, 0].set(POOL_DEV - 1)
    values = values.at[0, 1, 0].set(0)
    return values.astype(jnp.int32)


def draw_page_request(key, part):
    key = jax.random.fold_in(key, 23)
    owners = N_REPLICA * N_TENSOR
    streams = jax.random.split(key, 3)
    favored = jax.random.randint(streams[0], (), 0, owners)
    used = jax.random.randint(streams[1], (N_REPLICA, owners, CAP), 0, 2)
    column = jnp.arange(owners, dtype=jnp.int32)[None, :, None]
    used = jnp.where(column == favored, 1, used)
    labels = jax.random.randint(streams[2], (N_REPLICA, owners, CAP), 0, REQS)
    labels = jnp.where(used == 1, labels, -1)
    labels = labels.at[0, favored, 0].set(REQS - 1)
    spare = (favored + 1) % owners
    labels = labels.at[:, spare, CAP - 1].set(-1)
    return labels.astype(jnp.int32)


def draw_new_slot(key, part):
    key = jax.random.fold_in(key, 37)
    slots = N_TENSOR * POOL_DEV
    count = ROWS // PAGE
    streams = jax.random.split(key, N_REPLICA + 1)
    orders = jax.vmap(lambda single: jax.random.permutation(single, slots))(streams[1:])
    chosen = orders[:, :count].astype(jnp.int32)
    inner = (jax.random.permutation(streams[0], slots - 2)[:max(count - 2, 0)] + 1).astype(jnp.int32)
    first_row = jnp.concatenate([jnp.array([slots - 1, 0], dtype=jnp.int32), inner])[:count]
    return chosen.at[0].set(first_row).astype(jnp.int32)


def levels(rng, shape, shards, low, top_value):
    factor_of, own = 1.0, jax.random.fold_in(rng, 6)
    for dim, blocks in shards:
        heights = jnp.exp(jax.random.uniform(jax.random.fold_in(own, dim), (blocks,), jnp.float32, low / len(shards), top_value / len(shards)))
        factor_of = factor_of * jnp.repeat(heights, shape[dim] // blocks).reshape([-1 if axis == dim else 1 for axis in range(len(shape))])
    return factor_of


def profile(number_of, total, limit, skew):
    loads = [(1 << 20) // math.isqrt(standing ** skew) + 1 for standing in range(2, number_of + 1)]
    surplus, holding = total - limit - (number_of - 1), [1] * (number_of - 1)
    while surplus > 0:
        candidates = [i for i in range(number_of - 1) if holding[i] < limit]
        pool, budget = sum([loads[i] for i in candidates]), surplus
        for i in candidates:
            addition = min(limit - holding[i], max(1, budget * loads[i] // pool), surplus)
            holding[i] = holding[i] + addition
            surplus = surplus - addition
    return np.array([limit] + holding)


def ragged_sizes(key, number_of, total, reach, lean):
    if number_of == 2:
        one = jax.random.randint(key, (), max(1, total - reach), min(reach, total - 1) + 1)
        return jnp.stack([one, total - one])
    tallies = jnp.asarray(profile(number_of, total, reach, lean), jnp.int32)
    pairs = (number_of - 1) // 2
    source_of, taker = tallies[1:1 + 2 * pairs:2], tallies[2:2 + 2 * pairs:2]
    room = jnp.minimum(source_of - 1, reach - taker)
    shifted = jax.random.randint(jax.random.fold_in(key, 1), (pairs,), 0, 1 << 20) % (room + 1)
    tallies = tallies.at[1:1 + 2 * pairs:2].set(source_of - shifted).at[2:2 + 2 * pairs:2].set(taker + shifted)
    return tallies[jax.random.permutation(jax.random.fold_in(key, 2), number_of)]


def noise(own_key, extent, spread, bound, cuts=(), kind=jnp.bfloat16):
    level = levels(own_key, extent, cuts, -0.22, 0.18) if cuts else 1.0
    drawn = jax.random.normal(own_key, extent, jnp.float32) * spread * level
    return jnp.minimum(jnp.maximum(drawn, -bound), bound).astype(kind)


def setup_inputs(seed: int = 0, part: int = 0) -> dict:
    key_list = jax.random.split(jax.random.key(seed), 11)
    own_keys = jax.random.split(jax.random.fold_in(key_list[10], part), 11)
    tokens = noise(own_keys[0], (TOKENS, D), 0.5, 3.0, ((0, 16),))
    gain = jnp.clip(1.0 + 0.18 * jax.random.normal(key_list[1], (D,), jnp.float32), 0.099609375, 1.8984375).astype(jnp.bfloat16)
    w_query = noise(key_list[2], (D, HEADS * HEAD_DIM), D ** -0.5, 0.0625, ((1, 4),))
    w_keyvalue = noise(key_list[3], (D, 2 * KV_HEADS * HEAD_DIM), D ** -0.5, 0.0625, ((1, 4),))
    w_out = noise(key_list[4], (HEADS * HEAD_DIM, D), (4 * HEAD_DIM) ** -0.5, 0.25, ((0, 4),))
    kv_pool = draw_kv_pool(jax.random.fold_in(jax.random.fold_in(key_list[10], part), 71), part)
    suffix_pages = jax.vmap(lambda own: ragged_sizes(own, REQS, ROWS // UNIT, ROWS // UNIT // 2, 2))(jax.random.split(own_keys[6], N_REPLICA)).reshape((N_REPLICA, REQS)).astype(jnp.int32)
    page_index = draw_page_index(jax.random.fold_in(jax.random.fold_in(key_list[10], part), 71), part)
    page_request = draw_page_request(jax.random.fold_in(jax.random.fold_in(key_list[10], part), 71), part)
    new_slot = draw_new_slot(jax.random.fold_in(jax.random.fold_in(key_list[10], part), 71), part)
    return dict(tokens=tokens, gain=gain, w_query=w_query, w_keyvalue=w_keyvalue, w_out=w_out, kv_pool=kv_pool, suffix_pages=suffix_pages, page_index=page_index, page_request=page_request, new_slot=new_slot)


NEG_FILL = -1e+30
EPSILON = 1e-06

def normalize(rows, gain):
    values = rows.astype(jnp.float32)
    inverse = lax.rsqrt(lax.optimization_barrier(jnp.mean(values * values, axis=-1, keepdims=True)) + EPSILON)
    return (values * inverse * gain.astype(jnp.float32)).astype(jnp.bfloat16)

def row_segments(pages, total_rows):
    bounds = (jnp.cumsum(pages) * UNIT).astype(jnp.int32)
    positions = jnp.arange(total_rows, dtype=jnp.int32)
    return lax.optimization_barrier(jnp.sum((positions[:, None] >= bounds[None, :]).astype(jnp.int32), axis=1))

def reference(tokens, gain, w_query, w_keyvalue, w_out, kv_pool, suffix_pages, page_index, page_request, new_slot):
    owners = N_REPLICA * N_TENSOR
    group = HEADS // KV_HEADS
    local_width = HEADS // N_TENSOR * HEAD_DIM
    scale_factor = 1.0 / math.sqrt(HEAD_DIM)
    normed = normalize(tokens, gain)
    query = jnp.dot(normed, w_query, preferred_element_type=jnp.float32).astype(jnp.bfloat16)
    new_kv = jnp.dot(normed, w_keyvalue, preferred_element_type=jnp.float32).astype(jnp.bfloat16)
    owner_base = jnp.arange(owners, dtype=jnp.int32)[:, None] * POOL_DEV

    def one_replica(inputs):
        rows_in, query_rows, kv_rows, pages, index_rows, request_rows = inputs
        segments = row_segments(pages, ROWS)
        picked = kv_pool[(owner_base + index_rows).reshape(-1)]
        cached = picked.transpose(1, 0, 2, 3).reshape(KV_HEADS, owners * CAP * PAGE, 2 * HEAD_DIM)
        fresh = kv_rows.reshape(ROWS, KV_HEADS, 2 * HEAD_DIM).transpose(1, 0, 2)
        every_key = jnp.concatenate([cached, fresh], axis=1)
        key_groups = jnp.concatenate([jnp.repeat(request_rows.reshape(-1), PAGE), segments])
        key_order = jnp.concatenate([jnp.full((owners * CAP * PAGE,), -1, jnp.int32), jnp.arange(ROWS, dtype=jnp.int32)])
        row_order = jnp.arange(ROWS, dtype=jnp.int32)
        allowed = (key_groups[None, :] == segments[:, None]) & (key_order[None, :] <= row_order[:, None])
        heads_first = query_rows.reshape(ROWS, HEADS, HEAD_DIM).transpose(1, 0, 2)

        def one_head(items):
            head, head_query = items
            keys = lax.dynamic_index_in_dim(every_key, head // group, 0, keepdims=False)
            scores = jnp.dot(head_query, keys[:, :HEAD_DIM].T, preferred_element_type=jnp.float32) * scale_factor
            scores = jnp.where(allowed, scores, NEG_FILL)
            peak = lax.optimization_barrier(jnp.max(scores, axis=1, keepdims=True))
            probs = jnp.exp(scores - peak)
            total = lax.optimization_barrier(jnp.sum(probs, axis=1, keepdims=True))
            mixed = jnp.dot(probs.astype(jnp.bfloat16), keys[:, HEAD_DIM:], preferred_element_type=jnp.float32)
            return (mixed / total).astype(jnp.bfloat16)
        heads_out = lax.map(one_head, (jnp.arange(HEADS, dtype=jnp.int32), heads_first))
        attention = heads_out.transpose(1, 0, 2).reshape(ROWS, HEADS * HEAD_DIM)

        def add_part(carry, part_index):
            block = lax.dynamic_slice_in_dim(attention, part_index * local_width, local_width, 1)
            matrix = lax.dynamic_slice_in_dim(w_out, part_index * local_width, local_width, 0)
            term = jnp.dot(block, matrix, preferred_element_type=jnp.float32).astype(jnp.bfloat16)
            term = lax.optimization_barrier(term)
            return (carry + term.astype(jnp.float32), None)
        summed, _ = lax.scan(add_part, jnp.zeros((ROWS, D), jnp.float32), jnp.arange(N_TENSOR, dtype=jnp.int32))
        return (rows_in.astype(jnp.float32) + summed).astype(jnp.bfloat16)
    layer_out = lax.map(one_replica, (tokens.reshape(N_REPLICA, ROWS, D), query.reshape(N_REPLICA, ROWS, HEADS * HEAD_DIM), new_kv.reshape(N_REPLICA, ROWS, 2 * KV_HEADS * HEAD_DIM), suffix_pages, page_index, page_request))
    layer_out = layer_out.reshape(N_REPLICA * ROWS, D)
    fresh_pages = new_kv.reshape(N_REPLICA, ROWS // PAGE, PAGE, KV_HEADS, 2 * HEAD_DIM).transpose(0, 1, 3, 2, 4)
    fresh_pages = fresh_pages.reshape(N_REPLICA * (ROWS // PAGE), KV_HEADS, PAGE, 2 * HEAD_DIM)
    targets = (jnp.arange(N_REPLICA, dtype=jnp.int32)[:, None] * (N_TENSOR * POOL_DEV) + new_slot).reshape(-1)
    pool_out = kv_pool.at[targets].set(fresh_pages)
    return (layer_out, pool_out)
```

```python
import math

import jax
import jax.numpy as jnp
from jax import lax
from jax.experimental import pallas as pl
from jax.experimental.pallas import tpu as pltpu
from jax.sharding import PartitionSpec as P

KV_HEADS = 4
HEAD_DIM = 128
PAGE = 64
UNIT = 8


NEG_FILL = -1e30
EPSILON = 1e-06

F32 = jnp.float32
BF16 = jnp.bfloat16
MIB = 1 << 20
ANY = pl.BlockSpec(memory_space=pl.ANY)
SMEM = pl.BlockSpec(memory_space=pltpu.SMEM)
VMEM = pl.BlockSpec(memory_space=pltpu.VMEM)


def params(mib):
    return pltpu.CompilerParams(vmem_limit_bytes=mib * MIB)


def shape(dims, dtype=BF16):
    return jax.ShapeDtypeStruct(dims, dtype)


def normalize(rows, gain):
    values = rows.astype(jnp.float32)
    inverse = lax.rsqrt(jnp.mean(values * values, axis=-1, keepdims=True) + EPSILON)
    return (values * inverse * gain.astype(jnp.float32)).astype(jnp.bfloat16)


def row_segments(pages, total_rows):
    bounds = jnp.cumsum(pages) * UNIT
    positions = jnp.arange(total_rows, dtype=jnp.int32)
    return jnp.sum((positions[:, None] >= bounds[None, :]).astype(jnp.int32), axis=1)


def gathered_body(
    tokens,
    gain,
    w_query,
    w_keyvalue,
    w_out,
    kv_pool,
    suffix_pages,
    page_index,
    page_request,
    new_slot,
):
    replicas = lax.axis_size("replica")
    tensors = lax.axis_size("tensor")
    owners = replicas * tensors
    position = lax.axis_index("tensor")
    query_width = w_query.shape[1]
    local_heads = query_width // HEAD_DIM
    share = tensors // KV_HEADS
    my_head = position // share
    scale_factor = 1.0 / math.sqrt(HEAD_DIM)
    normed = normalize(tokens, gain)
    piece = lax.all_gather(normed, "tensor", axis=0, tiled=True)
    first = jnp.dot(piece, w_query, preferred_element_type=jnp.float32)
    second = jnp.dot(piece, w_keyvalue, preferred_element_type=jnp.float32)
    projected = jnp.concatenate([first, second], axis=1).astype(jnp.bfloat16)
    query = projected[:, :query_width]
    keyvalue = lax.all_gather(projected[:, query_width:], "tensor", axis=1, tiled=True)
    total_rows = query.shape[0]
    wanted = lax.all_to_all(
        page_index[0], ("replica", "tensor"), split_axis=0, concat_axis=0, tiled=True
    )
    slot_count = wanted.shape[1]
    sources = jnp.arange(owners, dtype=jnp.int32) % tensors
    source_heads = sources // share
    flat_pool = kv_pool.reshape(kv_pool.shape[0] * KV_HEADS, PAGE, 2 * HEAD_DIM)
    outgoing = flat_pool[wanted * KV_HEADS + source_heads[:, None]]
    sub_tokens = outgoing.shape[2]
    pulled = lax.all_to_all(
        outgoing, ("replica", "tensor"), split_axis=0, concat_axis=0, tiled=True
    )
    segments = row_segments(suffix_pages[0], total_rows)
    key_groups = page_request[0]
    stacked = (
        query.reshape(total_rows, local_heads, HEAD_DIM)
        .transpose(1, 0, 2)
        .reshape(local_heads * total_rows, HEAD_DIM)
    )
    own_new = lax.dynamic_index_in_dim(
        keyvalue.reshape(total_rows, KV_HEADS, 2 * HEAD_DIM), my_head, 1, keepdims=False
    )
    row_order = jnp.arange(total_rows, dtype=jnp.int32)
    causal = (segments[:, None] == segments[None, :]) & (row_order[None, :] <= row_order[:, None])

    def block_scores(queries, head_count, keys, allowed):
        raw = (
            jnp.dot(queries, keys[:, :HEAD_DIM].T, preferred_element_type=jnp.float32)
            * scale_factor
        )
        raw = raw.reshape(head_count, total_rows, keys.shape[0])
        return jnp.where(allowed[None], raw, NEG_FILL)

    first_scores = block_scores(stacked, local_heads, own_new, causal)
    running = jnp.max(first_scores, axis=2)
    probs = jnp.exp(first_scores - running[:, :, None])
    denominator = jnp.sum(probs, axis=2)
    numerator = jnp.dot(
        probs.astype(jnp.bfloat16).reshape(local_heads * total_rows, total_rows),
        own_new[:, HEAD_DIM:],
        preferred_element_type=jnp.float32,
    )
    block_owners = 16
    blocks = owners // block_owners

    def absorb(step, state):
        peak, total, mixed = state
        pages = lax.dynamic_slice_in_dim(pulled, step * block_owners, block_owners, 0)
        keys = pages.reshape(block_owners * slot_count * sub_tokens, 2 * HEAD_DIM)
        labels = lax.dynamic_slice_in_dim(key_groups, step * block_owners, block_owners, 0).reshape(
            -1
        )
        matches = (segments[:, None] == labels[None, :])[:, :, None]
        allowed = jnp.broadcast_to(matches, (total_rows, labels.shape[0], sub_tokens)).reshape(
            total_rows, labels.shape[0] * sub_tokens
        )
        scores = block_scores(stacked, local_heads, keys, allowed)
        updated = jnp.maximum(peak, jnp.max(scores, axis=2))
        rescale = jnp.exp(peak - updated)
        weights = jnp.where(allowed[None], jnp.exp(scores - updated[:, :, None]), 0.0)
        total = total * rescale + jnp.sum(weights, axis=2)
        flat_weights = weights.astype(jnp.bfloat16).reshape(local_heads * total_rows, keys.shape[0])
        mixed = mixed * rescale.reshape(-1)[:, None] + jnp.dot(
            flat_weights, keys[:, HEAD_DIM:], preferred_element_type=jnp.float32
        )
        return (updated, total, mixed)

    running, denominator, numerator = lax.fori_loop(
        0, blocks, absorb, (running, denominator, numerator)
    )
    attention = (numerator / denominator.reshape(-1)[:, None]).astype(jnp.bfloat16)
    attention = (
        attention.reshape(local_heads, total_rows, HEAD_DIM)
        .transpose(1, 0, 2)
        .reshape(total_rows, query_width)
    )
    summed = lax.psum_scatter(
        jnp.dot(attention, w_out, preferred_element_type=jnp.float32).astype(jnp.bfloat16),
        "tensor",
        scatter_dimension=0,
        tiled=True,
    ).astype(jnp.float32)
    layer_out = (tokens.astype(jnp.float32) + summed).astype(jnp.bfloat16)
    new_count = total_rows // PAGE
    fresh = (
        keyvalue.reshape(new_count, PAGE, KV_HEADS, 2 * HEAD_DIM)
        .transpose(0, 2, 1, 3)
        .reshape(new_count, KV_HEADS * PAGE * 2 * HEAD_DIM)
    )
    local_pages = kv_pool.shape[0]
    targets = position * local_pages + jnp.arange(local_pages, dtype=jnp.int32)
    match_table = new_slot[0][None, :] == targets[:, None]
    placed = jnp.dot(
        match_table.astype(jnp.bfloat16), fresh, preferred_element_type=jnp.float32
    ).astype(jnp.bfloat16)
    placed = placed.reshape(kv_pool.shape)
    landed = jnp.any(match_table, axis=1)
    pool_out = jnp.where(landed[:, None, None, None], placed, kv_pool)
    return (layer_out, pool_out)


def norm_rows(place, tokens, gain):
    rows, width = tokens.shape
    half = width // 2
    step = 16

    def kernel(place_ref, x_ref, g_ref, mine_ref, other_ref):
        core = place_ref[1]
        near = pl.multiple_of(core * half, half)
        far = pl.multiple_of((1 - core) * half, half)

        def block(i, carry):
            at = pl.ds(pl.multiple_of(i * step, step), step)
            total = jnp.zeros((step, 1), F32)
            for part in range(2):
                values = x_ref[at, part * half : (part + 1) * half].astype(F32)
                total += jnp.sum(values * values, axis=1, keepdims=True)
            inverse = lax.rsqrt(total * (1.0 / width) + EPSILON)
            for start, out in ((near, mine_ref), (far, other_ref)):
                cols = pl.ds(start, half)
                values = x_ref[at, cols].astype(F32)
                out[at, :] = (values * inverse * g_ref[:, cols].astype(F32)).astype(BF16)
            return carry

        lax.fori_loop(0, rows // step, block, 0)

    return pl.pallas_call(
        kernel,
        in_specs=[SMEM, VMEM, VMEM],
        out_specs=[VMEM, VMEM],
        out_shape=[shape((rows, half)), shape((rows, half))],
        compiler_params=params(16),
        name="norm_rows",
    )(place, tokens, gain.reshape(1, width))


def project(place, near, far, w_query, w_keyvalue, swap):
    count = len(near)
    rows, half = near[0].shape
    q_width, kv_width = w_query.shape[1], w_keyvalue.shape[1]
    steps = 8
    depth = 2 * half // steps

    def kernel(place_ref, *refs):
        near_refs, far_refs = refs[:count], refs[count : 2 * count]
        wq, wkv, q_ref, kv_ref, wq_buf, wkv_buf, q_acc, kv_acc, sems = refs[2 * count :]
        core = place_ref[1]

        def copies(j):
            base = core if j < steps // 2 else 1 - core
            start = pl.multiple_of(base * half + (j % (steps // 2)) * depth, depth)
            return (
                pltpu.make_async_copy(wq.at[pl.ds(start, depth)], wq_buf.at[j], sems.at[2 * j]),
                pltpu.make_async_copy(
                    wkv.at[pl.ds(start, depth)], wkv_buf.at[j], sems.at[2 * j + 1]
                ),
            )

        for j in range(steps):
            for copy in copies(j):
                copy.start()
        for j in range(steps):
            for copy in copies(j):
                copy.wait()
            group = near_refs if j < steps // 2 else far_refs
            cols = slice((j % (steps // 2)) * depth, (j % (steps // 2) + 1) * depth)
            x = group[0][:, cols]
            if count > 1:
                x = jnp.concatenate([ref[:, cols] for ref in group], axis=0)
            q_part = jnp.dot(x, wq_buf[j], preferred_element_type=F32)
            kv_part = jnp.dot(x, wkv_buf[j], preferred_element_type=F32)
            if j == 0:
                q_acc[...] = q_part
                kv_acc[...] = kv_part
            elif j < steps - 1:
                q_acc[...] += q_part
                kv_acc[...] += kv_part
            else:
                q_last = (q_acc[...] + q_part).astype(BF16)
                kv_last = (kv_acc[...] + kv_part).astype(BF16)
        for b in range(count):
            at = b * rows
            if swap:
                at = pl.multiple_of((core if b == 0 else 1 - core) * rows, rows)
            q_ref[pl.ds(at, rows), :] = q_last[b * rows : (b + 1) * rows]
            kv_ref[pl.ds(at, rows), :] = kv_last[b * rows : (b + 1) * rows]

    total = count * rows
    weights = 2 * half * (q_width + kv_width)
    return pl.pallas_call(
        kernel,
        in_specs=[SMEM] + [VMEM] * (2 * count) + [ANY, ANY],
        out_specs=[VMEM, VMEM],
        out_shape=[shape((total, q_width)), shape((total, kv_width))],
        scratch_shapes=[
            pltpu.VMEM((steps, depth, q_width), BF16),
            pltpu.VMEM((steps, depth, kv_width), BF16),
            pltpu.VMEM((total, q_width), F32),
            pltpu.VMEM((total, kv_width), F32),
            pltpu.SemaphoreType.DMA((2 * steps,)),
        ],
        compiler_params=params(40),
        cost_estimate=pl.CostEstimate(
            flops=2 * total * weights, bytes_accessed=2 * weights, transcendentals=0
        ),
        name="project",
    )(place, *near, *far, w_query, w_keyvalue)


def attend(place, pages_of, requests, query, fresh, bases, pulled, q_base, block_rows):
    rows, width = query.shape
    heads = width // HEAD_DIM
    blocks = rows // block_rows
    groups = len(pulled)
    per = pulled[0].shape[0]
    tensors = 4
    slots = per // tensors
    pages_step = 4
    steps = groups * per // pages_step
    fresh_rows = sum(f.shape[0] for f in fresh)
    keys_all = steps * pages_step * PAGE + fresh_rows
    stacked = heads * block_rows
    factor = math.log2(math.e) / math.sqrt(HEAD_DIM)
    count = len(fresh)

    def kernel(place_ref, sizes_ref, req_ref, q_ref, *refs):
        fresh_refs = refs[:count]
        page_refs = refs[count : count + groups]
        out_ref, scores = refs[count + groups :]
        me, side, rep = place_ref[0], place_ref[2], place_ref[3]
        bound = []
        running = jnp.int32(0)
        for k in range(4):
            running = running + sizes_ref[0, k] * UNIT
            bound.append(running)

        def segment_of(position):
            return sum((position >= b).astype(jnp.int32) for b in bound)

        def block(b, carry):
            start = pl.multiple_of(b * block_rows, block_rows)
            first_row = q_base(side) + start
            q = q_ref[pl.ds(start, block_rows), :]
            q_rows = jnp.concatenate(
                [q[:, h * HEAD_DIM : (h + 1) * HEAD_DIM] for h in range(heads)], axis=0
            )
            row_position = first_row + lax.broadcasted_iota(jnp.int32, (block_rows, 1), 0)
            row_segment = segment_of(row_position)
            peak = jnp.full((stacked, HEAD_DIM), NEG_FILL, F32)

            def add_scores(keys, allowed, column, peak):
                raw = lax.dot_general(
                    q_rows, keys, (((1,), (1,)), ((), ())), preferred_element_type=F32
                )
                n = keys.shape[0]
                masked = jnp.where(
                    allowed[None], raw.reshape(heads, block_rows, n), NEG_FILL
                ).reshape(stacked, n)
                scores[:, column : column + n] = masked
                for piece in range(0, n, HEAD_DIM):
                    peak = jnp.maximum(peak, masked[:, piece : piece + HEAD_DIM])
                return peak

            column = 0
            lanes = lax.broadcasted_iota(jnp.int32, (1, pages_step * PAGE), 1) // PAGE
            for g in range(groups):
                owner_row = lax.rem(rep - g + groups, groups)
                for p in range(0, per, pages_step):
                    label = jnp.full((1, pages_step * PAGE), -1, jnp.int32)
                    for j in range(pages_step):
                        owner = owner_row * tensors + jnp.bitwise_xor(me, (p + j) // slots)
                        value = req_ref[0, owner, (p + j) % slots]
                        label = jnp.where(lanes == j, value, label)
                    keys = page_refs[g][p : p + pages_step, :, :HEAD_DIM].reshape(
                        pages_step * PAGE, HEAD_DIM
                    )
                    peak = add_scores(keys, row_segment == label, column, peak)
                    column += pages_step * PAGE
            new_start = column
            new_keys = jnp.concatenate([f[:, :HEAD_DIM] for f in fresh_refs], axis=0)
            key_position = jnp.concatenate(
                [
                    base(side) + lax.broadcasted_iota(jnp.int32, (1, f.shape[0]), 1)
                    for base, f in zip(bases, fresh_refs)
                ],
                axis=1,
            )
            allowed = (row_segment == segment_of(key_position)) & (key_position <= row_position)
            raw = lax.dot_general(
                q_rows, new_keys, (((1,), (1,)), ((), ())), preferred_element_type=F32
            )
            masked = jnp.where(
                allowed[None], raw.reshape(heads, block_rows, fresh_rows), NEG_FILL
            ).reshape(stacked, fresh_rows)
            scores[:, new_start:keys_all] = masked
            top = jnp.maximum(
                jnp.max(peak, axis=1, keepdims=True), jnp.max(masked, axis=1, keepdims=True)
            )
            top = top * factor
            total = jnp.zeros((stacked, HEAD_DIM), F32)
            mixed = jnp.zeros((stacked, HEAD_DIM), F32)
            for g in range(groups):
                for p in range(0, per, pages_step):
                    column = (g * per + p) * PAGE
                    probs = jnp.exp2(scores[:, column : column + pages_step * PAGE] * factor - top)
                    for piece in range(0, pages_step * PAGE, HEAD_DIM):
                        total += probs[:, piece : piece + HEAD_DIM]
                    values = page_refs[g][p : p + pages_step, :, HEAD_DIM:].reshape(
                        pages_step * PAGE, HEAD_DIM
                    )
                    mixed += jnp.dot(probs.astype(BF16), values, preferred_element_type=F32)
            probs = jnp.exp2(scores[:, new_start:keys_all] * factor - top)
            denominator = jnp.sum(total, axis=1, keepdims=True) + jnp.sum(
                probs, axis=1, keepdims=True
            )
            new_values = jnp.concatenate([f[:, HEAD_DIM:] for f in fresh_refs], axis=0)
            mixed += jnp.dot(probs.astype(BF16), new_values, preferred_element_type=F32)
            result = (mixed / denominator).astype(BF16)
            for h in range(heads):
                out_ref[pl.ds(start, block_rows), h * HEAD_DIM : (h + 1) * HEAD_DIM] = result[
                    h * block_rows : (h + 1) * block_rows
                ]
            return carry

        if blocks == 1:
            block(0, 0)
        else:
            lax.fori_loop(0, blocks, block, 0)

    return pl.pallas_call(
        kernel,
        in_specs=[SMEM, SMEM, SMEM] + [VMEM] * (1 + count + groups),
        out_specs=VMEM,
        out_shape=shape((rows, width)),
        scratch_shapes=[pltpu.VMEM((stacked, keys_all), F32)],
        compiler_params=params(32),
        cost_estimate=pl.CostEstimate(
            flops=4 * rows * heads * keys_all * HEAD_DIM,
            bytes_accessed=4 * MIB,
            transcendentals=rows * heads * keys_all,
        ),
        name="attend",
    )(place, pages_of, requests, query, *fresh, *pulled)


def out_half(place, attention, w_out, near):
    rows, depth = attention.shape
    half = w_out.shape[1] // 2
    steps = 4
    wide = half // steps

    def kernel(place_ref, a_ref, w, out_ref, buf, sems):
        core = place_ref[1]
        base = (core if near else 1 - core) * half

        def copy(j):
            start = pl.multiple_of(base + j * wide, wide)
            return pltpu.make_async_copy(w.at[:, pl.ds(start, wide)], buf.at[j], sems.at[j])

        for j in range(steps):
            copy(j).start()
        for j in range(steps):
            copy(j).wait()
            out_ref[:, j * wide : (j + 1) * wide] = jnp.dot(
                a_ref[...], buf[j], preferred_element_type=F32
            ).astype(BF16)

    return pl.pallas_call(
        kernel,
        in_specs=[SMEM, VMEM, ANY],
        out_specs=VMEM,
        out_shape=shape((rows, half)),
        scratch_shapes=[
            pltpu.VMEM((steps, depth, wide), BF16),
            pltpu.SemaphoreType.DMA((steps,)),
        ],
        compiler_params=params(24),
        cost_estimate=pl.CostEstimate(
            flops=2 * rows * depth * half, bytes_accessed=2 * depth * half, transcendentals=0
        ),
        name="out_half",
    )(place, attention, w_out)


def out_local(place, attention, w_out):
    both, depth = attention.shape
    rows = both // 2
    width = w_out.shape[1]
    steps = 8
    wide = width // steps

    def kernel(place_ref, a_ref, w, own_ref, peer_ref, buf, sems):
        core = place_ref[1]
        own_at = pl.ds(pl.multiple_of(core * rows, rows), rows)
        peer_at = pl.ds(pl.multiple_of((1 - core) * rows, rows), rows)

        def copy(j):
            return pltpu.make_async_copy(
                w.at[:, j * wide : (j + 1) * wide], buf.at[j], sems.at[j]
            )

        for j in range(steps):
            copy(j).start()
        a = jnp.concatenate([a_ref[own_at, :], a_ref[peer_at, :]], axis=0)
        for j in range(steps):
            copy(j).wait()
            part = jnp.dot(a, buf[j], preferred_element_type=F32).astype(BF16)
            own_ref[:, j * wide : (j + 1) * wide] = part[:rows]
            peer_ref[:, j * wide : (j + 1) * wide] = part[rows:]

    return pl.pallas_call(
        kernel,
        in_specs=[SMEM, VMEM, ANY],
        out_specs=[VMEM, VMEM],
        out_shape=[shape((rows, width)), shape((rows, width))],
        scratch_shapes=[
            pltpu.VMEM((steps, depth, wide), BF16),
            pltpu.SemaphoreType.DMA((steps,)),
        ],
        compiler_params=params(36),
        cost_estimate=pl.CostEstimate(
            flops=2 * both * depth * width, bytes_accessed=2 * depth * width, transcendentals=0
        ),
        name="out_local",
    )(place, attention, w_out)


def finish(place, tokens, own, peer, near, far):
    rows, width = tokens.shape
    half = width // 2
    step = 16

    def kernel(place_ref, x_ref, own_ref, peer_ref, near_ref, far_ref, out_ref):
        core = place_ref[1]

        def block(i, carry):
            at = pl.ds(pl.multiple_of(i * step, step), step)
            for start, part in ((core, near_ref), (1 - core, far_ref)):
                cols = pl.ds(pl.multiple_of(start * half, half), half)
                local = own_ref[at, cols].astype(F32) + peer_ref[at, cols].astype(F32)
                total = local + part[at, :].astype(F32)
                out_ref[at, cols] = (x_ref[at, cols].astype(F32) + total).astype(BF16)
            return carry

        lax.fori_loop(0, rows // step, block, 0)

    return pl.pallas_call(
        kernel,
        in_specs=[SMEM] + [VMEM] * 5,
        out_specs=VMEM,
        out_shape=shape((rows, width)),
        compiler_params=params(16),
        name="finish",
    )(place, tokens, own, peer, near, far)


def pick_pages(place, wanted, own, core_pages, y_pages):
    replicas, _, slots = wanted.shape
    count, page, width = own.shape
    tensors = 4

    def kernel(place_ref, want_ref, own_ref, core_ref, y_ref, *refs):
        outs, sems = refs[:replicas], refs[replicas]
        me, rep = place_ref[0], place_ref[3]
        sources = (own_ref, core_ref.at[0], y_ref.at[0], core_ref.at[1])

        def copies():
            for k in range(replicas):
                asker = lax.rem(rep + k, replicas)
                for i in range(tensors):
                    owner = rep * tensors + jnp.bitwise_xor(me, i)
                    for s in range(slots):
                        at = i * slots + s
                        yield pltpu.make_async_copy(
                            sources[i].at[want_ref[asker, owner, s]],
                            outs[k].at[at],
                            sems.at[k * tensors * slots + at],
                        )

        for copy in copies():
            copy.start()
        for copy in copies():
            copy.wait()

    total = tensors * slots
    return pl.pallas_call(
        kernel,
        in_specs=[SMEM, SMEM] + [ANY] * 3,
        out_specs=[ANY] * replicas,
        out_shape=[shape((total, page, width))] * replicas,
        scratch_shapes=[pltpu.SemaphoreType.DMA((replicas * total,))],
        compiler_params=params(8),
        name="pick_pages",
    )(place, wanted, own, core_pages, y_pages)


def write_pool(place, slots, kv_pool, own, core_new, y_new):
    pages, heads = kv_pool.shape[:2]
    new_count = slots.shape[1]
    side_pages = new_count // 2

    def kernel(place_ref, slot_ref, pool_ref, own_ref, core_ref, y_ref, out_ref, sems):
        me, side = place_ref[0], place_ref[2]
        sources = (own_ref, core_ref.at[0], y_ref, core_ref.at[1])
        for p in range(pages):
            found = jnp.int32(-1)
            for j in range(new_count):
                found = jnp.where(slot_ref[0, j] == me * pages + p, j, found)
            far = (found >= side_pages).astype(jnp.int32)
            inner = jnp.maximum(found - far * side_pages, 0)

            @pl.when(found >= 0)
            def _():
                for i in range(heads):
                    origin = side if i < 2 else 1 - side
                    start = (jnp.bitwise_xor(far, origin) * side_pages + inner) * PAGE
                    pltpu.make_async_copy(
                        sources[i].at[pl.ds(pl.multiple_of(start, PAGE), PAGE)],
                        out_ref.at[p, jnp.bitwise_xor(me, i)],
                        sems.at[p * heads + i],
                    ).start()

            @pl.when(found < 0)
            def _():
                for i in range(heads):
                    at = jnp.bitwise_xor(me, i)
                    pltpu.make_async_copy(
                        pool_ref.at[p, at], out_ref.at[p, at], sems.at[p * heads + i]
                    ).start()

        for p in range(pages):
            for i in range(heads):
                at = jnp.bitwise_xor(me, i)
                pltpu.make_async_copy(
                    pool_ref.at[p, at], out_ref.at[p, at], sems.at[p * heads + i]
                ).wait()

    return pl.pallas_call(
        kernel,
        in_specs=[SMEM, SMEM] + [ANY] * 4,
        out_specs=ANY,
        out_shape=shape(kv_pool.shape),
        scratch_shapes=[pltpu.SemaphoreType.DMA((pages * heads,))],
        compiler_params=params(8),
        name="write_pool",
    )(place, slots, kv_pool, own, core_new, y_new)


def chip_pair_body(
    tokens,
    gain,
    w_query,
    w_keyvalue,
    w_out,
    kv_pool,
    suffix_pages,
    page_index,
    page_request,
    new_slot,
):
    replicas = lax.axis_size("replica")
    me = lax.axis_index("tensor")
    rep = lax.axis_index("replica")
    core = me % 2
    side = me // 2
    rows = tokens.shape[0]
    place = jnp.stack([me, core, side, rep]).astype(jnp.int32)

    def over_core(x):
        return lax.ppermute(x, "tensor", [(0, 1), (1, 0), (2, 3), (3, 2)])

    def over_y(x):
        return lax.ppermute(x, "tensor", [(0, 2), (2, 0), (1, 3), (3, 1)])

    def head_of(i):
        return lax.dynamic_index_in_dim(kv_pool, jnp.bitwise_xor(me, i), 1, keepdims=False)

    wanted = lax.all_gather(page_index[0], "replica", axis=0)
    y_pages = over_y(jnp.stack([head_of(2), head_of(3)]))
    core_pages = over_core(jnp.stack([head_of(1), y_pages[1]]))

    mine, other = norm_rows(place, tokens, gain)
    peer_near = over_core(other)
    peer_far = over_core(mine)
    is_first = core == 0
    first = over_y(jnp.where(is_first, mine, peer_near))
    second = over_y(jnp.where(is_first, peer_near, mine))

    picked = pick_pages(place, wanted, head_of(0), core_pages, y_pages)
    pulled = [picked[0]]
    for k in range(1, replicas):
        pulled.append(
            lax.ppermute(picked[k], "replica", [(i, (i + k) % replicas) for i in range(replicas)])
        )

    q_local, kv_local = project(
        place, [mine, peer_near], [other, peer_far], w_query, w_keyvalue, True
    )

    def local_base(s):
        return s * (2 * rows)

    def first_base(s):
        return (1 - s) * (2 * rows)

    def second_base(s):
        return (1 - s) * (2 * rows) + rows

    q_first, kv_first = project(place, [first], [over_core(first)], w_query, w_keyvalue, False)
    attended = attend(
        place, suffix_pages, page_request, q_first, [kv_local, kv_first],
        [local_base, first_base], pulled, first_base, rows,
    )
    away = over_core(out_half(place, attended, w_out, False))
    stay = out_half(place, attended, w_out, True)
    first_sum = over_y((stay.astype(F32) + away.astype(F32)).astype(BF16))

    q_second, kv_second = project(place, [second], [over_core(second)], w_query, w_keyvalue, False)
    fresh = [kv_local, kv_first, kv_second]
    bases = [local_base, first_base, second_base]
    attended = attend(
        place, suffix_pages, page_request, q_second, fresh, bases, pulled, second_base, rows
    )
    away = over_core(out_half(place, attended, w_out, False))
    stay = out_half(place, attended, w_out, True)
    second_sum = over_y((stay.astype(F32) + away.astype(F32)).astype(BF16))

    new_own = jnp.concatenate(fresh, axis=0)
    y_new = over_y(new_own)
    core_new = over_core(jnp.stack([new_own, y_new]))
    pool_out = write_pool(place, new_slot, kv_pool, new_own, core_new, y_new)

    attended = attend(
        place, suffix_pages, page_request, q_local, fresh, bases, pulled, local_base, rows
    )
    own_part, peer_part = out_local(place, attended, w_out)
    peer_part = over_core(peer_part)

    near = jnp.where(is_first, first_sum, second_sum)
    far = over_core(jnp.where(is_first, second_sum, first_sum))
    layer_out = finish(place, tokens, own_part, peer_part, near, far)
    return (layer_out, pool_out)


def solution(mesh):
    pair = mesh.shape["tensor"] == KV_HEADS
    return jax.shard_map(
        chip_pair_body if pair else gathered_body,
        mesh=mesh,
        in_specs=(
            P(("groups", "replica", "tensor"), None),
            P(),
            P(None, "tensor"),
            P(None, "tensor"),
            P("tensor", None),
            P(("groups", "replica", "tensor"), None, None, None),
            P(("groups", "replica"), None),
            P(("groups", "replica"), None, None),
            P(("groups", "replica"), None, None),
            P(("groups", "replica"), None),
        ),
        out_specs=(
            P(("groups", "replica", "tensor"), None),
            P(("groups", "replica", "tensor"), None, None, None),
        ),
        check_vma=False,
    )
```

```python
import math

import jax
import jax.numpy as jnp
from jax import lax
from jax.experimental import pallas as pl
from jax.experimental.pallas import tpu as pltpu
from jax.sharding import PartitionSpec as P

KV_HEADS = 4
HEAD_DIM = 128
PAGE = 64
UNIT = 8


NEG_FILL = -1e30
EPSILON = 1e-06

F32 = jnp.float32
BF16 = jnp.bfloat16
MIB = 1 << 20
ANY = pl.BlockSpec(memory_space=pl.ANY)
SMEM = pl.BlockSpec(memory_space=pltpu.SMEM)
VMEM = pl.BlockSpec(memory_space=pltpu.VMEM)
SMALL = pl.CostEstimate(flops=1024, bytes_accessed=1024, transcendentals=0)


def params(mib):
    return pltpu.CompilerParams(vmem_limit_bytes=mib * MIB)


def shape(dims, dtype=BF16):
    return jax.ShapeDtypeStruct(dims, dtype)


def normalize(rows, gain):
    values = rows.astype(jnp.float32)
    inverse = lax.rsqrt(jnp.mean(values * values, axis=-1, keepdims=True) + EPSILON)
    return (values * inverse * gain.astype(jnp.float32)).astype(jnp.bfloat16)


def row_segments(pages, total_rows):
    bounds = jnp.cumsum(pages) * UNIT
    positions = jnp.arange(total_rows, dtype=jnp.int32)
    return jnp.sum((positions[:, None] >= bounds[None, :]).astype(jnp.int32), axis=1)


def gathered_body(
    tokens,
    gain,
    w_query,
    w_keyvalue,
    w_out,
    kv_pool,
    suffix_pages,
    page_index,
    page_request,
    new_slot,
):
    replicas = lax.axis_size("replica")
    tensors = lax.axis_size("tensor")
    owners = replicas * tensors
    position = lax.axis_index("tensor")
    query_width = w_query.shape[1]
    local_heads = query_width // HEAD_DIM
    share = tensors // KV_HEADS
    my_head = position // share
    scale_factor = 1.0 / math.sqrt(HEAD_DIM)
    normed = normalize(tokens, gain)
    piece = lax.all_gather(normed, "tensor", axis=0, tiled=True)
    first = jnp.dot(piece, w_query, preferred_element_type=jnp.float32)
    second = jnp.dot(piece, w_keyvalue, preferred_element_type=jnp.float32)
    projected = jnp.concatenate([first, second], axis=1).astype(jnp.bfloat16)
    query = projected[:, :query_width]
    keyvalue = lax.all_gather(projected[:, query_width:], "tensor", axis=1, tiled=True)
    total_rows = query.shape[0]
    wanted = lax.all_to_all(
        page_index[0], ("replica", "tensor"), split_axis=0, concat_axis=0, tiled=True
    )
    slot_count = wanted.shape[1]
    sources = jnp.arange(owners, dtype=jnp.int32) % tensors
    source_heads = sources // share
    flat_pool = kv_pool.reshape(kv_pool.shape[0] * KV_HEADS, PAGE, 2 * HEAD_DIM)
    outgoing = flat_pool[wanted * KV_HEADS + source_heads[:, None]]
    sub_tokens = outgoing.shape[2]
    pulled = lax.all_to_all(
        outgoing, ("replica", "tensor"), split_axis=0, concat_axis=0, tiled=True
    )
    segments = row_segments(suffix_pages[0], total_rows)
    key_groups = page_request[0]
    stacked = (
        query.reshape(total_rows, local_heads, HEAD_DIM)
        .transpose(1, 0, 2)
        .reshape(local_heads * total_rows, HEAD_DIM)
    )
    own_new = lax.dynamic_index_in_dim(
        keyvalue.reshape(total_rows, KV_HEADS, 2 * HEAD_DIM), my_head, 1, keepdims=False
    )
    row_order = jnp.arange(total_rows, dtype=jnp.int32)
    causal = (segments[:, None] == segments[None, :]) & (row_order[None, :] <= row_order[:, None])

    def block_scores(queries, head_count, keys, allowed):
        raw = (
            jnp.dot(queries, keys[:, :HEAD_DIM].T, preferred_element_type=jnp.float32)
            * scale_factor
        )
        raw = raw.reshape(head_count, total_rows, keys.shape[0])
        return jnp.where(allowed[None], raw, NEG_FILL)

    first_scores = block_scores(stacked, local_heads, own_new, causal)
    running = jnp.max(first_scores, axis=2)
    probs = jnp.exp(first_scores - running[:, :, None])
    denominator = jnp.sum(probs, axis=2)
    numerator = jnp.dot(
        probs.astype(jnp.bfloat16).reshape(local_heads * total_rows, total_rows),
        own_new[:, HEAD_DIM:],
        preferred_element_type=jnp.float32,
    )
    block_owners = 16
    blocks = owners // block_owners

    def absorb(step, state):
        peak, total, mixed = state
        pages = lax.dynamic_slice_in_dim(pulled, step * block_owners, block_owners, 0)
        keys = pages.reshape(block_owners * slot_count * sub_tokens, 2 * HEAD_DIM)
        labels = lax.dynamic_slice_in_dim(key_groups, step * block_owners, block_owners, 0).reshape(
            -1
        )
        matches = (segments[:, None] == labels[None, :])[:, :, None]
        allowed = jnp.broadcast_to(matches, (total_rows, labels.shape[0], sub_tokens)).reshape(
            total_rows, labels.shape[0] * sub_tokens
        )
        scores = block_scores(stacked, local_heads, keys, allowed)
        updated = jnp.maximum(peak, jnp.max(scores, axis=2))
        rescale = jnp.exp(peak - updated)
        weights = jnp.where(allowed[None], jnp.exp(scores - updated[:, :, None]), 0.0)
        total = total * rescale + jnp.sum(weights, axis=2)
        flat_weights = weights.astype(jnp.bfloat16).reshape(local_heads * total_rows, keys.shape[0])
        mixed = mixed * rescale.reshape(-1)[:, None] + jnp.dot(
            flat_weights, keys[:, HEAD_DIM:], preferred_element_type=jnp.float32
        )
        return (updated, total, mixed)

    running, denominator, numerator = lax.fori_loop(
        0, blocks, absorb, (running, denominator, numerator)
    )
    attention = (numerator / denominator.reshape(-1)[:, None]).astype(jnp.bfloat16)
    attention = (
        attention.reshape(local_heads, total_rows, HEAD_DIM)
        .transpose(1, 0, 2)
        .reshape(total_rows, query_width)
    )
    summed = lax.psum_scatter(
        jnp.dot(attention, w_out, preferred_element_type=jnp.float32).astype(jnp.bfloat16),
        "tensor",
        scatter_dimension=0,
        tiled=True,
    ).astype(jnp.float32)
    layer_out = (tokens.astype(jnp.float32) + summed).astype(jnp.bfloat16)
    new_count = total_rows // PAGE
    fresh = (
        keyvalue.reshape(new_count, PAGE, KV_HEADS, 2 * HEAD_DIM)
        .transpose(0, 2, 1, 3)
        .reshape(new_count, KV_HEADS * PAGE * 2 * HEAD_DIM)
    )
    local_pages = kv_pool.shape[0]
    targets = position * local_pages + jnp.arange(local_pages, dtype=jnp.int32)
    match_table = new_slot[0][None, :] == targets[:, None]
    placed = jnp.dot(
        match_table.astype(jnp.bfloat16), fresh, preferred_element_type=jnp.float32
    ).astype(jnp.bfloat16)
    placed = placed.reshape(kv_pool.shape)
    landed = jnp.any(match_table, axis=1)
    pool_out = jnp.where(landed[:, None, None, None], placed, kv_pool)
    return (layer_out, pool_out)


def norm_rows(place, tokens, gain):
    rows, width = tokens.shape
    half = width // 2
    step = 16

    def kernel(place_ref, x_ref, g_ref, mine_ref, other_ref):
        core = place_ref[1]
        near = pl.multiple_of(core * half, half)
        far = pl.multiple_of((1 - core) * half, half)

        def block(i, carry):
            at = pl.ds(pl.multiple_of(i * step, step), step)
            total = jnp.zeros((step, 1), F32)
            for part in range(2):
                values = x_ref[at, part * half : (part + 1) * half].astype(F32)
                total += jnp.sum(values * values, axis=1, keepdims=True)
            inverse = lax.rsqrt(total * (1.0 / width) + EPSILON)
            for start, out in ((near, mine_ref), (far, other_ref)):
                cols = pl.ds(start, half)
                values = x_ref[at, cols].astype(F32)
                out[at, :] = (values * inverse * g_ref[:, cols].astype(F32)).astype(BF16)
            return carry

        lax.fori_loop(0, rows // step, block, 0)

    return pl.pallas_call(
        kernel,
        in_specs=[SMEM, VMEM, VMEM],
        out_specs=[VMEM, VMEM],
        out_shape=[shape((rows, half)), shape((rows, half))],
        compiler_params=params(16),
        cost_estimate=SMALL,
        name="norm_rows",
    )(place, tokens, gain.reshape(1, width))


def project_local(place, near, far, w_query, w_keyvalue, after):
    rows, half = near[0].shape
    q_width, kv_width = w_query.shape[1], w_keyvalue.shape[1]
    steps = 8
    depth = 2 * half // steps
    waits = len(after)

    def kernel(place_ref, near_own, near_peer, far_own, far_peer, wq, wkv, *refs):
        q_ref, kv_ref, wq_buf, wkv_buf, q_acc, kv_acc, sems = refs[waits:]
        core = place_ref[1]
        stream = weight_stream(core, half, steps, (wq, wkv), (wq_buf, wkv_buf), sems)
        for j in range(steps):
            for copy in stream(j):
                copy.start()
        for j in range(steps):
            for copy in stream(j):
                copy.wait()
            group = (near_own, near_peer) if j < steps // 2 else (far_own, far_peer)
            cols = slice((j % (steps // 2)) * depth, (j % (steps // 2) + 1) * depth)
            x = jnp.concatenate([ref[:, cols] for ref in group], axis=0)
            q_part = jnp.dot(x, wq_buf[j], preferred_element_type=F32)
            kv_part = jnp.dot(x, wkv_buf[j], preferred_element_type=F32)
            if j == 0:
                q_acc[...] = q_part
                kv_acc[...] = kv_part
            elif j < steps - 1:
                q_acc[...] += q_part
                kv_acc[...] += kv_part
            else:
                q_last = (q_acc[...] + q_part).astype(BF16)
                kv_last = (kv_acc[...] + kv_part).astype(BF16)
        for b in range(2):
            at = pl.ds(pl.multiple_of((core if b == 0 else 1 - core) * rows, rows), rows)
            q_ref[at, :] = q_last[b * rows : (b + 1) * rows]
            kv_ref[at, :] = kv_last[b * rows : (b + 1) * rows]

    total = 2 * rows
    return pl.pallas_call(
        kernel,
        in_specs=[SMEM] + [VMEM] * 4 + [ANY] * (2 + waits),
        out_specs=[VMEM, VMEM],
        out_shape=[shape((total, q_width)), shape((total, kv_width))],
        scratch_shapes=[
            pltpu.VMEM((steps, depth, q_width), BF16),
            pltpu.VMEM((steps, depth, kv_width), BF16),
            pltpu.VMEM((total, q_width), F32),
            pltpu.VMEM((total, kv_width), F32),
            pltpu.SemaphoreType.DMA((2 * steps,)),
        ],
        compiler_params=params(36),
        cost_estimate=SMALL,
        name="project_local",
    )(place, *near, *far, w_query, w_keyvalue, *after)


def weight_stream(core, half, steps, sources, buffers, sems):
    depth = 2 * half // steps

    def copies(j):
        base = core if j < steps // 2 else 1 - core
        start = pl.multiple_of(base * half + (j % (steps // 2)) * depth, depth)
        count = len(sources)
        return [
            pltpu.make_async_copy(w.at[pl.ds(start, depth)], buf.at[j], sems.at[count * j + i])
            for i, (w, buf) in enumerate(zip(sources, buffers))
        ]

    return copies


PAGES_STEP = 4


def attention_scratch(block_rows, heads, fresh_rows, slots):
    stacked = heads * block_rows
    return [
        pltpu.VMEM((stacked, fresh_rows + slots * PAGE), F32),
        pltpu.VMEM((stacked, HEAD_DIM), F32),
        pltpu.VMEM((stacked, HEAD_DIM), F32),
        pltpu.VMEM((slots * PAGE, 2 * HEAD_DIM), BF16),
        pltpu.SMEM((slots,), jnp.int32),
    ]


def attend_block(place_ref, sizes_ref, req_ref, q, first_row, fresh, pulled, scratch):
    scores, total_ref, mixed_ref, cache, labels = scratch
    me = place_ref[0]
    block_rows, width = q.shape
    heads = width // HEAD_DIM
    stacked = heads * block_rows
    groups, per = pulled.shape[:2]
    tensors = 4
    slots = per // tensors
    wide = PAGES_STEP * PAGE
    factor = math.log2(math.e) / math.sqrt(HEAD_DIM)
    bound = []
    running = jnp.int32(0)
    for k in range(sizes_ref.shape[1]):
        running = running + sizes_ref[0, k] * UNIT
        bound.append(running)

    def segment_of(position):
        return sum((position >= b).astype(jnp.int32) for b in bound)

    lowest = segment_of(first_row)
    highest = segment_of(first_row + block_rows - 1)
    count = jnp.int32(0)
    for g in range(groups):
        for p in range(per):
            owner = g * tensors + jnp.bitwise_xor(me, p // slots)
            label = req_ref[0, owner, p % slots]
            wanted = (label >= lowest) & (label <= highest)

            @pl.when(wanted)
            def _():
                cache[pl.ds(pl.multiple_of(count * PAGE, PAGE), PAGE), :] = pulled[g, p]
                labels[count] = label

            count = count + wanted.astype(jnp.int32)
    steps = (count + PAGES_STEP - 1) // PAGES_STEP
    for k in range(PAGES_STEP - 1):

        @pl.when(count + k < steps * PAGES_STEP)
        def _():
            cache[pl.ds(pl.multiple_of((count + k) * PAGE, PAGE), PAGE), :] = jnp.zeros(
                (PAGE, 2 * HEAD_DIM), BF16
            )
            labels[count + k] = jnp.int32(-1)

    q_rows = jnp.concatenate([q[:, h * HEAD_DIM : (h + 1) * HEAD_DIM] for h in range(heads)], axis=0)
    row_position = first_row + lax.broadcasted_iota(jnp.int32, (block_rows, 1), 0)
    row_segment = segment_of(row_position)

    def masked_scores(keys, allowed):
        raw = lax.dot_general(q_rows, keys, (((1,), (1,)), ((), ())), preferred_element_type=F32)
        n = keys.shape[0]
        return jnp.where(allowed[None], raw.reshape(heads, block_rows, n), NEG_FILL).reshape(
            stacked, n
        )

    def fold(values, combine):
        pieces = [values[:, i : i + HEAD_DIM] for i in range(0, values.shape[1], HEAD_DIM)]
        result = pieces[0]
        for piece in pieces[1:]:
            result = combine(result, piece)
        return result

    new = jnp.concatenate([rows for rows, _ in fresh], axis=0)
    fresh_rows = new.shape[0]
    key_position = jnp.concatenate(
        [
            base + lax.broadcasted_iota(jnp.int32, (1, rows.shape[0]), 1)
            for rows, base in fresh
        ],
        axis=1,
    )
    allowed = (row_segment == segment_of(key_position)) & (key_position <= row_position)
    masked = masked_scores(new[:, :HEAD_DIM], allowed)
    scores[:, :fresh_rows] = masked
    total_ref[...] = fold(masked, jnp.maximum)
    lanes = lax.broadcasted_iota(jnp.int32, (1, wide), 1) // PAGE

    def add_scores(g, carry):
        label = jnp.full((1, wide), -1, jnp.int32)
        for j in range(PAGES_STEP):
            label = jnp.where(lanes == j, labels[g * PAGES_STEP + j], label)
        keys = cache[pl.ds(pl.multiple_of(g * wide, wide), wide), :HEAD_DIM]
        masked = masked_scores(keys, row_segment == label)
        scores[:, pl.ds(pl.multiple_of(fresh_rows + g * wide, PAGE), wide)] = masked
        total_ref[...] = jnp.maximum(total_ref[...], fold(masked, jnp.maximum))
        return carry

    lax.fori_loop(0, steps, add_scores, 0)
    top = jnp.max(total_ref[...], axis=1, keepdims=True) * factor
    probs = jnp.exp2(scores[:, :fresh_rows] * factor - top)
    total_ref[...] = fold(probs, jnp.add)
    mixed_ref[...] = jnp.dot(probs.astype(BF16), new[:, HEAD_DIM:], preferred_element_type=F32)

    def add_values(g, carry):
        part = scores[:, pl.ds(pl.multiple_of(fresh_rows + g * wide, PAGE), wide)]
        probs = jnp.exp2(part * factor - top)
        values = cache[pl.ds(pl.multiple_of(g * wide, wide), wide), HEAD_DIM:]
        total_ref[...] += fold(probs, jnp.add)
        mixed_ref[...] += jnp.dot(probs.astype(BF16), values, preferred_element_type=F32)
        return carry

    lax.fori_loop(0, steps, add_values, 0)
    denominator = jnp.sum(total_ref[...], axis=1, keepdims=True)
    result = (mixed_ref[...] / denominator).astype(BF16)
    return jnp.concatenate(
        [result[h * block_rows : (h + 1) * block_rows] for h in range(heads)], axis=1
    )


def project_far(place, near, far, w_query, w_keyvalue, after):
    rows, half = near.shape
    q_width, kv_width = w_query.shape[1], w_keyvalue.shape[1]
    steps = 8
    depth = 2 * half // steps

    def kernel(place_ref, near_ref, far_ref, wq, wkv, *refs):
        q_ref, kv_ref, wq_buf, wkv_buf, sems = refs[len(after) :]
        stream = weight_stream(place_ref[1], half, steps, (wq, wkv), (wq_buf, wkv_buf), sems)
        for j in range(steps):
            for copy in stream(j):
                copy.start()
        q_sum = kv_sum = None
        for j in range(steps):
            for copy in stream(j):
                copy.wait()
            x_ref = near_ref if j < steps // 2 else far_ref
            x = x_ref[:, (j % (steps // 2)) * depth : (j % (steps // 2) + 1) * depth]
            q_part = jnp.dot(x, wq_buf[j], preferred_element_type=F32)
            kv_part = jnp.dot(x, wkv_buf[j], preferred_element_type=F32)
            q_sum = q_part if j == 0 else q_sum + q_part
            kv_sum = kv_part if j == 0 else kv_sum + kv_part
        q_ref[...] = q_sum.astype(BF16)
        kv_ref[...] = kv_sum.astype(BF16)

    return pl.pallas_call(
        kernel,
        in_specs=[SMEM] + [VMEM] * 2 + [ANY] * (2 + len(after)),
        out_specs=[VMEM] * 2,
        out_shape=[shape((rows, q_width)), shape((rows, kv_width))],
        scratch_shapes=[
            pltpu.VMEM((steps, depth, q_width), BF16),
            pltpu.VMEM((steps, depth, kv_width), BF16),
            pltpu.SemaphoreType.DMA((2 * steps,)),
        ],
        compiler_params=params(32),
        cost_estimate=SMALL,
        name="project_far",
    )(place, near, far, w_query, w_keyvalue, *after)


def attend_out(place, sizes, requests, query, fresh, bases, base, pulled, w_out):
    rows, depth = query.shape
    width = w_out.shape[1]
    half = width // 2
    heads = depth // HEAD_DIM
    out_steps = 4
    wide = half // out_steps
    known = len(fresh)
    count = sum(f.shape[0] for f in fresh)
    fresh_rows = -(-count // HEAD_DIM) * HEAD_DIM
    pad = fresh_rows - count

    def kernel(place_ref, sizes_ref, req_ref, q_ref, pulled_ref, *refs):
        fresh_refs = refs[:known]
        wo, there_ref, stay_ref, wo_buf, sems = refs[known : known + 5]
        core, side = place_ref[1], place_ref[2]

        def copy(j):
            first = 1 - core if j < out_steps else core
            start = pl.multiple_of(first * half + (j % out_steps) * wide, wide)
            return pltpu.make_async_copy(wo.at[:, pl.ds(start, wide)], wo_buf.at[j], sems.at[j])

        for j in range(2 * out_steps):
            copy(j).start()
        pairs = [(ref[...], at(side)) for ref, at in zip(fresh_refs, bases)]
        if pad:
            pairs.append((jnp.zeros((pad, 2 * HEAD_DIM), BF16), jnp.int32(1 << 20)))
        mixed = attend_block(
            place_ref, sizes_ref, req_ref, q_ref[...], base(side), pairs, pulled_ref,
            refs[known + 5 :],
        )
        for j in range(2 * out_steps):
            copy(j).wait()
            out_ref = there_ref if j < out_steps else stay_ref
            at = (j % out_steps) * wide
            out_ref[:, at : at + wide] = jnp.dot(
                mixed, wo_buf[j], preferred_element_type=F32
            ).astype(BF16)

    return pl.pallas_call(
        kernel,
        in_specs=[SMEM] * 3 + [VMEM] * (2 + known) + [ANY],
        out_specs=[VMEM] * 2,
        out_shape=[shape((rows, half)), shape((rows, half))],
        scratch_shapes=[
            pltpu.VMEM((2 * out_steps, depth, wide), BF16),
            pltpu.SemaphoreType.DMA((2 * out_steps,)),
        ]
        + attention_scratch(rows, heads, fresh_rows, pulled.shape[0] * pulled.shape[1]),
        compiler_params=params(36),
        cost_estimate=SMALL,
        name="attend_out",
    )(place, sizes, requests, query, pulled, *fresh, w_out)


def local_rows(place, sizes, requests, query, fresh, bases, base, pulled, w_out, after):
    both, depth = query.shape
    rows = both // 2
    width = w_out.shape[1]
    heads = depth // HEAD_DIM
    steps = 8
    wide = width // steps
    known = len(fresh)
    fresh_rows = sum(f.shape[0] for f in fresh)

    def kernel(place_ref, sizes_ref, req_ref, q_ref, pulled_ref, *refs):
        fresh_refs = refs[:known]
        wo = refs[known]
        rest = refs[known + 1 + len(after) :]
        own_ref, peer_ref, wo_buf, a_buf, sems = rest[:5]
        core, side = place_ref[1], place_ref[2]

        def out_copy(j):
            return pltpu.make_async_copy(
                wo.at[:, j * wide : (j + 1) * wide], wo_buf.at[j], sems.at[j]
            )

        for j in range(steps):
            out_copy(j).start()

        def block(b, carry):
            at = pl.ds(pl.multiple_of(b * rows, rows), rows)
            a_buf[at, :] = attend_block(
                place_ref,
                sizes_ref,
                req_ref,
                q_ref[at, :],
                base(side) + b * rows,
                [(ref[...], first(side)) for ref, first in zip(fresh_refs, bases)],
                pulled_ref,
                rest[5:],
            )
            return carry

        lax.fori_loop(0, 2, block, 0)
        own_at = pl.ds(pl.multiple_of(core * rows, rows), rows)
        peer_at = pl.ds(pl.multiple_of((1 - core) * rows, rows), rows)
        a = jnp.concatenate([a_buf[own_at, :], a_buf[peer_at, :]], axis=0)
        for j in range(steps):
            out_copy(j).wait()
            part = jnp.dot(a, wo_buf[j], preferred_element_type=F32).astype(BF16)
            own_ref[:, j * wide : (j + 1) * wide] = part[:rows]
            peer_ref[:, j * wide : (j + 1) * wide] = part[rows:]

    return pl.pallas_call(
        kernel,
        in_specs=[SMEM] * 3 + [VMEM] * (2 + known) + [ANY] * (1 + len(after)),
        out_specs=[VMEM, VMEM],
        out_shape=[shape((rows, width)), shape((rows, width))],
        scratch_shapes=[
            pltpu.VMEM((steps, depth, wide), BF16),
            pltpu.VMEM((both, depth), BF16),
            pltpu.SemaphoreType.DMA((steps,)),
        ]
        + attention_scratch(rows, heads, fresh_rows, pulled.shape[0] * pulled.shape[1]),
        compiler_params=params(40),
        cost_estimate=SMALL,
        name="local_rows",
    )(place, sizes, requests, query, pulled, *fresh, w_out, *after)


def add_pair(left, right):
    rows, width = left.shape
    step = 16

    def kernel(left_ref, right_ref, out_ref):
        def block(i, carry):
            at = pl.ds(pl.multiple_of(i * step, step), step)
            out_ref[at, :] = (left_ref[at, :].astype(F32) + right_ref[at, :].astype(F32)).astype(
                BF16
            )
            return carry

        lax.fori_loop(0, rows // step, block, 0)

    return pl.pallas_call(
        kernel,
        in_specs=[VMEM, VMEM],
        out_specs=VMEM,
        out_shape=shape((rows, width)),
        compiler_params=params(8),
        cost_estimate=SMALL,
        name="add_pair",
    )(left, right)


def finish(place, tokens, own, peer, near, far):
    rows, width = tokens.shape
    half = width // 2
    step = 16

    def kernel(place_ref, x_ref, own_ref, peer_ref, near_ref, far_ref, out_ref):
        core = place_ref[1]

        def block(i, carry):
            at = pl.ds(pl.multiple_of(i * step, step), step)
            for start, part in ((core, near_ref), (1 - core, far_ref)):
                cols = pl.ds(pl.multiple_of(start * half, half), half)
                local = own_ref[at, cols].astype(F32) + peer_ref[at, cols].astype(F32)
                total = local + part[at, :].astype(F32)
                out_ref[at, cols] = (x_ref[at, cols].astype(F32) + total).astype(BF16)
            return carry

        lax.fori_loop(0, rows // step, block, 0)

    return pl.pallas_call(
        kernel,
        in_specs=[SMEM] + [VMEM] * 5,
        out_specs=VMEM,
        out_shape=shape((rows, width)),
        compiler_params=params(16),
        cost_estimate=SMALL,
        name="finish",
    )(place, tokens, own, peer, near, far)


def pick_pages(place, wanted, own, core_pages, y_pages, after):
    replicas, tensors, slots = wanted.shape
    _, page, width = own.shape
    total = tensors * slots

    def kernel(place_ref, want_ref, own_ref, core_ref, y_ref, *refs):
        out_ref, sems = refs[len(after) :]
        me = place_ref[0]
        sources = (own_ref, core_ref.at[0], y_ref.at[0], core_ref.at[1])

        def copies():
            for r in range(replicas):
                for i in range(tensors):
                    for s in range(slots):
                        at = i * slots + s
                        yield pltpu.make_async_copy(
                            sources[i].at[want_ref[r, jnp.bitwise_xor(me, i), s]],
                            out_ref.at[r, at],
                            sems.at[r * total + at],
                        )

        for copy in copies():
            copy.start()
        for copy in copies():
            copy.wait()

    return pl.pallas_call(
        kernel,
        in_specs=[SMEM, SMEM] + [ANY] * (3 + len(after)),
        out_specs=ANY,
        out_shape=shape((replicas, total, page, width)),
        scratch_shapes=[pltpu.SemaphoreType.DMA((replicas * total,))],
        compiler_params=params(8),
        cost_estimate=SMALL,
        name="pick_pages",
    )(place, wanted, own, core_pages, y_pages, *after)


def write_pool(place, slots, kv_pool, own, core_new, y_new):
    pages, heads = kv_pool.shape[:2]
    new_count = slots.shape[1]
    side_pages = new_count // 2

    def kernel(place_ref, slot_ref, pool_ref, own_ref, core_ref, y_ref, out_ref, sems):
        me, side = place_ref[0], place_ref[2]
        sources = (own_ref, core_ref.at[0], y_ref, core_ref.at[1])
        for p in range(pages):
            found = jnp.int32(-1)
            for j in range(new_count):
                found = jnp.where(slot_ref[0, j] == me * pages + p, j, found)
            far = (found >= side_pages).astype(jnp.int32)
            inner = jnp.maximum(found - far * side_pages, 0)

            @pl.when(found >= 0)
            def _():
                for i in range(heads):
                    origin = side if i < 2 else 1 - side
                    start = (jnp.bitwise_xor(far, origin) * side_pages + inner) * PAGE
                    pltpu.make_async_copy(
                        sources[i].at[pl.ds(pl.multiple_of(start, PAGE), PAGE)],
                        out_ref.at[p, jnp.bitwise_xor(me, i)],
                        sems.at[p * heads + i],
                    ).start()

            @pl.when(found < 0)
            def _():
                for i in range(heads):
                    at = jnp.bitwise_xor(me, i)
                    pltpu.make_async_copy(
                        pool_ref.at[p, at], out_ref.at[p, at], sems.at[p * heads + i]
                    ).start()

        for p in range(pages):
            for i in range(heads):
                at = jnp.bitwise_xor(me, i)
                pltpu.make_async_copy(
                    pool_ref.at[p, at], out_ref.at[p, at], sems.at[p * heads + i]
                ).wait()

    return pl.pallas_call(
        kernel,
        in_specs=[SMEM, SMEM] + [ANY] * 4,
        out_specs=ANY,
        out_shape=shape(kv_pool.shape),
        scratch_shapes=[pltpu.SemaphoreType.DMA((pages * heads,))],
        compiler_params=params(8),
        cost_estimate=SMALL,
        name="write_pool",
    )(place, slots, kv_pool, own, core_new, y_new)


def chip_pair_body(
    tokens,
    gain,
    w_query,
    w_keyvalue,
    w_out,
    kv_pool,
    suffix_pages,
    page_index,
    page_request,
    new_slot,
):
    replicas = lax.axis_size("replica")
    me = lax.axis_index("tensor")
    core = me % 2
    side = me // 2
    rows = tokens.shape[0]
    place = jnp.stack([me, core, side]).astype(jnp.int32)

    def over_core(x):
        return lax.ppermute(x, "tensor", [(0, 1), (1, 0), (2, 3), (3, 2)])

    def over_y(x):
        return lax.ppermute(x, "tensor", [(0, 2), (2, 0), (1, 3), (3, 1)])

    def head_of(i):
        return lax.dynamic_index_in_dim(kv_pool, jnp.bitwise_xor(me, i), 1, keepdims=False)

    def to_replicas(x):
        return lax.all_to_all(x, "replica", split_axis=0, concat_axis=0, tiled=True)

    def tie(x, *others):
        return lax.optimization_barrier((x, *others))[0]

    wanted = to_replicas(page_index.reshape(replicas, -1, page_index.shape[2]))
    y_pages = over_y(jnp.stack([head_of(2), head_of(3)]))
    core_pages = over_core(jnp.stack([head_of(1), y_pages[1]]))

    mine, other = norm_rows(place, tokens, gain)
    peer_near = over_core(other)
    peer_far = over_core(mine)
    is_first = core == 0
    near_tied = tie(peer_near, y_pages)
    first_half = jnp.where(is_first, mine, near_tied)
    second_half = jnp.where(is_first, near_tied, mine)
    first = over_y(first_half)
    second = over_y(second_half)

    picked = pick_pages(
        place, wanted, head_of(0), core_pages, y_pages, [first_half, second_half]
    )
    pulled = to_replicas(picked)

    q_local, kv_local = project_local(
        place, [mine, peer_near], [other, peer_far], w_query, w_keyvalue, [picked]
    )

    def local_base(s):
        return s * (2 * rows)

    def first_base(s):
        return (1 - s) * (2 * rows)

    def second_base(s):
        return (1 - s) * (2 * rows) + rows

    first = tie(first, q_local)
    q_first, kv_first = project_far(place, first, over_core(first), w_query, w_keyvalue, [])
    there, stay = attend_out(
        place, suffix_pages, page_request, q_first, [kv_local, kv_first],
        [local_base, first_base], first_base, pulled, w_out,
    )
    there = tie(there, second)
    first_mix = add_pair(stay, over_core(there))
    first_sum = over_y(first_mix)

    second = tie(second, first_mix)
    q_second, kv_second = project_far(place, second, over_core(second), w_query, w_keyvalue, [])
    fresh = [kv_local, kv_first, kv_second]
    bases = [local_base, first_base, second_base]
    there, stay = attend_out(
        place, suffix_pages, page_request, q_second, fresh, bases, second_base, pulled, w_out
    )
    there = tie(there, first_sum)
    second_mix = add_pair(stay, over_core(there))


    new_own = jnp.concatenate(fresh, axis=0)
    y_new = over_y(new_own)
    core_new = over_core(jnp.stack([new_own, y_new]))
    second_sum = over_y(tie(second_mix, y_new))

    own_part, peer_part = local_rows(
        place, suffix_pages, page_request, q_local, fresh, bases, local_base, pulled, w_out,
        [second_mix],
    )
    peer_part = over_core(peer_part)
    pool_out = write_pool(place, new_slot, kv_pool, new_own, core_new, y_new)

    near = jnp.where(is_first, first_sum, second_sum)
    far = over_core(jnp.where(is_first, second_sum, first_sum))
    layer_out = finish(place, tokens, own_part, peer_part, near, far)
    return (layer_out, pool_out)


def solution(mesh):
    pair = mesh.shape["tensor"] == KV_HEADS
    return jax.shard_map(
        chip_pair_body if pair else gathered_body,
        mesh=mesh,
        in_specs=(
            P(("groups", "replica", "tensor"), None),
            P(),
            P(None, "tensor"),
            P(None, "tensor"),
            P("tensor", None),
            P(("groups", "replica", "tensor"), None, None, None),
            P(("groups", "replica"), None),
            P(("groups", "replica"), None, None),
            P(("groups", "replica"), None, None),
            P(("groups", "replica"), None),
        ),
        out_specs=(
            P(("groups", "replica", "tensor"), None),
            P(("groups", "replica", "tensor"), None, None, None),
        ),
        check_vma=False,
    )
```

```python
import math

import jax
import jax.numpy as jnp
from jax import lax
from jax.experimental import pallas as pl
from jax.experimental.pallas import tpu as pltpu
from jax.sharding import PartitionSpec as P

KV_HEADS = 4
HEAD_DIM = 128
PAGE = 64
UNIT = 8


NEG_FILL = -1e30
EPSILON = 1e-06

F32 = jnp.float32
BF16 = jnp.bfloat16
MIB = 1 << 20
ANY = pl.BlockSpec(memory_space=pl.ANY)
HBM = pl.BlockSpec(memory_space=pltpu.HBM)
SMEM = pl.BlockSpec(memory_space=pltpu.SMEM)
VMEM = pl.BlockSpec(memory_space=pltpu.VMEM)
SMALL = pl.CostEstimate(flops=1024, bytes_accessed=1024, transcendentals=0)


def params(mib):
    return pltpu.CompilerParams(vmem_limit_bytes=mib * MIB)


def shape(dims, dtype=BF16):
    return jax.ShapeDtypeStruct(dims, dtype)


def normalize(rows, gain):
    values = rows.astype(jnp.float32)
    inverse = lax.rsqrt(jnp.mean(values * values, axis=-1, keepdims=True) + EPSILON)
    return (values * inverse * gain.astype(jnp.float32)).astype(jnp.bfloat16)


def row_segments(pages, total_rows):
    bounds = jnp.cumsum(pages) * UNIT
    positions = jnp.arange(total_rows, dtype=jnp.int32)
    return jnp.sum((positions[:, None] >= bounds[None, :]).astype(jnp.int32), axis=1)


def gathered_body(
    tokens,
    gain,
    w_query,
    w_keyvalue,
    w_out,
    kv_pool,
    suffix_pages,
    page_index,
    page_request,
    new_slot,
):
    replicas = lax.axis_size("replica")
    tensors = lax.axis_size("tensor")
    owners = replicas * tensors
    position = lax.axis_index("tensor")
    query_width = w_query.shape[1]
    local_heads = query_width // HEAD_DIM
    share = tensors // KV_HEADS
    my_head = position // share
    scale_factor = 1.0 / math.sqrt(HEAD_DIM)
    normed = normalize(tokens, gain)
    piece = lax.all_gather(normed, "tensor", axis=0, tiled=True)
    first = jnp.dot(piece, w_query, preferred_element_type=jnp.float32)
    second = jnp.dot(piece, w_keyvalue, preferred_element_type=jnp.float32)
    projected = jnp.concatenate([first, second], axis=1).astype(jnp.bfloat16)
    query = projected[:, :query_width]
    keyvalue = lax.all_gather(projected[:, query_width:], "tensor", axis=1, tiled=True)
    total_rows = query.shape[0]
    wanted = lax.all_to_all(
        page_index[0], ("replica", "tensor"), split_axis=0, concat_axis=0, tiled=True
    )
    slot_count = wanted.shape[1]
    sources = jnp.arange(owners, dtype=jnp.int32) % tensors
    source_heads = sources // share
    flat_pool = kv_pool.reshape(kv_pool.shape[0] * KV_HEADS, PAGE, 2 * HEAD_DIM)
    outgoing = flat_pool[wanted * KV_HEADS + source_heads[:, None]]
    sub_tokens = outgoing.shape[2]
    pulled = lax.all_to_all(
        outgoing, ("replica", "tensor"), split_axis=0, concat_axis=0, tiled=True
    )
    segments = row_segments(suffix_pages[0], total_rows)
    key_groups = page_request[0]
    stacked = (
        query.reshape(total_rows, local_heads, HEAD_DIM)
        .transpose(1, 0, 2)
        .reshape(local_heads * total_rows, HEAD_DIM)
    )
    own_new = lax.dynamic_index_in_dim(
        keyvalue.reshape(total_rows, KV_HEADS, 2 * HEAD_DIM), my_head, 1, keepdims=False
    )
    row_order = jnp.arange(total_rows, dtype=jnp.int32)
    causal = (segments[:, None] == segments[None, :]) & (row_order[None, :] <= row_order[:, None])

    def block_scores(queries, head_count, keys, allowed):
        raw = (
            jnp.dot(queries, keys[:, :HEAD_DIM].T, preferred_element_type=jnp.float32)
            * scale_factor
        )
        raw = raw.reshape(head_count, total_rows, keys.shape[0])
        return jnp.where(allowed[None], raw, NEG_FILL)

    first_scores = block_scores(stacked, local_heads, own_new, causal)
    running = jnp.max(first_scores, axis=2)
    probs = jnp.exp(first_scores - running[:, :, None])
    denominator = jnp.sum(probs, axis=2)
    numerator = jnp.dot(
        probs.astype(jnp.bfloat16).reshape(local_heads * total_rows, total_rows),
        own_new[:, HEAD_DIM:],
        preferred_element_type=jnp.float32,
    )
    block_owners = 16
    blocks = owners // block_owners

    def absorb(step, state):
        peak, total, mixed = state
        pages = lax.dynamic_slice_in_dim(pulled, step * block_owners, block_owners, 0)
        keys = pages.reshape(block_owners * slot_count * sub_tokens, 2 * HEAD_DIM)
        labels = lax.dynamic_slice_in_dim(key_groups, step * block_owners, block_owners, 0).reshape(
            -1
        )
        matches = (segments[:, None] == labels[None, :])[:, :, None]
        allowed = jnp.broadcast_to(matches, (total_rows, labels.shape[0], sub_tokens)).reshape(
            total_rows, labels.shape[0] * sub_tokens
        )
        scores = block_scores(stacked, local_heads, keys, allowed)
        updated = jnp.maximum(peak, jnp.max(scores, axis=2))
        rescale = jnp.exp(peak - updated)
        weights = jnp.where(allowed[None], jnp.exp(scores - updated[:, :, None]), 0.0)
        total = total * rescale + jnp.sum(weights, axis=2)
        flat_weights = weights.astype(jnp.bfloat16).reshape(local_heads * total_rows, keys.shape[0])
        mixed = mixed * rescale.reshape(-1)[:, None] + jnp.dot(
            flat_weights, keys[:, HEAD_DIM:], preferred_element_type=jnp.float32
        )
        return (updated, total, mixed)

    running, denominator, numerator = lax.fori_loop(
        0, blocks, absorb, (running, denominator, numerator)
    )
    attention = (numerator / denominator.reshape(-1)[:, None]).astype(jnp.bfloat16)
    attention = (
        attention.reshape(local_heads, total_rows, HEAD_DIM)
        .transpose(1, 0, 2)
        .reshape(total_rows, query_width)
    )
    summed = lax.psum_scatter(
        jnp.dot(attention, w_out, preferred_element_type=jnp.float32).astype(jnp.bfloat16),
        "tensor",
        scatter_dimension=0,
        tiled=True,
    ).astype(jnp.float32)
    layer_out = (tokens.astype(jnp.float32) + summed).astype(jnp.bfloat16)
    new_count = total_rows // PAGE
    fresh = (
        keyvalue.reshape(new_count, PAGE, KV_HEADS, 2 * HEAD_DIM)
        .transpose(0, 2, 1, 3)
        .reshape(new_count, KV_HEADS * PAGE * 2 * HEAD_DIM)
    )
    local_pages = kv_pool.shape[0]
    targets = position * local_pages + jnp.arange(local_pages, dtype=jnp.int32)
    match_table = new_slot[0][None, :] == targets[:, None]
    placed = jnp.dot(
        match_table.astype(jnp.bfloat16), fresh, preferred_element_type=jnp.float32
    ).astype(jnp.bfloat16)
    placed = placed.reshape(kv_pool.shape)
    landed = jnp.any(match_table, axis=1)
    pool_out = jnp.where(landed[:, None, None, None], placed, kv_pool)
    return (layer_out, pool_out)


def norm_rows(place, tokens, gain):
    rows, width = tokens.shape
    half = width // 2
    step = 16

    def kernel(place_ref, x_ref, g_ref, mine_ref, other_ref):
        core = place_ref[1]
        near = pl.multiple_of(core * half, half)
        far = pl.multiple_of((1 - core) * half, half)

        def block(i, carry):
            at = pl.ds(pl.multiple_of(i * step, step), step)
            total = jnp.zeros((step, 1), F32)
            for part in range(2):
                values = x_ref[at, part * half : (part + 1) * half].astype(F32)
                total += jnp.sum(values * values, axis=1, keepdims=True)
            inverse = lax.rsqrt(total * (1.0 / width) + EPSILON)
            for start, out in ((near, mine_ref), (far, other_ref)):
                cols = pl.ds(start, half)
                values = x_ref[at, cols].astype(F32)
                out[at, :] = (values * inverse * g_ref[cols].astype(F32)[None, :]).astype(BF16)
            return carry

        lax.fori_loop(0, rows // step, block, 0)

    return pl.pallas_call(
        kernel,
        in_specs=[SMEM, VMEM, VMEM],
        out_specs=[VMEM, VMEM],
        out_shape=[shape((rows, half)), shape((rows, half))],
        compiler_params=params(16),
        cost_estimate=SMALL,
        name="norm_rows",
    )(place, tokens, gain)


def project_local(place, near, far, w_query, w_keyvalue, after):
    rows, half = near[0].shape
    q_width, kv_width = w_query.shape[1], w_keyvalue.shape[1]
    steps = 8
    depth = 2 * half // steps
    waits = len(after)

    def kernel(place_ref, near_own, near_peer, far_own, far_peer, wq, wkv, *refs):
        q_ref, kv_ref, wq_buf, wkv_buf, q_acc, kv_acc, sems = refs[waits:]
        core = place_ref[1]
        stream = weight_stream(core, half, steps, (wq, wkv), (wq_buf, wkv_buf), sems)
        for j in range(steps):
            for copy in stream(j):
                copy.start()
        for j in range(steps):
            for copy in stream(j):
                copy.wait()
            group = (near_own, near_peer) if j < steps // 2 else (far_own, far_peer)
            cols = slice((j % (steps // 2)) * depth, (j % (steps // 2) + 1) * depth)
            x = jnp.concatenate([ref[:, cols] for ref in group], axis=0)
            q_part = jnp.dot(x, wq_buf[j], preferred_element_type=F32)
            kv_part = jnp.dot(x, wkv_buf[j], preferred_element_type=F32)
            if j == 0:
                q_acc[...] = q_part
                kv_acc[...] = kv_part
            elif j < steps - 1:
                q_acc[...] += q_part
                kv_acc[...] += kv_part
            else:
                q_last = (q_acc[...] + q_part).astype(BF16)
                kv_last = (kv_acc[...] + kv_part).astype(BF16)
        for b in range(2):
            at = pl.ds(pl.multiple_of((core if b == 0 else 1 - core) * rows, rows), rows)
            q_ref[at, :] = q_last[b * rows : (b + 1) * rows]
            kv_ref[at, :] = kv_last[b * rows : (b + 1) * rows]

    total = 2 * rows
    return pl.pallas_call(
        kernel,
        in_specs=[SMEM] + [VMEM] * 4 + [HBM] * 2 + [ANY] * waits,
        out_specs=[VMEM, VMEM],
        out_shape=[shape((total, q_width)), shape((total, kv_width))],
        scratch_shapes=[
            pltpu.VMEM((steps, depth, q_width), BF16),
            pltpu.VMEM((steps, depth, kv_width), BF16),
            pltpu.VMEM((total, q_width), F32),
            pltpu.VMEM((total, kv_width), F32),
            pltpu.SemaphoreType.DMA((2 * steps,)),
        ],
        compiler_params=params(36),
        cost_estimate=SMALL,
        name="project_local",
    )(place, *near, *far, w_query, w_keyvalue, *after)


def weight_stream(core, half, steps, sources, buffers, sems):
    depth = 2 * half // steps

    def copies(j):
        base = core if j < steps // 2 else 1 - core
        start = pl.multiple_of(base * half + (j % (steps // 2)) * depth, depth)
        count = len(sources)
        return [
            pltpu.make_async_copy(w.at[pl.ds(start, depth)], buf.at[j], sems.at[count * j + i])
            for i, (w, buf) in enumerate(zip(sources, buffers))
        ]

    return copies


PAGES_STEP = 4


def attention_scratch(block_rows, heads, fresh_rows, slots):
    stacked = heads * block_rows
    return [
        pltpu.VMEM((stacked, fresh_rows + slots * PAGE), F32),
        pltpu.VMEM((stacked, HEAD_DIM), F32),
        pltpu.VMEM((stacked, HEAD_DIM), F32),
        pltpu.VMEM((slots * PAGE, 2 * HEAD_DIM), BF16),
        pltpu.SMEM((slots,), jnp.int32),
    ]


def attend_block(place_ref, sizes_ref, req_ref, q, first_row, fresh, pulled, scratch):
    scores, total_ref, mixed_ref, cache, labels = scratch
    me = place_ref[0]
    block_rows, width = q.shape
    heads = width // HEAD_DIM
    stacked = heads * block_rows
    groups, per = pulled.shape[:2]
    tensors = 4
    slots = per // tensors
    wide = PAGES_STEP * PAGE
    factor = math.log2(math.e) / math.sqrt(HEAD_DIM)
    bound = []
    running = jnp.int32(0)
    for k in range(sizes_ref.shape[1]):
        running = running + sizes_ref[0, k] * UNIT
        bound.append(running)

    def segment_of(position):
        return sum((position >= b).astype(jnp.int32) for b in bound)

    lowest = segment_of(first_row)
    highest = segment_of(first_row + block_rows - 1)
    count = jnp.int32(0)
    for g in range(groups):
        for p in range(per):
            owner = g * tensors + jnp.bitwise_xor(me, p // slots)
            label = req_ref[0, p % slots, owner]
            wanted = (label >= lowest) & (label <= highest)

            @pl.when(wanted)
            def _():
                cache[pl.ds(pl.multiple_of(count * PAGE, PAGE), PAGE), :] = pulled[g, p]
                labels[count] = label

            count = count + wanted.astype(jnp.int32)
    steps = (count + PAGES_STEP - 1) // PAGES_STEP
    for k in range(PAGES_STEP - 1):

        @pl.when(count + k < steps * PAGES_STEP)
        def _():
            cache[pl.ds(pl.multiple_of((count + k) * PAGE, PAGE), PAGE), :] = jnp.zeros(
                (PAGE, 2 * HEAD_DIM), BF16
            )
            labels[count + k] = jnp.int32(-1)

    q_rows = jnp.concatenate([q[:, h * HEAD_DIM : (h + 1) * HEAD_DIM] for h in range(heads)], axis=0)
    row_position = first_row + lax.broadcasted_iota(jnp.int32, (block_rows, 1), 0)
    row_segment = segment_of(row_position)

    def masked_scores(keys, allowed):
        raw = lax.dot_general(q_rows, keys, (((1,), (1,)), ((), ())), preferred_element_type=F32)
        n = keys.shape[0]
        return jnp.where(allowed[None], raw.reshape(heads, block_rows, n), NEG_FILL).reshape(
            stacked, n
        )

    def fold(values, combine):
        pieces = [values[:, i : i + HEAD_DIM] for i in range(0, values.shape[1], HEAD_DIM)]
        result = pieces[0]
        for piece in pieces[1:]:
            result = combine(result, piece)
        return result

    new = jnp.concatenate([rows for rows, _ in fresh], axis=0)
    fresh_rows = new.shape[0]
    key_position = jnp.concatenate(
        [
            base + lax.broadcasted_iota(jnp.int32, (1, rows.shape[0]), 1)
            for rows, base in fresh
        ],
        axis=1,
    )
    allowed = (row_segment == segment_of(key_position)) & (key_position <= row_position)
    masked = masked_scores(new[:, :HEAD_DIM], allowed)
    scores[:, :fresh_rows] = masked
    total_ref[...] = fold(masked, jnp.maximum)
    lanes = lax.broadcasted_iota(jnp.int32, (1, wide), 1) // PAGE

    def add_scores(g, carry):
        label = jnp.full((1, wide), -1, jnp.int32)
        for j in range(PAGES_STEP):
            label = jnp.where(lanes == j, labels[g * PAGES_STEP + j], label)
        keys = cache[pl.ds(pl.multiple_of(g * wide, wide), wide), :HEAD_DIM]
        masked = masked_scores(keys, row_segment == label)
        scores[:, pl.ds(pl.multiple_of(fresh_rows + g * wide, PAGE), wide)] = masked
        total_ref[...] = jnp.maximum(total_ref[...], fold(masked, jnp.maximum))
        return carry

    lax.fori_loop(0, steps, add_scores, 0)
    top = jnp.max(total_ref[...], axis=1, keepdims=True) * factor
    probs = jnp.exp2(scores[:, :fresh_rows] * factor - top)
    total_ref[...] = fold(probs, jnp.add)
    mixed_ref[...] = jnp.dot(probs.astype(BF16), new[:, HEAD_DIM:], preferred_element_type=F32)

    def add_values(g, carry):
        part = scores[:, pl.ds(pl.multiple_of(fresh_rows + g * wide, PAGE), wide)]
        probs = jnp.exp2(part * factor - top)
        values = cache[pl.ds(pl.multiple_of(g * wide, wide), wide), HEAD_DIM:]
        total_ref[...] += fold(probs, jnp.add)
        mixed_ref[...] += jnp.dot(probs.astype(BF16), values, preferred_element_type=F32)
        return carry

    lax.fori_loop(0, steps, add_values, 0)
    denominator = jnp.sum(total_ref[...], axis=1, keepdims=True)
    result = (mixed_ref[...] / denominator).astype(BF16)
    return jnp.concatenate(
        [result[h * block_rows : (h + 1) * block_rows] for h in range(heads)], axis=1
    )


def project_far(place, near, far, w_query, w_keyvalue, after):
    rows, half = near.shape
    q_width, kv_width = w_query.shape[1], w_keyvalue.shape[1]
    steps = 8
    depth = 2 * half // steps

    def kernel(place_ref, near_ref, far_ref, wq, wkv, *refs):
        q_ref, kv_ref, wq_buf, wkv_buf, sems = refs[len(after) :]
        stream = weight_stream(place_ref[1], half, steps, (wq, wkv), (wq_buf, wkv_buf), sems)
        for j in range(steps):
            for copy in stream(j):
                copy.start()
        q_sum = kv_sum = None
        for j in range(steps):
            for copy in stream(j):
                copy.wait()
            x_ref = near_ref if j < steps // 2 else far_ref
            x = x_ref[:, (j % (steps // 2)) * depth : (j % (steps // 2) + 1) * depth]
            q_part = jnp.dot(x, wq_buf[j], preferred_element_type=F32)
            kv_part = jnp.dot(x, wkv_buf[j], preferred_element_type=F32)
            q_sum = q_part if j == 0 else q_sum + q_part
            kv_sum = kv_part if j == 0 else kv_sum + kv_part
        q_ref[...] = q_sum.astype(BF16)
        kv_ref[...] = kv_sum.astype(BF16)

    return pl.pallas_call(
        kernel,
        in_specs=[SMEM] + [VMEM] * 2 + [HBM] * 2 + [ANY] * len(after),
        out_specs=[VMEM] * 2,
        out_shape=[shape((rows, q_width)), shape((rows, kv_width))],
        scratch_shapes=[
            pltpu.VMEM((steps, depth, q_width), BF16),
            pltpu.VMEM((steps, depth, kv_width), BF16),
            pltpu.SemaphoreType.DMA((2 * steps,)),
        ],
        compiler_params=params(32),
        cost_estimate=SMALL,
        name="project_far",
    )(place, near, far, w_query, w_keyvalue, *after)


def attend_out(place, sizes, requests, query, fresh, bases, base, pulled, w_out):
    rows, depth = query.shape
    width = w_out.shape[1]
    half = width // 2
    heads = depth // HEAD_DIM
    out_steps = 4
    wide = half // out_steps
    known = len(fresh)
    count = sum(f.shape[0] for f in fresh)
    fresh_rows = -(-count // HEAD_DIM) * HEAD_DIM
    pad = fresh_rows - count

    def kernel(place_ref, sizes_ref, req_ref, q_ref, pulled_ref, *refs):
        fresh_refs = refs[:known]
        wo, there_ref, stay_ref, wo_buf, sems = refs[known : known + 5]
        core, side = place_ref[1], place_ref[2]

        def copy(j):
            first = 1 - core if j < out_steps else core
            start = pl.multiple_of(first * half + (j % out_steps) * wide, wide)
            return pltpu.make_async_copy(wo.at[:, pl.ds(start, wide)], wo_buf.at[j], sems.at[j])

        for j in range(2 * out_steps):
            copy(j).start()
        pairs = [(ref[...], at(side)) for ref, at in zip(fresh_refs, bases)]
        if pad:
            pairs.append((jnp.zeros((pad, 2 * HEAD_DIM), BF16), jnp.int32(1 << 20)))
        mixed = attend_block(
            place_ref, sizes_ref, req_ref, q_ref[...], base(side), pairs, pulled_ref,
            refs[known + 5 :],
        )
        for j in range(2 * out_steps):
            copy(j).wait()
            out_ref = there_ref if j < out_steps else stay_ref
            at = (j % out_steps) * wide
            out_ref[:, at : at + wide] = jnp.dot(
                mixed, wo_buf[j], preferred_element_type=F32
            ).astype(BF16)

    return pl.pallas_call(
        kernel,
        in_specs=[SMEM] * 3 + [VMEM] * (2 + known) + [HBM],
        out_specs=[VMEM] * 2,
        out_shape=[shape((rows, half)), shape((rows, half))],
        scratch_shapes=[
            pltpu.VMEM((2 * out_steps, depth, wide), BF16),
            pltpu.SemaphoreType.DMA((2 * out_steps,)),
        ]
        + attention_scratch(rows, heads, fresh_rows, pulled.shape[0] * pulled.shape[1]),
        compiler_params=params(36),
        cost_estimate=SMALL,
        name="attend_out",
    )(place, sizes, requests, query, pulled, *fresh, w_out)


def local_rows(place, sizes, requests, query, fresh, bases, base, pulled, w_out, after):
    both, depth = query.shape
    rows = both // 2
    width = w_out.shape[1]
    heads = depth // HEAD_DIM
    steps = 8
    wide = width // steps
    known = len(fresh)
    fresh_rows = sum(f.shape[0] for f in fresh)

    def kernel(place_ref, sizes_ref, req_ref, q_ref, pulled_ref, *refs):
        fresh_refs = refs[:known]
        wo = refs[known]
        rest = refs[known + 1 + len(after) :]
        own_ref, peer_ref, wo_buf, a_buf, sems = rest[:5]
        core, side = place_ref[1], place_ref[2]

        def out_copy(j):
            return pltpu.make_async_copy(
                wo.at[:, j * wide : (j + 1) * wide], wo_buf.at[j], sems.at[j]
            )

        for j in range(steps):
            out_copy(j).start()

        def block(b, carry):
            at = pl.ds(pl.multiple_of(b * rows, rows), rows)
            a_buf[at, :] = attend_block(
                place_ref,
                sizes_ref,
                req_ref,
                q_ref[at, :],
                base(side) + b * rows,
                [(ref[...], first(side)) for ref, first in zip(fresh_refs, bases)],
                pulled_ref,
                rest[5:],
            )
            return carry

        lax.fori_loop(0, 2, block, 0)
        own_at = pl.ds(pl.multiple_of(core * rows, rows), rows)
        peer_at = pl.ds(pl.multiple_of((1 - core) * rows, rows), rows)
        a = jnp.concatenate([a_buf[own_at, :], a_buf[peer_at, :]], axis=0)
        for j in range(steps):
            out_copy(j).wait()
            part = jnp.dot(a, wo_buf[j], preferred_element_type=F32).astype(BF16)
            own_ref[:, j * wide : (j + 1) * wide] = part[:rows]
            peer_ref[:, j * wide : (j + 1) * wide] = part[rows:]

    return pl.pallas_call(
        kernel,
        in_specs=[SMEM] * 3 + [VMEM] * (2 + known) + [HBM] + [ANY] * len(after),
        out_specs=[VMEM, VMEM],
        out_shape=[shape((rows, width)), shape((rows, width))],
        scratch_shapes=[
            pltpu.VMEM((steps, depth, wide), BF16),
            pltpu.VMEM((both, depth), BF16),
            pltpu.SemaphoreType.DMA((steps,)),
        ]
        + attention_scratch(rows, heads, fresh_rows, pulled.shape[0] * pulled.shape[1]),
        compiler_params=params(40),
        cost_estimate=SMALL,
        name="local_rows",
    )(place, sizes, requests, query, pulled, *fresh, w_out, *after)


def add_pair(left, right):
    rows, width = left.shape
    step = 16

    def kernel(left_ref, right_ref, out_ref):
        def block(i, carry):
            at = pl.ds(pl.multiple_of(i * step, step), step)
            out_ref[at, :] = (left_ref[at, :].astype(F32) + right_ref[at, :].astype(F32)).astype(
                BF16
            )
            return carry

        lax.fori_loop(0, rows // step, block, 0)

    return pl.pallas_call(
        kernel,
        in_specs=[VMEM, VMEM],
        out_specs=VMEM,
        out_shape=shape((rows, width)),
        compiler_params=params(8),
        cost_estimate=SMALL,
        name="add_pair",
    )(left, right)


def finish(place, tokens, own, peer, near, far):
    rows, width = tokens.shape
    half = width // 2
    step = 16

    def kernel(place_ref, x_ref, own_ref, peer_ref, near_ref, far_ref, out_ref):
        core = place_ref[1]

        def block(i, carry):
            at = pl.ds(pl.multiple_of(i * step, step), step)
            for start, part in ((core, near_ref), (1 - core, far_ref)):
                cols = pl.ds(pl.multiple_of(start * half, half), half)
                local = own_ref[at, cols].astype(F32) + peer_ref[at, cols].astype(F32)
                total = local + part[at, :].astype(F32)
                out_ref[at, cols] = (x_ref[at, cols].astype(F32) + total).astype(BF16)
            return carry

        lax.fori_loop(0, rows // step, block, 0)

    return pl.pallas_call(
        kernel,
        in_specs=[SMEM] + [VMEM] * 5,
        out_specs=VMEM,
        out_shape=shape((rows, width)),
        compiler_params=params(16),
        cost_estimate=SMALL,
        name="finish",
    )(place, tokens, own, peer, near, far)


def pick_pages(place, wanted, held, after):
    replicas, tensors, slots = wanted.shape
    _, page, width = held[0].shape
    total = tensors * slots

    def kernel(place_ref, want_ref, *refs):
        sources = refs[:tensors]
        out_ref, sems = refs[tensors + len(after) :]
        me = place_ref[0]

        def copies():
            for r in range(replicas):
                for i in range(tensors):
                    for s in range(slots):
                        at = i * slots + s
                        yield pltpu.make_async_copy(
                            sources[i].at[want_ref[r, jnp.bitwise_xor(me, i), s]],
                            out_ref.at[r, at],
                            sems.at[r * total + at],
                        )

        for copy in copies():
            copy.start()
        for copy in copies():
            copy.wait()

    return pl.pallas_call(
        kernel,
        in_specs=[SMEM, SMEM] + [ANY] * (tensors + len(after)),
        out_specs=ANY,
        out_shape=shape((replicas, total, page, width)),
        scratch_shapes=[pltpu.SemaphoreType.DMA((replicas * total,))],
        compiler_params=params(8),
        cost_estimate=SMALL,
        name="pick_pages",
    )(place, wanted, *held, *after)


def write_pool(place, slots, kv_pool, own, core_new, y_new):
    pages, heads = kv_pool.shape[:2]
    new_count = slots.shape[1]
    side_pages = new_count // 2

    def kernel(place_ref, slot_ref, pool_ref, own_ref, core_ref, y_ref, out_ref, sems):
        me, side = place_ref[0], place_ref[2]
        sources = (own_ref, core_ref.at[0], y_ref, core_ref.at[1])
        for p in range(pages):
            found = jnp.int32(-1)
            for j in range(new_count):
                found = jnp.where(slot_ref[0, j] == me * pages + p, j, found)
            far = (found >= side_pages).astype(jnp.int32)
            inner = jnp.maximum(found - far * side_pages, 0)

            @pl.when(found >= 0)
            def _():
                for i in range(heads):
                    origin = side if i < 2 else 1 - side
                    start = (jnp.bitwise_xor(far, origin) * side_pages + inner) * PAGE
                    pltpu.make_async_copy(
                        sources[i].at[pl.ds(pl.multiple_of(start, PAGE), PAGE)],
                        out_ref.at[p, jnp.bitwise_xor(me, i)],
                        sems.at[p * heads + i],
                    ).start()

            @pl.when(found < 0)
            def _():
                for i in range(heads):
                    at = jnp.bitwise_xor(me, i)
                    pltpu.make_async_copy(
                        pool_ref.at[p, at], out_ref.at[p, at], sems.at[p * heads + i]
                    ).start()

        for p in range(pages):
            for i in range(heads):
                at = jnp.bitwise_xor(me, i)
                pltpu.make_async_copy(
                    pool_ref.at[p, at], out_ref.at[p, at], sems.at[p * heads + i]
                ).wait()

    return pl.pallas_call(
        kernel,
        in_specs=[SMEM, SMEM] + [ANY] * 4,
        out_specs=ANY,
        out_shape=shape(kv_pool.shape),
        scratch_shapes=[pltpu.SemaphoreType.DMA((pages * heads,))],
        compiler_params=params(8),
        cost_estimate=SMALL,
        name="write_pool",
    )(place, slots, kv_pool, own, core_new, y_new)


def chip_pair_body(
    tokens,
    gain,
    w_query,
    w_keyvalue,
    w_out,
    kv_pool,
    suffix_pages,
    page_index,
    page_request,
    new_slot,
):
    replicas = lax.axis_size("replica")
    me = lax.axis_index("tensor")
    core = me % 2
    side = me // 2
    rows = tokens.shape[0]
    place = jnp.stack([me, core, side]).astype(jnp.int32)

    def over_core(x):
        return lax.ppermute(x, "tensor", [(0, 1), (1, 0), (2, 3), (3, 2)])

    def over_y(x):
        return lax.ppermute(x, "tensor", [(0, 2), (2, 0), (1, 3), (3, 1)])

    def head_of(i):
        return lax.dynamic_index_in_dim(kv_pool, jnp.bitwise_xor(me, i), 1, keepdims=False)

    requests = jnp.swapaxes(page_request, 1, 2)

    def to_replicas(x):
        return lax.all_to_all(x, "replica", split_axis=0, concat_axis=0, tiled=True)

    def tie(x, *others):
        return lax.optimization_barrier((x, *others))[0]

    w_query = pltpu.with_memory_space_constraint(w_query, pltpu.HBM)
    w_keyvalue = pltpu.with_memory_space_constraint(w_keyvalue, pltpu.HBM)
    w_out = pltpu.with_memory_space_constraint(w_out, pltpu.HBM)
    held = [head_of(0)]
    for i in range(1, 4):
        held.append(lax.ppermute(head_of(i), "tensor", [(t, t ^ i) for t in range(4)]))

    mine, other = norm_rows(place, tokens, gain)
    peer_near = over_core(other)
    peer_far = over_core(mine)
    is_first = core == 0
    near_tied = tie(peer_near, held[2], held[3])
    first_half = jnp.where(is_first, mine, near_tied)
    second_half = jnp.where(is_first, near_tied, mine)
    first = over_y(first_half)
    second = over_y(second_half)

    numbers = page_index.reshape(replicas, -1, page_index.shape[2])
    wanted = to_replicas(tie(numbers, first_half))
    picked = pick_pages(place, wanted, held, [first_half, second_half])
    pulled = to_replicas(picked)

    q_local, kv_local = project_local(
        place, [mine, peer_near], [other, peer_far], w_query, w_keyvalue, [picked]
    )

    def local_base(s):
        return s * (2 * rows)

    def first_base(s):
        return (1 - s) * (2 * rows)

    def second_base(s):
        return (1 - s) * (2 * rows) + rows

    first = tie(first, q_local)
    q_first, kv_first = project_far(place, first, over_core(first), w_query, w_keyvalue, [])
    there, stay = attend_out(
        place, suffix_pages, requests, q_first, [kv_local, kv_first],
        [local_base, first_base], first_base, pulled, w_out,
    )
    there = tie(there, second)
    first_mix = add_pair(stay, over_core(there))
    first_sum = over_y(first_mix)

    second = tie(second, first_mix)
    q_second, kv_second = project_far(place, second, over_core(second), w_query, w_keyvalue, [])
    fresh = [kv_local, kv_first, kv_second]
    bases = [local_base, first_base, second_base]
    there, stay = attend_out(
        place, suffix_pages, requests, q_second, fresh, bases, second_base, pulled, w_out
    )
    there = tie(there, first_sum)
    second_mix = add_pair(stay, over_core(there))


    new_own = jnp.concatenate(fresh, axis=0)
    y_new = over_y(new_own)
    core_new = over_core(jnp.stack([new_own, y_new]))
    second_sum = over_y(tie(second_mix, y_new))

    pool_out = write_pool(place, new_slot, kv_pool, new_own, core_new, y_new)

    own_part, peer_part = local_rows(
        place, suffix_pages, requests, q_local, fresh, bases, local_base, pulled, w_out,
        [second_mix, pool_out],
    )
    peer_part = over_core(peer_part)

    near = jnp.where(is_first, first_sum, second_sum)
    far = over_core(jnp.where(is_first, second_sum, first_sum))
    layer_out = finish(place, tokens, own_part, peer_part, near, far)
    return (layer_out, pool_out)


def solution(mesh):
    pair = mesh.shape["tensor"] == KV_HEADS
    return jax.shard_map(
        chip_pair_body if pair else gathered_body,
        mesh=mesh,
        in_specs=(
            P(("groups", "replica", "tensor"), None),
            P(),
            P(None, "tensor"),
            P(None, "tensor"),
            P("tensor", None),
            P(("groups", "replica", "tensor"), None, None, None),
            P(("groups", "replica"), None),
            P(("groups", "replica"), None, None),
            P(("groups", "replica"), None, None),
            P(("groups", "replica"), None),
        ),
        out_specs=(
            P(("groups", "replica", "tensor"), None),
            P(("groups", "replica", "tensor"), None, None, None),
        ),
        check_vma=False,
    )
```

```python
import math

import jax
import jax.numpy as jnp
from jax import lax
from jax.experimental import pallas as pl
from jax.experimental.pallas import tpu as pltpu
from jax.sharding import PartitionSpec as P

KV_HEADS = 4
HEAD_DIM = 128
PAGE = 64
UNIT = 8


NEG_FILL = -1e30
EPSILON = 1e-06

F32 = jnp.float32
BF16 = jnp.bfloat16
MIB = 1 << 20
ANY = pl.BlockSpec(memory_space=pl.ANY)
HBM = pl.BlockSpec(memory_space=pltpu.HBM)
SMEM = pl.BlockSpec(memory_space=pltpu.SMEM)
VMEM = pl.BlockSpec(memory_space=pltpu.VMEM)
SMALL = pl.CostEstimate(flops=1024, bytes_accessed=1024, transcendentals=0)


def params(mib):
    return pltpu.CompilerParams(vmem_limit_bytes=mib * MIB)


def in_hbm(x):
    return pltpu.with_memory_space_constraint(x, pltpu.HBM)


def shape(dims, dtype=BF16):
    return jax.ShapeDtypeStruct(dims, dtype)


def normalize(rows, gain):
    values = rows.astype(jnp.float32)
    inverse = lax.rsqrt(jnp.mean(values * values, axis=-1, keepdims=True) + EPSILON)
    return (values * inverse * gain.astype(jnp.float32)).astype(jnp.bfloat16)


def row_segments(pages, total_rows):
    bounds = jnp.cumsum(pages) * UNIT
    positions = jnp.arange(total_rows, dtype=jnp.int32)
    return jnp.sum((positions[:, None] >= bounds[None, :]).astype(jnp.int32), axis=1)


def gathered_body(
    tokens,
    gain,
    w_query,
    w_keyvalue,
    w_out,
    kv_pool,
    suffix_pages,
    page_index,
    page_request,
    new_slot,
):
    replicas = lax.axis_size("replica")
    tensors = lax.axis_size("tensor")
    owners = replicas * tensors
    position = lax.axis_index("tensor")
    query_width = w_query.shape[1]
    local_heads = query_width // HEAD_DIM
    share = tensors // KV_HEADS
    my_head = position // share
    scale_factor = 1.0 / math.sqrt(HEAD_DIM)
    normed = normalize(tokens, gain)
    piece = lax.all_gather(normed, "tensor", axis=0, tiled=True)
    first = jnp.dot(piece, w_query, preferred_element_type=jnp.float32)
    second = jnp.dot(piece, w_keyvalue, preferred_element_type=jnp.float32)
    projected = jnp.concatenate([first, second], axis=1).astype(jnp.bfloat16)
    query = projected[:, :query_width]
    keyvalue = lax.all_gather(projected[:, query_width:], "tensor", axis=1, tiled=True)
    total_rows = query.shape[0]
    wanted = lax.all_to_all(
        page_index[0], ("replica", "tensor"), split_axis=0, concat_axis=0, tiled=True
    )
    slot_count = wanted.shape[1]
    sources = jnp.arange(owners, dtype=jnp.int32) % tensors
    source_heads = sources // share
    flat_pool = kv_pool.reshape(kv_pool.shape[0] * KV_HEADS, PAGE, 2 * HEAD_DIM)
    outgoing = flat_pool[wanted * KV_HEADS + source_heads[:, None]]
    sub_tokens = outgoing.shape[2]
    pulled = lax.all_to_all(
        outgoing, ("replica", "tensor"), split_axis=0, concat_axis=0, tiled=True
    )
    segments = row_segments(suffix_pages[0], total_rows)
    key_groups = page_request[0]
    stacked = (
        query.reshape(total_rows, local_heads, HEAD_DIM)
        .transpose(1, 0, 2)
        .reshape(local_heads * total_rows, HEAD_DIM)
    )
    own_new = lax.dynamic_index_in_dim(
        keyvalue.reshape(total_rows, KV_HEADS, 2 * HEAD_DIM), my_head, 1, keepdims=False
    )
    row_order = jnp.arange(total_rows, dtype=jnp.int32)
    causal = (segments[:, None] == segments[None, :]) & (row_order[None, :] <= row_order[:, None])

    def block_scores(queries, head_count, keys, allowed):
        raw = (
            jnp.dot(queries, keys[:, :HEAD_DIM].T, preferred_element_type=jnp.float32)
            * scale_factor
        )
        raw = raw.reshape(head_count, total_rows, keys.shape[0])
        return jnp.where(allowed[None], raw, NEG_FILL)

    first_scores = block_scores(stacked, local_heads, own_new, causal)
    running = jnp.max(first_scores, axis=2)
    probs = jnp.exp(first_scores - running[:, :, None])
    denominator = jnp.sum(probs, axis=2)
    numerator = jnp.dot(
        probs.astype(jnp.bfloat16).reshape(local_heads * total_rows, total_rows),
        own_new[:, HEAD_DIM:],
        preferred_element_type=jnp.float32,
    )
    block_owners = 16
    blocks = owners // block_owners

    def absorb(step, state):
        peak, total, mixed = state
        pages = lax.dynamic_slice_in_dim(pulled, step * block_owners, block_owners, 0)
        keys = pages.reshape(block_owners * slot_count * sub_tokens, 2 * HEAD_DIM)
        labels = lax.dynamic_slice_in_dim(key_groups, step * block_owners, block_owners, 0).reshape(
            -1
        )
        matches = (segments[:, None] == labels[None, :])[:, :, None]
        allowed = jnp.broadcast_to(matches, (total_rows, labels.shape[0], sub_tokens)).reshape(
            total_rows, labels.shape[0] * sub_tokens
        )
        scores = block_scores(stacked, local_heads, keys, allowed)
        updated = jnp.maximum(peak, jnp.max(scores, axis=2))
        rescale = jnp.exp(peak - updated)
        weights = jnp.where(allowed[None], jnp.exp(scores - updated[:, :, None]), 0.0)
        total = total * rescale + jnp.sum(weights, axis=2)
        flat_weights = weights.astype(jnp.bfloat16).reshape(local_heads * total_rows, keys.shape[0])
        mixed = mixed * rescale.reshape(-1)[:, None] + jnp.dot(
            flat_weights, keys[:, HEAD_DIM:], preferred_element_type=jnp.float32
        )
        return (updated, total, mixed)

    running, denominator, numerator = lax.fori_loop(
        0, blocks, absorb, (running, denominator, numerator)
    )
    attention = (numerator / denominator.reshape(-1)[:, None]).astype(jnp.bfloat16)
    attention = (
        attention.reshape(local_heads, total_rows, HEAD_DIM)
        .transpose(1, 0, 2)
        .reshape(total_rows, query_width)
    )
    summed = lax.psum_scatter(
        jnp.dot(attention, w_out, preferred_element_type=jnp.float32).astype(jnp.bfloat16),
        "tensor",
        scatter_dimension=0,
        tiled=True,
    ).astype(jnp.float32)
    layer_out = (tokens.astype(jnp.float32) + summed).astype(jnp.bfloat16)
    new_count = total_rows // PAGE
    fresh = (
        keyvalue.reshape(new_count, PAGE, KV_HEADS, 2 * HEAD_DIM)
        .transpose(0, 2, 1, 3)
        .reshape(new_count, KV_HEADS * PAGE * 2 * HEAD_DIM)
    )
    local_pages = kv_pool.shape[0]
    targets = position * local_pages + jnp.arange(local_pages, dtype=jnp.int32)
    match_table = new_slot[0][None, :] == targets[:, None]
    placed = jnp.dot(
        match_table.astype(jnp.bfloat16), fresh, preferred_element_type=jnp.float32
    ).astype(jnp.bfloat16)
    placed = placed.reshape(kv_pool.shape)
    landed = jnp.any(match_table, axis=1)
    pool_out = jnp.where(landed[:, None, None, None], placed, kv_pool)
    return (layer_out, pool_out)


def norm_rows(place, tokens, gain):
    rows, width = tokens.shape
    half = width // 2
    step = 16

    def kernel(place_ref, x_ref, g_ref, mine_ref, other_ref):
        core = place_ref[1]
        near = pl.multiple_of(core * half, half)
        far = pl.multiple_of((1 - core) * half, half)

        def block(i, carry):
            at = pl.ds(pl.multiple_of(i * step, step), step)
            total = jnp.zeros((step, 1), F32)
            for part in range(2):
                values = x_ref[at, part * half : (part + 1) * half].astype(F32)
                total += jnp.sum(values * values, axis=1, keepdims=True)
            inverse = lax.rsqrt(total * (1.0 / width) + EPSILON)
            for start, out in ((near, mine_ref), (far, other_ref)):
                cols = pl.ds(start, half)
                values = x_ref[at, cols].astype(F32)
                out[at, :] = (values * inverse * g_ref[cols].astype(F32)[None, :]).astype(BF16)
            return carry

        lax.fori_loop(0, rows // step, block, 0)

    return pl.pallas_call(
        kernel,
        in_specs=[SMEM, VMEM, VMEM],
        out_specs=[VMEM, VMEM],
        out_shape=[shape((rows, half)), shape((rows, half))],
        compiler_params=params(16),
        cost_estimate=SMALL,
        name="norm_rows",
    )(place, tokens, gain)


def project_local(place, near, far, w_query, w_keyvalue, after):
    rows, half = near[0].shape
    q_width, kv_width = w_query.shape[1], w_keyvalue.shape[1]
    steps = 8
    depth = 2 * half // steps
    waits = len(after)

    def kernel(place_ref, near_own, near_peer, far_own, far_peer, wq, wkv, *refs):
        q_ref, kv_ref, wq_buf, wkv_buf, q_acc, kv_acc, sems = refs[waits:]
        core = place_ref[1]
        stream = weight_stream(core, half, steps, (wq, wkv), (wq_buf, wkv_buf), sems)
        for j in range(steps):
            for copy in stream(j):
                copy.start()
        for j in range(steps):
            for copy in stream(j):
                copy.wait()
            group = (near_own, near_peer) if j < steps // 2 else (far_own, far_peer)
            cols = slice((j % (steps // 2)) * depth, (j % (steps // 2) + 1) * depth)
            x = jnp.concatenate([ref[:, cols] for ref in group], axis=0)
            q_part = jnp.dot(x, wq_buf[j], preferred_element_type=F32)
            kv_part = jnp.dot(x, wkv_buf[j], preferred_element_type=F32)
            if j == 0:
                q_acc[...] = q_part
                kv_acc[...] = kv_part
            elif j < steps - 1:
                q_acc[...] += q_part
                kv_acc[...] += kv_part
            else:
                q_last = (q_acc[...] + q_part).astype(BF16)
                kv_last = (kv_acc[...] + kv_part).astype(BF16)
        for b in range(2):
            at = pl.ds(pl.multiple_of((core if b == 0 else 1 - core) * rows, rows), rows)
            q_ref[at, :] = q_last[b * rows : (b + 1) * rows]
            kv_ref[at, :] = kv_last[b * rows : (b + 1) * rows]

    total = 2 * rows
    return pl.pallas_call(
        kernel,
        in_specs=[SMEM] + [VMEM] * 4 + [HBM] * 2 + [ANY] * waits,
        out_specs=[VMEM] * 4,
        out_shape=[
            shape((total, q_width)),
            shape((total, kv_width)),
            pltpu.VMEM((steps, depth, q_width), BF16),
            pltpu.VMEM((steps, depth, kv_width), BF16),
        ],
        scratch_shapes=[
            pltpu.VMEM((total, q_width), F32),
            pltpu.VMEM((total, kv_width), F32),
            pltpu.SemaphoreType.DMA((2 * steps,)),
        ],
        compiler_params=params(10),
        cost_estimate=SMALL,
        name="project_local",
    )(place, *near, *far, w_query, w_keyvalue, *after)


def weight_stream(core, half, steps, sources, buffers, sems):
    depth = 2 * half // steps

    def copies(j):
        base = core if j < steps // 2 else 1 - core
        start = pl.multiple_of(base * half + (j % (steps // 2)) * depth, depth)
        count = len(sources)
        return [
            pltpu.make_async_copy(w.at[pl.ds(start, depth)], buf.at[j], sems.at[count * j + i])
            for i, (w, buf) in enumerate(zip(sources, buffers))
        ]

    return copies


PAGES_STEP = 4
REQUESTS = 4
SIZES_AT = 4
REQUESTS_AT = 8


def attention_scratch(block_rows, heads, fresh_rows, slots):
    stacked = heads * block_rows
    return [
        pltpu.VMEM((stacked, fresh_rows + slots * PAGE), F32),
        pltpu.VMEM((stacked, HEAD_DIM), F32),
        pltpu.VMEM((stacked, HEAD_DIM), F32),
        pltpu.VMEM((slots * PAGE, 2 * HEAD_DIM), BF16),
        pltpu.SMEM((slots,), jnp.int32),
    ]


def attend_block(place_ref, q, first_row, fresh, pulled, scratch):
    scores, total_ref, mixed_ref, cache, labels = scratch
    me = place_ref[0]
    block_rows, width = q.shape
    heads = width // HEAD_DIM
    stacked = heads * block_rows
    groups, per = pulled.shape[:2]
    tensors = 4
    slots = per // tensors
    wide = PAGES_STEP * PAGE
    factor = math.log2(math.e) / math.sqrt(HEAD_DIM)
    bound = []
    running = jnp.int32(0)
    for k in range(REQUESTS):
        running = running + place_ref[SIZES_AT + k] * UNIT
        bound.append(running)

    def segment_of(position):
        return sum((position >= b).astype(jnp.int32) for b in bound)

    lowest = segment_of(first_row)
    highest = segment_of(first_row + block_rows - 1)
    count = jnp.int32(0)
    for g in range(groups):
        for p in range(per):
            owner = g * tensors + jnp.bitwise_xor(me, p // slots)
            label = place_ref[REQUESTS_AT + p % slots * groups * tensors + owner]
            wanted = (label >= lowest) & (label <= highest)

            @pl.when(wanted)
            def _():
                cache[pl.ds(pl.multiple_of(count * PAGE, PAGE), PAGE), :] = pulled[g, p]
                labels[count] = label

            count = count + wanted.astype(jnp.int32)
    steps = (count + PAGES_STEP - 1) // PAGES_STEP
    for k in range(PAGES_STEP - 1):

        @pl.when(count + k < steps * PAGES_STEP)
        def _():
            cache[pl.ds(pl.multiple_of((count + k) * PAGE, PAGE), PAGE), :] = jnp.zeros(
                (PAGE, 2 * HEAD_DIM), BF16
            )
            labels[count + k] = jnp.int32(-1)

    q_rows = jnp.concatenate([q[:, h * HEAD_DIM : (h + 1) * HEAD_DIM] for h in range(heads)], axis=0)
    row_position = first_row + lax.broadcasted_iota(jnp.int32, (block_rows, 1), 0)
    row_segment = segment_of(row_position)

    def masked_scores(keys, allowed):
        raw = lax.dot_general(q_rows, keys, (((1,), (1,)), ((), ())), preferred_element_type=F32)
        n = keys.shape[0]
        return jnp.where(allowed[None], raw.reshape(heads, block_rows, n), NEG_FILL).reshape(
            stacked, n
        )

    def fold(values, combine):
        pieces = [values[:, i : i + HEAD_DIM] for i in range(0, values.shape[1], HEAD_DIM)]
        result = pieces[0]
        for piece in pieces[1:]:
            result = combine(result, piece)
        return result

    new = jnp.concatenate([rows for rows, _ in fresh], axis=0)
    fresh_rows = new.shape[0]
    key_position = jnp.concatenate(
        [
            base + lax.broadcasted_iota(jnp.int32, (1, rows.shape[0]), 1)
            for rows, base in fresh
        ],
        axis=1,
    )
    allowed = (row_segment == segment_of(key_position)) & (key_position <= row_position)
    masked = masked_scores(new[:, :HEAD_DIM], allowed)
    scores[:, :fresh_rows] = masked
    total_ref[...] = fold(masked, jnp.maximum)
    lanes = lax.broadcasted_iota(jnp.int32, (1, wide), 1) // PAGE

    def add_scores(g, carry):
        label = jnp.full((1, wide), -1, jnp.int32)
        for j in range(PAGES_STEP):
            label = jnp.where(lanes == j, labels[g * PAGES_STEP + j], label)
        keys = cache[pl.ds(pl.multiple_of(g * wide, wide), wide), :HEAD_DIM]
        masked = masked_scores(keys, row_segment == label)
        scores[:, pl.ds(pl.multiple_of(fresh_rows + g * wide, PAGE), wide)] = masked
        total_ref[...] = jnp.maximum(total_ref[...], fold(masked, jnp.maximum))
        return carry

    lax.fori_loop(0, steps, add_scores, 0)
    top = jnp.max(total_ref[...], axis=1, keepdims=True) * factor
    probs = jnp.exp2(scores[:, :fresh_rows] * factor - top)
    total_ref[...] = fold(probs, jnp.add)
    mixed_ref[...] = jnp.dot(probs.astype(BF16), new[:, HEAD_DIM:], preferred_element_type=F32)

    def add_values(g, carry):
        part = scores[:, pl.ds(pl.multiple_of(fresh_rows + g * wide, PAGE), wide)]
        probs = jnp.exp2(part * factor - top)
        values = cache[pl.ds(pl.multiple_of(g * wide, wide), wide), HEAD_DIM:]
        total_ref[...] += fold(probs, jnp.add)
        mixed_ref[...] += jnp.dot(probs.astype(BF16), values, preferred_element_type=F32)
        return carry

    lax.fori_loop(0, steps, add_values, 0)
    denominator = jnp.sum(total_ref[...], axis=1, keepdims=True)
    result = (mixed_ref[...] / denominator).astype(BF16)
    return jnp.concatenate(
        [result[h * block_rows : (h + 1) * block_rows] for h in range(heads)], axis=1
    )


def project_held(near, far, w_query, w_keyvalue, after):
    rows, half = near.shape
    steps, depth, q_width = w_query.shape
    kv_width = w_keyvalue.shape[2]

    def kernel(near_ref, far_ref, wq, wkv, *refs):
        q_ref, kv_ref = refs[len(after) :]
        for w, out in ((wq, q_ref), (wkv, kv_ref)):
            total = None
            for j in range(steps):
                x_ref = near_ref if j < steps // 2 else far_ref
                x = x_ref[:, (j % (steps // 2)) * depth : (j % (steps // 2) + 1) * depth]
                part = jnp.dot(x, w[j], preferred_element_type=F32)
                total = part if j == 0 else total + part
            out[...] = total.astype(BF16)

    return pl.pallas_call(
        kernel,
        in_specs=[VMEM] * 4 + [ANY] * len(after),
        out_specs=[VMEM] * 2,
        out_shape=[shape((rows, q_width)), shape((rows, kv_width))],
        compiler_params=params(6),
        cost_estimate=SMALL,
        name="project_held",
    )(near, far, w_query, w_keyvalue, *after)


def project_far(place, near, far, w_query, w_keyvalue, after):
    rows, half = near.shape
    q_width, kv_width = w_query.shape[1], w_keyvalue.shape[1]
    steps = 8
    depth = 2 * half // steps

    def kernel(place_ref, near_ref, far_ref, wq, wkv, *refs):
        q_ref, kv_ref, wq_buf, wkv_buf, sems = refs[len(after) :]
        stream = weight_stream(place_ref[1], half, steps, (wq, wkv), (wq_buf, wkv_buf), sems)
        for j in range(steps):
            for copy in stream(j):
                copy.start()
        q_sum = kv_sum = None
        for j in range(steps):
            for copy in stream(j):
                copy.wait()
            x_ref = near_ref if j < steps // 2 else far_ref
            x = x_ref[:, (j % (steps // 2)) * depth : (j % (steps // 2) + 1) * depth]
            q_part = jnp.dot(x, wq_buf[j], preferred_element_type=F32)
            kv_part = jnp.dot(x, wkv_buf[j], preferred_element_type=F32)
            q_sum = q_part if j == 0 else q_sum + q_part
            kv_sum = kv_part if j == 0 else kv_sum + kv_part
        q_ref[...] = q_sum.astype(BF16)
        kv_ref[...] = kv_sum.astype(BF16)

    return pl.pallas_call(
        kernel,
        in_specs=[SMEM] + [VMEM] * 2 + [HBM] * 2 + [ANY] * len(after),
        out_specs=[VMEM] * 2,
        out_shape=[shape((rows, q_width)), shape((rows, kv_width))],
        scratch_shapes=[
            pltpu.VMEM((steps, depth, q_width), BF16),
            pltpu.VMEM((steps, depth, kv_width), BF16),
            pltpu.SemaphoreType.DMA((2 * steps,)),
        ],
        compiler_params=params(32),
        cost_estimate=SMALL,
        name="project_far",
    )(place, near, far, w_query, w_keyvalue, *after)


def attend_out(place, query, fresh, bases, base, pulled, w_out):
    rows, depth = query.shape
    width = w_out.shape[1]
    half = width // 2
    heads = depth // HEAD_DIM
    out_steps = 4
    wide = half // out_steps
    known = len(fresh)
    count = sum(f.shape[0] for f in fresh)
    fresh_rows = -(-count // HEAD_DIM) * HEAD_DIM
    pad = fresh_rows - count

    def kernel(place_ref, q_ref, pulled_ref, *refs):
        fresh_refs = refs[:known]
        wo, there_ref, stay_ref, wo_buf, q_buf, sems = refs[known : known + 6]
        core, side = place_ref[1], place_ref[2]

        def copy(j):
            first = 1 - core if j < out_steps else core
            start = pl.multiple_of(first * half + (j % out_steps) * wide, wide)
            return pltpu.make_async_copy(wo.at[:, pl.ds(start, wide)], wo_buf.at[j], sems.at[j])

        q_copy = pltpu.make_async_copy(q_ref, q_buf, sems.at[2 * out_steps])
        q_copy.start()
        for j in range(2 * out_steps):
            copy(j).start()
        q_copy.wait()
        pairs = [(ref[...], at(side)) for ref, at in zip(fresh_refs, bases)]
        if pad:
            pairs.append((jnp.zeros((pad, 2 * HEAD_DIM), BF16), jnp.int32(1 << 20)))
        mixed = attend_block(
            place_ref, q_buf[...], base(side), pairs, pulled_ref, refs[known + 6 :]
        )
        for j in range(2 * out_steps):
            copy(j).wait()
            out_ref = there_ref if j < out_steps else stay_ref
            at = (j % out_steps) * wide
            out_ref[:, at : at + wide] = jnp.dot(
                mixed, wo_buf[j], preferred_element_type=F32
            ).astype(BF16)

    return pl.pallas_call(
        kernel,
        in_specs=[SMEM, HBM] + [VMEM] * (1 + known) + [HBM],
        out_specs=[VMEM] * 2,
        out_shape=[shape((rows, half)), shape((rows, half))],
        scratch_shapes=[
            pltpu.VMEM((2 * out_steps, depth, wide), BF16),
            pltpu.VMEM((rows, depth), BF16),
            pltpu.SemaphoreType.DMA((2 * out_steps + 1,)),
        ]
        + attention_scratch(rows, heads, fresh_rows, pulled.shape[0] * pulled.shape[1]),
        compiler_params=params(30),
        cost_estimate=SMALL,
        name="attend_out",
    )(place, query, pulled, *fresh, w_out)


def local_rows(place, query, fresh, bases, base, pulled, w_out, after):
    both, depth = query.shape
    rows = both // 2
    width = w_out.shape[1]
    heads = depth // HEAD_DIM
    steps = 8
    wide = width // steps
    known = len(fresh)
    fresh_rows = sum(f.shape[0] for f in fresh)

    def kernel(place_ref, q_ref, pulled_ref, *refs):
        fresh_refs = refs[:known]
        wo = refs[known]
        rest = refs[known + 1 + len(after) :]
        own_ref, peer_ref, wo_buf, a_buf, sems = rest[:5]
        core, side = place_ref[1], place_ref[2]

        def out_copy(j):
            return pltpu.make_async_copy(
                wo.at[:, j * wide : (j + 1) * wide], wo_buf.at[j], sems.at[j]
            )

        for j in range(steps):
            out_copy(j).start()

        def block(b, carry):
            at = pl.ds(pl.multiple_of(b * rows, rows), rows)
            a_buf[at, :] = attend_block(
                place_ref,
                q_ref[at, :],
                base(side) + b * rows,
                [(ref[...], first(side)) for ref, first in zip(fresh_refs, bases)],
                pulled_ref,
                rest[5:],
            )
            return carry

        lax.fori_loop(0, 2, block, 0)
        own_at = pl.ds(pl.multiple_of(core * rows, rows), rows)
        peer_at = pl.ds(pl.multiple_of((1 - core) * rows, rows), rows)
        a = jnp.concatenate([a_buf[own_at, :], a_buf[peer_at, :]], axis=0)
        for j in range(steps):
            out_copy(j).wait()
            part = jnp.dot(a, wo_buf[j], preferred_element_type=F32).astype(BF16)
            own_ref[:, j * wide : (j + 1) * wide] = part[:rows]
            peer_ref[:, j * wide : (j + 1) * wide] = part[rows:]

    return pl.pallas_call(
        kernel,
        in_specs=[SMEM] + [VMEM] * (2 + known) + [HBM] + [ANY] * len(after),
        out_specs=[VMEM, VMEM],
        out_shape=[shape((rows, width)), shape((rows, width))],
        scratch_shapes=[
            pltpu.VMEM((steps, depth, wide), BF16),
            pltpu.VMEM((both, depth), BF16),
            pltpu.SemaphoreType.DMA((steps,)),
        ]
        + attention_scratch(rows, heads, fresh_rows, pulled.shape[0] * pulled.shape[1]),
        compiler_params=params(40),
        cost_estimate=SMALL,
        name="local_rows",
    )(place, query, pulled, *fresh, w_out, *after)


def add_pair(left, right):
    rows, width = left.shape
    step = 16

    def kernel(left_ref, right_ref, out_ref):
        def block(i, carry):
            at = pl.ds(pl.multiple_of(i * step, step), step)
            out_ref[at, :] = (left_ref[at, :].astype(F32) + right_ref[at, :].astype(F32)).astype(
                BF16
            )
            return carry

        lax.fori_loop(0, rows // step, block, 0)

    return pl.pallas_call(
        kernel,
        in_specs=[VMEM, VMEM],
        out_specs=VMEM,
        out_shape=shape((rows, width)),
        compiler_params=params(8),
        cost_estimate=SMALL,
        name="add_pair",
    )(left, right)


def finish(place, tokens, own, peer, near, far):
    rows, width = tokens.shape
    half = width // 2
    step = 16

    def kernel(place_ref, x_ref, own_ref, peer_ref, near_ref, far_ref, out_ref):
        core = place_ref[1]

        def block(i, carry):
            at = pl.ds(pl.multiple_of(i * step, step), step)
            for start, part in ((core, near_ref), (1 - core, far_ref)):
                cols = pl.ds(pl.multiple_of(start * half, half), half)
                local = own_ref[at, cols].astype(F32) + peer_ref[at, cols].astype(F32)
                total = local + part[at, :].astype(F32)
                out_ref[at, cols] = (x_ref[at, cols].astype(F32) + total).astype(BF16)
            return carry

        lax.fori_loop(0, rows // step, block, 0)

    return pl.pallas_call(
        kernel,
        in_specs=[SMEM] + [VMEM] * 5,
        out_specs=VMEM,
        out_shape=shape((rows, width)),
        compiler_params=params(16),
        cost_estimate=SMALL,
        name="finish",
    )(place, tokens, own, peer, near, far)


def pick_pages(place, wanted, held, after):
    replicas, tensors, slots = wanted.shape
    _, page, width = held[0].shape
    total = tensors * slots

    def kernel(place_ref, want_ref, *refs):
        sources = refs[:tensors]
        out_ref, sems = refs[tensors + len(after) :]
        me = place_ref[0]

        def copies():
            for r in range(replicas):
                for i in range(tensors):
                    for s in range(slots):
                        at = i * slots + s
                        yield pltpu.make_async_copy(
                            sources[i].at[want_ref[r, jnp.bitwise_xor(me, i), s]],
                            out_ref.at[r, at],
                            sems.at[r * total + at],
                        )

        for copy in copies():
            copy.start()
        for copy in copies():
            copy.wait()

    return pl.pallas_call(
        kernel,
        in_specs=[SMEM, SMEM] + [ANY] * (tensors + len(after)),
        out_specs=ANY,
        out_shape=shape((replicas, total, page, width)),
        scratch_shapes=[pltpu.SemaphoreType.DMA((replicas * total,))],
        compiler_params=params(8),
        cost_estimate=SMALL,
        name="pick_pages",
    )(place, wanted, *held, *after)


def write_pool(place, slots, kv_pool, own, core_new, y_new):
    pages, heads = kv_pool.shape[:2]
    new_count = slots.shape[1]
    side_pages = new_count // 2

    def kernel(place_ref, slot_ref, pool_ref, own_ref, core_ref, y_ref, out_ref, sems):
        me, side = place_ref[0], place_ref[2]
        sources = (own_ref, core_ref.at[0], y_ref, core_ref.at[1])
        for p in range(pages):
            found = jnp.int32(-1)
            for j in range(new_count):
                found = jnp.where(slot_ref[0, j] == me * pages + p, j, found)
            far = (found >= side_pages).astype(jnp.int32)
            inner = jnp.maximum(found - far * side_pages, 0)

            @pl.when(found >= 0)
            def _():
                for i in range(heads):
                    origin = side if i < 2 else 1 - side
                    start = (jnp.bitwise_xor(far, origin) * side_pages + inner) * PAGE
                    pltpu.make_async_copy(
                        sources[i].at[pl.ds(pl.multiple_of(start, PAGE), PAGE)],
                        out_ref.at[p, jnp.bitwise_xor(me, i)],
                        sems.at[p * heads + i],
                    ).start()

            @pl.when(found < 0)
            def _():
                for i in range(heads):
                    at = jnp.bitwise_xor(me, i)
                    pltpu.make_async_copy(
                        pool_ref.at[p, at], out_ref.at[p, at], sems.at[p * heads + i]
                    ).start()

        for p in range(pages):
            for i in range(heads):
                at = jnp.bitwise_xor(me, i)
                pltpu.make_async_copy(
                    pool_ref.at[p, at], out_ref.at[p, at], sems.at[p * heads + i]
                ).wait()

    return pl.pallas_call(
        kernel,
        in_specs=[SMEM, SMEM] + [ANY] * 4,
        out_specs=ANY,
        out_shape=shape(kv_pool.shape),
        scratch_shapes=[pltpu.SemaphoreType.DMA((pages * heads,))],
        compiler_params=params(8),
        cost_estimate=SMALL,
        name="write_pool",
    )(place, slots, kv_pool, own, core_new, y_new)


def chip_pair_body(
    tokens,
    gain,
    w_query,
    w_keyvalue,
    w_out,
    kv_pool,
    suffix_pages,
    page_index,
    page_request,
    new_slot,
):
    replicas = lax.axis_size("replica")
    me = lax.axis_index("tensor")
    core = me % 2
    side = me // 2
    rows = tokens.shape[0]
    requests = jnp.swapaxes(page_request, 1, 2).reshape(-1)
    place = jnp.stack([me, core, side, 0 * me]).astype(jnp.int32)
    place = in_hbm(jnp.concatenate([place, suffix_pages[0], requests]))

    def over_core(x):
        return lax.ppermute(x, "tensor", [(0, 1), (1, 0), (2, 3), (3, 2)])

    def over_y(x):
        return lax.ppermute(x, "tensor", [(0, 2), (2, 0), (1, 3), (3, 1)])

    def head_of(i):
        return lax.dynamic_index_in_dim(kv_pool, jnp.bitwise_xor(me, i), 1, keepdims=False)

    def to_replicas(x):
        return lax.all_to_all(x, "replica", split_axis=0, concat_axis=0, tiled=True)

    def tie(x, *others):
        return lax.optimization_barrier((x, *others))[0]

    w_query, w_keyvalue, w_out = in_hbm(w_query), in_hbm(w_keyvalue), in_hbm(w_out)
    held = [head_of(0)]
    for i in range(1, 4):
        held.append(lax.ppermute(head_of(i), "tensor", [(t, t ^ i) for t in range(4)]))

    numbers = page_index.reshape(replicas, -1, page_index.shape[2])
    wanted = to_replicas(numbers)

    mine, other = norm_rows(place, tokens, gain)
    peer_near = over_core(other)
    peer_far = over_core(mine)
    is_first = core == 0
    near_tied = tie(peer_near, held[2], held[3], wanted)
    first_half = jnp.where(is_first, mine, near_tied)
    second_half = jnp.where(is_first, near_tied, mine)
    first = over_y(first_half)
    second = over_y(second_half)

    picked = pick_pages(place, wanted, held, [first_half, second_half])
    pulled = to_replicas(picked)

    q_local, kv_local, wq, wkv = project_local(
        place, [mine, peer_near], [other, peer_far], w_query, w_keyvalue, [picked]
    )

    q_local = in_hbm(q_local)

    def local_base(s):
        return s * (2 * rows)

    def first_base(s):
        return (1 - s) * (2 * rows)

    def second_base(s):
        return (1 - s) * (2 * rows) + rows

    first = tie(first, q_local)
    q_first, kv_first = project_held(first, over_core(first), wq, wkv, [])
    q_first = in_hbm(q_first)
    there, stay = attend_out(
        place, q_first, [kv_local, kv_first],
        [local_base, first_base], first_base, pulled, w_out,
    )
    there = tie(there, second)
    first_mix = add_pair(stay, over_core(there))
    first_sum = over_y(first_mix)

    second = tie(second, first_mix)
    q_second, kv_second = project_far(place, second, over_core(second), w_query, w_keyvalue, [])
    fresh = [kv_local, kv_first, kv_second]
    bases = [local_base, first_base, second_base]
    there, stay = attend_out(
        place, q_second, fresh, bases, second_base, pulled, w_out
    )
    there = tie(there, first_sum)
    second_mix = add_pair(stay, over_core(there))


    new_own = jnp.concatenate(fresh, axis=0)
    y_new = over_y(new_own)
    core_new = over_core(jnp.stack([new_own, y_new]))
    second_sum = over_y(tie(second_mix, y_new))

    pool_out = write_pool(place, new_slot, kv_pool, new_own, core_new, y_new)

    own_part, peer_part = local_rows(
        place, q_local, fresh, bases, local_base, pulled, w_out,
        [second_mix, pool_out],
    )
    peer_part = over_core(peer_part)

    near = jnp.where(is_first, first_sum, second_sum)
    far = over_core(jnp.where(is_first, second_sum, first_sum))
    layer_out = finish(place, tokens, own_part, peer_part, near, far)
    return (layer_out, pool_out)


def solution(mesh):
    pair = mesh.shape["tensor"] == KV_HEADS
    return jax.shard_map(
        chip_pair_body if pair else gathered_body,
        mesh=mesh,
        in_specs=(
            P(("groups", "replica", "tensor"), None),
            P(),
            P(None, "tensor"),
            P(None, "tensor"),
            P("tensor", None),
            P(("groups", "replica", "tensor"), None, None, None),
            P(("groups", "replica"), None),
            P(("groups", "replica"), None, None),
            P(("groups", "replica"), None, None),
            P(("groups", "replica"), None),
        ),
        out_specs=(
            P(("groups", "replica", "tensor"), None),
            P(("groups", "replica", "tensor"), None, None, None),
        ),
        check_vma=False,
    )
```

```python
import math

import jax
import jax.numpy as jnp
from jax import lax
from jax.experimental import pallas as pl
from jax.experimental.pallas import tpu as pltpu
from jax.sharding import PartitionSpec as P

KV_HEADS = 4
HEAD_DIM = 128
PAGE = 64
UNIT = 8


NEG_FILL = -1e30
EPSILON = 1e-06

F32 = jnp.float32
BF16 = jnp.bfloat16
MIB = 1 << 20
ANY = pl.BlockSpec(memory_space=pl.ANY)
HBM = pl.BlockSpec(memory_space=pltpu.HBM)
SMEM = pl.BlockSpec(memory_space=pltpu.SMEM)
VMEM = pl.BlockSpec(memory_space=pltpu.VMEM)
SMALL = pl.CostEstimate(flops=1024, bytes_accessed=1024, transcendentals=0)


def params(mib):
    return pltpu.CompilerParams(vmem_limit_bytes=mib * MIB)


def in_hbm(x):
    return pltpu.with_memory_space_constraint(x, pltpu.HBM)


def shape(dims, dtype=BF16):
    return jax.ShapeDtypeStruct(dims, dtype)


def normalize(rows, gain):
    values = rows.astype(jnp.float32)
    inverse = lax.rsqrt(jnp.mean(values * values, axis=-1, keepdims=True) + EPSILON)
    return (values * inverse * gain.astype(jnp.float32)).astype(jnp.bfloat16)


def row_segments(pages, total_rows):
    bounds = jnp.cumsum(pages) * UNIT
    positions = jnp.arange(total_rows, dtype=jnp.int32)
    return jnp.sum((positions[:, None] >= bounds[None, :]).astype(jnp.int32), axis=1)


def gathered_body(
    tokens,
    gain,
    w_query,
    w_keyvalue,
    w_out,
    kv_pool,
    suffix_pages,
    page_index,
    page_request,
    new_slot,
):
    replicas = lax.axis_size("replica")
    tensors = lax.axis_size("tensor")
    owners = replicas * tensors
    position = lax.axis_index("tensor")
    query_width = w_query.shape[1]
    local_heads = query_width // HEAD_DIM
    share = tensors // KV_HEADS
    my_head = position // share
    scale_factor = 1.0 / math.sqrt(HEAD_DIM)
    normed = normalize(tokens, gain)
    piece = lax.all_gather(normed, "tensor", axis=0, tiled=True)
    first = jnp.dot(piece, w_query, preferred_element_type=jnp.float32)
    second = jnp.dot(piece, w_keyvalue, preferred_element_type=jnp.float32)
    projected = jnp.concatenate([first, second], axis=1).astype(jnp.bfloat16)
    query = projected[:, :query_width]
    keyvalue = lax.all_gather(projected[:, query_width:], "tensor", axis=1, tiled=True)
    total_rows = query.shape[0]
    wanted = lax.all_to_all(
        page_index[0], ("replica", "tensor"), split_axis=0, concat_axis=0, tiled=True
    )
    slot_count = wanted.shape[1]
    sources = jnp.arange(owners, dtype=jnp.int32) % tensors
    source_heads = sources // share
    flat_pool = kv_pool.reshape(kv_pool.shape[0] * KV_HEADS, PAGE, 2 * HEAD_DIM)
    outgoing = flat_pool[wanted * KV_HEADS + source_heads[:, None]]
    sub_tokens = outgoing.shape[2]
    pulled = lax.all_to_all(
        outgoing, ("replica", "tensor"), split_axis=0, concat_axis=0, tiled=True
    )
    segments = row_segments(suffix_pages[0], total_rows)
    key_groups = page_request[0]
    stacked = (
        query.reshape(total_rows, local_heads, HEAD_DIM)
        .transpose(1, 0, 2)
        .reshape(local_heads * total_rows, HEAD_DIM)
    )
    own_new = lax.dynamic_index_in_dim(
        keyvalue.reshape(total_rows, KV_HEADS, 2 * HEAD_DIM), my_head, 1, keepdims=False
    )
    row_order = jnp.arange(total_rows, dtype=jnp.int32)
    causal = (segments[:, None] == segments[None, :]) & (row_order[None, :] <= row_order[:, None])

    def block_scores(queries, head_count, keys, allowed):
        raw = (
            jnp.dot(queries, keys[:, :HEAD_DIM].T, preferred_element_type=jnp.float32)
            * scale_factor
        )
        raw = raw.reshape(head_count, total_rows, keys.shape[0])
        return jnp.where(allowed[None], raw, NEG_FILL)

    first_scores = block_scores(stacked, local_heads, own_new, causal)
    running = jnp.max(first_scores, axis=2)
    probs = jnp.exp(first_scores - running[:, :, None])
    denominator = jnp.sum(probs, axis=2)
    numerator = jnp.dot(
        probs.astype(jnp.bfloat16).reshape(local_heads * total_rows, total_rows),
        own_new[:, HEAD_DIM:],
        preferred_element_type=jnp.float32,
    )
    block_owners = 16
    blocks = owners // block_owners

    def absorb(step, state):
        peak, total, mixed = state
        pages = lax.dynamic_slice_in_dim(pulled, step * block_owners, block_owners, 0)
        keys = pages.reshape(block_owners * slot_count * sub_tokens, 2 * HEAD_DIM)
        labels = lax.dynamic_slice_in_dim(key_groups, step * block_owners, block_owners, 0).reshape(
            -1
        )
        matches = (segments[:, None] == labels[None, :])[:, :, None]
        allowed = jnp.broadcast_to(matches, (total_rows, labels.shape[0], sub_tokens)).reshape(
            total_rows, labels.shape[0] * sub_tokens
        )
        scores = block_scores(stacked, local_heads, keys, allowed)
        updated = jnp.maximum(peak, jnp.max(scores, axis=2))
        rescale = jnp.exp(peak - updated)
        weights = jnp.where(allowed[None], jnp.exp(scores - updated[:, :, None]), 0.0)
        total = total * rescale + jnp.sum(weights, axis=2)
        flat_weights = weights.astype(jnp.bfloat16).reshape(local_heads * total_rows, keys.shape[0])
        mixed = mixed * rescale.reshape(-1)[:, None] + jnp.dot(
            flat_weights, keys[:, HEAD_DIM:], preferred_element_type=jnp.float32
        )
        return (updated, total, mixed)

    running, denominator, numerator = lax.fori_loop(
        0, blocks, absorb, (running, denominator, numerator)
    )
    attention = (numerator / denominator.reshape(-1)[:, None]).astype(jnp.bfloat16)
    attention = (
        attention.reshape(local_heads, total_rows, HEAD_DIM)
        .transpose(1, 0, 2)
        .reshape(total_rows, query_width)
    )
    summed = lax.psum_scatter(
        jnp.dot(attention, w_out, preferred_element_type=jnp.float32).astype(jnp.bfloat16),
        "tensor",
        scatter_dimension=0,
        tiled=True,
    ).astype(jnp.float32)
    layer_out = (tokens.astype(jnp.float32) + summed).astype(jnp.bfloat16)
    new_count = total_rows // PAGE
    fresh = (
        keyvalue.reshape(new_count, PAGE, KV_HEADS, 2 * HEAD_DIM)
        .transpose(0, 2, 1, 3)
        .reshape(new_count, KV_HEADS * PAGE * 2 * HEAD_DIM)
    )
    local_pages = kv_pool.shape[0]
    targets = position * local_pages + jnp.arange(local_pages, dtype=jnp.int32)
    match_table = new_slot[0][None, :] == targets[:, None]
    placed = jnp.dot(
        match_table.astype(jnp.bfloat16), fresh, preferred_element_type=jnp.float32
    ).astype(jnp.bfloat16)
    placed = placed.reshape(kv_pool.shape)
    landed = jnp.any(match_table, axis=1)
    pool_out = jnp.where(landed[:, None, None, None], placed, kv_pool)
    return (layer_out, pool_out)


def prepare(place, tokens, gain, kv_pool):
    rows, width = tokens.shape
    half = width // 2
    step = 32
    pages, heads = kv_pool.shape[:2]
    blocks = rows // step

    def kernel(place_ref, x, g, pool, mine_ref, other_ref, *refs):
        held, (x_buf, g_buf, sems) = refs[:heads], refs[heads:]
        me, core = place_ref[0], place_ref[1]

        def head_copy(i):
            return pltpu.make_async_copy(
                pool.at[:, jnp.bitwise_xor(me, i)], held[i], sems.at[blocks + 1 + i]
            )

        def row_copy(b):
            at = pl.ds(b * step, step)
            return pltpu.make_async_copy(x.at[at], x_buf.at[at], sems.at[b])

        gain_copy = pltpu.make_async_copy(g, g_buf, sems.at[blocks])
        row_copy(0).start()
        gain_copy.start()
        for b in range(1, blocks):
            row_copy(b).start()
        for i in range(heads):
            head_copy(i).start()
        near = pl.multiple_of(core * half, half)
        far = pl.multiple_of((1 - core) * half, half)
        for b in range(blocks):
            row_copy(b).wait()
            if b == 0:
                gain_copy.wait()

            def block(i, carry):
                at = pl.ds(pl.multiple_of(b * step + i * 16, 16), 16)
                total = jnp.zeros((16, 1), F32)
                for part in range(2):
                    values = x_buf[at, part * half : (part + 1) * half].astype(F32)
                    total += jnp.sum(values * values, axis=1, keepdims=True)
                inverse = lax.rsqrt(total * (1.0 / width) + EPSILON)
                for start, out in ((near, mine_ref), (far, other_ref)):
                    cols = pl.ds(start, half)
                    values = x_buf[at, cols].astype(F32)
                    out[at, :] = (values * inverse * g_buf[cols].astype(F32)[None, :]).astype(BF16)
                return carry

            lax.fori_loop(0, step // 16, block, 0)
        for i in range(heads):
            head_copy(i).wait()

    return pl.pallas_call(
        kernel,
        in_specs=[SMEM] + [HBM] * 3,
        out_specs=[VMEM, VMEM] + [HBM] * heads,
        out_shape=[shape((rows, half))] * 2 + [shape((pages,) + kv_pool.shape[2:])] * heads,
        scratch_shapes=[
            pltpu.VMEM((rows, width), BF16),
            pltpu.VMEM((width,), BF16),
            pltpu.SemaphoreType.DMA((blocks + 1 + heads,)),
        ],
        compiler_params=params(16),
        cost_estimate=SMALL,
        name="prepare",
    )(place, tokens, gain, kv_pool)


def project_local(place, near, far, w_query, w_keyvalue, after):
    rows, half = near[0].shape
    q_width, kv_width = w_query.shape[1], w_keyvalue.shape[1]
    steps = 8
    depth = 2 * half // steps
    waits = len(after)

    def kernel(place_ref, near_own, near_peer, far_own, far_peer, wq, wkv, *refs):
        q_ref, kv_ref, wq_buf, wkv_buf, q_acc, kv_acc, sems = refs[waits:]
        core = place_ref[1]
        stream = weight_stream(core, half, steps, (wq, wkv), (wq_buf, wkv_buf), sems)
        for j in range(steps):
            for copy in stream(j):
                copy.start()
        for j in range(steps):
            for copy in stream(j):
                copy.wait()
            group = (near_own, near_peer) if j < steps // 2 else (far_own, far_peer)
            cols = slice((j % (steps // 2)) * depth, (j % (steps // 2) + 1) * depth)
            x = jnp.concatenate([ref[:, cols] for ref in group], axis=0)
            q_part = jnp.dot(x, wq_buf[j], preferred_element_type=F32)
            kv_part = jnp.dot(x, wkv_buf[j], preferred_element_type=F32)
            if j == 0:
                q_acc[...] = q_part
                kv_acc[...] = kv_part
            elif j < steps - 1:
                q_acc[...] += q_part
                kv_acc[...] += kv_part
            else:
                q_last = (q_acc[...] + q_part).astype(BF16)
                kv_last = (kv_acc[...] + kv_part).astype(BF16)
        for b in range(2):
            at = pl.ds(pl.multiple_of((core if b == 0 else 1 - core) * rows, rows), rows)
            q_ref[at, :] = q_last[b * rows : (b + 1) * rows]
            kv_ref[at, :] = kv_last[b * rows : (b + 1) * rows]

    total = 2 * rows
    return pl.pallas_call(
        kernel,
        in_specs=[SMEM] + [VMEM] * 4 + [HBM] * 2 + [ANY] * waits,
        out_specs=[VMEM] * 4,
        out_shape=[
            shape((total, q_width)),
            shape((total, kv_width)),
            pltpu.VMEM((steps, depth, q_width), BF16),
            pltpu.VMEM((steps, depth, kv_width), BF16),
        ],
        scratch_shapes=[
            pltpu.VMEM((total, q_width), F32),
            pltpu.VMEM((total, kv_width), F32),
            pltpu.SemaphoreType.DMA((2 * steps,)),
        ],
        compiler_params=params(10),
        cost_estimate=SMALL,
        name="project_local",
    )(place, *near, *far, w_query, w_keyvalue, *after)


def weight_stream(core, half, steps, sources, buffers, sems):
    depth = 2 * half // steps

    def copies(j):
        base = core if j < steps // 2 else 1 - core
        start = pl.multiple_of(base * half + (j % (steps // 2)) * depth, depth)
        count = len(sources)
        return [
            pltpu.make_async_copy(w.at[pl.ds(start, depth)], buf.at[j], sems.at[count * j + i])
            for i, (w, buf) in enumerate(zip(sources, buffers))
        ]

    return copies


PAGES_STEP = 4
REQUESTS = 4
SIZES_AT = 4
REQUESTS_AT = 8


def attention_scratch(block_rows, heads, fresh_rows, slots):
    stacked = heads * block_rows
    return [
        pltpu.VMEM((stacked, fresh_rows + slots * PAGE), F32),
        pltpu.VMEM((stacked, HEAD_DIM), F32),
        pltpu.VMEM((stacked, HEAD_DIM), F32),
        pltpu.VMEM((slots * PAGE, 2 * HEAD_DIM), BF16),
        pltpu.SMEM((slots,), jnp.int32),
    ]


def attend_block(place_ref, q, first_row, fresh, pulled, scratch):
    scores, total_ref, mixed_ref, cache, labels = scratch
    me = place_ref[0]
    block_rows, width = q.shape
    heads = width // HEAD_DIM
    stacked = heads * block_rows
    groups, per = pulled.shape[:2]
    tensors = 4
    slots = per // tensors
    wide = PAGES_STEP * PAGE
    factor = math.log2(math.e) / math.sqrt(HEAD_DIM)
    bound = []
    running = jnp.int32(0)
    for k in range(REQUESTS):
        running = running + place_ref[SIZES_AT + k] * UNIT
        bound.append(running)

    def segment_of(position):
        return sum((position >= b).astype(jnp.int32) for b in bound)

    lowest = segment_of(first_row)
    highest = segment_of(first_row + block_rows - 1)
    count = jnp.int32(0)
    for g in range(groups):
        for p in range(per):
            owner = g * tensors + jnp.bitwise_xor(me, p // slots)
            label = place_ref[REQUESTS_AT + p % slots * groups * tensors + owner]
            wanted = (label >= lowest) & (label <= highest)

            @pl.when(wanted)
            def _():
                cache[pl.ds(pl.multiple_of(count * PAGE, PAGE), PAGE), :] = pulled[g, p]
                labels[count] = label

            count = count + wanted.astype(jnp.int32)
    steps = (count + PAGES_STEP - 1) // PAGES_STEP
    for k in range(PAGES_STEP - 1):

        @pl.when(count + k < steps * PAGES_STEP)
        def _():
            cache[pl.ds(pl.multiple_of((count + k) * PAGE, PAGE), PAGE), :] = jnp.zeros(
                (PAGE, 2 * HEAD_DIM), BF16
            )
            labels[count + k] = jnp.int32(-1)

    q_rows = jnp.concatenate([q[:, h * HEAD_DIM : (h + 1) * HEAD_DIM] for h in range(heads)], axis=0)
    row_position = first_row + lax.broadcasted_iota(jnp.int32, (block_rows, 1), 0)
    row_segment = segment_of(row_position)

    def masked_scores(keys, allowed):
        raw = lax.dot_general(q_rows, keys, (((1,), (1,)), ((), ())), preferred_element_type=F32)
        n = keys.shape[0]
        return jnp.where(allowed[None], raw.reshape(heads, block_rows, n), NEG_FILL).reshape(
            stacked, n
        )

    def fold(values, combine):
        pieces = [values[:, i : i + HEAD_DIM] for i in range(0, values.shape[1], HEAD_DIM)]
        result = pieces[0]
        for piece in pieces[1:]:
            result = combine(result, piece)
        return result

    new = jnp.concatenate([rows for rows, _ in fresh], axis=0)
    fresh_rows = new.shape[0]
    key_position = jnp.concatenate(
        [
            base + lax.broadcasted_iota(jnp.int32, (1, rows.shape[0]), 1)
            for rows, base in fresh
        ],
        axis=1,
    )
    allowed = (row_segment == segment_of(key_position)) & (key_position <= row_position)
    masked = masked_scores(new[:, :HEAD_DIM], allowed)
    scores[:, :fresh_rows] = masked
    total_ref[...] = fold(masked, jnp.maximum)
    lanes = lax.broadcasted_iota(jnp.int32, (1, wide), 1) // PAGE

    def add_scores(g, carry):
        label = jnp.full((1, wide), -1, jnp.int32)
        for j in range(PAGES_STEP):
            label = jnp.where(lanes == j, labels[g * PAGES_STEP + j], label)
        keys = cache[pl.ds(pl.multiple_of(g * wide, wide), wide), :HEAD_DIM]
        masked = masked_scores(keys, row_segment == label)
        scores[:, pl.ds(pl.multiple_of(fresh_rows + g * wide, PAGE), wide)] = masked
        total_ref[...] = jnp.maximum(total_ref[...], fold(masked, jnp.maximum))
        return carry

    lax.fori_loop(0, steps, add_scores, 0)
    top = jnp.max(total_ref[...], axis=1, keepdims=True) * factor
    probs = jnp.exp2(scores[:, :fresh_rows] * factor - top)
    total_ref[...] = fold(probs, jnp.add)
    mixed_ref[...] = jnp.dot(probs.astype(BF16), new[:, HEAD_DIM:], preferred_element_type=F32)

    def add_values(g, carry):
        part = scores[:, pl.ds(pl.multiple_of(fresh_rows + g * wide, PAGE), wide)]
        probs = jnp.exp2(part * factor - top)
        values = cache[pl.ds(pl.multiple_of(g * wide, wide), wide), HEAD_DIM:]
        total_ref[...] += fold(probs, jnp.add)
        mixed_ref[...] += jnp.dot(probs.astype(BF16), values, preferred_element_type=F32)
        return carry

    lax.fori_loop(0, steps, add_values, 0)
    denominator = jnp.sum(total_ref[...], axis=1, keepdims=True)
    result = (mixed_ref[...] / denominator).astype(BF16)
    return jnp.concatenate(
        [result[h * block_rows : (h + 1) * block_rows] for h in range(heads)], axis=1
    )


def project_held(near, far, w_query, w_keyvalue, after):
    rows, half = near.shape
    steps, depth, q_width = w_query.shape
    kv_width = w_keyvalue.shape[2]

    def kernel(near_ref, far_ref, wq, wkv, *refs):
        q_ref, kv_ref = refs[len(after) :]
        for w, out in ((wq, q_ref), (wkv, kv_ref)):
            total = None
            for j in range(steps):
                x_ref = near_ref if j < steps // 2 else far_ref
                x = x_ref[:, (j % (steps // 2)) * depth : (j % (steps // 2) + 1) * depth]
                part = jnp.dot(x, w[j], preferred_element_type=F32)
                total = part if j == 0 else total + part
            out[...] = total.astype(BF16)

    return pl.pallas_call(
        kernel,
        in_specs=[VMEM] * 4 + [ANY] * len(after),
        out_specs=[VMEM] * 2,
        out_shape=[shape((rows, q_width)), shape((rows, kv_width))],
        compiler_params=params(6),
        cost_estimate=SMALL,
        name="project_held",
    )(near, far, w_query, w_keyvalue, *after)


def project_far(place, near, far, w_query, w_keyvalue, after):
    rows, half = near.shape
    q_width, kv_width = w_query.shape[1], w_keyvalue.shape[1]
    steps = 8
    depth = 2 * half // steps

    def kernel(place_ref, near_ref, far_ref, wq, wkv, *refs):
        q_ref, kv_ref, wq_buf, wkv_buf, sems = refs[len(after) :]
        stream = weight_stream(place_ref[1], half, steps, (wq, wkv), (wq_buf, wkv_buf), sems)
        for j in range(steps):
            for copy in stream(j):
                copy.start()
        q_sum = kv_sum = None
        for j in range(steps):
            for copy in stream(j):
                copy.wait()
            x_ref = near_ref if j < steps // 2 else far_ref
            x = x_ref[:, (j % (steps // 2)) * depth : (j % (steps // 2) + 1) * depth]
            q_part = jnp.dot(x, wq_buf[j], preferred_element_type=F32)
            kv_part = jnp.dot(x, wkv_buf[j], preferred_element_type=F32)
            q_sum = q_part if j == 0 else q_sum + q_part
            kv_sum = kv_part if j == 0 else kv_sum + kv_part
        q_ref[...] = q_sum.astype(BF16)
        kv_ref[...] = kv_sum.astype(BF16)

    return pl.pallas_call(
        kernel,
        in_specs=[SMEM] + [VMEM] * 2 + [HBM] * 2 + [ANY] * len(after),
        out_specs=[VMEM] * 2,
        out_shape=[shape((rows, q_width)), shape((rows, kv_width))],
        scratch_shapes=[
            pltpu.VMEM((steps, depth, q_width), BF16),
            pltpu.VMEM((steps, depth, kv_width), BF16),
            pltpu.SemaphoreType.DMA((2 * steps,)),
        ],
        compiler_params=params(32),
        cost_estimate=SMALL,
        name="project_far",
    )(place, near, far, w_query, w_keyvalue, *after)


def attend_out(place, query, fresh, bases, base, pulled, w_out):
    rows, depth = query.shape
    width = w_out.shape[1]
    half = width // 2
    heads = depth // HEAD_DIM
    out_steps = 4
    wide = half // out_steps
    known = len(fresh)
    count = sum(f.shape[0] for f in fresh)
    fresh_rows = -(-count // HEAD_DIM) * HEAD_DIM
    pad = fresh_rows - count

    def kernel(place_ref, q_ref, pulled_ref, *refs):
        fresh_refs = refs[:known]
        wo, there_ref, stay_ref, wo_buf, q_buf, sems = refs[known : known + 6]
        core, side = place_ref[1], place_ref[2]

        def copy(j):
            first = 1 - core if j < out_steps else core
            start = pl.multiple_of(first * half + (j % out_steps) * wide, wide)
            return pltpu.make_async_copy(wo.at[:, pl.ds(start, wide)], wo_buf.at[j], sems.at[j])

        q_copy = pltpu.make_async_copy(q_ref, q_buf, sems.at[2 * out_steps])
        q_copy.start()
        for j in range(2 * out_steps):
            copy(j).start()
        q_copy.wait()
        pairs = [(ref[...], at(side)) for ref, at in zip(fresh_refs, bases)]
        if pad:
            pairs.append((jnp.zeros((pad, 2 * HEAD_DIM), BF16), jnp.int32(1 << 20)))
        mixed = attend_block(
            place_ref, q_buf[...], base(side), pairs, pulled_ref, refs[known + 6 :]
        )
        for j in range(2 * out_steps):
            copy(j).wait()
            out_ref = there_ref if j < out_steps else stay_ref
            at = (j % out_steps) * wide
            out_ref[:, at : at + wide] = jnp.dot(
                mixed, wo_buf[j], preferred_element_type=F32
            ).astype(BF16)

    return pl.pallas_call(
        kernel,
        in_specs=[SMEM, HBM] + [VMEM] * (1 + known) + [HBM],
        out_specs=[VMEM] * 2,
        out_shape=[shape((rows, half)), shape((rows, half))],
        scratch_shapes=[
            pltpu.VMEM((2 * out_steps, depth, wide), BF16),
            pltpu.VMEM((rows, depth), BF16),
            pltpu.SemaphoreType.DMA((2 * out_steps + 1,)),
        ]
        + attention_scratch(rows, heads, fresh_rows, pulled.shape[0] * pulled.shape[1]),
        compiler_params=params(30),
        cost_estimate=SMALL,
        name="attend_out",
    )(place, query, pulled, *fresh, w_out)


def local_rows(place, query, fresh, bases, base, pulled, w_out, after):
    both, depth = query.shape
    rows = both // 2
    width = w_out.shape[1]
    heads = depth // HEAD_DIM
    steps = 8
    wide = width // steps
    known = len(fresh)
    fresh_rows = sum(f.shape[0] for f in fresh)

    def kernel(place_ref, q_ref, pulled_ref, *refs):
        fresh_refs = refs[:known]
        wo = refs[known]
        rest = refs[known + 1 + len(after) :]
        own_ref, peer_ref, wo_buf, a_buf, sems = rest[:5]
        core, side = place_ref[1], place_ref[2]

        def out_copy(j):
            return pltpu.make_async_copy(
                wo.at[:, j * wide : (j + 1) * wide], wo_buf.at[j], sems.at[j]
            )

        for j in range(steps):
            out_copy(j).start()

        def block(b, carry):
            at = pl.ds(pl.multiple_of(b * rows, rows), rows)
            a_buf[at, :] = attend_block(
                place_ref,
                q_ref[at, :],
                base(side) + b * rows,
                [(ref[...], first(side)) for ref, first in zip(fresh_refs, bases)],
                pulled_ref,
                rest[5:],
            )
            return carry

        lax.fori_loop(0, 2, block, 0)
        own_at = pl.ds(pl.multiple_of(core * rows, rows), rows)
        peer_at = pl.ds(pl.multiple_of((1 - core) * rows, rows), rows)
        a = jnp.concatenate([a_buf[own_at, :], a_buf[peer_at, :]], axis=0)
        for j in range(steps):
            out_copy(j).wait()
            part = jnp.dot(a, wo_buf[j], preferred_element_type=F32).astype(BF16)
            own_ref[:, j * wide : (j + 1) * wide] = part[:rows]
            peer_ref[:, j * wide : (j + 1) * wide] = part[rows:]

    return pl.pallas_call(
        kernel,
        in_specs=[SMEM] + [VMEM] * (2 + known) + [HBM] + [ANY] * len(after),
        out_specs=[VMEM, VMEM],
        out_shape=[shape((rows, width)), shape((rows, width))],
        scratch_shapes=[
            pltpu.VMEM((steps, depth, wide), BF16),
            pltpu.VMEM((both, depth), BF16),
            pltpu.SemaphoreType.DMA((steps,)),
        ]
        + attention_scratch(rows, heads, fresh_rows, pulled.shape[0] * pulled.shape[1]),
        compiler_params=params(40),
        cost_estimate=SMALL,
        name="local_rows",
    )(place, query, pulled, *fresh, w_out, *after)


def add_pair(left, right):
    rows, width = left.shape
    step = 16

    def kernel(left_ref, right_ref, out_ref):
        def block(i, carry):
            at = pl.ds(pl.multiple_of(i * step, step), step)
            out_ref[at, :] = (left_ref[at, :].astype(F32) + right_ref[at, :].astype(F32)).astype(
                BF16
            )
            return carry

        lax.fori_loop(0, rows // step, block, 0)

    return pl.pallas_call(
        kernel,
        in_specs=[VMEM, VMEM],
        out_specs=VMEM,
        out_shape=shape((rows, width)),
        compiler_params=params(8),
        cost_estimate=SMALL,
        name="add_pair",
    )(left, right)


def finish(place, tokens, own, peer, near, far):
    rows, width = tokens.shape
    half = width // 2
    step = 16

    def kernel(place_ref, x_ref, own_ref, peer_ref, near_ref, far_ref, out_ref):
        core = place_ref[1]

        def block(i, carry):
            at = pl.ds(pl.multiple_of(i * step, step), step)
            for start, part in ((core, near_ref), (1 - core, far_ref)):
                cols = pl.ds(pl.multiple_of(start * half, half), half)
                local = own_ref[at, cols].astype(F32) + peer_ref[at, cols].astype(F32)
                total = local + part[at, :].astype(F32)
                out_ref[at, cols] = (x_ref[at, cols].astype(F32) + total).astype(BF16)
            return carry

        lax.fori_loop(0, rows // step, block, 0)

    return pl.pallas_call(
        kernel,
        in_specs=[SMEM] + [VMEM] * 5,
        out_specs=VMEM,
        out_shape=shape((rows, width)),
        compiler_params=params(16),
        cost_estimate=SMALL,
        name="finish",
    )(place, tokens, own, peer, near, far)


def pick_pages(place, wanted, held, after):
    replicas = len(wanted)
    slots = wanted[0].shape[2]
    tensors = len(held)
    _, page, width = held[0].shape
    total = tensors * slots

    def kernel(place_ref, *refs):
        wants, sources = refs[:replicas], refs[replicas : replicas + tensors]
        out_ref, sems = refs[replicas + tensors + len(after) :]
        me, rep = place_ref[0], place_ref[3]

        def copies():
            for k in range(replicas):
                asker = lax.rem(rep + k, replicas)
                for i in range(tensors):
                    owner = rep * tensors + jnp.bitwise_xor(me, i)
                    for s in range(slots):
                        at = i * slots + s
                        yield pltpu.make_async_copy(
                            sources[i].at[wants[k][0, owner, s]],
                            out_ref.at[asker, at],
                            sems.at[k * total + at],
                        )

        for copy in copies():
            copy.start()
        for copy in copies():
            copy.wait()

    return pl.pallas_call(
        kernel,
        in_specs=[SMEM] * (1 + replicas) + [ANY] * (tensors + len(after)),
        out_specs=ANY,
        out_shape=shape((replicas, total, page, width)),
        scratch_shapes=[pltpu.SemaphoreType.DMA((replicas * total,))],
        compiler_params=params(8),
        cost_estimate=SMALL,
        name="pick_pages",
    )(place, *wanted, *held, *after)


def write_pool(place, slots, kv_pool, own, core_new, y_new):
    pages, heads = kv_pool.shape[:2]
    new_count = slots.shape[1]
    side_pages = new_count // 2

    def kernel(place_ref, slot_ref, pool_ref, own_ref, core_ref, y_ref, out_ref, sems):
        me, side = place_ref[0], place_ref[2]
        sources = (own_ref, core_ref.at[0], y_ref, core_ref.at[1])
        for p in range(pages):
            found = jnp.int32(-1)
            for j in range(new_count):
                found = jnp.where(slot_ref[0, j] == me * pages + p, j, found)
            far = (found >= side_pages).astype(jnp.int32)
            inner = jnp.maximum(found - far * side_pages, 0)

            @pl.when(found >= 0)
            def _():
                for i in range(heads):
                    origin = side if i < 2 else 1 - side
                    start = (jnp.bitwise_xor(far, origin) * side_pages + inner) * PAGE
                    pltpu.make_async_copy(
                        sources[i].at[pl.ds(pl.multiple_of(start, PAGE), PAGE)],
                        out_ref.at[p, jnp.bitwise_xor(me, i)],
                        sems.at[p * heads + i],
                    ).start()

            @pl.when(found < 0)
            def _():
                for i in range(heads):
                    at = jnp.bitwise_xor(me, i)
                    pltpu.make_async_copy(
                        pool_ref.at[p, at], out_ref.at[p, at], sems.at[p * heads + i]
                    ).start()

        for p in range(pages):
            for i in range(heads):
                at = jnp.bitwise_xor(me, i)
                pltpu.make_async_copy(
                    pool_ref.at[p, at], out_ref.at[p, at], sems.at[p * heads + i]
                ).wait()

    return pl.pallas_call(
        kernel,
        in_specs=[SMEM, SMEM] + [ANY] * 4,
        out_specs=ANY,
        out_shape=shape(kv_pool.shape),
        scratch_shapes=[pltpu.SemaphoreType.DMA((pages * heads,))],
        compiler_params=params(8),
        cost_estimate=SMALL,
        name="write_pool",
    )(place, slots, kv_pool, own, core_new, y_new)


def chip_pair_body(
    tokens,
    gain,
    w_query,
    w_keyvalue,
    w_out,
    kv_pool,
    suffix_pages,
    page_index,
    page_request,
    new_slot,
):
    replicas = lax.axis_size("replica")
    me = lax.axis_index("tensor")
    core = me % 2
    side = me // 2
    rows = tokens.shape[0]
    rep = lax.axis_index("replica")
    place = jnp.stack([me, core, side, rep]).astype(jnp.int32)
    requests = jnp.swapaxes(page_request, 1, 2).reshape(-1)
    scalars = in_hbm(jnp.concatenate([place, suffix_pages[0], requests]))

    def over_core(x):
        return lax.ppermute(x, "tensor", [(0, 1), (1, 0), (2, 3), (3, 2)])

    def over_y(x):
        return lax.ppermute(x, "tensor", [(0, 2), (2, 0), (1, 3), (3, 1)])

    def to_replicas(x):
        return lax.all_to_all(x, "replica", split_axis=0, concat_axis=0, tiled=True)

    def tie(x, *others):
        return lax.optimization_barrier((x, *others))[0]

    w_query, w_keyvalue, w_out = in_hbm(w_query), in_hbm(w_keyvalue), in_hbm(w_out)

    wanted = [page_index]
    for k in range(1, replicas):
        back = [(i, (i - k) % replicas) for i in range(replicas)]
        wanted.append(lax.ppermute(page_index, "replica", back))

    mine, other, *held = prepare(place, in_hbm(tokens), in_hbm(gain), in_hbm(kv_pool))
    for i in range(1, 4):
        held[i] = lax.ppermute(held[i], "tensor", [(t, t ^ i) for t in range(4)])

    peer_near = over_core(other)
    peer_far = over_core(mine)
    is_first = core == 0
    first_half = jnp.where(is_first, mine, peer_near)
    second_half = jnp.where(is_first, peer_near, mine)
    first = over_y(first_half)
    second = over_y(second_half)

    picked = pick_pages(place, wanted, held, [first_half, second_half])
    pulled = to_replicas(picked)

    q_local, kv_local, wq, wkv = project_local(
        place, [mine, peer_near], [other, peer_far], w_query, w_keyvalue, [picked, scalars]
    )

    q_local = in_hbm(q_local)

    def local_base(s):
        return s * (2 * rows)

    def first_base(s):
        return (1 - s) * (2 * rows)

    def second_base(s):
        return (1 - s) * (2 * rows) + rows

    first = tie(first, q_local)
    q_first, kv_first = project_held(first, over_core(first), wq, wkv, [])
    q_first = in_hbm(q_first)
    there, stay = attend_out(
        scalars, q_first, [kv_local, kv_first],
        [local_base, first_base], first_base, pulled, w_out,
    )
    there = tie(there, second)
    first_mix = add_pair(stay, over_core(there))
    first_sum = over_y(first_mix)

    second = tie(second, first_mix)
    q_second, kv_second = project_far(place, second, over_core(second), w_query, w_keyvalue, [])
    fresh = [kv_local, kv_first, kv_second]
    bases = [local_base, first_base, second_base]
    there, stay = attend_out(
        scalars, q_second, fresh, bases, second_base, pulled, w_out
    )
    there = tie(there, first_sum)
    second_mix = add_pair(stay, over_core(there))


    new_own = jnp.concatenate(fresh, axis=0)
    y_new = over_y(new_own)
    core_new = over_core(jnp.stack([new_own, y_new]))
    second_sum = over_y(tie(second_mix, y_new))

    pool_out = write_pool(place, new_slot, kv_pool, new_own, core_new, y_new)

    own_part, peer_part = local_rows(
        scalars, q_local, fresh, bases, local_base, pulled, w_out,
        [second_mix, pool_out],
    )
    peer_part = over_core(peer_part)

    near = jnp.where(is_first, first_sum, second_sum)
    far = over_core(jnp.where(is_first, second_sum, first_sum))
    layer_out = finish(place, tokens, own_part, peer_part, near, far)
    return (layer_out, pool_out)


def solution(mesh):
    pair = mesh.shape["tensor"] == KV_HEADS
    return jax.shard_map(
        chip_pair_body if pair else gathered_body,
        mesh=mesh,
        in_specs=(
            P(("groups", "replica", "tensor"), None),
            P(),
            P(None, "tensor"),
            P(None, "tensor"),
            P("tensor", None),
            P(("groups", "replica", "tensor"), None, None, None),
            P(("groups", "replica"), None),
            P(("groups", "replica"), None, None),
            P(("groups", "replica"), None, None),
            P(("groups", "replica"), None),
        ),
        out_specs=(
            P(("groups", "replica", "tensor"), None),
            P(("groups", "replica", "tensor"), None, None, None),
        ),
        check_vma=False,
    )
```

```python
import math

import jax
import jax.numpy as jnp
from jax import lax
from jax.experimental import pallas as pl
from jax.experimental.pallas import tpu as pltpu
from jax.sharding import PartitionSpec as P

KV_HEADS = 4
HEAD_DIM = 128
PAGE = 64
UNIT = 8


NEG_FILL = -1e30
EPSILON = 1e-06

F32 = jnp.float32
BF16 = jnp.bfloat16
MIB = 1 << 20
ANY = pl.BlockSpec(memory_space=pl.ANY)
HBM = pl.BlockSpec(memory_space=pltpu.HBM)
SMEM = pl.BlockSpec(memory_space=pltpu.SMEM)
VMEM = pl.BlockSpec(memory_space=pltpu.VMEM)
SMALL = pl.CostEstimate(flops=1024, bytes_accessed=1024, transcendentals=0)
LARGE = pl.CostEstimate(flops=20000000000, bytes_accessed=200000000, transcendentals=0)


def params(mib):
    return pltpu.CompilerParams(vmem_limit_bytes=mib * MIB)


def in_hbm(x):
    return pltpu.with_memory_space_constraint(x, pltpu.HBM)


def shape(dims, dtype=BF16):
    return jax.ShapeDtypeStruct(dims, dtype)


def normalize(rows, gain):
    values = rows.astype(jnp.float32)
    inverse = lax.rsqrt(jnp.mean(values * values, axis=-1, keepdims=True) + EPSILON)
    return (values * inverse * gain.astype(jnp.float32)).astype(jnp.bfloat16)


def row_segments(pages, total_rows):
    bounds = jnp.cumsum(pages) * UNIT
    positions = jnp.arange(total_rows, dtype=jnp.int32)
    return jnp.sum((positions[:, None] >= bounds[None, :]).astype(jnp.int32), axis=1)


def gathered_body(
    tokens,
    gain,
    w_query,
    w_keyvalue,
    w_out,
    kv_pool,
    suffix_pages,
    page_index,
    page_request,
    new_slot,
):
    replicas = lax.axis_size("replica")
    tensors = lax.axis_size("tensor")
    owners = replicas * tensors
    position = lax.axis_index("tensor")
    query_width = w_query.shape[1]
    local_heads = query_width // HEAD_DIM
    share = tensors // KV_HEADS
    my_head = position // share
    scale_factor = 1.0 / math.sqrt(HEAD_DIM)
    normed = normalize(tokens, gain)
    piece = lax.all_gather(normed, "tensor", axis=0, tiled=True)
    first = jnp.dot(piece, w_query, preferred_element_type=jnp.float32)
    second = jnp.dot(piece, w_keyvalue, preferred_element_type=jnp.float32)
    projected = jnp.concatenate([first, second], axis=1).astype(jnp.bfloat16)
    query = projected[:, :query_width]
    keyvalue = lax.all_gather(projected[:, query_width:], "tensor", axis=1, tiled=True)
    total_rows = query.shape[0]
    wanted = lax.all_to_all(
        page_index[0], ("replica", "tensor"), split_axis=0, concat_axis=0, tiled=True
    )
    slot_count = wanted.shape[1]
    sources = jnp.arange(owners, dtype=jnp.int32) % tensors
    source_heads = sources // share
    flat_pool = kv_pool.reshape(kv_pool.shape[0] * KV_HEADS, PAGE, 2 * HEAD_DIM)
    outgoing = flat_pool[wanted * KV_HEADS + source_heads[:, None]]
    sub_tokens = outgoing.shape[2]
    pulled = lax.all_to_all(
        outgoing, ("replica", "tensor"), split_axis=0, concat_axis=0, tiled=True
    )
    segments = row_segments(suffix_pages[0], total_rows)
    key_groups = page_request[0]
    stacked = (
        query.reshape(total_rows, local_heads, HEAD_DIM)
        .transpose(1, 0, 2)
        .reshape(local_heads * total_rows, HEAD_DIM)
    )
    own_new = lax.dynamic_index_in_dim(
        keyvalue.reshape(total_rows, KV_HEADS, 2 * HEAD_DIM), my_head, 1, keepdims=False
    )
    row_order = jnp.arange(total_rows, dtype=jnp.int32)
    causal = (segments[:, None] == segments[None, :]) & (row_order[None, :] <= row_order[:, None])

    def block_scores(queries, head_count, keys, allowed):
        raw = (
            jnp.dot(queries, keys[:, :HEAD_DIM].T, preferred_element_type=jnp.float32)
            * scale_factor
        )
        raw = raw.reshape(head_count, total_rows, keys.shape[0])
        return jnp.where(allowed[None], raw, NEG_FILL)

    first_scores = block_scores(stacked, local_heads, own_new, causal)
    running = jnp.max(first_scores, axis=2)
    probs = jnp.exp(first_scores - running[:, :, None])
    denominator = jnp.sum(probs, axis=2)
    numerator = jnp.dot(
        probs.astype(jnp.bfloat16).reshape(local_heads * total_rows, total_rows),
        own_new[:, HEAD_DIM:],
        preferred_element_type=jnp.float32,
    )
    block_owners = 16
    blocks = owners // block_owners

    def absorb(step, state):
        peak, total, mixed = state
        pages = lax.dynamic_slice_in_dim(pulled, step * block_owners, block_owners, 0)
        keys = pages.reshape(block_owners * slot_count * sub_tokens, 2 * HEAD_DIM)
        labels = lax.dynamic_slice_in_dim(key_groups, step * block_owners, block_owners, 0).reshape(
            -1
        )
        matches = (segments[:, None] == labels[None, :])[:, :, None]
        allowed = jnp.broadcast_to(matches, (total_rows, labels.shape[0], sub_tokens)).reshape(
            total_rows, labels.shape[0] * sub_tokens
        )
        scores = block_scores(stacked, local_heads, keys, allowed)
        updated = jnp.maximum(peak, jnp.max(scores, axis=2))
        rescale = jnp.exp(peak - updated)
        weights = jnp.where(allowed[None], jnp.exp(scores - updated[:, :, None]), 0.0)
        total = total * rescale + jnp.sum(weights, axis=2)
        flat_weights = weights.astype(jnp.bfloat16).reshape(local_heads * total_rows, keys.shape[0])
        mixed = mixed * rescale.reshape(-1)[:, None] + jnp.dot(
            flat_weights, keys[:, HEAD_DIM:], preferred_element_type=jnp.float32
        )
        return (updated, total, mixed)

    running, denominator, numerator = lax.fori_loop(
        0, blocks, absorb, (running, denominator, numerator)
    )
    attention = (numerator / denominator.reshape(-1)[:, None]).astype(jnp.bfloat16)
    attention = (
        attention.reshape(local_heads, total_rows, HEAD_DIM)
        .transpose(1, 0, 2)
        .reshape(total_rows, query_width)
    )
    summed = lax.psum_scatter(
        jnp.dot(attention, w_out, preferred_element_type=jnp.float32).astype(jnp.bfloat16),
        "tensor",
        scatter_dimension=0,
        tiled=True,
    ).astype(jnp.float32)
    layer_out = (tokens.astype(jnp.float32) + summed).astype(jnp.bfloat16)
    new_count = total_rows // PAGE
    fresh = (
        keyvalue.reshape(new_count, PAGE, KV_HEADS, 2 * HEAD_DIM)
        .transpose(0, 2, 1, 3)
        .reshape(new_count, KV_HEADS * PAGE * 2 * HEAD_DIM)
    )
    local_pages = kv_pool.shape[0]
    targets = position * local_pages + jnp.arange(local_pages, dtype=jnp.int32)
    match_table = new_slot[0][None, :] == targets[:, None]
    placed = jnp.dot(
        match_table.astype(jnp.bfloat16), fresh, preferred_element_type=jnp.float32
    ).astype(jnp.bfloat16)
    placed = placed.reshape(kv_pool.shape)
    landed = jnp.any(match_table, axis=1)
    pool_out = jnp.where(landed[:, None, None, None], placed, kv_pool)
    return (layer_out, pool_out)


def prepare(place, tokens, gain, kv_pool):
    rows, width = tokens.shape
    half = width // 2
    step = 32
    pages, heads = kv_pool.shape[:2]
    blocks = rows // step

    def kernel(place_ref, x, g, pool, mine_ref, other_ref, *refs):
        held, (x_buf, g_buf, pool_buf, sems) = refs[:heads], refs[heads:]
        me, core = place_ref[0], place_ref[1]
        pool_copy = pltpu.make_async_copy(pool, pool_buf, sems.at[blocks + 1])

        def row_copy(b):
            at = pl.ds(b * step, step)
            return pltpu.make_async_copy(x.at[at], x_buf.at[at], sems.at[b])

        gain_copy = pltpu.make_async_copy(g, g_buf, sems.at[blocks])
        row_copy(0).start()
        gain_copy.start()
        for b in range(1, blocks):
            row_copy(b).start()
        pool_copy.start()
        near = pl.multiple_of(core * half, half)
        far = pl.multiple_of((1 - core) * half, half)
        for b in range(blocks):
            row_copy(b).wait()
            if b == 0:
                gain_copy.wait()

            def block(i, carry):
                at = pl.ds(pl.multiple_of(b * step + i * 16, 16), 16)
                total = jnp.zeros((16, 1), F32)
                for part in range(2):
                    values = x_buf[at, part * half : (part + 1) * half].astype(F32)
                    total += jnp.sum(values * values, axis=1, keepdims=True)
                inverse = lax.rsqrt(total * (1.0 / width) + EPSILON)
                for start, out in ((near, mine_ref), (far, other_ref)):
                    cols = pl.ds(start, half)
                    values = x_buf[at, cols].astype(F32)
                    out[at, :] = (values * inverse * g_buf[cols].astype(F32)[None, :]).astype(BF16)
                return carry

            lax.fori_loop(0, step // 16, block, 0)
        pool_copy.wait()
        for i in range(heads):
            for p in range(pages):
                held[i][p] = pool_buf[p, jnp.bitwise_xor(me, i)]

    return pl.pallas_call(
        kernel,
        in_specs=[SMEM] + [HBM] * 3,
        out_specs=[VMEM] * (2 + heads),
        out_shape=[shape((rows, half))] * 2 + [shape((pages,) + kv_pool.shape[2:])] * heads,
        scratch_shapes=[
            pltpu.VMEM((rows, width), BF16),
            pltpu.VMEM((width,), BF16),
            pltpu.VMEM(kv_pool.shape, BF16),
            pltpu.SemaphoreType.DMA((blocks + 2,)),
        ],
        compiler_params=params(16),
        cost_estimate=SMALL,
        name="prepare",
    )(place, tokens, gain, kv_pool)


def project_local(place, near, far, w_query, w_keyvalue, after):
    rows, half = near[0].shape
    q_width, kv_width = w_query.shape[1], w_keyvalue.shape[1]
    steps = 8
    depth = 2 * half // steps
    waits = len(after)

    def kernel(place_ref, near_own, near_peer, far_own, far_peer, wq, wkv, *refs):
        q_ref, kv_ref, wq_buf, wkv_buf, q_acc, kv_acc, sems = refs[waits:]
        core = place_ref[1]
        stream = weight_stream(core, half, steps, (wq, wkv), (wq_buf, wkv_buf), sems)
        for j in range(steps):
            for copy in stream(j):
                copy.start()
        for j in range(steps):
            for copy in stream(j):
                copy.wait()
            group = (near_own, near_peer) if j < steps // 2 else (far_own, far_peer)
            cols = slice((j % (steps // 2)) * depth, (j % (steps // 2) + 1) * depth)
            x = jnp.concatenate([ref[:, cols] for ref in group], axis=0)
            q_part = jnp.dot(x, wq_buf[j], preferred_element_type=F32)
            kv_part = jnp.dot(x, wkv_buf[j], preferred_element_type=F32)
            if j == 0:
                q_acc[...] = q_part
                kv_acc[...] = kv_part
            elif j < steps - 1:
                q_acc[...] += q_part
                kv_acc[...] += kv_part
            else:
                q_last = (q_acc[...] + q_part).astype(BF16)
                kv_last = (kv_acc[...] + kv_part).astype(BF16)
        for b in range(2):
            at = pl.ds(pl.multiple_of((core if b == 0 else 1 - core) * rows, rows), rows)
            q_ref[at, :] = q_last[b * rows : (b + 1) * rows]
            kv_ref[at, :] = kv_last[b * rows : (b + 1) * rows]

    total = 2 * rows
    return pl.pallas_call(
        kernel,
        in_specs=[SMEM] + [VMEM] * 4 + [HBM] * 2 + [ANY] * waits,
        out_specs=[VMEM] * 4,
        out_shape=[
            shape((total, q_width)),
            shape((total, kv_width)),
            pltpu.VMEM((steps, depth, q_width), BF16),
            pltpu.VMEM((steps, depth, kv_width), BF16),
        ],
        scratch_shapes=[
            pltpu.VMEM((total, q_width), F32),
            pltpu.VMEM((total, kv_width), F32),
            pltpu.SemaphoreType.DMA((2 * steps,)),
        ],
        compiler_params=params(10),
        cost_estimate=LARGE,
        name="project_local",
    )(place, *near, *far, w_query, w_keyvalue, *after)


def weight_stream(core, half, steps, sources, buffers, sems):
    depth = 2 * half // steps

    def copies(j):
        base = core if j < steps // 2 else 1 - core
        start = pl.multiple_of(base * half + (j % (steps // 2)) * depth, depth)
        count = len(sources)
        return [
            pltpu.make_async_copy(w.at[pl.ds(start, depth)], buf.at[j], sems.at[count * j + i])
            for i, (w, buf) in enumerate(zip(sources, buffers))
        ]

    return copies


PAGES_STEP = 4
REQUESTS = 4
SIZES_AT = 4
REQUESTS_AT = 8


def attention_scratch(block_rows, heads, fresh_rows, slots):
    stacked = heads * block_rows
    return [
        pltpu.VMEM((stacked, fresh_rows + slots * PAGE), F32),
        pltpu.VMEM((stacked, HEAD_DIM), F32),
        pltpu.VMEM((stacked, HEAD_DIM), F32),
        pltpu.VMEM((slots * PAGE, 2 * HEAD_DIM), BF16),
        pltpu.SMEM((slots,), jnp.int32),
    ]


def attend_block(place_ref, q, first_row, fresh, pulled, scratch):
    scores, total_ref, mixed_ref, cache, labels = scratch
    me = place_ref[0]
    block_rows, width = q.shape
    heads = width // HEAD_DIM
    stacked = heads * block_rows
    groups, per = pulled.shape[:2]
    tensors = 4
    slots = per // tensors
    wide = PAGES_STEP * PAGE
    factor = math.log2(math.e) / math.sqrt(HEAD_DIM)
    bound = []
    running = jnp.int32(0)
    for k in range(REQUESTS):
        running = running + place_ref[SIZES_AT + k] * UNIT
        bound.append(running)

    def segment_of(position):
        return sum((position >= b).astype(jnp.int32) for b in bound)

    lowest = segment_of(first_row)
    highest = segment_of(first_row + block_rows - 1)
    count = jnp.int32(0)
    for g in range(groups):
        for p in range(per):
            owner = g * tensors + jnp.bitwise_xor(me, p // slots)
            label = place_ref[REQUESTS_AT + p % slots * groups * tensors + owner]
            wanted = (label >= lowest) & (label <= highest)

            @pl.when(wanted)
            def _():
                cache[pl.ds(pl.multiple_of(count * PAGE, PAGE), PAGE), :] = pulled[g, p]
                labels[count] = label

            count = count + wanted.astype(jnp.int32)
    steps = (count + PAGES_STEP - 1) // PAGES_STEP
    for k in range(PAGES_STEP - 1):

        @pl.when(count + k < steps * PAGES_STEP)
        def _():
            cache[pl.ds(pl.multiple_of((count + k) * PAGE, PAGE), PAGE), :] = jnp.zeros(
                (PAGE, 2 * HEAD_DIM), BF16
            )
            labels[count + k] = jnp.int32(-1)

    q_rows = jnp.concatenate([q[:, h * HEAD_DIM : (h + 1) * HEAD_DIM] for h in range(heads)], axis=0)
    row_position = first_row + lax.broadcasted_iota(jnp.int32, (block_rows, 1), 0)
    row_segment = segment_of(row_position)

    def masked_scores(keys, allowed):
        raw = lax.dot_general(q_rows, keys, (((1,), (1,)), ((), ())), preferred_element_type=F32)
        n = keys.shape[0]
        return jnp.where(allowed[None], raw.reshape(heads, block_rows, n), NEG_FILL).reshape(
            stacked, n
        )

    def fold(values, combine):
        pieces = [values[:, i : i + HEAD_DIM] for i in range(0, values.shape[1], HEAD_DIM)]
        result = pieces[0]
        for piece in pieces[1:]:
            result = combine(result, piece)
        return result

    new = jnp.concatenate([rows for rows, _ in fresh], axis=0)
    fresh_rows = new.shape[0]
    key_position = jnp.concatenate(
        [
            base + lax.broadcasted_iota(jnp.int32, (1, rows.shape[0]), 1)
            for rows, base in fresh
        ],
        axis=1,
    )
    allowed = (row_segment == segment_of(key_position)) & (key_position <= row_position)
    masked = masked_scores(new[:, :HEAD_DIM], allowed)
    scores[:, :fresh_rows] = masked
    total_ref[...] = fold(masked, jnp.maximum)
    lanes = lax.broadcasted_iota(jnp.int32, (1, wide), 1) // PAGE

    def add_scores(g, carry):
        label = jnp.full((1, wide), -1, jnp.int32)
        for j in range(PAGES_STEP):
            label = jnp.where(lanes == j, labels[g * PAGES_STEP + j], label)
        keys = cache[pl.ds(pl.multiple_of(g * wide, wide), wide), :HEAD_DIM]
        masked = masked_scores(keys, row_segment == label)
        scores[:, pl.ds(pl.multiple_of(fresh_rows + g * wide, PAGE), wide)] = masked
        total_ref[...] = jnp.maximum(total_ref[...], fold(masked, jnp.maximum))
        return carry

    lax.fori_loop(0, steps, add_scores, 0)
    top = jnp.max(total_ref[...], axis=1, keepdims=True) * factor
    probs = jnp.exp2(scores[:, :fresh_rows] * factor - top)
    total_ref[...] = fold(probs, jnp.add)
    mixed_ref[...] = jnp.dot(probs.astype(BF16), new[:, HEAD_DIM:], preferred_element_type=F32)

    def add_values(g, carry):
        part = scores[:, pl.ds(pl.multiple_of(fresh_rows + g * wide, PAGE), wide)]
        probs = jnp.exp2(part * factor - top)
        values = cache[pl.ds(pl.multiple_of(g * wide, wide), wide), HEAD_DIM:]
        total_ref[...] += fold(probs, jnp.add)
        mixed_ref[...] += jnp.dot(probs.astype(BF16), values, preferred_element_type=F32)
        return carry

    lax.fori_loop(0, steps, add_values, 0)
    denominator = jnp.sum(total_ref[...], axis=1, keepdims=True)
    result = (mixed_ref[...] / denominator).astype(BF16)
    return jnp.concatenate(
        [result[h * block_rows : (h + 1) * block_rows] for h in range(heads)], axis=1
    )


def project_held(near, far, w_query, w_keyvalue):
    rows, half = near.shape
    pieces = len(far)
    steps, depth, q_width = w_query.shape
    kv_width = w_keyvalue.shape[2]

    def kernel(near_ref, *refs):
        far_refs = refs[:pieces]
        wq, wkv, q_ref, kv_ref = refs[pieces:]
        for w, out in ((wq, q_ref), (wkv, kv_ref)):
            total = None
            for j in range(steps):
                at = j * depth
                if at < half:
                    x = near_ref[:, at : at + depth]
                else:
                    wide = half // pieces
                    x = far_refs[(at - half) // wide][:, at % wide : at % wide + depth]
                part = jnp.dot(x, w[j], preferred_element_type=F32)
                total = part if j == 0 else total + part
            out[...] = total.astype(BF16)

    return pl.pallas_call(
        kernel,
        in_specs=[VMEM] * (3 + pieces),
        out_specs=[VMEM] * 2,
        out_shape=[shape((rows, q_width)), shape((rows, kv_width))],
        compiler_params=params(6),
        cost_estimate=SMALL,
        name="project_held",
    )(near, *far, w_query, w_keyvalue)


def project_far(place, near, far, w_query, w_keyvalue, after):
    rows, half = near.shape
    q_width, kv_width = w_query.shape[1], w_keyvalue.shape[1]
    steps = 8
    depth = 2 * half // steps

    def kernel(place_ref, near_ref, far_ref, wq, wkv, *refs):
        q_ref, kv_ref, wq_buf, wkv_buf, sems = refs[len(after) :]
        stream = weight_stream(place_ref[1], half, steps, (wq, wkv), (wq_buf, wkv_buf), sems)
        for j in range(steps):
            for copy in stream(j):
                copy.start()
        q_sum = kv_sum = None
        for j in range(steps):
            for copy in stream(j):
                copy.wait()
            x_ref = near_ref if j < steps // 2 else far_ref
            x = x_ref[:, (j % (steps // 2)) * depth : (j % (steps // 2) + 1) * depth]
            q_part = jnp.dot(x, wq_buf[j], preferred_element_type=F32)
            kv_part = jnp.dot(x, wkv_buf[j], preferred_element_type=F32)
            q_sum = q_part if j == 0 else q_sum + q_part
            kv_sum = kv_part if j == 0 else kv_sum + kv_part
        q_ref[...] = q_sum.astype(BF16)
        kv_ref[...] = kv_sum.astype(BF16)

    return pl.pallas_call(
        kernel,
        in_specs=[SMEM] + [VMEM] * 2 + [HBM] * 2 + [ANY] * len(after),
        out_specs=[VMEM] * 2,
        out_shape=[shape((rows, q_width)), shape((rows, kv_width))],
        scratch_shapes=[
            pltpu.VMEM((steps, depth, q_width), BF16),
            pltpu.VMEM((steps, depth, kv_width), BF16),
            pltpu.SemaphoreType.DMA((2 * steps,)),
        ],
        compiler_params=params(32),
        cost_estimate=SMALL,
        name="project_far",
    )(place, near, far, w_query, w_keyvalue, *after)


def attend_out(place, query, fresh, bases, base, pulled, w_out):
    rows, depth = query.shape
    width = w_out.shape[1]
    half = width // 2
    heads = depth // HEAD_DIM
    out_steps = 4
    wide = half // out_steps
    known = len(fresh)
    count = sum(f.shape[0] for f in fresh)
    fresh_rows = -(-count // HEAD_DIM) * HEAD_DIM
    pad = fresh_rows - count

    def kernel(place_ref, q_ref, pulled_ref, *refs):
        fresh_refs = refs[:known]
        wo, there_ref, stay_ref, wo_buf, sems = refs[known : known + 5]
        core, side = place_ref[1], place_ref[2]

        def copy(j):
            first = 1 - core if j < out_steps else core
            start = pl.multiple_of(first * half + (j % out_steps) * wide, wide)
            return pltpu.make_async_copy(wo.at[:, pl.ds(start, wide)], wo_buf.at[j], sems.at[j])

        for j in range(2 * out_steps):
            copy(j).start()
        pairs = [(ref[...], at(side)) for ref, at in zip(fresh_refs, bases)]
        if pad:
            pairs.append((jnp.zeros((pad, 2 * HEAD_DIM), BF16), jnp.int32(1 << 20)))
        mixed = attend_block(
            place_ref, q_ref[...], base(side), pairs, pulled_ref, refs[known + 5 :]
        )
        for j in range(2 * out_steps):
            copy(j).wait()
            out_ref = there_ref if j < out_steps else stay_ref
            at = (j % out_steps) * wide
            out_ref[:, at : at + wide] = jnp.dot(
                mixed, wo_buf[j], preferred_element_type=F32
            ).astype(BF16)

    return pl.pallas_call(
        kernel,
        in_specs=[SMEM] + [VMEM] * (2 + known) + [HBM],
        out_specs=[VMEM] * 2,
        out_shape=[shape((rows, half)), shape((rows, half))],
        scratch_shapes=[
            pltpu.VMEM((2 * out_steps, depth, wide), BF16),
            pltpu.SemaphoreType.DMA((2 * out_steps,)),
        ]
        + attention_scratch(rows, heads, fresh_rows, pulled.shape[0] * pulled.shape[1]),
        compiler_params=params(30),
        cost_estimate=SMALL,
        name="attend_out",
    )(place, query, pulled, *fresh, w_out)


def local_rows(place, query, fresh, bases, base, pulled, w_out, after):
    both, depth = query.shape
    rows = both // 2
    width = w_out.shape[1]
    heads = depth // HEAD_DIM
    steps = 8
    wide = width // steps
    known = len(fresh)
    fresh_rows = sum(f.shape[0] for f in fresh)

    def kernel(place_ref, q_ref, pulled_ref, *refs):
        fresh_refs = refs[:known]
        wo = refs[known]
        rest = refs[known + 1 + len(after) :]
        own_ref, peer_ref, wo_buf, a_buf, sems = rest[:5]
        core, side = place_ref[1], place_ref[2]

        def out_copy(j):
            return pltpu.make_async_copy(
                wo.at[:, j * wide : (j + 1) * wide], wo_buf.at[j], sems.at[j]
            )

        for j in range(steps):
            out_copy(j).start()

        def block(b, carry):
            at = pl.ds(pl.multiple_of(b * rows, rows), rows)
            a_buf[at, :] = attend_block(
                place_ref,
                q_ref[at, :],
                base(side) + b * rows,
                [(ref[...], first(side)) for ref, first in zip(fresh_refs, bases)],
                pulled_ref,
                rest[5:],
            )
            return carry

        lax.fori_loop(0, 2, block, 0)
        own_at = pl.ds(pl.multiple_of(core * rows, rows), rows)
        peer_at = pl.ds(pl.multiple_of((1 - core) * rows, rows), rows)
        a = jnp.concatenate([a_buf[own_at, :], a_buf[peer_at, :]], axis=0)
        for j in range(steps):
            out_copy(j).wait()
            part = jnp.dot(a, wo_buf[j], preferred_element_type=F32).astype(BF16)
            own_ref[:, j * wide : (j + 1) * wide] = part[:rows]
            peer_ref[:, j * wide : (j + 1) * wide] = part[rows:]

    return pl.pallas_call(
        kernel,
        in_specs=[SMEM] + [VMEM] * (2 + known) + [HBM] + [ANY] * len(after),
        out_specs=[VMEM, VMEM],
        out_shape=[shape((rows, width)), shape((rows, width))],
        scratch_shapes=[
            pltpu.VMEM((steps, depth, wide), BF16),
            pltpu.VMEM((both, depth), BF16),
            pltpu.SemaphoreType.DMA((steps,)),
        ]
        + attention_scratch(rows, heads, fresh_rows, pulled.shape[0] * pulled.shape[1]),
        compiler_params=params(40),
        cost_estimate=SMALL,
        name="local_rows",
    )(place, query, pulled, *fresh, w_out, *after)


def add_pair(left, right):
    rows, width = left.shape
    step = 16

    def kernel(left_ref, right_ref, out_ref):
        def block(i, carry):
            at = pl.ds(pl.multiple_of(i * step, step), step)
            out_ref[at, :] = (left_ref[at, :].astype(F32) + right_ref[at, :].astype(F32)).astype(
                BF16
            )
            return carry

        lax.fori_loop(0, rows // step, block, 0)

    return pl.pallas_call(
        kernel,
        in_specs=[VMEM, VMEM],
        out_specs=VMEM,
        out_shape=shape((rows, width)),
        compiler_params=params(8),
        cost_estimate=SMALL,
        name="add_pair",
    )(left, right)


def finish(place, tokens, own, peer, near, far):
    rows, width = tokens.shape
    half = width // 2
    step = 16

    def kernel(place_ref, x_ref, own_ref, peer_ref, near_ref, far_ref, out_ref):
        core = place_ref[1]

        def block(i, carry):
            at = pl.ds(pl.multiple_of(i * step, step), step)
            for start, part in ((core, near_ref), (1 - core, far_ref)):
                cols = pl.ds(pl.multiple_of(start * half, half), half)
                local = own_ref[at, cols].astype(F32) + peer_ref[at, cols].astype(F32)
                total = local + part[at, :].astype(F32)
                out_ref[at, cols] = (x_ref[at, cols].astype(F32) + total).astype(BF16)
            return carry

        lax.fori_loop(0, rows // step, block, 0)

    return pl.pallas_call(
        kernel,
        in_specs=[SMEM] + [VMEM] * 5,
        out_specs=VMEM,
        out_shape=shape((rows, width)),
        compiler_params=params(16),
        cost_estimate=SMALL,
        name="finish",
    )(place, tokens, own, peer, near, far)


def pick_pages(place, wanted, held, after):
    replicas = len(wanted)
    slots = wanted[0].shape[1]
    tensors = len(held)
    _, page, width = held[0].shape
    total = tensors * slots

    def kernel(place_ref, *refs):
        wants, sources = refs[:replicas], refs[replicas : replicas + tensors]
        out_ref = refs[replicas + tensors + len(after)]
        me, rep = place_ref[0], place_ref[3]
        for k in range(replicas):
            asker = lax.rem(rep + k, replicas)
            for i in range(tensors):
                owner = rep * tensors + jnp.bitwise_xor(me, i)
                for s in range(slots):
                    out_ref[asker, i * slots + s] = sources[i][wants[k][0, s, owner]]

    return pl.pallas_call(
        kernel,
        in_specs=[SMEM] * (1 + replicas) + [VMEM] * tensors + [ANY] * len(after),
        out_specs=VMEM,
        out_shape=shape((replicas, total, page, width)),
        compiler_params=params(8),
        cost_estimate=SMALL,
        name="pick_pages",
    )(place, *wanted, *held, *after)


def write_pool(place, slots, kv_pool, own, core_new, y_new):
    pages, heads = kv_pool.shape[:2]
    new_count = slots.shape[1]
    side_pages = new_count // 2

    def kernel(place_ref, slot_ref, pool_ref, own_ref, core_ref, y_ref, out_ref, sems):
        me, side = place_ref[0], place_ref[2]
        sources = (own_ref, core_ref.at[0], y_ref, core_ref.at[1])
        for p in range(pages):
            found = jnp.int32(-1)
            for j in range(new_count):
                found = jnp.where(slot_ref[0, j] == me * pages + p, j, found)
            far = (found >= side_pages).astype(jnp.int32)
            inner = jnp.maximum(found - far * side_pages, 0)

            @pl.when(found >= 0)
            def _():
                for i in range(heads):
                    origin = side if i < 2 else 1 - side
                    start = (jnp.bitwise_xor(far, origin) * side_pages + inner) * PAGE
                    pltpu.make_async_copy(
                        sources[i].at[pl.ds(pl.multiple_of(start, PAGE), PAGE)],
                        out_ref.at[p, jnp.bitwise_xor(me, i)],
                        sems.at[p * heads + i],
                    ).start()

            @pl.when(found < 0)
            def _():
                for i in range(heads):
                    at = jnp.bitwise_xor(me, i)
                    pltpu.make_async_copy(
                        pool_ref.at[p, at], out_ref.at[p, at], sems.at[p * heads + i]
                    ).start()

        for p in range(pages):
            for i in range(heads):
                at = jnp.bitwise_xor(me, i)
                pltpu.make_async_copy(
                    pool_ref.at[p, at], out_ref.at[p, at], sems.at[p * heads + i]
                ).wait()

    return pl.pallas_call(
        kernel,
        in_specs=[SMEM, SMEM] + [ANY] * 4,
        out_specs=ANY,
        out_shape=shape(kv_pool.shape),
        scratch_shapes=[pltpu.SemaphoreType.DMA((pages * heads,))],
        compiler_params=params(8),
        cost_estimate=SMALL,
        name="write_pool",
    )(place, slots, kv_pool, own, core_new, y_new)


def chip_pair_body(
    tokens,
    gain,
    w_query,
    w_keyvalue,
    w_out,
    kv_pool,
    suffix_pages,
    page_index,
    page_request,
    new_slot,
):
    replicas = lax.axis_size("replica")
    me = lax.axis_index("tensor")
    core = me % 2
    side = me // 2
    rows = tokens.shape[0]
    rep = lax.axis_index("replica")
    place = jnp.stack([me, core, side, rep]).astype(jnp.int32)
    requests = jnp.swapaxes(page_request, 1, 2).reshape(-1)
    scalars = jnp.concatenate([place, suffix_pages[0], requests])

    def over_core(x):
        return lax.ppermute(x, "tensor", [(0, 1), (1, 0), (2, 3), (3, 2)])

    def over_y(x):
        return lax.ppermute(x, "tensor", [(0, 2), (2, 0), (1, 3), (3, 1)])

    def tie(x, *others):
        return lax.optimization_barrier((x, *others))[0]

    w_query, w_keyvalue, w_out = in_hbm(w_query), in_hbm(w_keyvalue), in_hbm(w_out)

    wanted = [jnp.swapaxes(page_index, 1, 2)]
    for k in range(1, replicas):
        back = [(i, (i - k) % replicas) for i in range(replicas)]
        wanted.append(lax.ppermute(wanted[0], "replica", back))

    mine, other, *held = prepare(place, in_hbm(tokens), in_hbm(gain), in_hbm(kv_pool))
    for i in range(1, 4):
        held[i] = lax.ppermute(held[i], "tensor", [(t, t ^ i) for t in range(4)])

    peer_near = over_core(other)
    peer_far = over_core(mine)
    is_first = core == 0
    near_tied = tie(peer_near, held[2], held[3])
    first_half = jnp.where(is_first, mine, near_tied)
    second_half = jnp.where(is_first, near_tied, mine)
    first = over_y(first_half)
    second = over_y(second_half)

    picked = pick_pages(place, wanted, held, [first_half, second_half])
    pulled = lax.all_to_all(picked, "replica", split_axis=0, concat_axis=0, tiled=True)

    q_local, kv_local, wq, wkv = project_local(
        place, [mine, peer_near], [other, peer_far], w_query, w_keyvalue, [picked, scalars]
    )


    def local_base(s):
        return s * (2 * rows)

    def first_base(s):
        return (1 - s) * (2 * rows)

    def second_base(s):
        return (1 - s) * (2 * rows) + rows

    first = tie(first, q_local)
    wide = first.shape[1] // 4
    pieces = [over_core(first[:, i * wide : (i + 1) * wide]) for i in range(4)]
    q_first, kv_first = project_held(first, pieces, wq, wkv)
    there, stay = attend_out(
        scalars, q_first, [kv_local, kv_first],
        [local_base, first_base], first_base, pulled, w_out,
    )
    there = tie(there, second)
    first_mix = add_pair(stay, over_core(there))
    first_sum = over_y(first_mix)

    second = tie(second, first_mix)
    q_second, kv_second = project_far(place, second, over_core(second), w_query, w_keyvalue, [])
    fresh = [kv_local, kv_first, kv_second]
    bases = [local_base, first_base, second_base]
    there, stay = attend_out(
        scalars, q_second, fresh, bases, second_base, pulled, w_out
    )
    there = tie(there, first_sum)
    second_mix = add_pair(stay, over_core(there))


    new_own = jnp.concatenate(fresh, axis=0)
    y_new = over_y(new_own)
    core_new = over_core(jnp.stack([new_own, y_new]))
    second_sum = over_y(tie(second_mix, y_new))

    pool_out = write_pool(place, new_slot, kv_pool, new_own, core_new, y_new)

    own_part, peer_part = local_rows(
        scalars, q_local, fresh, bases, local_base, pulled, w_out,
        [second_mix, pool_out],
    )
    peer_part = over_core(peer_part)

    near = jnp.where(is_first, first_sum, second_sum)
    far = over_core(jnp.where(is_first, second_sum, first_sum))
    layer_out = finish(place, tokens, own_part, peer_part, near, far)
    return (layer_out, pool_out)


def solution(mesh):
    pair = mesh.shape["tensor"] == KV_HEADS
    return jax.shard_map(
        chip_pair_body if pair else gathered_body,
        mesh=mesh,
        in_specs=(
            P(("groups", "replica", "tensor"), None),
            P(),
            P(None, "tensor"),
            P(None, "tensor"),
            P("tensor", None),
            P(("groups", "replica", "tensor"), None, None, None),
            P(("groups", "replica"), None),
            P(("groups", "replica"), None, None),
            P(("groups", "replica"), None, None),
            P(("groups", "replica"), None),
        ),
        out_specs=(
            P(("groups", "replica", "tensor"), None),
            P(("groups", "replica", "tensor"), None, None, None),
        ),
        check_vma=False,
    )
```

```python
import math

import jax
import jax.numpy as jnp
from jax import lax
from jax.experimental import pallas as pl
from jax.experimental.pallas import tpu as pltpu
from jax.sharding import PartitionSpec as P

KV_HEADS = 4
HEAD_DIM = 128
PAGE = 64
UNIT = 8


NEG_FILL = -1e30
EPSILON = 1e-06

F32 = jnp.float32
BF16 = jnp.bfloat16
MIB = 1 << 20
ANY = pl.BlockSpec(memory_space=pl.ANY)
HBM = pl.BlockSpec(memory_space=pltpu.HBM)
SMEM = pl.BlockSpec(memory_space=pltpu.SMEM)
VMEM = pl.BlockSpec(memory_space=pltpu.VMEM)
SMALL = pl.CostEstimate(flops=1024, bytes_accessed=1024, transcendentals=0)
MEDIUM = pl.CostEstimate(flops=1024, bytes_accessed=4000000, transcendentals=0)
LARGE = pl.CostEstimate(flops=20000000000, bytes_accessed=200000000, transcendentals=0)


def params(mib):
    return pltpu.CompilerParams(vmem_limit_bytes=mib * MIB)


def in_hbm(x):
    return pltpu.with_memory_space_constraint(x, pltpu.HBM)


def shape(dims, dtype=BF16):
    return jax.ShapeDtypeStruct(dims, dtype)


def normalize(rows, gain):
    values = rows.astype(jnp.float32)
    inverse = lax.rsqrt(jnp.mean(values * values, axis=-1, keepdims=True) + EPSILON)
    return (values * inverse * gain.astype(jnp.float32)).astype(jnp.bfloat16)


def row_segments(pages, total_rows):
    bounds = jnp.cumsum(pages) * UNIT
    positions = jnp.arange(total_rows, dtype=jnp.int32)
    return jnp.sum((positions[:, None] >= bounds[None, :]).astype(jnp.int32), axis=1)


def gathered_body(
    tokens,
    gain,
    w_query,
    w_keyvalue,
    w_out,
    kv_pool,
    suffix_pages,
    page_index,
    page_request,
    new_slot,
):
    replicas = lax.axis_size("replica")
    tensors = lax.axis_size("tensor")
    owners = replicas * tensors
    position = lax.axis_index("tensor")
    query_width = w_query.shape[1]
    local_heads = query_width // HEAD_DIM
    share = tensors // KV_HEADS
    my_head = position // share
    scale_factor = 1.0 / math.sqrt(HEAD_DIM)
    normed = normalize(tokens, gain)
    piece = lax.all_gather(normed, "tensor", axis=0, tiled=True)
    first = jnp.dot(piece, w_query, preferred_element_type=jnp.float32)
    second = jnp.dot(piece, w_keyvalue, preferred_element_type=jnp.float32)
    projected = jnp.concatenate([first, second], axis=1).astype(jnp.bfloat16)
    query = projected[:, :query_width]
    keyvalue = lax.all_gather(projected[:, query_width:], "tensor", axis=1, tiled=True)
    total_rows = query.shape[0]
    wanted = lax.all_to_all(
        page_index[0], ("replica", "tensor"), split_axis=0, concat_axis=0, tiled=True
    )
    slot_count = wanted.shape[1]
    sources = jnp.arange(owners, dtype=jnp.int32) % tensors
    source_heads = sources // share
    flat_pool = kv_pool.reshape(kv_pool.shape[0] * KV_HEADS, PAGE, 2 * HEAD_DIM)
    outgoing = flat_pool[wanted * KV_HEADS + source_heads[:, None]]
    sub_tokens = outgoing.shape[2]
    pulled = lax.all_to_all(
        outgoing, ("replica", "tensor"), split_axis=0, concat_axis=0, tiled=True
    )
    segments = row_segments(suffix_pages[0], total_rows)
    key_groups = page_request[0]
    stacked = (
        query.reshape(total_rows, local_heads, HEAD_DIM)
        .transpose(1, 0, 2)
        .reshape(local_heads * total_rows, HEAD_DIM)
    )
    own_new = lax.dynamic_index_in_dim(
        keyvalue.reshape(total_rows, KV_HEADS, 2 * HEAD_DIM), my_head, 1, keepdims=False
    )
    row_order = jnp.arange(total_rows, dtype=jnp.int32)
    causal = (segments[:, None] == segments[None, :]) & (row_order[None, :] <= row_order[:, None])

    def block_scores(queries, head_count, keys, allowed):
        raw = (
            jnp.dot(queries, keys[:, :HEAD_DIM].T, preferred_element_type=jnp.float32)
            * scale_factor
        )
        raw = raw.reshape(head_count, total_rows, keys.shape[0])
        return jnp.where(allowed[None], raw, NEG_FILL)

    first_scores = block_scores(stacked, local_heads, own_new, causal)
    running = jnp.max(first_scores, axis=2)
    probs = jnp.exp(first_scores - running[:, :, None])
    denominator = jnp.sum(probs, axis=2)
    numerator = jnp.dot(
        probs.astype(jnp.bfloat16).reshape(local_heads * total_rows, total_rows),
        own_new[:, HEAD_DIM:],
        preferred_element_type=jnp.float32,
    )
    block_owners = 16
    blocks = owners // block_owners

    def absorb(step, state):
        peak, total, mixed = state
        pages = lax.dynamic_slice_in_dim(pulled, step * block_owners, block_owners, 0)
        keys = pages.reshape(block_owners * slot_count * sub_tokens, 2 * HEAD_DIM)
        labels = lax.dynamic_slice_in_dim(key_groups, step * block_owners, block_owners, 0).reshape(
            -1
        )
        matches = (segments[:, None] == labels[None, :])[:, :, None]
        allowed = jnp.broadcast_to(matches, (total_rows, labels.shape[0], sub_tokens)).reshape(
            total_rows, labels.shape[0] * sub_tokens
        )
        scores = block_scores(stacked, local_heads, keys, allowed)
        updated = jnp.maximum(peak, jnp.max(scores, axis=2))
        rescale = jnp.exp(peak - updated)
        weights = jnp.where(allowed[None], jnp.exp(scores - updated[:, :, None]), 0.0)
        total = total * rescale + jnp.sum(weights, axis=2)
        flat_weights = weights.astype(jnp.bfloat16).reshape(local_heads * total_rows, keys.shape[0])
        mixed = mixed * rescale.reshape(-1)[:, None] + jnp.dot(
            flat_weights, keys[:, HEAD_DIM:], preferred_element_type=jnp.float32
        )
        return (updated, total, mixed)

    running, denominator, numerator = lax.fori_loop(
        0, blocks, absorb, (running, denominator, numerator)
    )
    attention = (numerator / denominator.reshape(-1)[:, None]).astype(jnp.bfloat16)
    attention = (
        attention.reshape(local_heads, total_rows, HEAD_DIM)
        .transpose(1, 0, 2)
        .reshape(total_rows, query_width)
    )
    summed = lax.psum_scatter(
        jnp.dot(attention, w_out, preferred_element_type=jnp.float32).astype(jnp.bfloat16),
        "tensor",
        scatter_dimension=0,
        tiled=True,
    ).astype(jnp.float32)
    layer_out = (tokens.astype(jnp.float32) + summed).astype(jnp.bfloat16)
    new_count = total_rows // PAGE
    fresh = (
        keyvalue.reshape(new_count, PAGE, KV_HEADS, 2 * HEAD_DIM)
        .transpose(0, 2, 1, 3)
        .reshape(new_count, KV_HEADS * PAGE * 2 * HEAD_DIM)
    )
    local_pages = kv_pool.shape[0]
    targets = position * local_pages + jnp.arange(local_pages, dtype=jnp.int32)
    match_table = new_slot[0][None, :] == targets[:, None]
    placed = jnp.dot(
        match_table.astype(jnp.bfloat16), fresh, preferred_element_type=jnp.float32
    ).astype(jnp.bfloat16)
    placed = placed.reshape(kv_pool.shape)
    landed = jnp.any(match_table, axis=1)
    pool_out = jnp.where(landed[:, None, None, None], placed, kv_pool)
    return (layer_out, pool_out)


def prepare(place, tokens, gain, kv_pool):
    rows, width = tokens.shape
    half = width // 2
    step = 32
    pages, heads = kv_pool.shape[:2]
    blocks = rows // step

    def kernel(place_ref, x, g, pool, mine_ref, other_ref, *refs):
        held, (x_buf, g_buf, pool_buf, sems) = refs[:heads], refs[heads:]
        me, core = place_ref[0], place_ref[1]
        pool_copy = pltpu.make_async_copy(pool, pool_buf, sems.at[blocks + 1])

        def row_copy(b):
            at = pl.ds(b * step, step)
            return pltpu.make_async_copy(x.at[at], x_buf.at[at], sems.at[b])

        gain_copy = pltpu.make_async_copy(g, g_buf, sems.at[blocks])
        row_copy(0).start()
        gain_copy.start()
        for b in range(1, blocks):
            row_copy(b).start()
        pool_copy.start()
        near = pl.multiple_of(core * half, half)
        far = pl.multiple_of((1 - core) * half, half)
        for b in range(blocks):
            row_copy(b).wait()
            if b == 0:
                gain_copy.wait()

            def block(i, carry):
                at = pl.ds(pl.multiple_of(b * step + i * 16, 16), 16)
                total = jnp.zeros((16, 1), F32)
                for part in range(2):
                    values = x_buf[at, part * half : (part + 1) * half].astype(F32)
                    total += jnp.sum(values * values, axis=1, keepdims=True)
                inverse = lax.rsqrt(total * (1.0 / width) + EPSILON)
                for start, out in ((near, mine_ref), (far, other_ref)):
                    cols = pl.ds(start, half)
                    values = x_buf[at, cols].astype(F32)
                    out[at, :] = (values * inverse * g_buf[cols].astype(F32)[None, :]).astype(BF16)
                return carry

            lax.fori_loop(0, step // 16, block, 0)
        pool_copy.wait()
        for i in range(heads):
            for p in range(pages):
                held[i][p] = pool_buf[p, jnp.bitwise_xor(me, i)]

    return pl.pallas_call(
        kernel,
        in_specs=[SMEM] + [HBM] * 3,
        out_specs=[VMEM] * (2 + heads),
        out_shape=[shape((rows, half))] * 2 + [shape((pages,) + kv_pool.shape[2:])] * heads,
        scratch_shapes=[
            pltpu.VMEM((rows, width), BF16),
            pltpu.VMEM((width,), BF16),
            pltpu.VMEM(kv_pool.shape, BF16),
            pltpu.SemaphoreType.DMA((blocks + 2,)),
        ],
        compiler_params=params(16),
        cost_estimate=SMALL,
        name="prepare",
    )(place, tokens, gain, kv_pool)


def project_local(place, near, far, w_query, w_keyvalue, after):
    rows, half = near[0].shape
    q_width, kv_width = w_query.shape[1], w_keyvalue.shape[1]
    steps = 8
    depth = 2 * half // steps
    waits = len(after)

    def kernel(place_ref, near_own, near_peer, far_own, far_peer, wq, wkv, *refs):
        q_ref, kv_ref, wq_buf, wkv_buf, q_acc, kv_acc, sems = refs[waits:]
        core = place_ref[1]
        stream = weight_stream(core, half, steps, (wq, wkv), (wq_buf, wkv_buf), sems)
        for j in range(steps):
            for copy in stream(j):
                copy.start()
        for j in range(steps):
            for copy in stream(j):
                copy.wait()
            group = (near_own, near_peer) if j < steps // 2 else (far_own, far_peer)
            cols = slice((j % (steps // 2)) * depth, (j % (steps // 2) + 1) * depth)
            x = jnp.concatenate([ref[:, cols] for ref in group], axis=0)
            q_part = jnp.dot(x, wq_buf[j], preferred_element_type=F32)
            kv_part = jnp.dot(x, wkv_buf[j], preferred_element_type=F32)
            if j == 0:
                q_acc[...] = q_part
                kv_acc[...] = kv_part
            elif j < steps - 1:
                q_acc[...] += q_part
                kv_acc[...] += kv_part
            else:
                q_last = (q_acc[...] + q_part).astype(BF16)
                kv_last = (kv_acc[...] + kv_part).astype(BF16)
        for b in range(2):
            at = pl.ds(pl.multiple_of((core if b == 0 else 1 - core) * rows, rows), rows)
            q_ref[at, :] = q_last[b * rows : (b + 1) * rows]
            kv_ref[at, :] = kv_last[b * rows : (b + 1) * rows]

    total = 2 * rows
    return pl.pallas_call(
        kernel,
        in_specs=[SMEM] + [VMEM] * 4 + [HBM] * 2 + [ANY] * waits,
        out_specs=[VMEM] * 4,
        out_shape=[
            shape((total, q_width)),
            shape((total, kv_width)),
            pltpu.VMEM((steps, depth, q_width), BF16),
            pltpu.VMEM((steps, depth, kv_width), BF16),
        ],
        scratch_shapes=[
            pltpu.VMEM((total, q_width), F32),
            pltpu.VMEM((total, kv_width), F32),
            pltpu.SemaphoreType.DMA((2 * steps,)),
        ],
        compiler_params=params(10),
        cost_estimate=LARGE,
        name="project_local",
    )(place, *near, *far, w_query, w_keyvalue, *after)


def weight_stream(core, half, steps, sources, buffers, sems):
    depth = 2 * half // steps

    def copies(j):
        base = core if j < steps // 2 else 1 - core
        start = pl.multiple_of(base * half + (j % (steps // 2)) * depth, depth)
        count = len(sources)
        return [
            pltpu.make_async_copy(w.at[pl.ds(start, depth)], buf.at[j], sems.at[count * j + i])
            for i, (w, buf) in enumerate(zip(sources, buffers))
        ]

    return copies


PAGES_STEP = 4
REQUESTS = 4
SIZES_AT = 4
REQUESTS_AT = 8


def attention_scratch(block_rows, heads, fresh_rows, slots):
    stacked = heads * block_rows
    return [
        pltpu.VMEM((stacked, fresh_rows + slots * PAGE), F32),
        pltpu.VMEM((stacked, HEAD_DIM), F32),
        pltpu.VMEM((stacked, HEAD_DIM), F32),
        pltpu.VMEM((slots * PAGE, 2 * HEAD_DIM), BF16),
        pltpu.SMEM((slots,), jnp.int32),
    ]


def attend_block(place_ref, q, first_row, fresh, pulled, scratch):
    scores, total_ref, mixed_ref, cache, labels = scratch
    me = place_ref[0]
    block_rows, width = q.shape
    heads = width // HEAD_DIM
    stacked = heads * block_rows
    groups, per = pulled.shape[:2]
    tensors = 4
    slots = per // tensors
    wide = PAGES_STEP * PAGE
    factor = math.log2(math.e) / math.sqrt(HEAD_DIM)
    bound = []
    running = jnp.int32(0)
    for k in range(REQUESTS):
        running = running + place_ref[SIZES_AT + k] * UNIT
        bound.append(running)

    def segment_of(position):
        return sum((position >= b).astype(jnp.int32) for b in bound)

    lowest = segment_of(first_row)
    highest = segment_of(first_row + block_rows - 1)
    count = jnp.int32(0)
    for g in range(groups):
        for p in range(per):
            owner = g * tensors + jnp.bitwise_xor(me, p // slots)
            label = place_ref[REQUESTS_AT + p % slots * groups * tensors + owner]
            wanted = (label >= lowest) & (label <= highest)

            @pl.when(wanted)
            def _():
                cache[pl.ds(pl.multiple_of(count * PAGE, PAGE), PAGE), :] = pulled[g, p]
                labels[count] = label

            count = count + wanted.astype(jnp.int32)
    steps = (count + PAGES_STEP - 1) // PAGES_STEP
    for k in range(PAGES_STEP - 1):

        @pl.when(count + k < steps * PAGES_STEP)
        def _():
            cache[pl.ds(pl.multiple_of((count + k) * PAGE, PAGE), PAGE), :] = jnp.zeros(
                (PAGE, 2 * HEAD_DIM), BF16
            )
            labels[count + k] = jnp.int32(-1)

    q_rows = jnp.concatenate([q[:, h * HEAD_DIM : (h + 1) * HEAD_DIM] for h in range(heads)], axis=0)
    row_position = first_row + lax.broadcasted_iota(jnp.int32, (block_rows, 1), 0)
    row_segment = segment_of(row_position)

    def masked_scores(keys, allowed):
        raw = lax.dot_general(q_rows, keys, (((1,), (1,)), ((), ())), preferred_element_type=F32)
        n = keys.shape[0]
        return jnp.where(allowed[None], raw.reshape(heads, block_rows, n), NEG_FILL).reshape(
            stacked, n
        )

    def fold(values, combine):
        pieces = [values[:, i : i + HEAD_DIM] for i in range(0, values.shape[1], HEAD_DIM)]
        result = pieces[0]
        for piece in pieces[1:]:
            result = combine(result, piece)
        return result

    new = jnp.concatenate([rows for rows, _ in fresh], axis=0)
    fresh_rows = new.shape[0]
    key_position = jnp.concatenate(
        [
            base + lax.broadcasted_iota(jnp.int32, (1, rows.shape[0]), 1)
            for rows, base in fresh
        ],
        axis=1,
    )
    allowed = (row_segment == segment_of(key_position)) & (key_position <= row_position)
    masked = masked_scores(new[:, :HEAD_DIM], allowed)
    scores[:, :fresh_rows] = masked
    total_ref[...] = fold(masked, jnp.maximum)
    lanes = lax.broadcasted_iota(jnp.int32, (1, wide), 1) // PAGE

    def add_scores(g, carry):
        label = jnp.full((1, wide), -1, jnp.int32)
        for j in range(PAGES_STEP):
            label = jnp.where(lanes == j, labels[g * PAGES_STEP + j], label)
        keys = cache[pl.ds(pl.multiple_of(g * wide, wide), wide), :HEAD_DIM]
        masked = masked_scores(keys, row_segment == label)
        scores[:, pl.ds(pl.multiple_of(fresh_rows + g * wide, PAGE), wide)] = masked
        total_ref[...] = jnp.maximum(total_ref[...], fold(masked, jnp.maximum))
        return carry

    lax.fori_loop(0, steps, add_scores, 0)
    top = jnp.max(total_ref[...], axis=1, keepdims=True) * factor
    probs = jnp.exp2(scores[:, :fresh_rows] * factor - top)
    total_ref[...] = fold(probs, jnp.add)
    mixed_ref[...] = jnp.dot(probs.astype(BF16), new[:, HEAD_DIM:], preferred_element_type=F32)

    def add_values(g, carry):
        part = scores[:, pl.ds(pl.multiple_of(fresh_rows + g * wide, PAGE), wide)]
        probs = jnp.exp2(part * factor - top)
        values = cache[pl.ds(pl.multiple_of(g * wide, wide), wide), HEAD_DIM:]
        total_ref[...] += fold(probs, jnp.add)
        mixed_ref[...] += jnp.dot(probs.astype(BF16), values, preferred_element_type=F32)
        return carry

    lax.fori_loop(0, steps, add_values, 0)
    denominator = jnp.sum(total_ref[...], axis=1, keepdims=True)
    result = (mixed_ref[...] / denominator).astype(BF16)
    return jnp.concatenate(
        [result[h * block_rows : (h + 1) * block_rows] for h in range(heads)], axis=1
    )


def project_held(near, far, w_query, w_keyvalue):
    rows, half = near.shape
    pieces = len(far)
    steps, depth, q_width = w_query.shape
    kv_width = w_keyvalue.shape[2]

    def kernel(near_ref, *refs):
        far_refs = refs[:pieces]
        wq, wkv, q_ref, kv_ref = refs[pieces:]
        for w, out in ((wq, q_ref), (wkv, kv_ref)):
            total = None
            for j in range(steps):
                at = j * depth
                if at < half:
                    x = near_ref[:, at : at + depth]
                else:
                    wide = half // pieces
                    x = far_refs[(at - half) // wide][:, at % wide : at % wide + depth]
                part = jnp.dot(x, w[j], preferred_element_type=F32)
                total = part if j == 0 else total + part
            out[...] = total.astype(BF16)

    return pl.pallas_call(
        kernel,
        in_specs=[VMEM] * (3 + pieces),
        out_specs=[VMEM] * 2,
        out_shape=[shape((rows, q_width)), shape((rows, kv_width))],
        compiler_params=params(6),
        cost_estimate=SMALL,
        name="project_held",
    )(near, *far, w_query, w_keyvalue)


def project_far(place, near, far, w_query, w_keyvalue, after):
    rows, half = near.shape
    q_width, kv_width = w_query.shape[1], w_keyvalue.shape[1]
    steps = 8
    depth = 2 * half // steps

    def kernel(place_ref, near_ref, far_ref, wq, wkv, *refs):
        q_ref, kv_ref, wq_buf, wkv_buf, sems = refs[len(after) :]
        stream = weight_stream(place_ref[1], half, steps, (wq, wkv), (wq_buf, wkv_buf), sems)
        for j in range(steps):
            for copy in stream(j):
                copy.start()
        q_sum = kv_sum = None
        for j in range(steps):
            for copy in stream(j):
                copy.wait()
            x_ref = near_ref if j < steps // 2 else far_ref
            x = x_ref[:, (j % (steps // 2)) * depth : (j % (steps // 2) + 1) * depth]
            q_part = jnp.dot(x, wq_buf[j], preferred_element_type=F32)
            kv_part = jnp.dot(x, wkv_buf[j], preferred_element_type=F32)
            q_sum = q_part if j == 0 else q_sum + q_part
            kv_sum = kv_part if j == 0 else kv_sum + kv_part
        q_ref[...] = q_sum.astype(BF16)
        kv_ref[...] = kv_sum.astype(BF16)

    return pl.pallas_call(
        kernel,
        in_specs=[SMEM] + [VMEM] * 2 + [HBM] * 2 + [ANY] * len(after),
        out_specs=[VMEM] * 2,
        out_shape=[shape((rows, q_width)), shape((rows, kv_width))],
        scratch_shapes=[
            pltpu.VMEM((steps, depth, q_width), BF16),
            pltpu.VMEM((steps, depth, kv_width), BF16),
            pltpu.SemaphoreType.DMA((2 * steps,)),
        ],
        compiler_params=params(32),
        cost_estimate=SMALL,
        name="project_far",
    )(place, near, far, w_query, w_keyvalue, *after)


def attend_out(place, query, fresh, bases, base, pulled, w_out):
    rows, depth = query.shape
    width = w_out.shape[1]
    half = width // 2
    heads = depth // HEAD_DIM
    out_steps = 4
    wide = half // out_steps
    known = len(fresh)
    count = sum(f.shape[0] for f in fresh)
    fresh_rows = -(-count // HEAD_DIM) * HEAD_DIM
    pad = fresh_rows - count

    def kernel(place_ref, q_ref, pulled_ref, *refs):
        fresh_refs = refs[:known]
        wo = refs[known]
        there_refs, refs_after = refs[known + 1 : known + 1 + out_steps], refs[known + 1 + out_steps :]
        stay_ref, wo_buf, sems = refs_after[:3]
        core, side = place_ref[1], place_ref[2]

        def copy(j):
            first = 1 - core if j < out_steps else core
            start = pl.multiple_of(first * half + (j % out_steps) * wide, wide)
            return pltpu.make_async_copy(wo.at[:, pl.ds(start, wide)], wo_buf.at[j], sems.at[j])

        for j in range(2 * out_steps):
            copy(j).start()
        pairs = [(ref[...], at(side)) for ref, at in zip(fresh_refs, bases)]
        if pad:
            pairs.append((jnp.zeros((pad, 2 * HEAD_DIM), BF16), jnp.int32(1 << 20)))
        mixed = attend_block(
            place_ref, q_ref[...], base(side), pairs, pulled_ref, refs_after[3:]
        )
        for j in range(2 * out_steps):
            copy(j).wait()
            part = jnp.dot(mixed, wo_buf[j], preferred_element_type=F32).astype(BF16)
            if j < out_steps:
                there_refs[j][...] = part
            else:
                at = (j - out_steps) * wide
                stay_ref[:, at : at + wide] = part

    return pl.pallas_call(
        kernel,
        in_specs=[SMEM] + [VMEM] * (2 + known) + [HBM],
        out_specs=[VMEM] * (out_steps + 1),
        out_shape=[shape((rows, wide))] * out_steps + [shape((rows, half))],
        scratch_shapes=[
            pltpu.VMEM((2 * out_steps, depth, wide), BF16),
            pltpu.SemaphoreType.DMA((2 * out_steps,)),
        ]
        + attention_scratch(rows, heads, fresh_rows, pulled.shape[0] * pulled.shape[1]),
        compiler_params=params(30),
        cost_estimate=MEDIUM,
        name="attend_out",
    )(place, query, pulled, *fresh, w_out)


def local_rows(place, query, fresh, bases, base, pulled, w_out, after):
    both, depth = query.shape
    rows = both // 2
    width = w_out.shape[1]
    heads = depth // HEAD_DIM
    steps = 8
    wide = width // steps
    known = len(fresh)
    fresh_rows = sum(f.shape[0] for f in fresh)

    def kernel(place_ref, q_ref, pulled_ref, *refs):
        fresh_refs = refs[:known]
        wo = refs[known]
        rest = refs[known + 1 + len(after) :]
        own_ref, peer_ref, wo_buf, a_buf, sems = rest[:5]
        core, side = place_ref[1], place_ref[2]

        def out_copy(j):
            return pltpu.make_async_copy(
                wo.at[:, j * wide : (j + 1) * wide], wo_buf.at[j], sems.at[j]
            )

        for j in range(steps):
            out_copy(j).start()

        def block(b, carry):
            at = pl.ds(pl.multiple_of(b * rows, rows), rows)
            a_buf[at, :] = attend_block(
                place_ref,
                q_ref[at, :],
                base(side) + b * rows,
                [(ref[...], first(side)) for ref, first in zip(fresh_refs, bases)],
                pulled_ref,
                rest[5:],
            )
            return carry

        lax.fori_loop(0, 2, block, 0)
        own_at = pl.ds(pl.multiple_of(core * rows, rows), rows)
        peer_at = pl.ds(pl.multiple_of((1 - core) * rows, rows), rows)
        a = jnp.concatenate([a_buf[own_at, :], a_buf[peer_at, :]], axis=0)
        for j in range(steps):
            out_copy(j).wait()
            part = jnp.dot(a, wo_buf[j], preferred_element_type=F32).astype(BF16)
            own_ref[:, j * wide : (j + 1) * wide] = part[:rows]
            peer_ref[:, j * wide : (j + 1) * wide] = part[rows:]

    return pl.pallas_call(
        kernel,
        in_specs=[SMEM] + [VMEM] * (2 + known) + [HBM] + [ANY] * len(after),
        out_specs=[VMEM, VMEM],
        out_shape=[shape((rows, width)), shape((rows, width))],
        scratch_shapes=[
            pltpu.VMEM((steps, depth, wide), BF16),
            pltpu.VMEM((both, depth), BF16),
            pltpu.SemaphoreType.DMA((steps,)),
        ]
        + attention_scratch(rows, heads, fresh_rows, pulled.shape[0] * pulled.shape[1]),
        compiler_params=params(40),
        cost_estimate=SMALL,
        name="local_rows",
    )(place, query, pulled, *fresh, w_out, *after)


def add_pair(left, pieces):
    rows, width = left.shape
    count = len(pieces)
    wide = width // count

    def kernel(left_ref, *refs):
        out_ref = refs[count]
        for i in range(count):
            cols = slice(i * wide, (i + 1) * wide)
            out_ref[:, cols] = (left_ref[:, cols].astype(F32) + refs[i][...].astype(F32)).astype(
                BF16
            )

    return pl.pallas_call(
        kernel,
        in_specs=[VMEM] * (1 + count),
        out_specs=VMEM,
        out_shape=shape((rows, width)),
        compiler_params=params(8),
        cost_estimate=SMALL,
        name="add_pair",
    )(left, *pieces)


def finish(place, tokens, own, peer, near, far):
    rows, width = tokens.shape
    half = width // 2
    step = 16

    def kernel(place_ref, x_ref, own_ref, peer_ref, near_ref, far_ref, out_ref):
        core = place_ref[1]

        def block(i, carry):
            at = pl.ds(pl.multiple_of(i * step, step), step)
            for start, part in ((core, near_ref), (1 - core, far_ref)):
                cols = pl.ds(pl.multiple_of(start * half, half), half)
                local = own_ref[at, cols].astype(F32) + peer_ref[at, cols].astype(F32)
                total = local + part[at, :].astype(F32)
                out_ref[at, cols] = (x_ref[at, cols].astype(F32) + total).astype(BF16)
            return carry

        lax.fori_loop(0, rows // step, block, 0)

    return pl.pallas_call(
        kernel,
        in_specs=[SMEM] + [VMEM] * 5,
        out_specs=VMEM,
        out_shape=shape((rows, width)),
        compiler_params=params(16),
        cost_estimate=SMALL,
        name="finish",
    )(place, tokens, own, peer, near, far)


def pick_pages(place, wanted, held, after):
    replicas = len(wanted)
    slots = wanted[0].shape[1]
    tensors = len(held)
    _, page, width = held[0].shape
    total = tensors * slots

    def kernel(place_ref, *refs):
        wants, sources = refs[:replicas], refs[replicas : replicas + tensors]
        out_ref = refs[replicas + tensors + len(after)]
        me, rep = place_ref[0], place_ref[3]
        for k in range(replicas):
            asker = lax.rem(rep + k, replicas)
            for i in range(tensors):
                owner = rep * tensors + jnp.bitwise_xor(me, i)
                for s in range(slots):
                    out_ref[asker, i * slots + s] = sources[i][wants[k][0, s, owner]]

    return pl.pallas_call(
        kernel,
        in_specs=[SMEM] * (1 + replicas) + [VMEM] * tensors + [ANY] * len(after),
        out_specs=VMEM,
        out_shape=shape((replicas, total, page, width)),
        compiler_params=params(8),
        cost_estimate=SMALL,
        name="pick_pages",
    )(place, *wanted, *held, *after)


def write_pool(place, slots, kv_pool, early, late):
    pages, heads = kv_pool.shape[:2]
    new_count = slots.shape[1]
    early_rows, late_rows = early[0].shape[0], late[0].shape[0]
    side_rows = (early_rows + late_rows) // 2
    total_rows = early_rows + late_rows

    def kernel(place_ref, slot_ref, pool_ref, *refs):
        early_refs, late_refs, (out_ref, rows_ref) = refs[:3], refs[3:6], refs[6:]
        me, side = place_ref[0], place_ref[2]

        def source(group, i):
            own, y, core = group
            return (own, core.at[0], y, core.at[1])[i]

        for i in range(heads):
            rows_ref[i, :early_rows] = source(early_refs, i)[...]
            rows_ref[i, early_rows:] = source(late_refs, i)[...]
        for p in range(pages):
            found = jnp.int32(-1)
            for j in range(new_count):
                found = jnp.where(slot_ref[0, j] == me * pages + p, j, found)
            first = jnp.maximum(found, 0) * PAGE
            far = (first >= side_rows).astype(jnp.int32)
            inner = first - far * side_rows
            for i in range(heads):
                origin = side if i < 2 else 1 - side
                start = jnp.bitwise_xor(far, origin) * side_rows + inner
                at = jnp.bitwise_xor(me, i)

                @pl.when(found >= 0)
                def _():
                    out_ref[p, at] = rows_ref[i, pl.ds(pl.multiple_of(start, PAGE), PAGE), :]

                @pl.when(found < 0)
                def _():
                    out_ref[p, at] = pool_ref[p, at]

    return pl.pallas_call(
        kernel,
        in_specs=[SMEM, SMEM] + [VMEM] * 7,
        out_specs=VMEM,
        out_shape=shape(kv_pool.shape),
        scratch_shapes=[pltpu.VMEM((heads, total_rows, kv_pool.shape[3]), BF16)],
        compiler_params=params(12),
        cost_estimate=SMALL,
        name="write_pool",
    )(place, slots, kv_pool, *early, *late)


def chip_pair_body(
    tokens,
    gain,
    w_query,
    w_keyvalue,
    w_out,
    kv_pool,
    suffix_pages,
    page_index,
    page_request,
    new_slot,
):
    replicas = lax.axis_size("replica")
    me = lax.axis_index("tensor")
    core = me % 2
    side = me // 2
    rows = tokens.shape[0]
    rep = lax.axis_index("replica")
    place = jnp.stack([me, core, side, rep]).astype(jnp.int32)
    requests = jnp.swapaxes(page_request, 1, 2).reshape(-1)
    scalars = jnp.concatenate([place, suffix_pages[0], requests])

    def over_core(x):
        return lax.ppermute(x, "tensor", [(0, 1), (1, 0), (2, 3), (3, 2)])

    def over_y(x):
        return lax.ppermute(x, "tensor", [(0, 2), (2, 0), (1, 3), (3, 1)])

    def tie(x, *others):
        return lax.optimization_barrier((x, *others))[0]

    w_query, w_keyvalue, w_out = in_hbm(w_query), in_hbm(w_keyvalue), in_hbm(w_out)

    wanted = [jnp.swapaxes(page_index, 1, 2)]
    for k in range(1, replicas):
        back = [(i, (i - k) % replicas) for i in range(replicas)]
        wanted.append(lax.ppermute(wanted[0], "replica", back))

    mine, other, *held = prepare(place, in_hbm(tokens), in_hbm(gain), in_hbm(kv_pool))
    for i in range(1, 4):
        held[i] = lax.ppermute(held[i], "tensor", [(t, t ^ i) for t in range(4)])

    peer_near = over_core(other)
    peer_far = over_core(mine)
    is_first = core == 0
    near_tied = tie(peer_near, held[2], held[3])
    first_half = jnp.where(is_first, mine, near_tied)
    second_half = jnp.where(is_first, near_tied, mine)
    first = over_y(first_half)
    second = over_y(second_half)

    picked = pick_pages(place, wanted, held, [first_half, second_half])
    pulled = lax.all_to_all(picked, "replica", split_axis=0, concat_axis=0, tiled=True)

    q_local, kv_local, wq, wkv = project_local(
        place, [mine, peer_near], [other, peer_far], w_query, w_keyvalue, [picked, scalars]
    )


    def local_base(s):
        return s * (2 * rows)

    def first_base(s):
        return (1 - s) * (2 * rows)

    def second_base(s):
        return (1 - s) * (2 * rows) + rows

    first = tie(first, q_local)
    wide = first.shape[1] // 4
    pieces = [over_core(first[:, i * wide : (i + 1) * wide]) for i in range(4)]
    q_first, kv_first = project_held(first, pieces, wq, wkv)
    early_own = jnp.concatenate([kv_local, kv_first], axis=0)
    early_y = over_y(early_own)
    *there, stay = attend_out(
        scalars, q_first, [kv_local, kv_first], [local_base, first_base], first_base, pulled, w_out
    )
    first_mix = add_pair(stay, [over_core(tie(part, early_y)) for part in there])
    first_sum = over_y(first_mix)

    second = tie(second, first_mix)
    q_second, kv_second = project_far(place, second, over_core(second), w_query, w_keyvalue, [])
    fresh = [kv_local, kv_first, kv_second]
    bases = [local_base, first_base, second_base]
    *there, stay = attend_out(scalars, q_second, fresh, bases, second_base, pulled, w_out)
    second_mix = add_pair(stay, [over_core(part) for part in there])
    late_y = over_y(kv_second)
    second_sum = over_y(tie(second_mix, late_y, first_sum))

    own_part, peer_part = local_rows(
        scalars, q_local, fresh, bases, local_base, pulled, w_out, [second_mix]
    )
    peer_part = over_core(peer_part)

    early = over_core(jnp.stack([early_own, early_y]))
    late = over_core(jnp.stack([kv_second, late_y]))
    pool_out = write_pool(
        place, new_slot, kv_pool, [early_own, early_y, early], [kv_second, late_y, late]
    )

    near = jnp.where(is_first, first_sum, second_sum)
    far = over_core(jnp.where(is_first, second_sum, first_sum))
    layer_out = finish(place, tokens, own_part, peer_part, near, far)
    return (layer_out, pool_out)


def solution(mesh):
    pair = mesh.shape["tensor"] == KV_HEADS
    return jax.shard_map(
        chip_pair_body if pair else gathered_body,
        mesh=mesh,
        in_specs=(
            P(("groups", "replica", "tensor"), None),
            P(),
            P(None, "tensor"),
            P(None, "tensor"),
            P("tensor", None),
            P(("groups", "replica", "tensor"), None, None, None),
            P(("groups", "replica"), None),
            P(("groups", "replica"), None, None),
            P(("groups", "replica"), None, None),
            P(("groups", "replica"), None),
        ),
        out_specs=(
            P(("groups", "replica", "tensor"), None),
            P(("groups", "replica", "tensor"), None, None, None),
        ),
        check_vma=False,
    )
```

```python
import math

import jax
import jax.numpy as jnp
from jax import lax
from jax.experimental import pallas as pl
from jax.experimental.pallas import tpu as pltpu
from jax.sharding import PartitionSpec as P

KV_HEADS = 4
HEAD_DIM = 128
PAGE = 64
UNIT = 8


NEG_FILL = -1e30
EPSILON = 1e-06

F32 = jnp.float32
BF16 = jnp.bfloat16
MIB = 1 << 20
ANY = pl.BlockSpec(memory_space=pl.ANY)
HBM = pl.BlockSpec(memory_space=pltpu.HBM)
SMEM = pl.BlockSpec(memory_space=pltpu.SMEM)
VMEM = pl.BlockSpec(memory_space=pltpu.VMEM)
SMALL = pl.CostEstimate(flops=1024, bytes_accessed=1024, transcendentals=0)
MEDIUM = pl.CostEstimate(flops=1024, bytes_accessed=4000000, transcendentals=0)
LARGE = pl.CostEstimate(flops=20000000000, bytes_accessed=200000000, transcendentals=0)


def params(mib):
    return pltpu.CompilerParams(vmem_limit_bytes=mib * MIB)


def in_hbm(x):
    return pltpu.with_memory_space_constraint(x, pltpu.HBM)


def shape(dims, dtype=BF16):
    return jax.ShapeDtypeStruct(dims, dtype)


def normalize(rows, gain):
    values = rows.astype(jnp.float32)
    inverse = lax.rsqrt(jnp.mean(values * values, axis=-1, keepdims=True) + EPSILON)
    return (values * inverse * gain.astype(jnp.float32)).astype(jnp.bfloat16)


def row_segments(pages, total_rows):
    bounds = jnp.cumsum(pages) * UNIT
    positions = jnp.arange(total_rows, dtype=jnp.int32)
    return jnp.sum((positions[:, None] >= bounds[None, :]).astype(jnp.int32), axis=1)


def gathered_body(
    tokens,
    gain,
    w_query,
    w_keyvalue,
    w_out,
    kv_pool,
    suffix_pages,
    page_index,
    page_request,
    new_slot,
):
    replicas = lax.axis_size("replica")
    tensors = lax.axis_size("tensor")
    owners = replicas * tensors
    position = lax.axis_index("tensor")
    query_width = w_query.shape[1]
    local_heads = query_width // HEAD_DIM
    share = tensors // KV_HEADS
    my_head = position // share
    scale_factor = 1.0 / math.sqrt(HEAD_DIM)
    normed = normalize(tokens, gain)
    piece = lax.all_gather(normed, "tensor", axis=0, tiled=True)
    first = jnp.dot(piece, w_query, preferred_element_type=jnp.float32)
    second = jnp.dot(piece, w_keyvalue, preferred_element_type=jnp.float32)
    projected = jnp.concatenate([first, second], axis=1).astype(jnp.bfloat16)
    query = projected[:, :query_width]
    keyvalue = lax.all_gather(projected[:, query_width:], "tensor", axis=1, tiled=True)
    total_rows = query.shape[0]
    wanted = lax.all_to_all(
        page_index[0], ("replica", "tensor"), split_axis=0, concat_axis=0, tiled=True
    )
    slot_count = wanted.shape[1]
    sources = jnp.arange(owners, dtype=jnp.int32) % tensors
    source_heads = sources // share
    flat_pool = kv_pool.reshape(kv_pool.shape[0] * KV_HEADS, PAGE, 2 * HEAD_DIM)
    outgoing = flat_pool[wanted * KV_HEADS + source_heads[:, None]]
    sub_tokens = outgoing.shape[2]
    pulled = lax.all_to_all(
        outgoing, ("replica", "tensor"), split_axis=0, concat_axis=0, tiled=True
    )
    segments = row_segments(suffix_pages[0], total_rows)
    key_groups = page_request[0]
    stacked = (
        query.reshape(total_rows, local_heads, HEAD_DIM)
        .transpose(1, 0, 2)
        .reshape(local_heads * total_rows, HEAD_DIM)
    )
    own_new = lax.dynamic_index_in_dim(
        keyvalue.reshape(total_rows, KV_HEADS, 2 * HEAD_DIM), my_head, 1, keepdims=False
    )
    row_order = jnp.arange(total_rows, dtype=jnp.int32)
    causal = (segments[:, None] == segments[None, :]) & (row_order[None, :] <= row_order[:, None])

    def block_scores(queries, head_count, keys, allowed):
        raw = (
            jnp.dot(queries, keys[:, :HEAD_DIM].T, preferred_element_type=jnp.float32)
            * scale_factor
        )
        raw = raw.reshape(head_count, total_rows, keys.shape[0])
        return jnp.where(allowed[None], raw, NEG_FILL)

    first_scores = block_scores(stacked, local_heads, own_new, causal)
    running = jnp.max(first_scores, axis=2)
    probs = jnp.exp(first_scores - running[:, :, None])
    denominator = jnp.sum(probs, axis=2)
    numerator = jnp.dot(
        probs.astype(jnp.bfloat16).reshape(local_heads * total_rows, total_rows),
        own_new[:, HEAD_DIM:],
        preferred_element_type=jnp.float32,
    )
    block_owners = 16
    blocks = owners // block_owners

    def absorb(step, state):
        peak, total, mixed = state
        pages = lax.dynamic_slice_in_dim(pulled, step * block_owners, block_owners, 0)
        keys = pages.reshape(block_owners * slot_count * sub_tokens, 2 * HEAD_DIM)
        labels = lax.dynamic_slice_in_dim(key_groups, step * block_owners, block_owners, 0).reshape(
            -1
        )
        matches = (segments[:, None] == labels[None, :])[:, :, None]
        allowed = jnp.broadcast_to(matches, (total_rows, labels.shape[0], sub_tokens)).reshape(
            total_rows, labels.shape[0] * sub_tokens
        )
        scores = block_scores(stacked, local_heads, keys, allowed)
        updated = jnp.maximum(peak, jnp.max(scores, axis=2))
        rescale = jnp.exp(peak - updated)
        weights = jnp.where(allowed[None], jnp.exp(scores - updated[:, :, None]), 0.0)
        total = total * rescale + jnp.sum(weights, axis=2)
        flat_weights = weights.astype(jnp.bfloat16).reshape(local_heads * total_rows, keys.shape[0])
        mixed = mixed * rescale.reshape(-1)[:, None] + jnp.dot(
            flat_weights, keys[:, HEAD_DIM:], preferred_element_type=jnp.float32
        )
        return (updated, total, mixed)

    running, denominator, numerator = lax.fori_loop(
        0, blocks, absorb, (running, denominator, numerator)
    )
    attention = (numerator / denominator.reshape(-1)[:, None]).astype(jnp.bfloat16)
    attention = (
        attention.reshape(local_heads, total_rows, HEAD_DIM)
        .transpose(1, 0, 2)
        .reshape(total_rows, query_width)
    )
    summed = lax.psum_scatter(
        jnp.dot(attention, w_out, preferred_element_type=jnp.float32).astype(jnp.bfloat16),
        "tensor",
        scatter_dimension=0,
        tiled=True,
    ).astype(jnp.float32)
    layer_out = (tokens.astype(jnp.float32) + summed).astype(jnp.bfloat16)
    new_count = total_rows // PAGE
    fresh = (
        keyvalue.reshape(new_count, PAGE, KV_HEADS, 2 * HEAD_DIM)
        .transpose(0, 2, 1, 3)
        .reshape(new_count, KV_HEADS * PAGE * 2 * HEAD_DIM)
    )
    local_pages = kv_pool.shape[0]
    targets = position * local_pages + jnp.arange(local_pages, dtype=jnp.int32)
    match_table = new_slot[0][None, :] == targets[:, None]
    placed = jnp.dot(
        match_table.astype(jnp.bfloat16), fresh, preferred_element_type=jnp.float32
    ).astype(jnp.bfloat16)
    placed = placed.reshape(kv_pool.shape)
    landed = jnp.any(match_table, axis=1)
    pool_out = jnp.where(landed[:, None, None, None], placed, kv_pool)
    return (layer_out, pool_out)


def prepare(place, tokens, gain, kv_pool):
    rows, width = tokens.shape
    half = width // 2
    step = 32
    pages, heads = kv_pool.shape[:2]
    blocks = rows // step

    def kernel(place_ref, x, g, pool, mine_ref, other_ref, *refs):
        held, (x_buf, g_buf, pool_buf, sems) = refs[:heads], refs[heads:]
        me, core = place_ref[0], place_ref[1]
        pool_copy = pltpu.make_async_copy(pool, pool_buf, sems.at[blocks + 1])

        def row_copy(b):
            at = pl.ds(b * step, step)
            return pltpu.make_async_copy(x.at[at], x_buf.at[at], sems.at[b])

        gain_copy = pltpu.make_async_copy(g, g_buf, sems.at[blocks])
        row_copy(0).start()
        gain_copy.start()
        for b in range(1, blocks):
            row_copy(b).start()
        pool_copy.start()
        near = pl.multiple_of(core * half, half)
        far = pl.multiple_of((1 - core) * half, half)
        for b in range(blocks):
            row_copy(b).wait()
            if b == 0:
                gain_copy.wait()

            def block(i, carry):
                at = pl.ds(pl.multiple_of(b * step + i * 16, 16), 16)
                total = jnp.zeros((16, 1), F32)
                for part in range(2):
                    values = x_buf[at, part * half : (part + 1) * half].astype(F32)
                    total += jnp.sum(values * values, axis=1, keepdims=True)
                inverse = lax.rsqrt(total * (1.0 / width) + EPSILON)
                for start, out in ((near, mine_ref), (far, other_ref)):
                    cols = pl.ds(start, half)
                    values = x_buf[at, cols].astype(F32)
                    out[at, :] = (values * inverse * g_buf[cols].astype(F32)[None, :]).astype(BF16)
                return carry

            lax.fori_loop(0, step // 16, block, 0)
        pool_copy.wait()
        for i in range(heads):
            for p in range(pages):
                held[i][p] = pool_buf[p, jnp.bitwise_xor(me, i)]

    return pl.pallas_call(
        kernel,
        in_specs=[SMEM] + [HBM] * 3,
        out_specs=[VMEM] * (2 + heads),
        out_shape=[shape((rows, half))] * 2 + [shape((pages,) + kv_pool.shape[2:])] * heads,
        scratch_shapes=[
            pltpu.VMEM((rows, width), BF16),
            pltpu.VMEM((width,), BF16),
            pltpu.VMEM(kv_pool.shape, BF16),
            pltpu.SemaphoreType.DMA((blocks + 2,)),
        ],
        compiler_params=params(16),
        cost_estimate=SMALL,
        name="prepare",
    )(place, tokens, gain, kv_pool)


def project_local(place, near, far, w_query, w_keyvalue, after):
    rows, half = near[0].shape
    q_width, kv_width = w_query.shape[1], w_keyvalue.shape[1]
    steps = 8
    depth = 2 * half // steps
    waits = len(after)

    def kernel(place_ref, near_own, near_peer, far_own, far_peer, wq, wkv, *refs):
        q_ref, kv_ref, wq_buf, wkv_buf, q_acc, kv_acc, sems = refs[waits:]
        core = place_ref[1]
        stream = weight_stream(core, half, steps, (wq, wkv), (wq_buf, wkv_buf), sems)
        for j in range(steps):
            for copy in stream(j):
                copy.start()
        for j in range(steps):
            for copy in stream(j):
                copy.wait()
            group = (near_own, near_peer) if j < steps // 2 else (far_own, far_peer)
            cols = slice((j % (steps // 2)) * depth, (j % (steps // 2) + 1) * depth)
            x = jnp.concatenate([ref[:, cols] for ref in group], axis=0)
            q_part = jnp.dot(x, wq_buf[j], preferred_element_type=F32)
            kv_part = jnp.dot(x, wkv_buf[j], preferred_element_type=F32)
            if j == 0:
                q_acc[...] = q_part
                kv_acc[...] = kv_part
            elif j < steps - 1:
                q_acc[...] += q_part
                kv_acc[...] += kv_part
            else:
                q_last = (q_acc[...] + q_part).astype(BF16)
                kv_last = (kv_acc[...] + kv_part).astype(BF16)
        for b in range(2):
            at = pl.ds(pl.multiple_of((core if b == 0 else 1 - core) * rows, rows), rows)
            q_ref[at, :] = q_last[b * rows : (b + 1) * rows]
            kv_ref[at, :] = kv_last[b * rows : (b + 1) * rows]

    total = 2 * rows
    return pl.pallas_call(
        kernel,
        in_specs=[SMEM] + [VMEM] * 4 + [HBM] * 2 + [ANY] * waits,
        out_specs=[VMEM] * 4,
        out_shape=[
            shape((total, q_width)),
            shape((total, kv_width)),
            pltpu.VMEM((steps, depth, q_width), BF16),
            pltpu.VMEM((steps, depth, kv_width), BF16),
        ],
        scratch_shapes=[
            pltpu.VMEM((total, q_width), F32),
            pltpu.VMEM((total, kv_width), F32),
            pltpu.SemaphoreType.DMA((2 * steps,)),
        ],
        compiler_params=params(10),
        cost_estimate=LARGE,
        name="project_local",
    )(place, *near, *far, w_query, w_keyvalue, *after)


def weight_stream(core, half, steps, sources, buffers, sems):
    depth = 2 * half // steps

    def copies(j):
        base = core if j < steps // 2 else 1 - core
        start = pl.multiple_of(base * half + (j % (steps // 2)) * depth, depth)
        count = len(sources)
        return [
            pltpu.make_async_copy(w.at[pl.ds(start, depth)], buf.at[j], sems.at[count * j + i])
            for i, (w, buf) in enumerate(zip(sources, buffers))
        ]

    return copies


PAGES_STEP = 4
REQUESTS = 4
SIZES_AT = 4
REQUESTS_AT = 8


def attention_scratch(block_rows, heads, fresh_rows, slots):
    stacked = heads * block_rows
    return [
        pltpu.VMEM((stacked, fresh_rows + slots * PAGE), F32),
        pltpu.VMEM((stacked, HEAD_DIM), F32),
        pltpu.VMEM((stacked, HEAD_DIM), F32),
        pltpu.VMEM((slots * PAGE, 2 * HEAD_DIM), BF16),
        pltpu.SMEM((slots,), jnp.int32),
    ]


def attend_block(place_ref, q, first_row, fresh, pulled, scratch):
    scores, total_ref, mixed_ref, cache, labels = scratch
    me = place_ref[0]
    block_rows, width = q.shape
    heads = width // HEAD_DIM
    stacked = heads * block_rows
    groups, per = pulled.shape[:2]
    tensors = 4
    slots = per // tensors
    wide = PAGES_STEP * PAGE
    factor = math.log2(math.e) / math.sqrt(HEAD_DIM)
    bound = []
    running = jnp.int32(0)
    for k in range(REQUESTS):
        running = running + place_ref[SIZES_AT + k] * UNIT
        bound.append(running)

    def segment_of(position):
        return sum((position >= b).astype(jnp.int32) for b in bound)

    lowest = segment_of(first_row)
    highest = segment_of(first_row + block_rows - 1)
    count = jnp.int32(0)
    for g in range(groups):
        for p in range(per):
            owner = g * tensors + jnp.bitwise_xor(me, p // slots)
            label = place_ref[REQUESTS_AT + p % slots * groups * tensors + owner]
            wanted = (label >= lowest) & (label <= highest)

            @pl.when(wanted)
            def _():
                cache[pl.ds(pl.multiple_of(count * PAGE, PAGE), PAGE), :] = pulled[g, p]
                labels[count] = label

            count = count + wanted.astype(jnp.int32)
    steps = (count + PAGES_STEP - 1) // PAGES_STEP
    for k in range(PAGES_STEP - 1):

        @pl.when(count + k < steps * PAGES_STEP)
        def _():
            cache[pl.ds(pl.multiple_of((count + k) * PAGE, PAGE), PAGE), :] = jnp.zeros(
                (PAGE, 2 * HEAD_DIM), BF16
            )
            labels[count + k] = jnp.int32(-1)

    q_rows = jnp.concatenate([q[:, h * HEAD_DIM : (h + 1) * HEAD_DIM] for h in range(heads)], axis=0)
    row_position = first_row + lax.broadcasted_iota(jnp.int32, (block_rows, 1), 0)
    row_segment = segment_of(row_position)

    def masked_scores(keys, allowed):
        raw = lax.dot_general(q_rows, keys, (((1,), (1,)), ((), ())), preferred_element_type=F32)
        n = keys.shape[0]
        return jnp.where(allowed[None], raw.reshape(heads, block_rows, n), NEG_FILL).reshape(
            stacked, n
        )

    def fold(values, combine):
        pieces = [values[:, i : i + HEAD_DIM] for i in range(0, values.shape[1], HEAD_DIM)]
        result = pieces[0]
        for piece in pieces[1:]:
            result = combine(result, piece)
        return result

    new = jnp.concatenate([rows for rows, _ in fresh], axis=0)
    fresh_rows = new.shape[0]
    key_position = jnp.concatenate(
        [
            base + lax.broadcasted_iota(jnp.int32, (1, rows.shape[0]), 1)
            for rows, base in fresh
        ],
        axis=1,
    )
    allowed = (row_segment == segment_of(key_position)) & (key_position <= row_position)
    masked = masked_scores(new[:, :HEAD_DIM], allowed)
    scores[:, :fresh_rows] = masked
    total_ref[...] = fold(masked, jnp.maximum)
    lanes = lax.broadcasted_iota(jnp.int32, (1, wide), 1) // PAGE

    def add_scores(g, carry):
        label = jnp.full((1, wide), -1, jnp.int32)
        for j in range(PAGES_STEP):
            label = jnp.where(lanes == j, labels[g * PAGES_STEP + j], label)
        keys = cache[pl.ds(pl.multiple_of(g * wide, wide), wide), :HEAD_DIM]
        masked = masked_scores(keys, row_segment == label)
        scores[:, pl.ds(pl.multiple_of(fresh_rows + g * wide, PAGE), wide)] = masked
        total_ref[...] = jnp.maximum(total_ref[...], fold(masked, jnp.maximum))
        return carry

    lax.fori_loop(0, steps, add_scores, 0)
    top = jnp.max(total_ref[...], axis=1, keepdims=True) * factor
    probs = jnp.exp2(scores[:, :fresh_rows] * factor - top)
    total_ref[...] = fold(probs, jnp.add)
    mixed_ref[...] = jnp.dot(probs.astype(BF16), new[:, HEAD_DIM:], preferred_element_type=F32)

    def add_values(g, carry):
        part = scores[:, pl.ds(pl.multiple_of(fresh_rows + g * wide, PAGE), wide)]
        probs = jnp.exp2(part * factor - top)
        values = cache[pl.ds(pl.multiple_of(g * wide, wide), wide), HEAD_DIM:]
        total_ref[...] += fold(probs, jnp.add)
        mixed_ref[...] += jnp.dot(probs.astype(BF16), values, preferred_element_type=F32)
        return carry

    lax.fori_loop(0, steps, add_values, 0)
    denominator = jnp.sum(total_ref[...], axis=1, keepdims=True)
    result = (mixed_ref[...] / denominator).astype(BF16)
    return jnp.concatenate(
        [result[h * block_rows : (h + 1) * block_rows] for h in range(heads)], axis=1
    )


def project_held(near, far, w_query, w_keyvalue, after):
    rows, half = near.shape
    pieces = len(far)
    steps, depth, q_width = w_query.shape
    kv_width = w_keyvalue.shape[2]

    def kernel(near_ref, *refs):
        far_refs = refs[:pieces]
        wq, wkv = refs[pieces : pieces + 2]
        q_ref, kv_ref = refs[pieces + 2 + len(after) :]
        for w, out in ((wq, q_ref), (wkv, kv_ref)):
            total = None
            for j in range(steps):
                at = j * depth
                if at < half:
                    x = near_ref[:, at : at + depth]
                else:
                    wide = half // pieces
                    x = far_refs[(at - half) // wide][:, at % wide : at % wide + depth]
                part = jnp.dot(x, w[j], preferred_element_type=F32)
                total = part if j == 0 else total + part
            out[...] = total.astype(BF16)

    return pl.pallas_call(
        kernel,
        in_specs=[VMEM] * (3 + pieces) + [ANY] * len(after),
        out_specs=[VMEM] * 2,
        out_shape=[shape((rows, q_width)), shape((rows, kv_width))],
        compiler_params=params(6),
        cost_estimate=SMALL,
        name="project_held",
    )(near, *far, w_query, w_keyvalue, *after)


def project_far(place, near, far, w_query, w_keyvalue, after):
    rows, half = near.shape
    q_width, kv_width = w_query.shape[1], w_keyvalue.shape[1]
    steps = 8
    depth = 2 * half // steps

    def kernel(place_ref, near_ref, far_ref, wq, wkv, *refs):
        q_ref, kv_ref, wq_buf, wkv_buf, sems = refs[len(after) :]
        stream = weight_stream(place_ref[1], half, steps, (wq, wkv), (wq_buf, wkv_buf), sems)
        for j in range(steps):
            for copy in stream(j):
                copy.start()
        q_sum = kv_sum = None
        for j in range(steps):
            for copy in stream(j):
                copy.wait()
            x_ref = near_ref if j < steps // 2 else far_ref
            x = x_ref[:, (j % (steps // 2)) * depth : (j % (steps // 2) + 1) * depth]
            q_part = jnp.dot(x, wq_buf[j], preferred_element_type=F32)
            kv_part = jnp.dot(x, wkv_buf[j], preferred_element_type=F32)
            q_sum = q_part if j == 0 else q_sum + q_part
            kv_sum = kv_part if j == 0 else kv_sum + kv_part
        q_ref[...] = q_sum.astype(BF16)
        kv_ref[...] = kv_sum.astype(BF16)

    return pl.pallas_call(
        kernel,
        in_specs=[SMEM] + [VMEM] * 2 + [HBM] * 2 + [ANY] * len(after),
        out_specs=[VMEM] * 2,
        out_shape=[shape((rows, q_width)), shape((rows, kv_width))],
        scratch_shapes=[
            pltpu.VMEM((steps, depth, q_width), BF16),
            pltpu.VMEM((steps, depth, kv_width), BF16),
            pltpu.SemaphoreType.DMA((2 * steps,)),
        ],
        compiler_params=params(32),
        cost_estimate=SMALL,
        name="project_far",
    )(place, near, far, w_query, w_keyvalue, *after)


def attend_out(place, query, fresh, bases, base, pulled, w_out):
    rows, depth = query.shape
    width = w_out.shape[1]
    half = width // 2
    heads = depth // HEAD_DIM
    out_steps = 4
    wide = half // out_steps
    known = len(fresh)
    count = sum(f.shape[0] for f in fresh)
    fresh_rows = -(-count // HEAD_DIM) * HEAD_DIM
    pad = fresh_rows - count

    def kernel(place_ref, q_ref, pulled_ref, *refs):
        fresh_refs = refs[:known]
        wo = refs[known]
        there_refs, refs_after = refs[known + 1 : known + 1 + out_steps], refs[known + 1 + out_steps :]
        stay_ref, wo_buf, sems = refs_after[:3]
        core, side = place_ref[1], place_ref[2]

        def copy(j):
            first = 1 - core if j < out_steps else core
            start = pl.multiple_of(first * half + (j % out_steps) * wide, wide)
            return pltpu.make_async_copy(wo.at[:, pl.ds(start, wide)], wo_buf.at[j], sems.at[j])

        for j in range(2 * out_steps):
            copy(j).start()
        pairs = [(ref[...], at(side)) for ref, at in zip(fresh_refs, bases)]
        if pad:
            pairs.append((jnp.zeros((pad, 2 * HEAD_DIM), BF16), jnp.int32(1 << 20)))
        mixed = attend_block(
            place_ref, q_ref[...], base(side), pairs, pulled_ref, refs_after[3:]
        )
        for j in range(2 * out_steps):
            copy(j).wait()
            part = jnp.dot(mixed, wo_buf[j], preferred_element_type=F32).astype(BF16)
            if j < out_steps:
                there_refs[j][...] = part
            else:
                at = (j - out_steps) * wide
                stay_ref[:, at : at + wide] = part

    return pl.pallas_call(
        kernel,
        in_specs=[SMEM] + [VMEM] * (2 + known) + [HBM],
        out_specs=[VMEM] * (out_steps + 1),
        out_shape=[shape((rows, wide))] * out_steps + [shape((rows, half))],
        scratch_shapes=[
            pltpu.VMEM((2 * out_steps, depth, wide), BF16),
            pltpu.SemaphoreType.DMA((2 * out_steps,)),
        ]
        + attention_scratch(rows, heads, fresh_rows, pulled.shape[0] * pulled.shape[1]),
        compiler_params=params(30),
        cost_estimate=MEDIUM,
        name="attend_out",
    )(place, query, pulled, *fresh, w_out)


def local_rows(place, query, fresh, bases, base, pulled, w_out, after):
    both, depth = query.shape
    rows = both // 2
    width = w_out.shape[1]
    heads = depth // HEAD_DIM
    steps = 8
    wide = width // steps
    known = len(fresh)
    fresh_rows = sum(f.shape[0] for f in fresh)

    def kernel(place_ref, q_ref, pulled_ref, *refs):
        fresh_refs = refs[:known]
        wo = refs[known]
        rest = refs[known + 1 + len(after) :]
        own_ref, peer_ref, wo_buf, a_buf, sems = rest[:5]
        core, side = place_ref[1], place_ref[2]

        def out_copy(j):
            return pltpu.make_async_copy(
                wo.at[:, j * wide : (j + 1) * wide], wo_buf.at[j], sems.at[j]
            )

        for j in range(steps):
            out_copy(j).start()

        def block(b, carry):
            at = pl.ds(pl.multiple_of(b * rows, rows), rows)
            a_buf[at, :] = attend_block(
                place_ref,
                q_ref[at, :],
                base(side) + b * rows,
                [(ref[...], first(side)) for ref, first in zip(fresh_refs, bases)],
                pulled_ref,
                rest[5:],
            )
            return carry

        lax.fori_loop(0, 2, block, 0)
        own_at = pl.ds(pl.multiple_of(core * rows, rows), rows)
        peer_at = pl.ds(pl.multiple_of((1 - core) * rows, rows), rows)
        a = jnp.concatenate([a_buf[own_at, :], a_buf[peer_at, :]], axis=0)
        for j in range(steps):
            out_copy(j).wait()
            part = jnp.dot(a, wo_buf[j], preferred_element_type=F32).astype(BF16)
            own_ref[:, j * wide : (j + 1) * wide] = part[:rows]
            peer_ref[:, j * wide : (j + 1) * wide] = part[rows:]

    return pl.pallas_call(
        kernel,
        in_specs=[SMEM] + [VMEM] * (2 + known) + [HBM] + [ANY] * len(after),
        out_specs=[VMEM, VMEM],
        out_shape=[shape((rows, width)), shape((rows, width))],
        scratch_shapes=[
            pltpu.VMEM((steps, depth, wide), BF16),
            pltpu.VMEM((both, depth), BF16),
            pltpu.SemaphoreType.DMA((steps,)),
        ]
        + attention_scratch(rows, heads, fresh_rows, pulled.shape[0] * pulled.shape[1]),
        compiler_params=params(40),
        cost_estimate=SMALL,
        name="local_rows",
    )(place, query, pulled, *fresh, w_out, *after)


def add_pair(left, pieces):
    rows, width = left.shape
    count = len(pieces)
    wide = width // count

    def kernel(left_ref, *refs):
        out_ref = refs[count]
        for i in range(count):
            cols = slice(i * wide, (i + 1) * wide)
            out_ref[:, cols] = (left_ref[:, cols].astype(F32) + refs[i][...].astype(F32)).astype(
                BF16
            )

    return pl.pallas_call(
        kernel,
        in_specs=[VMEM] * (1 + count),
        out_specs=VMEM,
        out_shape=shape((rows, width)),
        compiler_params=params(8),
        cost_estimate=SMALL,
        name="add_pair",
    )(left, *pieces)


def finish(place, tokens, own, peer, near, far):
    rows, width = tokens.shape
    half = width // 2
    step = 16

    def kernel(place_ref, x_ref, own_ref, peer_ref, near_ref, far_ref, out_ref):
        core = place_ref[1]

        def block(i, carry):
            at = pl.ds(pl.multiple_of(i * step, step), step)
            for start, part in ((core, near_ref), (1 - core, far_ref)):
                cols = pl.ds(pl.multiple_of(start * half, half), half)
                local = own_ref[at, cols].astype(F32) + peer_ref[at, cols].astype(F32)
                total = local + part[at, :].astype(F32)
                out_ref[at, cols] = (x_ref[at, cols].astype(F32) + total).astype(BF16)
            return carry

        lax.fori_loop(0, rows // step, block, 0)

    return pl.pallas_call(
        kernel,
        in_specs=[SMEM] + [VMEM] * 5,
        out_specs=VMEM,
        out_shape=shape((rows, width)),
        compiler_params=params(16),
        cost_estimate=SMALL,
        name="finish",
    )(place, tokens, own, peer, near, far)


def pick_pages(place, wanted, held, after):
    replicas = len(wanted)
    slots = wanted[0].shape[1]
    tensors = len(held)
    _, page, width = held[0].shape
    total = tensors * slots

    def kernel(place_ref, *refs):
        wants, sources = refs[:replicas], refs[replicas : replicas + tensors]
        out_ref = refs[replicas + tensors + len(after)]
        me, rep = place_ref[0], place_ref[3]
        for k in range(replicas):
            asker = lax.rem(rep + k, replicas)
            for i in range(tensors):
                owner = rep * tensors + jnp.bitwise_xor(me, i)
                for s in range(slots):
                    out_ref[asker, i * slots + s] = sources[i][wants[k][0, s, owner]]

    return pl.pallas_call(
        kernel,
        in_specs=[SMEM] * (1 + replicas) + [VMEM] * tensors + [ANY] * len(after),
        out_specs=VMEM,
        out_shape=shape((replicas, total, page, width)),
        compiler_params=params(8),
        cost_estimate=SMALL,
        name="pick_pages",
    )(place, *wanted, *held, *after)


def write_pool(place, slots, kv_pool, early, late):
    pages, heads = kv_pool.shape[:2]
    new_count = slots.shape[1]
    early_rows, late_rows = early[0].shape[0], late[0].shape[0]
    side_rows = (early_rows + late_rows) // 2
    total_rows = early_rows + late_rows

    def kernel(place_ref, slot_ref, pool_ref, *refs):
        early_refs, late_refs, (out_ref, rows_ref) = refs[:3], refs[3:6], refs[6:]
        me, side = place_ref[0], place_ref[2]

        def source(group, i):
            own, y, core = group
            return (own, core.at[0], y, core.at[1])[i]

        for i in range(heads):
            rows_ref[i, :early_rows] = source(early_refs, i)[...]
            rows_ref[i, early_rows:] = source(late_refs, i)[...]
        for p in range(pages):
            found = jnp.int32(-1)
            for j in range(new_count):
                found = jnp.where(slot_ref[0, j] == me * pages + p, j, found)
            first = jnp.maximum(found, 0) * PAGE
            far = (first >= side_rows).astype(jnp.int32)
            inner = first - far * side_rows
            for i in range(heads):
                origin = side if i < 2 else 1 - side
                start = jnp.bitwise_xor(far, origin) * side_rows + inner
                at = jnp.bitwise_xor(me, i)

                @pl.when(found >= 0)
                def _():
                    out_ref[p, at] = rows_ref[i, pl.ds(pl.multiple_of(start, PAGE), PAGE), :]

                @pl.when(found < 0)
                def _():
                    out_ref[p, at] = pool_ref[p, at]

    return pl.pallas_call(
        kernel,
        in_specs=[SMEM, SMEM] + [VMEM] * 7,
        out_specs=VMEM,
        out_shape=shape(kv_pool.shape),
        scratch_shapes=[pltpu.VMEM((heads, total_rows, kv_pool.shape[3]), BF16)],
        compiler_params=params(12),
        cost_estimate=SMALL,
        name="write_pool",
    )(place, slots, kv_pool, *early, *late)


def chip_pair_body(
    tokens,
    gain,
    w_query,
    w_keyvalue,
    w_out,
    kv_pool,
    suffix_pages,
    page_index,
    page_request,
    new_slot,
):
    replicas = lax.axis_size("replica")
    me = lax.axis_index("tensor")
    core = me % 2
    side = me // 2
    rows = tokens.shape[0]
    rep = lax.axis_index("replica")
    place = jnp.stack([me, core, side, rep]).astype(jnp.int32)
    requests = jnp.swapaxes(page_request, 1, 2).reshape(-1)
    scalars = jnp.concatenate([place, suffix_pages[0], requests])

    def over_core(x):
        return lax.ppermute(x, "tensor", [(0, 1), (1, 0), (2, 3), (3, 2)])

    def over_y(x):
        return lax.ppermute(x, "tensor", [(0, 2), (2, 0), (1, 3), (3, 1)])

    def tie(x, *others):
        return lax.optimization_barrier((x, *others))[0]

    w_query, w_keyvalue, w_out = in_hbm(w_query), in_hbm(w_keyvalue), in_hbm(w_out)

    wanted = [jnp.swapaxes(page_index, 1, 2)]
    for k in range(1, replicas):
        back = [(i, (i - k) % replicas) for i in range(replicas)]
        wanted.append(lax.ppermute(wanted[0], "replica", back))

    mine, other, *held = prepare(place, in_hbm(tokens), in_hbm(gain), in_hbm(kv_pool))
    for i in range(1, 4):
        held[i] = lax.ppermute(held[i], "tensor", [(t, t ^ i) for t in range(4)])

    peer_near = over_core(other)
    peer_far = over_core(mine)
    is_first = core == 0
    near_tied = tie(peer_near, held[2], held[3])
    first_half = jnp.where(is_first, mine, near_tied)
    second_half = jnp.where(is_first, near_tied, mine)
    first = over_y(first_half)
    second = over_y(second_half)

    picked = pick_pages(place, wanted, held, [first_half, second_half])
    pulled = lax.all_to_all(picked, "replica", split_axis=0, concat_axis=0, tiled=True)

    q_local, kv_local, wq, wkv = project_local(
        place, [mine, peer_near], [other, peer_far], w_query, w_keyvalue, [picked, scalars]
    )


    def local_base(s):
        return s * (2 * rows)

    def first_base(s):
        return (1 - s) * (2 * rows)

    def second_base(s):
        return (1 - s) * (2 * rows) + rows

    first = tie(first, q_local)
    wide = first.shape[1] // 4
    pieces = [over_core(first[:, i * wide : (i + 1) * wide]) for i in range(4)]
    q_first, kv_first = project_held(first, pieces, wq, wkv, [])
    early_own = jnp.concatenate([kv_local, kv_first], axis=0)
    early_y = over_y(early_own)
    *there, stay = attend_out(
        scalars, q_first, [kv_local, kv_first], [local_base, first_base], first_base, pulled, w_out
    )
    first_mix = add_pair(stay, [over_core(tie(part, early_y)) for part in there])
    first_sum = over_y(first_mix)

    second = tie(second, first_mix)
    q_second, kv_second = project_far(place, second, over_core(second), w_query, w_keyvalue, [])
    fresh = [kv_local, kv_first, kv_second]
    bases = [local_base, first_base, second_base]
    *there, stay = attend_out(scalars, q_second, fresh, bases, second_base, pulled, w_out)
    late_y = over_y(kv_second)
    second_mix = add_pair(stay, [over_core(tie(part, late_y)) for part in there])
    second_sum = over_y(tie(second_mix, first_sum))

    own_part, peer_part = local_rows(
        scalars, q_local, fresh, bases, local_base, pulled, w_out, [second_mix]
    )
    peer_part = over_core(peer_part)

    early = over_core(jnp.stack([early_own, early_y]))
    late = over_core(jnp.stack([kv_second, late_y]))
    pool_out = write_pool(
        place, new_slot, kv_pool, [early_own, early_y, early], [kv_second, late_y, late]
    )

    second_sum = tie(second_sum, pool_out)
    near = jnp.where(is_first, first_sum, second_sum)
    far = over_core(jnp.where(is_first, second_sum, first_sum))
    layer_out = finish(place, tokens, own_part, peer_part, near, far)
    return (layer_out, pool_out)


def solution(mesh):
    pair = mesh.shape["tensor"] == KV_HEADS
    return jax.shard_map(
        chip_pair_body if pair else gathered_body,
        mesh=mesh,
        in_specs=(
            P(("groups", "replica", "tensor"), None),
            P(),
            P(None, "tensor"),
            P(None, "tensor"),
            P("tensor", None),
            P(("groups", "replica", "tensor"), None, None, None),
            P(("groups", "replica"), None),
            P(("groups", "replica"), None, None),
            P(("groups", "replica"), None, None),
            P(("groups", "replica"), None),
        ),
        out_specs=(
            P(("groups", "replica", "tensor"), None),
            P(("groups", "replica", "tensor"), None, None, None),
        ),
        check_vma=False,
    )
```

```python
import math

import jax
import jax.numpy as jnp
from jax import lax
from jax.experimental import pallas as pl
from jax.experimental.pallas import tpu as pltpu
from jax.sharding import PartitionSpec as P

KV_HEADS = 4
HEAD_DIM = 128
PAGE = 64
UNIT = 8


NEG_FILL = -1e30
EPSILON = 1e-06

F32 = jnp.float32
BF16 = jnp.bfloat16
MIB = 1 << 20
ANY = pl.BlockSpec(memory_space=pl.ANY)
HBM = pl.BlockSpec(memory_space=pltpu.HBM)
SMEM = pl.BlockSpec(memory_space=pltpu.SMEM)
VMEM = pl.BlockSpec(memory_space=pltpu.VMEM)
SMALL = pl.CostEstimate(flops=1024, bytes_accessed=1024, transcendentals=0)
MEDIUM = pl.CostEstimate(flops=1024, bytes_accessed=4000000, transcendentals=0)
LARGE = pl.CostEstimate(flops=20000000000, bytes_accessed=200000000, transcendentals=0)


def params(mib):
    return pltpu.CompilerParams(vmem_limit_bytes=mib * MIB)


def in_hbm(x):
    return pltpu.with_memory_space_constraint(x, pltpu.HBM)


def shape(dims, dtype=BF16):
    return jax.ShapeDtypeStruct(dims, dtype)


def normalize(rows, gain):
    values = rows.astype(jnp.float32)
    inverse = lax.rsqrt(jnp.mean(values * values, axis=-1, keepdims=True) + EPSILON)
    return (values * inverse * gain.astype(jnp.float32)).astype(jnp.bfloat16)


def row_segments(pages, total_rows):
    bounds = jnp.cumsum(pages) * UNIT
    positions = jnp.arange(total_rows, dtype=jnp.int32)
    return jnp.sum((positions[:, None] >= bounds[None, :]).astype(jnp.int32), axis=1)


def gathered_body(
    tokens,
    gain,
    w_query,
    w_keyvalue,
    w_out,
    kv_pool,
    suffix_pages,
    page_index,
    page_request,
    new_slot,
):
    replicas = lax.axis_size("replica")
    tensors = lax.axis_size("tensor")
    owners = replicas * tensors
    position = lax.axis_index("tensor")
    query_width = w_query.shape[1]
    local_heads = query_width // HEAD_DIM
    share = tensors // KV_HEADS
    my_head = position // share
    scale_factor = 1.0 / math.sqrt(HEAD_DIM)
    normed = normalize(tokens, gain)
    piece = lax.all_gather(normed, "tensor", axis=0, tiled=True)
    first = jnp.dot(piece, w_query, preferred_element_type=jnp.float32)
    second = jnp.dot(piece, w_keyvalue, preferred_element_type=jnp.float32)
    projected = jnp.concatenate([first, second], axis=1).astype(jnp.bfloat16)
    query = projected[:, :query_width]
    keyvalue = lax.all_gather(projected[:, query_width:], "tensor", axis=1, tiled=True)
    total_rows = query.shape[0]
    wanted = lax.all_to_all(
        page_index[0], ("replica", "tensor"), split_axis=0, concat_axis=0, tiled=True
    )
    slot_count = wanted.shape[1]
    sources = jnp.arange(owners, dtype=jnp.int32) % tensors
    source_heads = sources // share
    flat_pool = kv_pool.reshape(kv_pool.shape[0] * KV_HEADS, PAGE, 2 * HEAD_DIM)
    outgoing = flat_pool[wanted * KV_HEADS + source_heads[:, None]]
    sub_tokens = outgoing.shape[2]
    pulled = lax.all_to_all(
        outgoing, ("replica", "tensor"), split_axis=0, concat_axis=0, tiled=True
    )
    segments = row_segments(suffix_pages[0], total_rows)
    key_groups = page_request[0]
    stacked = (
        query.reshape(total_rows, local_heads, HEAD_DIM)
        .transpose(1, 0, 2)
        .reshape(local_heads * total_rows, HEAD_DIM)
    )
    own_new = lax.dynamic_index_in_dim(
        keyvalue.reshape(total_rows, KV_HEADS, 2 * HEAD_DIM), my_head, 1, keepdims=False
    )
    row_order = jnp.arange(total_rows, dtype=jnp.int32)
    causal = (segments[:, None] == segments[None, :]) & (row_order[None, :] <= row_order[:, None])

    def block_scores(queries, head_count, keys, allowed):
        raw = (
            jnp.dot(queries, keys[:, :HEAD_DIM].T, preferred_element_type=jnp.float32)
            * scale_factor
        )
        raw = raw.reshape(head_count, total_rows, keys.shape[0])
        return jnp.where(allowed[None], raw, NEG_FILL)

    first_scores = block_scores(stacked, local_heads, own_new, causal)
    running = jnp.max(first_scores, axis=2)
    probs = jnp.exp(first_scores - running[:, :, None])
    denominator = jnp.sum(probs, axis=2)
    numerator = jnp.dot(
        probs.astype(jnp.bfloat16).reshape(local_heads * total_rows, total_rows),
        own_new[:, HEAD_DIM:],
        preferred_element_type=jnp.float32,
    )
    block_owners = 16
    blocks = owners // block_owners

    def absorb(step, state):
        peak, total, mixed = state
        pages = lax.dynamic_slice_in_dim(pulled, step * block_owners, block_owners, 0)
        keys = pages.reshape(block_owners * slot_count * sub_tokens, 2 * HEAD_DIM)
        labels = lax.dynamic_slice_in_dim(key_groups, step * block_owners, block_owners, 0).reshape(
            -1
        )
        matches = (segments[:, None] == labels[None, :])[:, :, None]
        allowed = jnp.broadcast_to(matches, (total_rows, labels.shape[0], sub_tokens)).reshape(
            total_rows, labels.shape[0] * sub_tokens
        )
        scores = block_scores(stacked, local_heads, keys, allowed)
        updated = jnp.maximum(peak, jnp.max(scores, axis=2))
        rescale = jnp.exp(peak - updated)
        weights = jnp.where(allowed[None], jnp.exp(scores - updated[:, :, None]), 0.0)
        total = total * rescale + jnp.sum(weights, axis=2)
        flat_weights = weights.astype(jnp.bfloat16).reshape(local_heads * total_rows, keys.shape[0])
        mixed = mixed * rescale.reshape(-1)[:, None] + jnp.dot(
            flat_weights, keys[:, HEAD_DIM:], preferred_element_type=jnp.float32
        )
        return (updated, total, mixed)

    running, denominator, numerator = lax.fori_loop(
        0, blocks, absorb, (running, denominator, numerator)
    )
    attention = (numerator / denominator.reshape(-1)[:, None]).astype(jnp.bfloat16)
    attention = (
        attention.reshape(local_heads, total_rows, HEAD_DIM)
        .transpose(1, 0, 2)
        .reshape(total_rows, query_width)
    )
    summed = lax.psum_scatter(
        jnp.dot(attention, w_out, preferred_element_type=jnp.float32).astype(jnp.bfloat16),
        "tensor",
        scatter_dimension=0,
        tiled=True,
    ).astype(jnp.float32)
    layer_out = (tokens.astype(jnp.float32) + summed).astype(jnp.bfloat16)
    new_count = total_rows // PAGE
    fresh = (
        keyvalue.reshape(new_count, PAGE, KV_HEADS, 2 * HEAD_DIM)
        .transpose(0, 2, 1, 3)
        .reshape(new_count, KV_HEADS * PAGE * 2 * HEAD_DIM)
    )
    local_pages = kv_pool.shape[0]
    targets = position * local_pages + jnp.arange(local_pages, dtype=jnp.int32)
    match_table = new_slot[0][None, :] == targets[:, None]
    placed = jnp.dot(
        match_table.astype(jnp.bfloat16), fresh, preferred_element_type=jnp.float32
    ).astype(jnp.bfloat16)
    placed = placed.reshape(kv_pool.shape)
    landed = jnp.any(match_table, axis=1)
    pool_out = jnp.where(landed[:, None, None, None], placed, kv_pool)
    return (layer_out, pool_out)


def prepare(place, tokens, gain, kv_pool):
    rows, width = tokens.shape
    half = width // 2
    step = 32
    pages, heads = kv_pool.shape[:2]
    blocks = rows // step

    def kernel(place_ref, x, g, pool, mine_ref, other_ref, *refs):
        held, (x_buf, g_buf, pool_buf, sems) = refs[:heads], refs[heads:]
        me, core = place_ref[0], place_ref[1]
        pool_copy = pltpu.make_async_copy(pool, pool_buf, sems.at[blocks + 1])

        def row_copy(b):
            at = pl.ds(b * step, step)
            return pltpu.make_async_copy(x.at[at], x_buf.at[at], sems.at[b])

        gain_copy = pltpu.make_async_copy(g, g_buf, sems.at[blocks])
        row_copy(0).start()
        gain_copy.start()
        for b in range(1, blocks):
            row_copy(b).start()
        pool_copy.start()
        near = pl.multiple_of(core * half, half)
        far = pl.multiple_of((1 - core) * half, half)
        for b in range(blocks):
            row_copy(b).wait()
            if b == 0:
                gain_copy.wait()

            def block(i, carry):
                at = pl.ds(pl.multiple_of(b * step + i * 16, 16), 16)
                total = jnp.zeros((16, 1), F32)
                for part in range(2):
                    values = x_buf[at, part * half : (part + 1) * half].astype(F32)
                    total += jnp.sum(values * values, axis=1, keepdims=True)
                inverse = lax.rsqrt(total * (1.0 / width) + EPSILON)
                for start, out in ((near, mine_ref), (far, other_ref)):
                    cols = pl.ds(start, half)
                    values = x_buf[at, cols].astype(F32)
                    out[at, :] = (values * inverse * g_buf[cols].astype(F32)[None, :]).astype(BF16)
                return carry

            lax.fori_loop(0, step // 16, block, 0)
        pool_copy.wait()
        for i in range(heads):
            for p in range(pages):
                held[i][p] = pool_buf[p, jnp.bitwise_xor(me, i)]

    return pl.pallas_call(
        kernel,
        in_specs=[SMEM] + [HBM] * 3,
        out_specs=[VMEM] * (2 + heads),
        out_shape=[shape((rows, half))] * 2 + [shape((pages,) + kv_pool.shape[2:])] * heads,
        scratch_shapes=[
            pltpu.VMEM((rows, width), BF16),
            pltpu.VMEM((width,), BF16),
            pltpu.VMEM(kv_pool.shape, BF16),
            pltpu.SemaphoreType.DMA((blocks + 2,)),
        ],
        compiler_params=params(16),
        cost_estimate=SMALL,
        name="prepare",
    )(place, tokens, gain, kv_pool)


def project_local(place, near, far, w_query, w_keyvalue, after):
    rows, half = near[0].shape
    q_width, kv_width = w_query.shape[1], w_keyvalue.shape[1]
    steps = 8
    depth = 2 * half // steps
    waits = len(after)

    def kernel(place_ref, near_own, near_peer, far_own, far_peer, wq, wkv, *refs):
        q_ref, kv_ref, wq_buf, wkv_buf, q_acc, kv_acc, sems = refs[waits:]
        core = place_ref[1]
        stream = weight_stream(core, half, steps, (wq, wkv), (wq_buf, wkv_buf), sems)
        for j in range(steps):
            for copy in stream(j):
                copy.start()
        for j in range(steps):
            for copy in stream(j):
                copy.wait()
            group = (near_own, near_peer) if j < steps // 2 else (far_own, far_peer)
            cols = slice((j % (steps // 2)) * depth, (j % (steps // 2) + 1) * depth)
            x = jnp.concatenate([ref[:, cols] for ref in group], axis=0)
            q_part = jnp.dot(x, wq_buf[j], preferred_element_type=F32)
            kv_part = jnp.dot(x, wkv_buf[j], preferred_element_type=F32)
            if j == 0:
                q_acc[...] = q_part
                kv_acc[...] = kv_part
            elif j < steps - 1:
                q_acc[...] += q_part
                kv_acc[...] += kv_part
            else:
                q_last = (q_acc[...] + q_part).astype(BF16)
                kv_last = (kv_acc[...] + kv_part).astype(BF16)
        for b in range(2):
            at = pl.ds(pl.multiple_of((core if b == 0 else 1 - core) * rows, rows), rows)
            q_ref[at, :] = q_last[b * rows : (b + 1) * rows]
            kv_ref[at, :] = kv_last[b * rows : (b + 1) * rows]

    total = 2 * rows
    return pl.pallas_call(
        kernel,
        in_specs=[SMEM] + [VMEM] * 4 + [HBM] * 2 + [ANY] * waits,
        out_specs=[VMEM] * 4,
        out_shape=[
            shape((total, q_width)),
            shape((total, kv_width)),
            pltpu.VMEM((steps, depth, q_width), BF16),
            pltpu.VMEM((steps, depth, kv_width), BF16),
        ],
        scratch_shapes=[
            pltpu.VMEM((total, q_width), F32),
            pltpu.VMEM((total, kv_width), F32),
            pltpu.SemaphoreType.DMA((2 * steps,)),
        ],
        compiler_params=params(10),
        cost_estimate=LARGE,
        name="project_local",
    )(place, *near, *far, w_query, w_keyvalue, *after)


def weight_stream(core, half, steps, sources, buffers, sems):
    depth = 2 * half // steps

    def copies(j):
        base = core if j < steps // 2 else 1 - core
        start = pl.multiple_of(base * half + (j % (steps // 2)) * depth, depth)
        count = len(sources)
        return [
            pltpu.make_async_copy(w.at[pl.ds(start, depth)], buf.at[j], sems.at[count * j + i])
            for i, (w, buf) in enumerate(zip(sources, buffers))
        ]

    return copies


PAGES_STEP = 4
REQUESTS = 4
SIZES_AT = 4
REQUESTS_AT = 8


def attention_scratch(block_rows, heads, fresh_rows, slots):
    stacked = heads * block_rows
    return [
        pltpu.VMEM((stacked, fresh_rows + slots * PAGE), F32),
        pltpu.VMEM((stacked, HEAD_DIM), F32),
        pltpu.VMEM((stacked, HEAD_DIM), F32),
        pltpu.VMEM((slots * PAGE, 2 * HEAD_DIM), BF16),
        pltpu.SMEM((slots,), jnp.int32),
    ]


def attend_block(place_ref, q, first_row, fresh, pulled, scratch):
    scores, total_ref, mixed_ref, cache, labels = scratch
    me = place_ref[0]
    block_rows, width = q.shape
    heads = width // HEAD_DIM
    stacked = heads * block_rows
    groups, per = pulled.shape[:2]
    tensors = 4
    slots = per // tensors
    wide = PAGES_STEP * PAGE
    factor = math.log2(math.e) / math.sqrt(HEAD_DIM)
    bound = []
    running = jnp.int32(0)
    for k in range(REQUESTS):
        running = running + place_ref[SIZES_AT + k] * UNIT
        bound.append(running)

    def segment_of(position):
        return sum((position >= b).astype(jnp.int32) for b in bound)

    lowest = segment_of(first_row)
    highest = segment_of(first_row + block_rows - 1)
    count = jnp.int32(0)
    for g in range(groups):
        for p in range(per):
            owner = g * tensors + jnp.bitwise_xor(me, p // slots)
            label = place_ref[REQUESTS_AT + p % slots * groups * tensors + owner]
            wanted = (label >= lowest) & (label <= highest)

            @pl.when(wanted)
            def _():
                cache[pl.ds(pl.multiple_of(count * PAGE, PAGE), PAGE), :] = pulled[g, p]
                labels[count] = label

            count = count + wanted.astype(jnp.int32)
    steps = (count + PAGES_STEP - 1) // PAGES_STEP
    for k in range(PAGES_STEP - 1):

        @pl.when(count + k < steps * PAGES_STEP)
        def _():
            cache[pl.ds(pl.multiple_of((count + k) * PAGE, PAGE), PAGE), :] = jnp.zeros(
                (PAGE, 2 * HEAD_DIM), BF16
            )
            labels[count + k] = jnp.int32(-1)

    q_rows = jnp.concatenate([q[:, h * HEAD_DIM : (h + 1) * HEAD_DIM] for h in range(heads)], axis=0)
    row_position = first_row + lax.broadcasted_iota(jnp.int32, (block_rows, 1), 0)
    row_segment = segment_of(row_position)

    def masked_scores(keys, allowed):
        raw = lax.dot_general(q_rows, keys, (((1,), (1,)), ((), ())), preferred_element_type=F32)
        n = keys.shape[0]
        return jnp.where(allowed[None], raw.reshape(heads, block_rows, n), NEG_FILL).reshape(
            stacked, n
        )

    def fold(values, combine):
        pieces = [values[:, i : i + HEAD_DIM] for i in range(0, values.shape[1], HEAD_DIM)]
        result = pieces[0]
        for piece in pieces[1:]:
            result = combine(result, piece)
        return result

    new = jnp.concatenate([rows for rows, _ in fresh], axis=0)
    fresh_rows = new.shape[0]
    key_position = jnp.concatenate(
        [
            base + lax.broadcasted_iota(jnp.int32, (1, rows.shape[0]), 1)
            for rows, base in fresh
        ],
        axis=1,
    )
    allowed = (row_segment == segment_of(key_position)) & (key_position <= row_position)
    masked = masked_scores(new[:, :HEAD_DIM], allowed)
    scores[:, :fresh_rows] = masked
    total_ref[...] = fold(masked, jnp.maximum)
    lanes = lax.broadcasted_iota(jnp.int32, (1, wide), 1) // PAGE

    def add_scores(g, carry):
        label = jnp.full((1, wide), -1, jnp.int32)
        for j in range(PAGES_STEP):
            label = jnp.where(lanes == j, labels[g * PAGES_STEP + j], label)
        keys = cache[pl.ds(pl.multiple_of(g * wide, wide), wide), :HEAD_DIM]
        masked = masked_scores(keys, row_segment == label)
        scores[:, pl.ds(pl.multiple_of(fresh_rows + g * wide, PAGE), wide)] = masked
        total_ref[...] = jnp.maximum(total_ref[...], fold(masked, jnp.maximum))
        return carry

    lax.fori_loop(0, steps, add_scores, 0)
    top = jnp.max(total_ref[...], axis=1, keepdims=True) * factor
    probs = jnp.exp2(scores[:, :fresh_rows] * factor - top)
    total_ref[...] = fold(probs, jnp.add)
    mixed_ref[...] = jnp.dot(probs.astype(BF16), new[:, HEAD_DIM:], preferred_element_type=F32)

    def add_values(g, carry):
        part = scores[:, pl.ds(pl.multiple_of(fresh_rows + g * wide, PAGE), wide)]
        probs = jnp.exp2(part * factor - top)
        values = cache[pl.ds(pl.multiple_of(g * wide, wide), wide), HEAD_DIM:]
        total_ref[...] += fold(probs, jnp.add)
        mixed_ref[...] += jnp.dot(probs.astype(BF16), values, preferred_element_type=F32)
        return carry

    lax.fori_loop(0, steps, add_values, 0)
    denominator = jnp.sum(total_ref[...], axis=1, keepdims=True)
    result = (mixed_ref[...] / denominator).astype(BF16)
    return jnp.concatenate(
        [result[h * block_rows : (h + 1) * block_rows] for h in range(heads)], axis=1
    )


def project_held(near, far, w_query, w_keyvalue, after):
    rows, half = near.shape
    pieces = len(far)
    steps, depth, q_width = w_query.shape
    kv_width = w_keyvalue.shape[2]

    def kernel(near_ref, *refs):
        far_refs = refs[:pieces]
        wq, wkv = refs[pieces : pieces + 2]
        q_ref, kv_ref = refs[pieces + 2 + len(after) :]
        for w, out in ((wq, q_ref), (wkv, kv_ref)):
            total = None
            for j in range(steps):
                at = j * depth
                if at < half:
                    x = near_ref[:, at : at + depth]
                else:
                    wide = half // pieces
                    x = far_refs[(at - half) // wide][:, at % wide : at % wide + depth]
                part = jnp.dot(x, w[j], preferred_element_type=F32)
                total = part if j == 0 else total + part
            out[...] = total.astype(BF16)

    return pl.pallas_call(
        kernel,
        in_specs=[VMEM] * (3 + pieces) + [ANY] * len(after),
        out_specs=[VMEM] * 2,
        out_shape=[shape((rows, q_width)), shape((rows, kv_width))],
        compiler_params=params(6),
        cost_estimate=SMALL,
        name="project_held",
    )(near, *far, w_query, w_keyvalue, *after)


def project_far(place, near, far, w_query, w_keyvalue, after):
    rows, half = near.shape
    q_width, kv_width = w_query.shape[1], w_keyvalue.shape[1]
    steps = 8
    depth = 2 * half // steps

    def kernel(place_ref, near_ref, far_ref, wq, wkv, *refs):
        q_ref, kv_ref, wq_buf, wkv_buf, x_buf, sems = refs[len(after) :]
        rows_in = [
            pltpu.make_async_copy(ref, x_buf.at[i], sems.at[2 * steps + i])
            for i, ref in enumerate((near_ref, far_ref))
        ]
        stream = weight_stream(place_ref[1], half, steps, (wq, wkv), (wq_buf, wkv_buf), sems)
        for j in range(steps):
            for copy in stream(j):
                copy.start()
            if j < 2:
                rows_in[j].start()
        q_sum = kv_sum = None
        for j in range(steps):
            for copy in stream(j):
                copy.wait()
            group, inner = divmod(j, steps // 2)
            if inner == 0:
                rows_in[group].wait()
            x = x_buf[group, :, inner * depth : (inner + 1) * depth]
            q_part = jnp.dot(x, wq_buf[j], preferred_element_type=F32)
            kv_part = jnp.dot(x, wkv_buf[j], preferred_element_type=F32)
            q_sum = q_part if j == 0 else q_sum + q_part
            kv_sum = kv_part if j == 0 else kv_sum + kv_part
        q_ref[...] = q_sum.astype(BF16)
        kv_ref[...] = kv_sum.astype(BF16)

    return pl.pallas_call(
        kernel,
        in_specs=[SMEM] + [ANY] * 2 + [HBM] * 2 + [ANY] * len(after),
        out_specs=[VMEM] * 2,
        out_shape=[shape((rows, q_width)), shape((rows, kv_width))],
        scratch_shapes=[
            pltpu.VMEM((steps, depth, q_width), BF16),
            pltpu.VMEM((steps, depth, kv_width), BF16),
            pltpu.VMEM((2, rows, half), BF16),
            pltpu.SemaphoreType.DMA((2 * steps + 2,)),
        ],
        compiler_params=params(32),
        cost_estimate=SMALL,
        name="project_far",
    )(place, near, far, w_query, w_keyvalue, *after)


def attend_out(place, query, fresh, bases, base, pulled, w_out):
    rows, depth = query.shape
    width = w_out.shape[1]
    half = width // 2
    heads = depth // HEAD_DIM
    out_steps = 4
    wide = half // out_steps
    known = len(fresh)
    count = sum(f.shape[0] for f in fresh)
    fresh_rows = -(-count // HEAD_DIM) * HEAD_DIM
    pad = fresh_rows - count

    def kernel(place_ref, q_ref, pulled_ref, *refs):
        fresh_refs = refs[:known]
        wo = refs[known]
        there_refs, refs_after = refs[known + 1 : known + 1 + out_steps], refs[known + 1 + out_steps :]
        stay_ref, wo_buf, sems = refs_after[:3]
        core, side = place_ref[1], place_ref[2]

        def copy(j):
            first = 1 - core if j < out_steps else core
            start = pl.multiple_of(first * half + (j % out_steps) * wide, wide)
            return pltpu.make_async_copy(wo.at[:, pl.ds(start, wide)], wo_buf.at[j], sems.at[j])

        for j in range(2 * out_steps):
            copy(j).start()
        pairs = [(ref[...], at(side)) for ref, at in zip(fresh_refs, bases)]
        if pad:
            pairs.append((jnp.zeros((pad, 2 * HEAD_DIM), BF16), jnp.int32(1 << 20)))
        mixed = attend_block(
            place_ref, q_ref[...], base(side), pairs, pulled_ref, refs_after[3:]
        )
        for j in range(2 * out_steps):
            copy(j).wait()
            part = jnp.dot(mixed, wo_buf[j], preferred_element_type=F32).astype(BF16)
            if j < out_steps:
                there_refs[j][...] = part
            else:
                at = (j - out_steps) * wide
                stay_ref[:, at : at + wide] = part

    return pl.pallas_call(
        kernel,
        in_specs=[SMEM] + [VMEM] * (2 + known) + [HBM],
        out_specs=[VMEM] * (out_steps + 1),
        out_shape=[shape((rows, wide))] * out_steps + [shape((rows, half))],
        scratch_shapes=[
            pltpu.VMEM((2 * out_steps, depth, wide), BF16),
            pltpu.SemaphoreType.DMA((2 * out_steps,)),
        ]
        + attention_scratch(rows, heads, fresh_rows, pulled.shape[0] * pulled.shape[1]),
        compiler_params=params(30),
        cost_estimate=MEDIUM,
        name="attend_out",
    )(place, query, pulled, *fresh, w_out)


def local_rows(place, query, fresh, bases, base, pulled, w_out, after):
    both, depth = query.shape
    rows = both // 2
    width = w_out.shape[1]
    heads = depth // HEAD_DIM
    steps = 8
    wide = width // steps
    known = len(fresh)
    fresh_rows = sum(f.shape[0] for f in fresh)

    def kernel(place_ref, q_ref, pulled_ref, *refs):
        fresh_refs = refs[:known]
        wo = refs[known]
        rest = refs[known + 1 + len(after) :]
        own_ref, peer_ref, wo_buf, a_buf, sems = rest[:5]
        core, side = place_ref[1], place_ref[2]

        def out_copy(j):
            return pltpu.make_async_copy(
                wo.at[:, j * wide : (j + 1) * wide], wo_buf.at[j], sems.at[j]
            )

        for j in range(steps):
            out_copy(j).start()

        def block(b, carry):
            at = pl.ds(pl.multiple_of(b * rows, rows), rows)
            a_buf[at, :] = attend_block(
                place_ref,
                q_ref[at, :],
                base(side) + b * rows,
                [(ref[...], first(side)) for ref, first in zip(fresh_refs, bases)],
                pulled_ref,
                rest[5:],
            )
            return carry

        lax.fori_loop(0, 2, block, 0)
        own_at = pl.ds(pl.multiple_of(core * rows, rows), rows)
        peer_at = pl.ds(pl.multiple_of((1 - core) * rows, rows), rows)
        a = jnp.concatenate([a_buf[own_at, :], a_buf[peer_at, :]], axis=0)
        for j in range(steps):
            out_copy(j).wait()
            part = jnp.dot(a, wo_buf[j], preferred_element_type=F32).astype(BF16)
            own_ref[:, j * wide : (j + 1) * wide] = part[:rows]
            peer_ref[:, j * wide : (j + 1) * wide] = part[rows:]

    return pl.pallas_call(
        kernel,
        in_specs=[SMEM] + [VMEM] * (2 + known) + [HBM] + [ANY] * len(after),
        out_specs=[VMEM, VMEM],
        out_shape=[shape((rows, width)), shape((rows, width))],
        scratch_shapes=[
            pltpu.VMEM((steps, depth, wide), BF16),
            pltpu.VMEM((both, depth), BF16),
            pltpu.SemaphoreType.DMA((steps,)),
        ]
        + attention_scratch(rows, heads, fresh_rows, pulled.shape[0] * pulled.shape[1]),
        compiler_params=params(40),
        cost_estimate=SMALL,
        name="local_rows",
    )(place, query, pulled, *fresh, w_out, *after)


def add_pair(left, pieces):
    rows, width = left.shape
    count = len(pieces)
    wide = width // count

    def kernel(left_ref, *refs):
        out_ref = refs[count]
        for i in range(count):
            cols = slice(i * wide, (i + 1) * wide)
            out_ref[:, cols] = (left_ref[:, cols].astype(F32) + refs[i][...].astype(F32)).astype(
                BF16
            )

    return pl.pallas_call(
        kernel,
        in_specs=[VMEM] * (1 + count),
        out_specs=VMEM,
        out_shape=shape((rows, width)),
        compiler_params=params(8),
        cost_estimate=SMALL,
        name="add_pair",
    )(left, *pieces)


def finish(place, tokens, own, peer, near, far):
    rows, width = tokens.shape
    half = width // 2
    step = 16

    def kernel(place_ref, x_ref, own_ref, peer_ref, near_ref, far_ref, out_ref):
        core = place_ref[1]

        def block(i, carry):
            at = pl.ds(pl.multiple_of(i * step, step), step)
            for start, part in ((core, near_ref), (1 - core, far_ref)):
                cols = pl.ds(pl.multiple_of(start * half, half), half)
                local = own_ref[at, cols].astype(F32) + peer_ref[at, cols].astype(F32)
                total = local + part[at, :].astype(F32)
                out_ref[at, cols] = (x_ref[at, cols].astype(F32) + total).astype(BF16)
            return carry

        lax.fori_loop(0, rows // step, block, 0)

    return pl.pallas_call(
        kernel,
        in_specs=[SMEM] + [VMEM] * 5,
        out_specs=VMEM,
        out_shape=shape((rows, width)),
        compiler_params=params(16),
        cost_estimate=SMALL,
        name="finish",
    )(place, tokens, own, peer, near, far)


def pick_pages(place, wanted, held, after):
    replicas = len(wanted)
    slots = wanted[0].shape[1]
    tensors = len(held)
    _, page, width = held[0].shape
    total = tensors * slots

    def kernel(place_ref, *refs):
        wants, sources = refs[:replicas], refs[replicas : replicas + tensors]
        out_ref = refs[replicas + tensors + len(after)]
        me, rep = place_ref[0], place_ref[3]
        for k in range(replicas):
            asker = lax.rem(rep + k, replicas)
            for i in range(tensors):
                owner = rep * tensors + jnp.bitwise_xor(me, i)
                for s in range(slots):
                    out_ref[asker, i * slots + s] = sources[i][wants[k][0, s, owner]]

    return pl.pallas_call(
        kernel,
        in_specs=[SMEM] * (1 + replicas) + [VMEM] * tensors + [ANY] * len(after),
        out_specs=VMEM,
        out_shape=shape((replicas, total, page, width)),
        compiler_params=params(8),
        cost_estimate=SMALL,
        name="pick_pages",
    )(place, *wanted, *held, *after)


def write_pool(place, slots, kv_pool, early, late):
    pages, heads = kv_pool.shape[:2]
    new_count = slots.shape[1]
    early_rows, late_rows = early[0].shape[0], late[0].shape[0]
    side_rows = (early_rows + late_rows) // 2
    total_rows = early_rows + late_rows

    def kernel(place_ref, slot_ref, pool_ref, *refs):
        early_refs, late_refs, (out_ref, rows_ref) = refs[:3], refs[3:6], refs[6:]
        me, side = place_ref[0], place_ref[2]

        def source(group, i):
            own, y, core = group
            return (own, core.at[0], y, core.at[1])[i]

        for i in range(heads):
            rows_ref[i, :early_rows] = source(early_refs, i)[...]
            rows_ref[i, early_rows:] = source(late_refs, i)[...]
        for p in range(pages):
            found = jnp.int32(-1)
            for j in range(new_count):
                found = jnp.where(slot_ref[0, j] == me * pages + p, j, found)
            first = jnp.maximum(found, 0) * PAGE
            far = (first >= side_rows).astype(jnp.int32)
            inner = first - far * side_rows
            for i in range(heads):
                origin = side if i < 2 else 1 - side
                start = jnp.bitwise_xor(far, origin) * side_rows + inner
                at = jnp.bitwise_xor(me, i)

                @pl.when(found >= 0)
                def _():
                    out_ref[p, at] = rows_ref[i, pl.ds(pl.multiple_of(start, PAGE), PAGE), :]

                @pl.when(found < 0)
                def _():
                    out_ref[p, at] = pool_ref[p, at]

    return pl.pallas_call(
        kernel,
        in_specs=[SMEM, SMEM] + [VMEM] * 7,
        out_specs=VMEM,
        out_shape=shape(kv_pool.shape),
        scratch_shapes=[pltpu.VMEM((heads, total_rows, kv_pool.shape[3]), BF16)],
        compiler_params=params(12),
        cost_estimate=SMALL,
        name="write_pool",
    )(place, slots, kv_pool, *early, *late)


def chip_pair_body(
    tokens,
    gain,
    w_query,
    w_keyvalue,
    w_out,
    kv_pool,
    suffix_pages,
    page_index,
    page_request,
    new_slot,
):
    replicas = lax.axis_size("replica")
    me = lax.axis_index("tensor")
    core = me % 2
    side = me // 2
    rows = tokens.shape[0]
    rep = lax.axis_index("replica")
    place = jnp.stack([me, core, side, rep]).astype(jnp.int32)
    def over_core(x):
        return lax.ppermute(x, "tensor", [(0, 1), (1, 0), (2, 3), (3, 2)])

    def over_y(x):
        return lax.ppermute(x, "tensor", [(0, 2), (2, 0), (1, 3), (3, 1)])

    def tie(x, *others):
        return lax.optimization_barrier((x, *others))[0]

    w_query, w_keyvalue, w_out = in_hbm(w_query), in_hbm(w_keyvalue), in_hbm(w_out)

    wanted = [jnp.swapaxes(page_index, 1, 2)]
    for k in range(1, replicas):
        back = [(i, (i - k) % replicas) for i in range(replicas)]
        wanted.append(lax.ppermute(wanted[0], "replica", back))

    mine, other, *held = prepare(place, in_hbm(tokens), in_hbm(gain), in_hbm(kv_pool))
    for i in range(1, 4):
        held[i] = lax.ppermute(held[i], "tensor", [(t, t ^ i) for t in range(4)])

    peer_near = over_core(other)
    peer_far = over_core(mine)
    is_first = core == 0
    near_tied = tie(peer_near, held[2], held[3])
    first_half = jnp.where(is_first, mine, near_tied)
    second_half = jnp.where(is_first, near_tied, mine)
    first = over_y(first_half)
    second = over_y(second_half)

    picked = pick_pages(place, wanted, held, [first_half, second_half])
    sizes, requests = lax.optimization_barrier((suffix_pages, page_request, picked))[:2]
    requests = jnp.swapaxes(requests, 1, 2).reshape(-1)
    scalars = jnp.concatenate([place, sizes[0], requests])
    pulled = lax.all_to_all(picked, "replica", split_axis=0, concat_axis=0, tiled=True)

    q_local, kv_local, wq, wkv = project_local(
        place, [mine, peer_near], [other, peer_far], w_query, w_keyvalue, [picked, scalars]
    )


    def local_base(s):
        return s * (2 * rows)

    def first_base(s):
        return (1 - s) * (2 * rows)

    def second_base(s):
        return (1 - s) * (2 * rows) + rows

    first = tie(first, q_local)
    wide = first.shape[1] // 4
    pieces = [over_core(first[:, i * wide : (i + 1) * wide]) for i in range(4)]
    q_first, kv_first = project_held(first, pieces, wq, wkv, [])
    early_own = jnp.concatenate([kv_local, kv_first], axis=0)
    early_y = over_y(early_own)
    *there, stay = attend_out(
        scalars, q_first, [kv_local, kv_first], [local_base, first_base], first_base, pulled, w_out
    )
    first_mix = add_pair(stay, [over_core(tie(part, early_y)) for part in there])
    first_sum = over_y(first_mix)

    second = tie(second, first_mix)
    q_second, kv_second = project_far(place, second, over_core(second), w_query, w_keyvalue, [])
    fresh = [kv_local, kv_first, kv_second]
    bases = [local_base, first_base, second_base]
    *there, stay = attend_out(scalars, q_second, fresh, bases, second_base, pulled, w_out)
    late_y = over_y(kv_second)
    second_mix = add_pair(stay, [over_core(tie(part, late_y)) for part in there])
    second_sum = over_y(tie(second_mix, first_sum))

    own_part, peer_part = local_rows(
        scalars, q_local, fresh, bases, local_base, pulled, w_out, [second_mix]
    )
    peer_part = over_core(peer_part)

    early = over_core(jnp.stack([early_own, early_y]))
    late = over_core(jnp.stack([kv_second, late_y]))
    pool_out = write_pool(
        place, new_slot, kv_pool, [early_own, early_y, early], [kv_second, late_y, late]
    )

    second_sum = tie(second_sum, pool_out)
    near = jnp.where(is_first, first_sum, second_sum)
    far = over_core(jnp.where(is_first, second_sum, first_sum))
    layer_out = finish(place, tokens, own_part, peer_part, near, far)
    return (layer_out, pool_out)


def solution(mesh):
    pair = mesh.shape["tensor"] == KV_HEADS
    return jax.shard_map(
        chip_pair_body if pair else gathered_body,
        mesh=mesh,
        in_specs=(
            P(("groups", "replica", "tensor"), None),
            P(),
            P(None, "tensor"),
            P(None, "tensor"),
            P("tensor", None),
            P(("groups", "replica", "tensor"), None, None, None),
            P(("groups", "replica"), None),
            P(("groups", "replica"), None, None),
            P(("groups", "replica"), None, None),
            P(("groups", "replica"), None),
        ),
        out_specs=(
            P(("groups", "replica", "tensor"), None),
            P(("groups", "replica", "tensor"), None, None, None),
        ),
        check_vma=False,
    )
```

```python
import math

import jax
import jax.numpy as jnp
from jax import lax
from jax.experimental import pallas as pl
from jax.experimental.pallas import tpu as pltpu
from jax.sharding import PartitionSpec as P

KV_HEADS = 4
HEAD_DIM = 128
PAGE = 64
UNIT = 8


NEG_FILL = -1e30
EPSILON = 1e-06

F32 = jnp.float32
BF16 = jnp.bfloat16
MIB = 1 << 20
ANY = pl.BlockSpec(memory_space=pl.ANY)
HBM = pl.BlockSpec(memory_space=pltpu.HBM)
SMEM = pl.BlockSpec(memory_space=pltpu.SMEM)
VMEM = pl.BlockSpec(memory_space=pltpu.VMEM)
SMALL = pl.CostEstimate(flops=1024, bytes_accessed=1024, transcendentals=0)
MEDIUM = pl.CostEstimate(flops=1024, bytes_accessed=4000000, transcendentals=0)
LARGE = pl.CostEstimate(flops=20000000000, bytes_accessed=200000000, transcendentals=0)


def params(mib):
    return pltpu.CompilerParams(vmem_limit_bytes=mib * MIB)


def in_hbm(x):
    return pltpu.with_memory_space_constraint(x, pltpu.HBM)


def shape(dims, dtype=BF16):
    return jax.ShapeDtypeStruct(dims, dtype)


def normalize(rows, gain):
    values = rows.astype(jnp.float32)
    inverse = lax.rsqrt(jnp.mean(values * values, axis=-1, keepdims=True) + EPSILON)
    return (values * inverse * gain.astype(jnp.float32)).astype(jnp.bfloat16)


def row_segments(pages, total_rows):
    bounds = jnp.cumsum(pages) * UNIT
    positions = jnp.arange(total_rows, dtype=jnp.int32)
    return jnp.sum((positions[:, None] >= bounds[None, :]).astype(jnp.int32), axis=1)


def gathered_body(
    tokens,
    gain,
    w_query,
    w_keyvalue,
    w_out,
    kv_pool,
    suffix_pages,
    page_index,
    page_request,
    new_slot,
):
    replicas = lax.axis_size("replica")
    tensors = lax.axis_size("tensor")
    owners = replicas * tensors
    position = lax.axis_index("tensor")
    query_width = w_query.shape[1]
    local_heads = query_width // HEAD_DIM
    share = tensors // KV_HEADS
    my_head = position // share
    scale_factor = 1.0 / math.sqrt(HEAD_DIM)
    normed = normalize(tokens, gain)
    piece = lax.all_gather(normed, "tensor", axis=0, tiled=True)
    first = jnp.dot(piece, w_query, preferred_element_type=jnp.float32)
    second = jnp.dot(piece, w_keyvalue, preferred_element_type=jnp.float32)
    projected = jnp.concatenate([first, second], axis=1).astype(jnp.bfloat16)
    query = projected[:, :query_width]
    keyvalue = lax.all_gather(projected[:, query_width:], "tensor", axis=1, tiled=True)
    total_rows = query.shape[0]
    wanted = lax.all_to_all(
        page_index[0], ("replica", "tensor"), split_axis=0, concat_axis=0, tiled=True
    )
    slot_count = wanted.shape[1]
    sources = jnp.arange(owners, dtype=jnp.int32) % tensors
    source_heads = sources // share
    flat_pool = kv_pool.reshape(kv_pool.shape[0] * KV_HEADS, PAGE, 2 * HEAD_DIM)
    outgoing = flat_pool[wanted * KV_HEADS + source_heads[:, None]]
    sub_tokens = outgoing.shape[2]
    pulled = lax.all_to_all(
        outgoing, ("replica", "tensor"), split_axis=0, concat_axis=0, tiled=True
    )
    segments = row_segments(suffix_pages[0], total_rows)
    key_groups = page_request[0]
    stacked = (
        query.reshape(total_rows, local_heads, HEAD_DIM)
        .transpose(1, 0, 2)
        .reshape(local_heads * total_rows, HEAD_DIM)
    )
    own_new = lax.dynamic_index_in_dim(
        keyvalue.reshape(total_rows, KV_HEADS, 2 * HEAD_DIM), my_head, 1, keepdims=False
    )
    row_order = jnp.arange(total_rows, dtype=jnp.int32)
    causal = (segments[:, None] == segments[None, :]) & (row_order[None, :] <= row_order[:, None])

    def block_scores(queries, head_count, keys, allowed):
        raw = (
            jnp.dot(queries, keys[:, :HEAD_DIM].T, preferred_element_type=jnp.float32)
            * scale_factor
        )
        raw = raw.reshape(head_count, total_rows, keys.shape[0])
        return jnp.where(allowed[None], raw, NEG_FILL)

    first_scores = block_scores(stacked, local_heads, own_new, causal)
    running = jnp.max(first_scores, axis=2)
    probs = jnp.exp(first_scores - running[:, :, None])
    denominator = jnp.sum(probs, axis=2)
    numerator = jnp.dot(
        probs.astype(jnp.bfloat16).reshape(local_heads * total_rows, total_rows),
        own_new[:, HEAD_DIM:],
        preferred_element_type=jnp.float32,
    )
    block_owners = 16
    blocks = owners // block_owners

    def absorb(step, state):
        peak, total, mixed = state
        pages = lax.dynamic_slice_in_dim(pulled, step * block_owners, block_owners, 0)
        keys = pages.reshape(block_owners * slot_count * sub_tokens, 2 * HEAD_DIM)
        labels = lax.dynamic_slice_in_dim(key_groups, step * block_owners, block_owners, 0).reshape(
            -1
        )
        matches = (segments[:, None] == labels[None, :])[:, :, None]
        allowed = jnp.broadcast_to(matches, (total_rows, labels.shape[0], sub_tokens)).reshape(
            total_rows, labels.shape[0] * sub_tokens
        )
        scores = block_scores(stacked, local_heads, keys, allowed)
        updated = jnp.maximum(peak, jnp.max(scores, axis=2))
        rescale = jnp.exp(peak - updated)
        weights = jnp.where(allowed[None], jnp.exp(scores - updated[:, :, None]), 0.0)
        total = total * rescale + jnp.sum(weights, axis=2)
        flat_weights = weights.astype(jnp.bfloat16).reshape(local_heads * total_rows, keys.shape[0])
        mixed = mixed * rescale.reshape(-1)[:, None] + jnp.dot(
            flat_weights, keys[:, HEAD_DIM:], preferred_element_type=jnp.float32
        )
        return (updated, total, mixed)

    running, denominator, numerator = lax.fori_loop(
        0, blocks, absorb, (running, denominator, numerator)
    )
    attention = (numerator / denominator.reshape(-1)[:, None]).astype(jnp.bfloat16)
    attention = (
        attention.reshape(local_heads, total_rows, HEAD_DIM)
        .transpose(1, 0, 2)
        .reshape(total_rows, query_width)
    )
    summed = lax.psum_scatter(
        jnp.dot(attention, w_out, preferred_element_type=jnp.float32).astype(jnp.bfloat16),
        "tensor",
        scatter_dimension=0,
        tiled=True,
    ).astype(jnp.float32)
    layer_out = (tokens.astype(jnp.float32) + summed).astype(jnp.bfloat16)
    new_count = total_rows // PAGE
    fresh = (
        keyvalue.reshape(new_count, PAGE, KV_HEADS, 2 * HEAD_DIM)
        .transpose(0, 2, 1, 3)
        .reshape(new_count, KV_HEADS * PAGE * 2 * HEAD_DIM)
    )
    local_pages = kv_pool.shape[0]
    targets = position * local_pages + jnp.arange(local_pages, dtype=jnp.int32)
    match_table = new_slot[0][None, :] == targets[:, None]
    placed = jnp.dot(
        match_table.astype(jnp.bfloat16), fresh, preferred_element_type=jnp.float32
    ).astype(jnp.bfloat16)
    placed = placed.reshape(kv_pool.shape)
    landed = jnp.any(match_table, axis=1)
    pool_out = jnp.where(landed[:, None, None, None], placed, kv_pool)
    return (layer_out, pool_out)


def prepare(place, tokens, gain, kv_pool):
    rows, width = tokens.shape
    half = width // 2
    step = 32
    pages, heads = kv_pool.shape[:2]
    blocks = rows // step

    def kernel(place_ref, x, g, pool, mine_ref, other_ref, *refs):
        held, (x_buf, g_buf, pool_buf, sems) = refs[:heads], refs[heads:]
        me, core = place_ref[0], place_ref[1]
        pool_copy = pltpu.make_async_copy(pool, pool_buf, sems.at[blocks + 1])

        def row_copy(b):
            at = pl.ds(b * step, step)
            return pltpu.make_async_copy(x.at[at], x_buf.at[at], sems.at[b])

        gain_copy = pltpu.make_async_copy(g, g_buf, sems.at[blocks])
        row_copy(0).start()
        gain_copy.start()
        for b in range(1, blocks):
            row_copy(b).start()
        pool_copy.start()
        near = pl.multiple_of(core * half, half)
        far = pl.multiple_of((1 - core) * half, half)
        for b in range(blocks):
            row_copy(b).wait()
            if b == 0:
                gain_copy.wait()

            def block(i, carry):
                at = pl.ds(pl.multiple_of(b * step + i * 16, 16), 16)
                total = jnp.zeros((16, 1), F32)
                for part in range(2):
                    values = x_buf[at, part * half : (part + 1) * half].astype(F32)
                    total += jnp.sum(values * values, axis=1, keepdims=True)
                inverse = lax.rsqrt(total * (1.0 / width) + EPSILON)
                for start, out in ((near, mine_ref), (far, other_ref)):
                    cols = pl.ds(start, half)
                    values = x_buf[at, cols].astype(F32)
                    out[at, :] = (values * inverse * g_buf[cols].astype(F32)[None, :]).astype(BF16)
                return carry

            lax.fori_loop(0, step // 16, block, 0)
        pool_copy.wait()
        for i in range(heads):
            for p in range(pages):
                held[i][p] = pool_buf[p, jnp.bitwise_xor(me, i)]

    return pl.pallas_call(
        kernel,
        in_specs=[SMEM] + [HBM] * 3,
        out_specs=[VMEM] * (2 + heads),
        out_shape=[shape((rows, half))] * 2 + [shape((pages,) + kv_pool.shape[2:])] * heads,
        scratch_shapes=[
            pltpu.VMEM((rows, width), BF16),
            pltpu.VMEM((width,), BF16),
            pltpu.VMEM(kv_pool.shape, BF16),
            pltpu.SemaphoreType.DMA((blocks + 2,)),
        ],
        compiler_params=params(16),
        cost_estimate=SMALL,
        name="prepare",
    )(place, tokens, gain, kv_pool)


def project_local(place, near, far, w_query, w_keyvalue, after):
    rows, half = near[0].shape
    q_width, kv_width = w_query.shape[1], w_keyvalue.shape[1]
    steps = 8
    depth = 2 * half // steps
    waits = len(after)

    def kernel(place_ref, near_own, near_peer, far_own, far_peer, wq, wkv, *refs):
        q_ref, kv_ref, wq_buf, wkv_buf, q_acc, kv_acc, sems = refs[waits:]
        core = place_ref[1]
        stream = weight_stream(core, half, steps, (wq, wkv), (wq_buf, wkv_buf), sems)
        for j in range(steps):
            for copy in stream(j):
                copy.start()
        for j in range(steps):
            for copy in stream(j):
                copy.wait()
            group = (near_own, near_peer) if j < steps // 2 else (far_own, far_peer)
            cols = slice((j % (steps // 2)) * depth, (j % (steps // 2) + 1) * depth)
            x = jnp.concatenate([ref[:, cols] for ref in group], axis=0)
            q_part = jnp.dot(x, wq_buf[j], preferred_element_type=F32)
            kv_part = jnp.dot(x, wkv_buf[j], preferred_element_type=F32)
            if j == 0:
                q_acc[...] = q_part
                kv_acc[...] = kv_part
            elif j < steps - 1:
                q_acc[...] += q_part
                kv_acc[...] += kv_part
            else:
                q_last = (q_acc[...] + q_part).astype(BF16)
                kv_last = (kv_acc[...] + kv_part).astype(BF16)
        for b in range(2):
            at = pl.ds(pl.multiple_of((core if b == 0 else 1 - core) * rows, rows), rows)
            q_ref[at, :] = q_last[b * rows : (b + 1) * rows]
            kv_ref[at, :] = kv_last[b * rows : (b + 1) * rows]

    total = 2 * rows
    return pl.pallas_call(
        kernel,
        in_specs=[SMEM] + [VMEM] * 4 + [HBM] * 2 + [ANY] * waits,
        out_specs=[VMEM] * 4,
        out_shape=[
            shape((total, q_width)),
            shape((total, kv_width)),
            pltpu.VMEM((steps, depth, q_width), BF16),
            pltpu.VMEM((steps, depth, kv_width), BF16),
        ],
        scratch_shapes=[
            pltpu.VMEM((total, q_width), F32),
            pltpu.VMEM((total, kv_width), F32),
            pltpu.SemaphoreType.DMA((2 * steps,)),
        ],
        compiler_params=params(10),
        cost_estimate=LARGE,
        name="project_local",
    )(place, *near, *far, w_query, w_keyvalue, *after)


def weight_stream(core, half, steps, sources, buffers, sems):
    depth = 2 * half // steps

    def copies(j):
        base = core if j < steps // 2 else 1 - core
        start = pl.multiple_of(base * half + (j % (steps // 2)) * depth, depth)
        count = len(sources)
        return [
            pltpu.make_async_copy(w.at[pl.ds(start, depth)], buf.at[j], sems.at[count * j + i])
            for i, (w, buf) in enumerate(zip(sources, buffers))
        ]

    return copies


PAGES_STEP = 4
REQUESTS = 4
SIZES_AT = 4
REQUESTS_AT = 8


def attention_scratch(block_rows, heads, fresh_rows, slots):
    stacked = heads * block_rows
    return [
        pltpu.VMEM((stacked, fresh_rows + slots * PAGE), F32),
        pltpu.VMEM((stacked, HEAD_DIM), F32),
        pltpu.VMEM((stacked, HEAD_DIM), F32),
        pltpu.VMEM((slots * PAGE, 2 * HEAD_DIM), BF16),
        pltpu.SMEM((slots,), jnp.int32),
    ]


def attend_block(place_ref, q, first_row, fresh, pulled, scratch):
    scores, total_ref, mixed_ref, cache, labels = scratch
    me = place_ref[0]
    block_rows, width = q.shape
    heads = width // HEAD_DIM
    stacked = heads * block_rows
    groups, per = pulled.shape[:2]
    tensors = 4
    slots = per // tensors
    wide = PAGES_STEP * PAGE
    factor = math.log2(math.e) / math.sqrt(HEAD_DIM)
    bound = []
    running = jnp.int32(0)
    for k in range(REQUESTS):
        running = running + place_ref[SIZES_AT + k] * UNIT
        bound.append(running)

    def segment_of(position):
        return sum((position >= b).astype(jnp.int32) for b in bound)

    lowest = segment_of(first_row)
    highest = segment_of(first_row + block_rows - 1)
    count = jnp.int32(0)
    for g in range(groups):
        for p in range(per):
            owner = g * tensors + jnp.bitwise_xor(me, p // slots)
            label = place_ref[REQUESTS_AT + p % slots * groups * tensors + owner]
            wanted = (label >= lowest) & (label <= highest)

            @pl.when(wanted)
            def _():
                cache[pl.ds(pl.multiple_of(count * PAGE, PAGE), PAGE), :] = pulled[g, p]
                labels[count] = label

            count = count + wanted.astype(jnp.int32)
    steps = (count + PAGES_STEP - 1) // PAGES_STEP
    for k in range(PAGES_STEP - 1):

        @pl.when(count + k < steps * PAGES_STEP)
        def _():
            cache[pl.ds(pl.multiple_of((count + k) * PAGE, PAGE), PAGE), :] = jnp.zeros(
                (PAGE, 2 * HEAD_DIM), BF16
            )
            labels[count + k] = jnp.int32(-1)

    q_rows = jnp.concatenate([q[:, h * HEAD_DIM : (h + 1) * HEAD_DIM] for h in range(heads)], axis=0)
    row_position = first_row + lax.broadcasted_iota(jnp.int32, (block_rows, 1), 0)
    row_segment = segment_of(row_position)

    def masked_scores(keys, allowed):
        raw = lax.dot_general(q_rows, keys, (((1,), (1,)), ((), ())), preferred_element_type=F32)
        n = keys.shape[0]
        return jnp.where(allowed[None], raw.reshape(heads, block_rows, n), NEG_FILL).reshape(
            stacked, n
        )

    def fold(values, combine):
        pieces = [values[:, i : i + HEAD_DIM] for i in range(0, values.shape[1], HEAD_DIM)]
        result = pieces[0]
        for piece in pieces[1:]:
            result = combine(result, piece)
        return result

    new = jnp.concatenate([rows for rows, _ in fresh], axis=0)
    fresh_rows = new.shape[0]
    key_position = jnp.concatenate(
        [
            base + lax.broadcasted_iota(jnp.int32, (1, rows.shape[0]), 1)
            for rows, base in fresh
        ],
        axis=1,
    )
    allowed = (row_segment == segment_of(key_position)) & (key_position <= row_position)
    masked = masked_scores(new[:, :HEAD_DIM], allowed)
    scores[:, :fresh_rows] = masked
    total_ref[...] = fold(masked, jnp.maximum)
    lanes = lax.broadcasted_iota(jnp.int32, (1, wide), 1) // PAGE

    def add_scores(g, carry):
        label = jnp.full((1, wide), -1, jnp.int32)
        for j in range(PAGES_STEP):
            label = jnp.where(lanes == j, labels[g * PAGES_STEP + j], label)
        keys = cache[pl.ds(pl.multiple_of(g * wide, wide), wide), :HEAD_DIM]
        masked = masked_scores(keys, row_segment == label)
        scores[:, pl.ds(pl.multiple_of(fresh_rows + g * wide, PAGE), wide)] = masked
        total_ref[...] = jnp.maximum(total_ref[...], fold(masked, jnp.maximum))
        return carry

    lax.fori_loop(0, steps, add_scores, 0)
    top = jnp.max(total_ref[...], axis=1, keepdims=True) * factor
    probs = jnp.exp2(scores[:, :fresh_rows] * factor - top)
    total_ref[...] = fold(probs, jnp.add)
    mixed_ref[...] = jnp.dot(probs.astype(BF16), new[:, HEAD_DIM:], preferred_element_type=F32)

    def add_values(g, carry):
        part = scores[:, pl.ds(pl.multiple_of(fresh_rows + g * wide, PAGE), wide)]
        probs = jnp.exp2(part * factor - top)
        values = cache[pl.ds(pl.multiple_of(g * wide, wide), wide), HEAD_DIM:]
        total_ref[...] += fold(probs, jnp.add)
        mixed_ref[...] += jnp.dot(probs.astype(BF16), values, preferred_element_type=F32)
        return carry

    lax.fori_loop(0, steps, add_values, 0)
    denominator = jnp.sum(total_ref[...], axis=1, keepdims=True)
    result = (mixed_ref[...] / denominator).astype(BF16)
    return jnp.concatenate(
        [result[h * block_rows : (h + 1) * block_rows] for h in range(heads)], axis=1
    )


def project_held(near, far, w_query, w_keyvalue, after):
    rows, half = near.shape
    pieces = len(far)
    steps, depth, q_width = w_query.shape
    kv_width = w_keyvalue.shape[2]

    def kernel(near_ref, *refs):
        far_refs = refs[:pieces]
        wq, wkv = refs[pieces : pieces + 2]
        q_ref, kv_ref = refs[pieces + 2 + len(after) :]
        for w, out in ((wq, q_ref), (wkv, kv_ref)):
            total = None
            for j in range(steps):
                at = j * depth
                if at < half:
                    x = near_ref[:, at : at + depth]
                else:
                    wide = half // pieces
                    x = far_refs[(at - half) // wide][:, at % wide : at % wide + depth]
                part = jnp.dot(x, w[j], preferred_element_type=F32)
                total = part if j == 0 else total + part
            out[...] = total.astype(BF16)

    return pl.pallas_call(
        kernel,
        in_specs=[VMEM] * (3 + pieces) + [ANY] * len(after),
        out_specs=[VMEM] * 2,
        out_shape=[shape((rows, q_width)), shape((rows, kv_width))],
        compiler_params=params(6),
        cost_estimate=SMALL,
        name="project_held",
    )(near, *far, w_query, w_keyvalue, *after)


def project_far(place, near, far, w_query, w_keyvalue, after):
    rows, half = near.shape
    q_width, kv_width = w_query.shape[1], w_keyvalue.shape[1]
    steps = 8
    depth = 2 * half // steps

    def kernel(place_ref, near_ref, far_ref, wq, wkv, *refs):
        q_ref, kv_ref, wq_buf, wkv_buf, x_buf, sems = refs[len(after) :]
        rows_in = [
            pltpu.make_async_copy(ref, x_buf.at[i], sems.at[2 * steps + i])
            for i, ref in enumerate((near_ref, far_ref))
        ]
        stream = weight_stream(place_ref[1], half, steps, (wq, wkv), (wq_buf, wkv_buf), sems)
        for j in range(steps):
            for copy in stream(j):
                copy.start()
            if j < 2:
                rows_in[j].start()
        q_sum = kv_sum = None
        for j in range(steps):
            for copy in stream(j):
                copy.wait()
            group, inner = divmod(j, steps // 2)
            if inner == 0:
                rows_in[group].wait()
            x = x_buf[group, :, inner * depth : (inner + 1) * depth]
            q_part = jnp.dot(x, wq_buf[j], preferred_element_type=F32)
            kv_part = jnp.dot(x, wkv_buf[j], preferred_element_type=F32)
            q_sum = q_part if j == 0 else q_sum + q_part
            kv_sum = kv_part if j == 0 else kv_sum + kv_part
        q_ref[...] = q_sum.astype(BF16)
        kv_ref[...] = kv_sum.astype(BF16)

    return pl.pallas_call(
        kernel,
        in_specs=[SMEM] + [ANY] * 2 + [HBM] * 2 + [ANY] * len(after),
        out_specs=[VMEM] * 2,
        out_shape=[shape((rows, q_width)), shape((rows, kv_width))],
        scratch_shapes=[
            pltpu.VMEM((steps, depth, q_width), BF16),
            pltpu.VMEM((steps, depth, kv_width), BF16),
            pltpu.VMEM((2, rows, half), BF16),
            pltpu.SemaphoreType.DMA((2 * steps + 2,)),
        ],
        compiler_params=params(32),
        cost_estimate=SMALL,
        name="project_far",
    )(place, near, far, w_query, w_keyvalue, *after)


def attend_out(place, query, fresh, bases, base, pulled, w_out):
    rows, depth = query.shape
    width = w_out.shape[1]
    half = width // 2
    heads = depth // HEAD_DIM
    out_steps = 4
    wide = half // out_steps
    known = len(fresh)
    count = sum(f.shape[0] for f in fresh)
    fresh_rows = -(-count // HEAD_DIM) * HEAD_DIM
    pad = fresh_rows - count

    def kernel(place_ref, q_ref, pulled_ref, *refs):
        fresh_refs = refs[:known]
        wo = refs[known]
        there_refs, refs_after = refs[known + 1 : known + 1 + out_steps], refs[known + 1 + out_steps :]
        stay_ref, wo_buf, sems = refs_after[:3]
        core, side = place_ref[1], place_ref[2]

        def copy(j):
            first = 1 - core if j < out_steps else core
            start = pl.multiple_of(first * half + (j % out_steps) * wide, wide)
            return pltpu.make_async_copy(wo.at[:, pl.ds(start, wide)], wo_buf.at[j], sems.at[j])

        for j in range(2 * out_steps):
            copy(j).start()
        pairs = [(ref[...], at(side)) for ref, at in zip(fresh_refs, bases)]
        if pad:
            pairs.append((jnp.zeros((pad, 2 * HEAD_DIM), BF16), jnp.int32(1 << 20)))
        mixed = attend_block(
            place_ref, q_ref[...], base(side), pairs, pulled_ref, refs_after[3:]
        )
        for j in range(2 * out_steps):
            copy(j).wait()
            part = jnp.dot(mixed, wo_buf[j], preferred_element_type=F32).astype(BF16)
            if j < out_steps:
                there_refs[j][...] = part
            else:
                at = (j - out_steps) * wide
                stay_ref[:, at : at + wide] = part

    return pl.pallas_call(
        kernel,
        in_specs=[SMEM] + [VMEM] * (2 + known) + [HBM],
        out_specs=[VMEM] * (out_steps + 1),
        out_shape=[shape((rows, wide))] * out_steps + [shape((rows, half))],
        scratch_shapes=[
            pltpu.VMEM((2 * out_steps, depth, wide), BF16),
            pltpu.SemaphoreType.DMA((2 * out_steps,)),
        ]
        + attention_scratch(rows, heads, fresh_rows, pulled.shape[0] * pulled.shape[1]),
        compiler_params=params(30),
        cost_estimate=MEDIUM,
        name="attend_out",
    )(place, query, pulled, *fresh, w_out)


def local_rows(place, query, fresh, bases, base, pulled, w_out, after):
    both, depth = query.shape
    rows = both // 2
    width = w_out.shape[1]
    heads = depth // HEAD_DIM
    steps = 8
    wide = width // steps
    known = len(fresh)
    fresh_rows = sum(f.shape[0] for f in fresh)

    def kernel(place_ref, q_ref, pulled_ref, *refs):
        fresh_refs = refs[:known]
        wo = refs[known]
        rest = refs[known + 1 + len(after) :]
        own_ref, peer_ref, wo_buf, a_buf, sems = rest[:5]
        core, side = place_ref[1], place_ref[2]

        def out_copy(j):
            return pltpu.make_async_copy(
                wo.at[:, j * wide : (j + 1) * wide], wo_buf.at[j], sems.at[j]
            )

        for j in range(steps):
            out_copy(j).start()

        def block(b, carry):
            at = pl.ds(pl.multiple_of(b * rows, rows), rows)
            a_buf[at, :] = attend_block(
                place_ref,
                q_ref[at, :],
                base(side) + b * rows,
                [(ref[...], first(side)) for ref, first in zip(fresh_refs, bases)],
                pulled_ref,
                rest[5:],
            )
            return carry

        lax.fori_loop(0, 2, block, 0)
        own_at = pl.ds(pl.multiple_of(core * rows, rows), rows)
        peer_at = pl.ds(pl.multiple_of((1 - core) * rows, rows), rows)
        a = jnp.concatenate([a_buf[own_at, :], a_buf[peer_at, :]], axis=0)
        for j in range(steps):
            out_copy(j).wait()
            part = jnp.dot(a, wo_buf[j], preferred_element_type=F32).astype(BF16)
            own_ref[:, j * wide : (j + 1) * wide] = part[:rows]
            peer_ref[:, j * wide : (j + 1) * wide] = part[rows:]

    return pl.pallas_call(
        kernel,
        in_specs=[SMEM] + [VMEM] * (2 + known) + [HBM] + [ANY] * len(after),
        out_specs=[VMEM, VMEM],
        out_shape=[shape((rows, width)), shape((rows, width))],
        scratch_shapes=[
            pltpu.VMEM((steps, depth, wide), BF16),
            pltpu.VMEM((both, depth), BF16),
            pltpu.SemaphoreType.DMA((steps,)),
        ]
        + attention_scratch(rows, heads, fresh_rows, pulled.shape[0] * pulled.shape[1]),
        compiler_params=params(40),
        cost_estimate=SMALL,
        name="local_rows",
    )(place, query, pulled, *fresh, w_out, *after)


def add_pair(left, pieces):
    rows, width = left.shape
    count = len(pieces)
    wide = width // count

    def kernel(left_ref, *refs):
        out_ref = refs[count]
        for i in range(count):
            cols = slice(i * wide, (i + 1) * wide)
            out_ref[:, cols] = (left_ref[:, cols].astype(F32) + refs[i][...].astype(F32)).astype(
                BF16
            )

    return pl.pallas_call(
        kernel,
        in_specs=[VMEM] * (1 + count),
        out_specs=VMEM,
        out_shape=shape((rows, width)),
        compiler_params=params(8),
        cost_estimate=SMALL,
        name="add_pair",
    )(left, *pieces)


def finish_near(place, tokens, own, peer, near):
    rows, width = tokens.shape
    half = width // 2
    step = 16

    def kernel(place_ref, x_ref, own_ref, peer_ref, near_ref, done_ref, local_ref):
        core = place_ref[1]
        near_cols = pl.ds(pl.multiple_of(core * half, half), half)
        far_cols = pl.ds(pl.multiple_of((1 - core) * half, half), half)

        def block(i, carry):
            at = pl.ds(pl.multiple_of(i * step, step), step)
            local = own_ref[at, near_cols].astype(F32) + peer_ref[at, near_cols].astype(F32)
            total = local + near_ref[at, :].astype(F32)
            done_ref[at, :] = (x_ref[at, near_cols].astype(F32) + total).astype(BF16)
            local_ref[at, :] = own_ref[at, far_cols].astype(F32) + peer_ref[at, far_cols].astype(F32)
            return carry

        lax.fori_loop(0, rows // step, block, 0)

    return pl.pallas_call(
        kernel,
        in_specs=[SMEM] + [VMEM] * 4,
        out_specs=[VMEM] * 2,
        out_shape=[shape((rows, half)), shape((rows, half), F32)],
        compiler_params=params(16),
        cost_estimate=SMALL,
        name="finish_near",
    )(place, tokens, own, peer, near)


def finish(place, tokens, done, local, far):
    rows, width = tokens.shape
    half = width // 2
    step = 32
    blocks = rows // step

    def kernel(place_ref, x_ref, done_ref, local_ref, far_ref, out_ref, buf, sems):
        core = place_ref[1]
        near_cols = pl.ds(pl.multiple_of(core * half, half), half)
        far_cols = pl.ds(pl.multiple_of((1 - core) * half, half), half)

        def near_copy():
            return pltpu.make_async_copy(done_ref, out_ref.at[:, near_cols], sems.at[blocks])

        def far_copy(b):
            at = pl.ds(b * step, step)
            return pltpu.make_async_copy(buf.at[at], out_ref.at[at, far_cols], sems.at[b])

        near_copy().start()
        for b in range(blocks):
            for i in range(0, step, 16):
                at = slice(b * step + i, b * step + i + 16)
                total = local_ref[at, :] + far_ref[at, :].astype(F32)
                buf[at, :] = (x_ref[at, far_cols].astype(F32) + total).astype(BF16)
            far_copy(b).start()
        near_copy().wait()
        for b in range(blocks):
            far_copy(b).wait()

    return pl.pallas_call(
        kernel,
        in_specs=[SMEM] + [VMEM] * 4,
        out_specs=ANY,
        out_shape=shape((rows, width)),
        scratch_shapes=[
            pltpu.VMEM((rows, half), BF16),
            pltpu.SemaphoreType.DMA((blocks + 1,)),
        ],
        compiler_params=params(16),
        cost_estimate=SMALL,
        name="finish",
    )(place, tokens, done, local, far)


def pick_pages(place, wanted, held, after):
    replicas = len(wanted)
    slots = wanted[0].shape[1]
    tensors = len(held)
    _, page, width = held[0].shape
    total = tensors * slots

    def kernel(place_ref, *refs):
        wants, sources = refs[:replicas], refs[replicas : replicas + tensors]
        out_ref = refs[replicas + tensors + len(after)]
        me, rep = place_ref[0], place_ref[3]
        for k in range(replicas):
            asker = lax.rem(rep + k, replicas)
            for i in range(tensors):
                owner = rep * tensors + jnp.bitwise_xor(me, i)
                for s in range(slots):
                    out_ref[asker, i * slots + s] = sources[i][wants[k][0, s, owner]]

    return pl.pallas_call(
        kernel,
        in_specs=[SMEM] * (1 + replicas) + [VMEM] * tensors + [ANY] * len(after),
        out_specs=VMEM,
        out_shape=shape((replicas, total, page, width)),
        compiler_params=params(8),
        cost_estimate=SMALL,
        name="pick_pages",
    )(place, *wanted, *held, *after)


def write_pool(place, slots, kv_pool, early, late):
    pages, heads = kv_pool.shape[:2]
    new_count = slots.shape[1]
    early_rows, late_rows = early[0].shape[0], late[0].shape[0]
    side_rows = (early_rows + late_rows) // 2
    total_rows = early_rows + late_rows

    def kernel(place_ref, slot_ref, pool_ref, *refs):
        early_refs, late_refs, (out_ref, rows_ref) = refs[:3], refs[3:6], refs[6:]
        me, side = place_ref[0], place_ref[2]

        def source(group, i):
            own, y, core = group
            return (own, core.at[0], y, core.at[1])[i]

        for i in range(heads):
            rows_ref[i, :early_rows] = source(early_refs, i)[...]
            rows_ref[i, early_rows:] = source(late_refs, i)[...]
        for p in range(pages):
            found = jnp.int32(-1)
            for j in range(new_count):
                found = jnp.where(slot_ref[0, j] == me * pages + p, j, found)
            first = jnp.maximum(found, 0) * PAGE
            far = (first >= side_rows).astype(jnp.int32)
            inner = first - far * side_rows
            for i in range(heads):
                origin = side if i < 2 else 1 - side
                start = jnp.bitwise_xor(far, origin) * side_rows + inner
                at = jnp.bitwise_xor(me, i)

                @pl.when(found >= 0)
                def _():
                    out_ref[p, at] = rows_ref[i, pl.ds(pl.multiple_of(start, PAGE), PAGE), :]

                @pl.when(found < 0)
                def _():
                    out_ref[p, at] = pool_ref[p, at]

    return pl.pallas_call(
        kernel,
        in_specs=[SMEM, SMEM] + [VMEM] * 7,
        out_specs=VMEM,
        out_shape=shape(kv_pool.shape),
        scratch_shapes=[pltpu.VMEM((heads, total_rows, kv_pool.shape[3]), BF16)],
        compiler_params=params(12),
        cost_estimate=SMALL,
        name="write_pool",
    )(place, slots, kv_pool, *early, *late)


def chip_pair_body(
    tokens,
    gain,
    w_query,
    w_keyvalue,
    w_out,
    kv_pool,
    suffix_pages,
    page_index,
    page_request,
    new_slot,
):
    replicas = lax.axis_size("replica")
    me = lax.axis_index("tensor")
    core = me % 2
    side = me // 2
    rows = tokens.shape[0]
    rep = lax.axis_index("replica")
    place = jnp.stack([me, core, side, rep]).astype(jnp.int32)
    def over_core(x):
        return lax.ppermute(x, "tensor", [(0, 1), (1, 0), (2, 3), (3, 2)])

    def over_y(x):
        return lax.ppermute(x, "tensor", [(0, 2), (2, 0), (1, 3), (3, 1)])

    def tie(x, *others):
        return lax.optimization_barrier((x, *others))[0]

    w_query, w_keyvalue, w_out = in_hbm(w_query), in_hbm(w_keyvalue), in_hbm(w_out)

    wanted = [jnp.swapaxes(page_index, 1, 2)]
    for k in range(1, replicas):
        back = [(i, (i - k) % replicas) for i in range(replicas)]
        wanted.append(lax.ppermute(wanted[0], "replica", back))

    mine, other, *held = prepare(place, in_hbm(tokens), in_hbm(gain), in_hbm(kv_pool))
    for i in range(1, 4):
        held[i] = lax.ppermute(held[i], "tensor", [(t, t ^ i) for t in range(4)])

    peer_near = over_core(other)
    peer_far = over_core(mine)
    is_first = core == 0
    near_tied = tie(peer_near, held[2], held[3])
    first_half = jnp.where(is_first, mine, near_tied)
    second_half = jnp.where(is_first, near_tied, mine)
    first = over_y(first_half)
    second = over_y(second_half)

    picked = pick_pages(place, wanted, held, [first_half, second_half])
    sizes, requests = lax.optimization_barrier((suffix_pages, page_request, picked))[:2]
    requests = jnp.swapaxes(requests, 1, 2).reshape(-1)
    scalars = jnp.concatenate([place, sizes[0], requests])
    pulled = lax.all_to_all(picked, "replica", split_axis=0, concat_axis=0, tiled=True)

    q_local, kv_local, wq, wkv = project_local(
        place, [mine, peer_near], [other, peer_far], w_query, w_keyvalue, [picked, scalars]
    )


    def local_base(s):
        return s * (2 * rows)

    def first_base(s):
        return (1 - s) * (2 * rows)

    def second_base(s):
        return (1 - s) * (2 * rows) + rows

    first = tie(first, q_local)
    wide = first.shape[1] // 4
    pieces = [over_core(first[:, i * wide : (i + 1) * wide]) for i in range(4)]
    q_first, kv_first = project_held(first, pieces, wq, wkv, [])
    early_own = jnp.concatenate([kv_local, kv_first], axis=0)
    early_y = over_y(early_own)
    *there, stay = attend_out(
        scalars, q_first, [kv_local, kv_first], [local_base, first_base], first_base, pulled, w_out
    )
    first_mix = add_pair(stay, [over_core(tie(part, early_y)) for part in there])
    first_sum = over_y(first_mix)

    second = tie(second, first_mix)
    q_second, kv_second = project_far(place, second, over_core(second), w_query, w_keyvalue, [])
    fresh = [kv_local, kv_first, kv_second]
    bases = [local_base, first_base, second_base]
    *there, stay = attend_out(scalars, q_second, fresh, bases, second_base, pulled, w_out)
    late_y = over_y(kv_second)
    second_mix = add_pair(stay, [over_core(tie(part, late_y)) for part in there])
    second_sum = over_y(tie(second_mix, first_sum))

    own_part, peer_part = local_rows(
        scalars, q_local, fresh, bases, local_base, pulled, w_out, [second_mix]
    )
    peer_part = over_core(peer_part)

    early = over_core(jnp.stack([early_own, early_y]))
    late = over_core(jnp.stack([kv_second, late_y]))
    pool_out = write_pool(
        place, new_slot, kv_pool, [early_own, early_y, early], [kv_second, late_y, late]
    )

    second_sum = tie(second_sum, pool_out)
    near = jnp.where(is_first, first_sum, second_sum)
    far = over_core(jnp.where(is_first, second_sum, first_sum))
    done, local = finish_near(place, tokens, own_part, peer_part, near)
    layer_out = finish(place, tokens, done, local, far)
    return (layer_out, pool_out)


def solution(mesh):
    pair = mesh.shape["tensor"] == KV_HEADS
    return jax.shard_map(
        chip_pair_body if pair else gathered_body,
        mesh=mesh,
        in_specs=(
            P(("groups", "replica", "tensor"), None),
            P(),
            P(None, "tensor"),
            P(None, "tensor"),
            P("tensor", None),
            P(("groups", "replica", "tensor"), None, None, None),
            P(("groups", "replica"), None),
            P(("groups", "replica"), None, None),
            P(("groups", "replica"), None, None),
            P(("groups", "replica"), None),
        ),
        out_specs=(
            P(("groups", "replica", "tensor"), None),
            P(("groups", "replica", "tensor"), None, None, None),
        ),
        check_vma=False,
    )
```

```python
import math

import jax
import jax.numpy as jnp
from jax import lax
from jax.experimental import pallas as pl
from jax.experimental.pallas import tpu as pltpu
from jax.sharding import PartitionSpec as P

KV_HEADS = 4
HEAD_DIM = 128
PAGE = 64
UNIT = 8


NEG_FILL = -1e30
EPSILON = 1e-06

F32 = jnp.float32
BF16 = jnp.bfloat16
MIB = 1 << 20
ANY = pl.BlockSpec(memory_space=pl.ANY)
HBM = pl.BlockSpec(memory_space=pltpu.HBM)
SMEM = pl.BlockSpec(memory_space=pltpu.SMEM)
VMEM = pl.BlockSpec(memory_space=pltpu.VMEM)
SMALL = pl.CostEstimate(flops=1024, bytes_accessed=1024, transcendentals=0)
MEDIUM = pl.CostEstimate(flops=1024, bytes_accessed=4000000, transcendentals=0)
LARGE = pl.CostEstimate(flops=20000000000, bytes_accessed=200000000, transcendentals=0)


def params(mib):
    return pltpu.CompilerParams(vmem_limit_bytes=mib * MIB)


def in_hbm(x):
    return pltpu.with_memory_space_constraint(x, pltpu.HBM)


def shape(dims, dtype=BF16):
    return jax.ShapeDtypeStruct(dims, dtype)


def normalize(rows, gain):
    values = rows.astype(jnp.float32)
    inverse = lax.rsqrt(jnp.mean(values * values, axis=-1, keepdims=True) + EPSILON)
    return (values * inverse * gain.astype(jnp.float32)).astype(jnp.bfloat16)


def row_segments(pages, total_rows):
    bounds = jnp.cumsum(pages) * UNIT
    positions = jnp.arange(total_rows, dtype=jnp.int32)
    return jnp.sum((positions[:, None] >= bounds[None, :]).astype(jnp.int32), axis=1)


def gathered_body(
    tokens,
    gain,
    w_query,
    w_keyvalue,
    w_out,
    kv_pool,
    suffix_pages,
    page_index,
    page_request,
    new_slot,
):
    replicas = lax.axis_size("replica")
    tensors = lax.axis_size("tensor")
    owners = replicas * tensors
    position = lax.axis_index("tensor")
    query_width = w_query.shape[1]
    local_heads = query_width // HEAD_DIM
    share = tensors // KV_HEADS
    my_head = position // share
    scale_factor = 1.0 / math.sqrt(HEAD_DIM)
    normed = normalize(tokens, gain)
    piece = lax.all_gather(normed, "tensor", axis=0, tiled=True)
    first = jnp.dot(piece, w_query, preferred_element_type=jnp.float32)
    second = jnp.dot(piece, w_keyvalue, preferred_element_type=jnp.float32)
    projected = jnp.concatenate([first, second], axis=1).astype(jnp.bfloat16)
    query = projected[:, :query_width]
    keyvalue = lax.all_gather(projected[:, query_width:], "tensor", axis=1, tiled=True)
    total_rows = query.shape[0]
    wanted = lax.all_to_all(
        page_index[0], ("replica", "tensor"), split_axis=0, concat_axis=0, tiled=True
    )
    slot_count = wanted.shape[1]
    sources = jnp.arange(owners, dtype=jnp.int32) % tensors
    source_heads = sources // share
    flat_pool = kv_pool.reshape(kv_pool.shape[0] * KV_HEADS, PAGE, 2 * HEAD_DIM)
    outgoing = flat_pool[wanted * KV_HEADS + source_heads[:, None]]
    sub_tokens = outgoing.shape[2]
    pulled = lax.all_to_all(
        outgoing, ("replica", "tensor"), split_axis=0, concat_axis=0, tiled=True
    )
    segments = row_segments(suffix_pages[0], total_rows)
    key_groups = page_request[0]
    stacked = (
        query.reshape(total_rows, local_heads, HEAD_DIM)
        .transpose(1, 0, 2)
        .reshape(local_heads * total_rows, HEAD_DIM)
    )
    own_new = lax.dynamic_index_in_dim(
        keyvalue.reshape(total_rows, KV_HEADS, 2 * HEAD_DIM), my_head, 1, keepdims=False
    )
    row_order = jnp.arange(total_rows, dtype=jnp.int32)
    causal = (segments[:, None] == segments[None, :]) & (row_order[None, :] <= row_order[:, None])

    def block_scores(queries, head_count, keys, allowed):
        raw = (
            jnp.dot(queries, keys[:, :HEAD_DIM].T, preferred_element_type=jnp.float32)
            * scale_factor
        )
        raw = raw.reshape(head_count, total_rows, keys.shape[0])
        return jnp.where(allowed[None], raw, NEG_FILL)

    first_scores = block_scores(stacked, local_heads, own_new, causal)
    running = jnp.max(first_scores, axis=2)
    probs = jnp.exp(first_scores - running[:, :, None])
    denominator = jnp.sum(probs, axis=2)
    numerator = jnp.dot(
        probs.astype(jnp.bfloat16).reshape(local_heads * total_rows, total_rows),
        own_new[:, HEAD_DIM:],
        preferred_element_type=jnp.float32,
    )
    block_owners = 16
    blocks = owners // block_owners

    def absorb(step, state):
        peak, total, mixed = state
        pages = lax.dynamic_slice_in_dim(pulled, step * block_owners, block_owners, 0)
        keys = pages.reshape(block_owners * slot_count * sub_tokens, 2 * HEAD_DIM)
        labels = lax.dynamic_slice_in_dim(key_groups, step * block_owners, block_owners, 0).reshape(
            -1
        )
        matches = (segments[:, None] == labels[None, :])[:, :, None]
        allowed = jnp.broadcast_to(matches, (total_rows, labels.shape[0], sub_tokens)).reshape(
            total_rows, labels.shape[0] * sub_tokens
        )
        scores = block_scores(stacked, local_heads, keys, allowed)
        updated = jnp.maximum(peak, jnp.max(scores, axis=2))
        rescale = jnp.exp(peak - updated)
        weights = jnp.where(allowed[None], jnp.exp(scores - updated[:, :, None]), 0.0)
        total = total * rescale + jnp.sum(weights, axis=2)
        flat_weights = weights.astype(jnp.bfloat16).reshape(local_heads * total_rows, keys.shape[0])
        mixed = mixed * rescale.reshape(-1)[:, None] + jnp.dot(
            flat_weights, keys[:, HEAD_DIM:], preferred_element_type=jnp.float32
        )
        return (updated, total, mixed)

    running, denominator, numerator = lax.fori_loop(
        0, blocks, absorb, (running, denominator, numerator)
    )
    attention = (numerator / denominator.reshape(-1)[:, None]).astype(jnp.bfloat16)
    attention = (
        attention.reshape(local_heads, total_rows, HEAD_DIM)
        .transpose(1, 0, 2)
        .reshape(total_rows, query_width)
    )
    summed = lax.psum_scatter(
        jnp.dot(attention, w_out, preferred_element_type=jnp.float32).astype(jnp.bfloat16),
        "tensor",
        scatter_dimension=0,
        tiled=True,
    ).astype(jnp.float32)
    layer_out = (tokens.astype(jnp.float32) + summed).astype(jnp.bfloat16)
    new_count = total_rows // PAGE
    fresh = (
        keyvalue.reshape(new_count, PAGE, KV_HEADS, 2 * HEAD_DIM)
        .transpose(0, 2, 1, 3)
        .reshape(new_count, KV_HEADS * PAGE * 2 * HEAD_DIM)
    )
    local_pages = kv_pool.shape[0]
    targets = position * local_pages + jnp.arange(local_pages, dtype=jnp.int32)
    match_table = new_slot[0][None, :] == targets[:, None]
    placed = jnp.dot(
        match_table.astype(jnp.bfloat16), fresh, preferred_element_type=jnp.float32
    ).astype(jnp.bfloat16)
    placed = placed.reshape(kv_pool.shape)
    landed = jnp.any(match_table, axis=1)
    pool_out = jnp.where(landed[:, None, None, None], placed, kv_pool)
    return (layer_out, pool_out)


def prepare(place, tokens, gain, kv_pool):
    rows, width = tokens.shape
    half = width // 2
    step = 32
    pages, heads = kv_pool.shape[:2]
    blocks = rows // step

    def kernel(place_ref, x, g, pool, mine_ref, other_ref, *refs):
        held, (x_buf, g_buf, pool_buf, sems) = refs[:heads], refs[heads:]
        me, core = place_ref[0], place_ref[1]
        pool_copy = pltpu.make_async_copy(pool, pool_buf, sems.at[blocks + 1])

        def row_copy(b):
            at = pl.ds(b * step, step)
            return pltpu.make_async_copy(x.at[at], x_buf.at[at], sems.at[b])

        gain_copy = pltpu.make_async_copy(g, g_buf, sems.at[blocks])
        row_copy(0).start()
        gain_copy.start()
        for b in range(1, blocks):
            row_copy(b).start()
        pool_copy.start()
        near = pl.multiple_of(core * half, half)
        far = pl.multiple_of((1 - core) * half, half)
        for b in range(blocks):
            row_copy(b).wait()
            if b == 0:
                gain_copy.wait()

            def block(i, carry):
                at = pl.ds(pl.multiple_of(b * step + i * 16, 16), 16)
                total = jnp.zeros((16, 1), F32)
                for part in range(2):
                    values = x_buf[at, part * half : (part + 1) * half].astype(F32)
                    total += jnp.sum(values * values, axis=1, keepdims=True)
                inverse = lax.rsqrt(total * (1.0 / width) + EPSILON)
                for start, out in ((near, mine_ref), (far, other_ref)):
                    cols = pl.ds(start, half)
                    values = x_buf[at, cols].astype(F32)
                    out[at, :] = (values * inverse * g_buf[cols].astype(F32)[None, :]).astype(BF16)
                return carry

            lax.fori_loop(0, step // 16, block, 0)
        pool_copy.wait()
        for i in range(heads):
            for p in range(pages):
                held[i][p] = pool_buf[p, jnp.bitwise_xor(me, i)]

    return pl.pallas_call(
        kernel,
        in_specs=[SMEM] + [HBM] * 3,
        out_specs=[VMEM] * (2 + heads),
        out_shape=[shape((rows, half))] * 2 + [shape((pages,) + kv_pool.shape[2:])] * heads,
        scratch_shapes=[
            pltpu.VMEM((rows, width), BF16),
            pltpu.VMEM((width,), BF16),
            pltpu.VMEM(kv_pool.shape, BF16),
            pltpu.SemaphoreType.DMA((blocks + 2,)),
        ],
        compiler_params=params(16),
        cost_estimate=SMALL,
        name="prepare",
    )(place, tokens, gain, kv_pool)


def project_local(place, near, far, w_query, w_keyvalue, after):
    rows, half = near[0].shape
    q_width, kv_width = w_query.shape[1], w_keyvalue.shape[1]
    steps = 8
    depth = 2 * half // steps
    waits = len(after)

    def kernel(place_ref, near_own, near_peer, far_own, far_peer, wq, wkv, *refs):
        q_ref, kv_ref, wq_buf, wkv_buf, q_acc, kv_acc, sems = refs[waits:]
        core = place_ref[1]
        stream = weight_stream(core, half, steps, (wq, wkv), (wq_buf, wkv_buf), sems)
        for j in range(steps):
            for copy in stream(j):
                copy.start()
        for j in range(steps):
            for copy in stream(j):
                copy.wait()
            group = (near_own, near_peer) if j < steps // 2 else (far_own, far_peer)
            cols = slice((j % (steps // 2)) * depth, (j % (steps // 2) + 1) * depth)
            x = jnp.concatenate([ref[:, cols] for ref in group], axis=0)
            q_part = jnp.dot(x, wq_buf[j], preferred_element_type=F32)
            kv_part = jnp.dot(x, wkv_buf[j], preferred_element_type=F32)
            if j == 0:
                q_acc[...] = q_part
                kv_acc[...] = kv_part
            elif j < steps - 1:
                q_acc[...] += q_part
                kv_acc[...] += kv_part
            else:
                q_last = (q_acc[...] + q_part).astype(BF16)
                kv_last = (kv_acc[...] + kv_part).astype(BF16)
        for b in range(2):
            at = pl.ds(pl.multiple_of((core if b == 0 else 1 - core) * rows, rows), rows)
            q_ref[at, :] = q_last[b * rows : (b + 1) * rows]
            kv_ref[at, :] = kv_last[b * rows : (b + 1) * rows]

    total = 2 * rows
    return pl.pallas_call(
        kernel,
        in_specs=[SMEM] + [VMEM] * 4 + [HBM] * 2 + [ANY] * waits,
        out_specs=[VMEM] * 4,
        out_shape=[
            shape((total, q_width)),
            shape((total, kv_width)),
            pltpu.VMEM((steps, depth, q_width), BF16),
            pltpu.VMEM((steps, depth, kv_width), BF16),
        ],
        scratch_shapes=[
            pltpu.VMEM((total, q_width), F32),
            pltpu.VMEM((total, kv_width), F32),
            pltpu.SemaphoreType.DMA((2 * steps,)),
        ],
        compiler_params=params(10),
        cost_estimate=LARGE,
        name="project_local",
    )(place, *near, *far, w_query, w_keyvalue, *after)


def weight_stream(core, half, steps, sources, buffers, sems):
    depth = 2 * half // steps

    def copies(j):
        base = core if j < steps // 2 else 1 - core
        start = pl.multiple_of(base * half + (j % (steps // 2)) * depth, depth)
        count = len(sources)
        return [
            pltpu.make_async_copy(w.at[pl.ds(start, depth)], buf.at[j], sems.at[count * j + i])
            for i, (w, buf) in enumerate(zip(sources, buffers))
        ]

    return copies


PAGES_STEP = 4
REQUESTS = 4
SIZES_AT = 4
REQUESTS_AT = 8


def attention_scratch(block_rows, heads, fresh_rows, slots):
    stacked = heads * block_rows
    return [
        pltpu.VMEM((stacked, fresh_rows + slots * PAGE), F32),
        pltpu.VMEM((stacked, HEAD_DIM), F32),
        pltpu.VMEM((stacked, HEAD_DIM), F32),
        pltpu.VMEM((slots * PAGE, 2 * HEAD_DIM), BF16),
        pltpu.SMEM((slots,), jnp.int32),
    ]


def attend_block(place_ref, q, first_row, fresh, pulled, scratch):
    scores, total_ref, mixed_ref, cache, labels = scratch
    me = place_ref[0]
    block_rows, width = q.shape
    heads = width // HEAD_DIM
    stacked = heads * block_rows
    groups, per = pulled.shape[:2]
    tensors = 4
    slots = per // tensors
    wide = PAGES_STEP * PAGE
    factor = math.log2(math.e) / math.sqrt(HEAD_DIM)
    bound = []
    running = jnp.int32(0)
    for k in range(REQUESTS):
        running = running + place_ref[SIZES_AT + k] * UNIT
        bound.append(running)

    def segment_of(position):
        return sum((position >= b).astype(jnp.int32) for b in bound)

    lowest = segment_of(first_row)
    highest = segment_of(first_row + block_rows - 1)
    count = jnp.int32(0)
    for g in range(groups):
        for p in range(per):
            owner = g * tensors + jnp.bitwise_xor(me, p // slots)
            label = place_ref[REQUESTS_AT + p % slots * groups * tensors + owner]
            wanted = (label >= lowest) & (label <= highest)

            @pl.when(wanted)
            def _():
                cache[pl.ds(pl.multiple_of(count * PAGE, PAGE), PAGE), :] = pulled[g, p]
                labels[count] = label

            count = count + wanted.astype(jnp.int32)
    steps = (count + PAGES_STEP - 1) // PAGES_STEP
    for k in range(PAGES_STEP - 1):

        @pl.when(count + k < steps * PAGES_STEP)
        def _():
            cache[pl.ds(pl.multiple_of((count + k) * PAGE, PAGE), PAGE), :] = jnp.zeros(
                (PAGE, 2 * HEAD_DIM), BF16
            )
            labels[count + k] = jnp.int32(-1)

    q_rows = jnp.concatenate([q[:, h * HEAD_DIM : (h + 1) * HEAD_DIM] for h in range(heads)], axis=0)
    row_position = first_row + lax.broadcasted_iota(jnp.int32, (block_rows, 1), 0)
    row_segment = segment_of(row_position)

    def masked_scores(keys, allowed):
        raw = lax.dot_general(q_rows, keys, (((1,), (1,)), ((), ())), preferred_element_type=F32)
        n = keys.shape[0]
        return jnp.where(allowed[None], raw.reshape(heads, block_rows, n), NEG_FILL).reshape(
            stacked, n
        )

    def fold(values, combine):
        pieces = [values[:, i : i + HEAD_DIM] for i in range(0, values.shape[1], HEAD_DIM)]
        result = pieces[0]
        for piece in pieces[1:]:
            result = combine(result, piece)
        return result

    new = jnp.concatenate([rows for rows, _ in fresh], axis=0)
    fresh_rows = new.shape[0]
    key_position = jnp.concatenate(
        [
            base + lax.broadcasted_iota(jnp.int32, (1, rows.shape[0]), 1)
            for rows, base in fresh
        ],
        axis=1,
    )
    allowed = (row_segment == segment_of(key_position)) & (key_position <= row_position)
    masked = masked_scores(new[:, :HEAD_DIM], allowed)
    scores[:, :fresh_rows] = masked
    total_ref[...] = fold(masked, jnp.maximum)
    lanes = lax.broadcasted_iota(jnp.int32, (1, wide), 1) // PAGE

    def add_scores(g, carry):
        label = jnp.full((1, wide), -1, jnp.int32)
        for j in range(PAGES_STEP):
            label = jnp.where(lanes == j, labels[g * PAGES_STEP + j], label)
        keys = cache[pl.ds(pl.multiple_of(g * wide, wide), wide), :HEAD_DIM]
        masked = masked_scores(keys, row_segment == label)
        scores[:, pl.ds(pl.multiple_of(fresh_rows + g * wide, PAGE), wide)] = masked
        total_ref[...] = jnp.maximum(total_ref[...], fold(masked, jnp.maximum))
        return carry

    lax.fori_loop(0, steps, add_scores, 0)
    top = jnp.max(total_ref[...], axis=1, keepdims=True) * factor
    probs = jnp.exp2(scores[:, :fresh_rows] * factor - top)
    total_ref[...] = fold(probs, jnp.add)
    mixed_ref[...] = jnp.dot(probs.astype(BF16), new[:, HEAD_DIM:], preferred_element_type=F32)

    def add_values(g, carry):
        part = scores[:, pl.ds(pl.multiple_of(fresh_rows + g * wide, PAGE), wide)]
        probs = jnp.exp2(part * factor - top)
        values = cache[pl.ds(pl.multiple_of(g * wide, wide), wide), HEAD_DIM:]
        total_ref[...] += fold(probs, jnp.add)
        mixed_ref[...] += jnp.dot(probs.astype(BF16), values, preferred_element_type=F32)
        return carry

    lax.fori_loop(0, steps, add_values, 0)
    denominator = jnp.sum(total_ref[...], axis=1, keepdims=True)
    result = (mixed_ref[...] / denominator).astype(BF16)
    return jnp.concatenate(
        [result[h * block_rows : (h + 1) * block_rows] for h in range(heads)], axis=1
    )


def project_held(near, far, w_query, w_keyvalue, after):
    rows, half = near.shape
    pieces = len(far)
    steps, depth, q_width = w_query.shape
    kv_width = w_keyvalue.shape[2]

    def kernel(near_ref, *refs):
        far_refs = refs[:pieces]
        wq, wkv = refs[pieces : pieces + 2]
        q_ref, kv_ref = refs[pieces + 2 + len(after) :]
        for w, out in ((wq, q_ref), (wkv, kv_ref)):
            total = None
            for j in range(steps):
                at = j * depth
                if at < half:
                    x = near_ref[:, at : at + depth]
                else:
                    wide = half // pieces
                    x = far_refs[(at - half) // wide][:, at % wide : at % wide + depth]
                part = jnp.dot(x, w[j], preferred_element_type=F32)
                total = part if j == 0 else total + part
            out[...] = total.astype(BF16)

    return pl.pallas_call(
        kernel,
        in_specs=[VMEM] * (3 + pieces) + [ANY] * len(after),
        out_specs=[VMEM] * 2,
        out_shape=[shape((rows, q_width)), shape((rows, kv_width))],
        compiler_params=params(6),
        cost_estimate=SMALL,
        name="project_held",
    )(near, *far, w_query, w_keyvalue, *after)


def project_far(place, near, far, w_query, w_keyvalue, after):
    rows, half = near.shape
    q_width, kv_width = w_query.shape[1], w_keyvalue.shape[1]
    steps = 8
    depth = 2 * half // steps

    def kernel(place_ref, near_ref, far_ref, wq, wkv, *refs):
        q_ref, kv_ref, wq_buf, wkv_buf, x_buf, sems = refs[len(after) :]
        rows_in = [
            pltpu.make_async_copy(ref, x_buf.at[i], sems.at[2 * steps + i])
            for i, ref in enumerate((near_ref, far_ref))
        ]
        stream = weight_stream(place_ref[1], half, steps, (wq, wkv), (wq_buf, wkv_buf), sems)
        for j in range(steps):
            for copy in stream(j):
                copy.start()
            if j < 2:
                rows_in[j].start()
        q_sum = kv_sum = None
        for j in range(steps):
            for copy in stream(j):
                copy.wait()
            group, inner = divmod(j, steps // 2)
            if inner == 0:
                rows_in[group].wait()
            x = x_buf[group, :, inner * depth : (inner + 1) * depth]
            q_part = jnp.dot(x, wq_buf[j], preferred_element_type=F32)
            kv_part = jnp.dot(x, wkv_buf[j], preferred_element_type=F32)
            q_sum = q_part if j == 0 else q_sum + q_part
            kv_sum = kv_part if j == 0 else kv_sum + kv_part
        q_ref[...] = q_sum.astype(BF16)
        kv_ref[...] = kv_sum.astype(BF16)

    return pl.pallas_call(
        kernel,
        in_specs=[SMEM] + [ANY] * 2 + [HBM] * 2 + [ANY] * len(after),
        out_specs=[VMEM] * 2,
        out_shape=[shape((rows, q_width)), shape((rows, kv_width))],
        scratch_shapes=[
            pltpu.VMEM((steps, depth, q_width), BF16),
            pltpu.VMEM((steps, depth, kv_width), BF16),
            pltpu.VMEM((2, rows, half), BF16),
            pltpu.SemaphoreType.DMA((2 * steps + 2,)),
        ],
        compiler_params=params(32),
        cost_estimate=SMALL,
        name="project_far",
    )(place, near, far, w_query, w_keyvalue, *after)


def attend_out(place, query, fresh, bases, base, pulled, w_out):
    rows, depth = query.shape
    width = w_out.shape[1]
    half = width // 2
    heads = depth // HEAD_DIM
    out_steps = 4
    wide = half // out_steps
    known = len(fresh)
    count = sum(f.shape[0] for f in fresh)
    fresh_rows = -(-count // HEAD_DIM) * HEAD_DIM
    pad = fresh_rows - count

    def kernel(place_ref, q_ref, pulled_ref, *refs):
        fresh_refs = refs[:known]
        wo = refs[known]
        there_refs, refs_after = refs[known + 1 : known + 1 + out_steps], refs[known + 1 + out_steps :]
        stay_ref, wo_buf, sems = refs_after[:3]
        core, side = place_ref[1], place_ref[2]

        def copy(j):
            first = 1 - core if j < out_steps else core
            start = pl.multiple_of(first * half + (j % out_steps) * wide, wide)
            return pltpu.make_async_copy(wo.at[:, pl.ds(start, wide)], wo_buf.at[j], sems.at[j])

        for j in range(2 * out_steps):
            copy(j).start()
        pairs = [(ref[...], at(side)) for ref, at in zip(fresh_refs, bases)]
        if pad:
            pairs.append((jnp.zeros((pad, 2 * HEAD_DIM), BF16), jnp.int32(1 << 20)))
        mixed = attend_block(
            place_ref, q_ref[...], base(side), pairs, pulled_ref, refs_after[3:]
        )
        for j in range(2 * out_steps):
            copy(j).wait()
            part = jnp.dot(mixed, wo_buf[j], preferred_element_type=F32).astype(BF16)
            if j < out_steps:
                there_refs[j][...] = part
            else:
                at = (j - out_steps) * wide
                stay_ref[:, at : at + wide] = part

    return pl.pallas_call(
        kernel,
        in_specs=[SMEM] + [VMEM] * (2 + known) + [HBM],
        out_specs=[VMEM] * (out_steps + 1),
        out_shape=[shape((rows, wide))] * out_steps + [shape((rows, half))],
        scratch_shapes=[
            pltpu.VMEM((2 * out_steps, depth, wide), BF16),
            pltpu.SemaphoreType.DMA((2 * out_steps,)),
        ]
        + attention_scratch(rows, heads, fresh_rows, pulled.shape[0] * pulled.shape[1]),
        compiler_params=params(30),
        cost_estimate=MEDIUM,
        name="attend_out",
    )(place, query, pulled, *fresh, w_out)


def local_rows(place, query, fresh, bases, base, pulled, w_out, after):
    both, depth = query.shape
    rows = both // 2
    width = w_out.shape[1]
    heads = depth // HEAD_DIM
    steps = 8
    wide = width // steps
    known = len(fresh)
    fresh_rows = sum(f.shape[0] for f in fresh)

    def kernel(place_ref, q_ref, pulled_ref, *refs):
        fresh_refs = refs[:known]
        wo = refs[known]
        rest = refs[known + 1 + len(after) :]
        own_ref, peer_ref, wo_buf, a_buf, sems = rest[:5]
        core, side = place_ref[1], place_ref[2]

        def out_copy(j):
            return pltpu.make_async_copy(
                wo.at[:, j * wide : (j + 1) * wide], wo_buf.at[j], sems.at[j]
            )

        for j in range(steps):
            out_copy(j).start()

        def block(b, carry):
            at = pl.ds(pl.multiple_of(b * rows, rows), rows)
            a_buf[at, :] = attend_block(
                place_ref,
                q_ref[at, :],
                base(side) + b * rows,
                [(ref[...], first(side)) for ref, first in zip(fresh_refs, bases)],
                pulled_ref,
                rest[5:],
            )
            return carry

        lax.fori_loop(0, 2, block, 0)
        own_at = pl.ds(pl.multiple_of(core * rows, rows), rows)
        peer_at = pl.ds(pl.multiple_of((1 - core) * rows, rows), rows)
        a = jnp.concatenate([a_buf[own_at, :], a_buf[peer_at, :]], axis=0)
        for j in range(steps):
            out_copy(j).wait()
            part = jnp.dot(a, wo_buf[j], preferred_element_type=F32).astype(BF16)
            own_ref[:, j * wide : (j + 1) * wide] = part[:rows]
            peer_ref[:, j * wide : (j + 1) * wide] = part[rows:]

    return pl.pallas_call(
        kernel,
        in_specs=[SMEM] + [VMEM] * (2 + known) + [HBM] + [ANY] * len(after),
        out_specs=[VMEM, VMEM],
        out_shape=[shape((rows, width)), shape((rows, width))],
        scratch_shapes=[
            pltpu.VMEM((steps, depth, wide), BF16),
            pltpu.VMEM((both, depth), BF16),
            pltpu.SemaphoreType.DMA((steps,)),
        ]
        + attention_scratch(rows, heads, fresh_rows, pulled.shape[0] * pulled.shape[1]),
        compiler_params=params(40),
        cost_estimate=SMALL,
        name="local_rows",
    )(place, query, pulled, *fresh, w_out, *after)


def add_pair(left, pieces):
    rows, width = left.shape
    count = len(pieces)
    wide = width // count

    def kernel(left_ref, *refs):
        out_ref = refs[count]
        for i in range(count):
            cols = slice(i * wide, (i + 1) * wide)
            out_ref[:, cols] = (left_ref[:, cols].astype(F32) + refs[i][...].astype(F32)).astype(
                BF16
            )

    return pl.pallas_call(
        kernel,
        in_specs=[VMEM] * (1 + count),
        out_specs=VMEM,
        out_shape=shape((rows, width)),
        compiler_params=params(8),
        cost_estimate=SMALL,
        name="add_pair",
    )(left, *pieces)


def finish_near(place, tokens, own, peer, near):
    rows, width = tokens.shape
    half = width // 2
    step = 16

    def kernel(place_ref, x_ref, own_ref, peer_ref, near_ref, done_ref, local_ref):
        core = place_ref[1]
        near_cols = pl.ds(pl.multiple_of(core * half, half), half)
        far_cols = pl.ds(pl.multiple_of((1 - core) * half, half), half)

        def block(i, carry):
            at = pl.ds(pl.multiple_of(i * step, step), step)
            local = own_ref[at, near_cols].astype(F32) + peer_ref[at, near_cols].astype(F32)
            total = local + near_ref[at, :].astype(F32)
            done_ref[at, :] = (x_ref[at, near_cols].astype(F32) + total).astype(BF16)
            local_ref[at, :] = own_ref[at, far_cols].astype(F32) + peer_ref[at, far_cols].astype(F32)
            return carry

        lax.fori_loop(0, rows // step, block, 0)

    return pl.pallas_call(
        kernel,
        in_specs=[SMEM] + [VMEM] * 4,
        out_specs=[VMEM] * 2,
        out_shape=[shape((rows, half)), shape((rows, half), F32)],
        compiler_params=params(16),
        cost_estimate=SMALL,
        name="finish_near",
    )(place, tokens, own, peer, near)


def finish(place, tokens, done, local, far):
    rows, width = tokens.shape
    half = width // 2
    step = 32
    blocks = rows // step

    def kernel(place_ref, x_ref, done_ref, local_ref, far_ref, out_ref, buf, sems):
        core = place_ref[1]
        near_cols = pl.ds(pl.multiple_of(core * half, half), half)
        far_cols = pl.ds(pl.multiple_of((1 - core) * half, half), half)

        def near_copy():
            return pltpu.make_async_copy(done_ref, out_ref.at[:, near_cols], sems.at[blocks])

        def far_copy(b):
            at = pl.ds(b * step, step)
            return pltpu.make_async_copy(buf.at[at], out_ref.at[at, far_cols], sems.at[b])

        near_copy().start()
        for b in range(blocks):
            for i in range(0, step, 16):
                at = slice(b * step + i, b * step + i + 16)
                total = local_ref[at, :] + far_ref[at, :].astype(F32)
                buf[at, :] = (x_ref[at, far_cols].astype(F32) + total).astype(BF16)
            far_copy(b).start()
        near_copy().wait()
        for b in range(blocks):
            far_copy(b).wait()

    return pl.pallas_call(
        kernel,
        in_specs=[SMEM] + [VMEM] * 4,
        out_specs=ANY,
        out_shape=shape((rows, width)),
        scratch_shapes=[
            pltpu.VMEM((rows, half), BF16),
            pltpu.SemaphoreType.DMA((blocks + 1,)),
        ],
        compiler_params=params(16),
        cost_estimate=SMALL,
        name="finish",
    )(place, tokens, done, local, far)


def pick_pages(place, wanted, held, after):
    replicas = len(wanted)
    slots = wanted[0].shape[1]
    tensors = len(held)
    _, page, width = held[0].shape
    total = tensors * slots

    def kernel(place_ref, *refs):
        wants, sources = refs[:replicas], refs[replicas : replicas + tensors]
        out_ref = refs[replicas + tensors + len(after)]
        me, rep = place_ref[0], place_ref[3]
        for k in range(replicas):
            asker = lax.rem(rep + k, replicas)
            for i in range(tensors):
                owner = rep * tensors + jnp.bitwise_xor(me, i)
                for s in range(slots):
                    out_ref[asker, i * slots + s] = sources[i][wants[k][0, s, owner]]

    return pl.pallas_call(
        kernel,
        in_specs=[SMEM] * (1 + replicas) + [VMEM] * tensors + [ANY] * len(after),
        out_specs=VMEM,
        out_shape=shape((replicas, total, page, width)),
        compiler_params=params(8),
        cost_estimate=SMALL,
        name="pick_pages",
    )(place, *wanted, *held, *after)


def write_pool(place, slots, kv_pool, early, late):
    pages, heads = kv_pool.shape[:2]
    new_count = slots.shape[1]
    early_rows, late_rows = early[0].shape[0], late[0].shape[0]
    side_rows = (early_rows + late_rows) // 2
    total_rows = early_rows + late_rows

    def kernel(place_ref, slot_ref, pool_ref, *refs):
        early_refs, late_refs, (out_ref, rows_ref) = refs[:3], refs[3:6], refs[6:]
        me, side = place_ref[0], place_ref[2]

        def source(group, i):
            own, y, core = group
            return (own, core.at[0], y, core.at[1])[i]

        for i in range(heads):
            rows_ref[i, :early_rows] = source(early_refs, i)[...]
            rows_ref[i, early_rows:] = source(late_refs, i)[...]
        for p in range(pages):
            found = jnp.int32(-1)
            for j in range(new_count):
                found = jnp.where(slot_ref[0, j] == me * pages + p, j, found)
            first = jnp.maximum(found, 0) * PAGE
            far = (first >= side_rows).astype(jnp.int32)
            inner = first - far * side_rows
            for i in range(heads):
                origin = side if i < 2 else 1 - side
                start = jnp.bitwise_xor(far, origin) * side_rows + inner
                at = jnp.bitwise_xor(me, i)

                @pl.when(found >= 0)
                def _():
                    out_ref[p, at] = rows_ref[i, pl.ds(pl.multiple_of(start, PAGE), PAGE), :]

                @pl.when(found < 0)
                def _():
                    out_ref[p, at] = pool_ref[p, at]

    return pl.pallas_call(
        kernel,
        in_specs=[SMEM, SMEM] + [VMEM] * 7,
        out_specs=VMEM,
        out_shape=shape(kv_pool.shape),
        scratch_shapes=[pltpu.VMEM((heads, total_rows, kv_pool.shape[3]), BF16)],
        compiler_params=params(12),
        cost_estimate=SMALL,
        name="write_pool",
    )(place, slots, kv_pool, *early, *late)


def chip_pair_body(
    tokens,
    gain,
    w_query,
    w_keyvalue,
    w_out,
    kv_pool,
    suffix_pages,
    page_index,
    page_request,
    new_slot,
):
    replicas = lax.axis_size("replica")
    me = lax.axis_index("tensor")
    core = me % 2
    side = me // 2
    rows = tokens.shape[0]
    rep = lax.axis_index("replica")
    place = jnp.stack([me, core, side, rep]).astype(jnp.int32)
    def over_core(x):
        return lax.ppermute(x, "tensor", [(0, 1), (1, 0), (2, 3), (3, 2)])

    def over_y(x):
        return lax.ppermute(x, "tensor", [(0, 2), (2, 0), (1, 3), (3, 1)])

    def tie(x, *others):
        return lax.optimization_barrier((x, *others))[0]

    w_query, w_keyvalue, w_out = in_hbm(w_query), in_hbm(w_keyvalue), in_hbm(w_out)

    wanted = [jnp.swapaxes(page_index, 1, 2)]
    for k in range(1, replicas):
        back = [(i, (i - k) % replicas) for i in range(replicas)]
        wanted.append(lax.ppermute(wanted[0], "replica", back))

    mine, other, *held = prepare(place, in_hbm(tokens), in_hbm(gain), in_hbm(kv_pool))
    for i in range(1, 4):
        held[i] = lax.ppermute(held[i], "tensor", [(t, t ^ i) for t in range(4)])

    peer_near = over_core(other)
    peer_far = over_core(mine)
    is_first = core == 0
    near_tied = tie(peer_near, held[2], held[3])
    first_half = jnp.where(is_first, mine, near_tied)
    second_half = jnp.where(is_first, near_tied, mine)
    first = over_y(first_half)
    second = over_y(second_half)

    picked = pick_pages(place, wanted, held, [first_half, second_half])
    sizes, requests = lax.optimization_barrier((suffix_pages, page_request, picked))[:2]
    requests = jnp.swapaxes(requests, 1, 2).reshape(-1)
    scalars = jnp.concatenate([place, sizes[0], requests])
    pulled = lax.all_to_all(picked, "replica", split_axis=0, concat_axis=0, tiled=True)

    q_local, kv_local, wq, wkv = project_local(
        place, [mine, peer_near], [other, peer_far], w_query, w_keyvalue, [picked, scalars]
    )


    def local_base(s):
        return s * (2 * rows)

    def first_base(s):
        return (1 - s) * (2 * rows)

    def second_base(s):
        return (1 - s) * (2 * rows) + rows

    first = tie(first, q_local)
    wide = first.shape[1] // 4
    pieces = [over_core(first[:, i * wide : (i + 1) * wide]) for i in range(4)]
    q_first, kv_first = project_held(first, pieces, wq, wkv, [])
    early_own = jnp.concatenate([kv_local, kv_first], axis=0)
    early_y = over_y(early_own)
    *there, stay = attend_out(
        scalars, q_first, [kv_local, kv_first], [local_base, first_base], first_base, pulled, w_out
    )
    first_mix = add_pair(stay, [over_core(tie(part, early_y)) for part in there])
    first_sum = over_y(first_mix)

    second = tie(second, first_mix)
    q_second, kv_second = project_far(place, second, over_core(second), w_query, w_keyvalue, [])
    fresh = [kv_local, kv_first, kv_second]
    bases = [local_base, first_base, second_base]
    *there, stay = attend_out(scalars, q_second, fresh, bases, second_base, pulled, w_out)
    late_y = over_y(kv_second)
    there[-1] = tie(there[-1], late_y)
    second_mix = add_pair(stay, [over_core(part) for part in there])
    second_sum = over_y(tie(second_mix, first_sum))

    own_part, peer_part = local_rows(
        scalars, q_local, fresh, bases, local_base, pulled, w_out, [second_mix]
    )
    peer_part = over_core(peer_part)

    early = over_core(jnp.stack([early_own, early_y]))
    late = over_core(jnp.stack([kv_second, late_y]))
    pool_out = write_pool(
        place, new_slot, kv_pool, [early_own, early_y, early], [kv_second, late_y, late]
    )

    second_sum = tie(second_sum, pool_out)
    near = jnp.where(is_first, first_sum, second_sum)
    far = over_core(jnp.where(is_first, second_sum, first_sum))
    done, local = finish_near(place, tokens, own_part, peer_part, near)
    layer_out = finish(place, tokens, done, local, far)
    return (layer_out, pool_out)


def solution(mesh):
    pair = mesh.shape["tensor"] == KV_HEADS
    return jax.shard_map(
        chip_pair_body if pair else gathered_body,
        mesh=mesh,
        in_specs=(
            P(("groups", "replica", "tensor"), None),
            P(),
            P(None, "tensor"),
            P(None, "tensor"),
            P("tensor", None),
            P(("groups", "replica", "tensor"), None, None, None),
            P(("groups", "replica"), None),
            P(("groups", "replica"), None, None),
            P(("groups", "replica"), None, None),
            P(("groups", "replica"), None),
        ),
        out_specs=(
            P(("groups", "replica", "tensor"), None),
            P(("groups", "replica", "tensor"), None, None, None),
        ),
        check_vma=False,
    )
```

```python
import math

import jax
import jax.numpy as jnp
from jax import lax
from jax.experimental import pallas as pl
from jax.experimental.pallas import tpu as pltpu
from jax.sharding import PartitionSpec as P

KV_HEADS = 4
HEAD_DIM = 128
PAGE = 64
UNIT = 8


NEG_FILL = -1e30
EPSILON = 1e-06

F32 = jnp.float32
BF16 = jnp.bfloat16
MIB = 1 << 20
ANY = pl.BlockSpec(memory_space=pl.ANY)
HBM = pl.BlockSpec(memory_space=pltpu.HBM)
SMEM = pl.BlockSpec(memory_space=pltpu.SMEM)
VMEM = pl.BlockSpec(memory_space=pltpu.VMEM)
SMALL = pl.CostEstimate(flops=1024, bytes_accessed=1024, transcendentals=0)
MEDIUM = pl.CostEstimate(flops=1024, bytes_accessed=4000000, transcendentals=0)
LARGE = pl.CostEstimate(flops=20000000000, bytes_accessed=200000000, transcendentals=0)


def params(mib):
    return pltpu.CompilerParams(vmem_limit_bytes=mib * MIB)


def in_hbm(x):
    return pltpu.with_memory_space_constraint(x, pltpu.HBM)


def shape(dims, dtype=BF16):
    return jax.ShapeDtypeStruct(dims, dtype)


def normalize(rows, gain):
    values = rows.astype(jnp.float32)
    inverse = lax.rsqrt(jnp.mean(values * values, axis=-1, keepdims=True) + EPSILON)
    return (values * inverse * gain.astype(jnp.float32)).astype(jnp.bfloat16)


def row_segments(pages, total_rows):
    bounds = jnp.cumsum(pages) * UNIT
    positions = jnp.arange(total_rows, dtype=jnp.int32)
    return jnp.sum((positions[:, None] >= bounds[None, :]).astype(jnp.int32), axis=1)


def gathered_body(
    tokens,
    gain,
    w_query,
    w_keyvalue,
    w_out,
    kv_pool,
    suffix_pages,
    page_index,
    page_request,
    new_slot,
):
    replicas = lax.axis_size("replica")
    tensors = lax.axis_size("tensor")
    owners = replicas * tensors
    position = lax.axis_index("tensor")
    query_width = w_query.shape[1]
    local_heads = query_width // HEAD_DIM
    share = tensors // KV_HEADS
    my_head = position // share
    scale_factor = 1.0 / math.sqrt(HEAD_DIM)
    normed = normalize(tokens, gain)
    piece = lax.all_gather(normed, "tensor", axis=0, tiled=True)
    first = jnp.dot(piece, w_query, preferred_element_type=jnp.float32)
    second = jnp.dot(piece, w_keyvalue, preferred_element_type=jnp.float32)
    projected = jnp.concatenate([first, second], axis=1).astype(jnp.bfloat16)
    query = projected[:, :query_width]
    keyvalue = lax.all_gather(projected[:, query_width:], "tensor", axis=1, tiled=True)
    total_rows = query.shape[0]
    wanted = lax.all_to_all(
        page_index[0], ("replica", "tensor"), split_axis=0, concat_axis=0, tiled=True
    )
    slot_count = wanted.shape[1]
    sources = jnp.arange(owners, dtype=jnp.int32) % tensors
    source_heads = sources // share
    flat_pool = kv_pool.reshape(kv_pool.shape[0] * KV_HEADS, PAGE, 2 * HEAD_DIM)
    outgoing = flat_pool[wanted * KV_HEADS + source_heads[:, None]]
    sub_tokens = outgoing.shape[2]
    pulled = lax.all_to_all(
        outgoing, ("replica", "tensor"), split_axis=0, concat_axis=0, tiled=True
    )
    segments = row_segments(suffix_pages[0], total_rows)
    key_groups = page_request[0]
    stacked = (
        query.reshape(total_rows, local_heads, HEAD_DIM)
        .transpose(1, 0, 2)
        .reshape(local_heads * total_rows, HEAD_DIM)
    )
    own_new = lax.dynamic_index_in_dim(
        keyvalue.reshape(total_rows, KV_HEADS, 2 * HEAD_DIM), my_head, 1, keepdims=False
    )
    row_order = jnp.arange(total_rows, dtype=jnp.int32)
    causal = (segments[:, None] == segments[None, :]) & (row_order[None, :] <= row_order[:, None])

    def block_scores(queries, head_count, keys, allowed):
        raw = (
            jnp.dot(queries, keys[:, :HEAD_DIM].T, preferred_element_type=jnp.float32)
            * scale_factor
        )
        raw = raw.reshape(head_count, total_rows, keys.shape[0])
        return jnp.where(allowed[None], raw, NEG_FILL)

    first_scores = block_scores(stacked, local_heads, own_new, causal)
    running = jnp.max(first_scores, axis=2)
    probs = jnp.exp(first_scores - running[:, :, None])
    denominator = jnp.sum(probs, axis=2)
    numerator = jnp.dot(
        probs.astype(jnp.bfloat16).reshape(local_heads * total_rows, total_rows),
        own_new[:, HEAD_DIM:],
        preferred_element_type=jnp.float32,
    )
    block_owners = 16
    blocks = owners // block_owners

    def absorb(step, state):
        peak, total, mixed = state
        pages = lax.dynamic_slice_in_dim(pulled, step * block_owners, block_owners, 0)
        keys = pages.reshape(block_owners * slot_count * sub_tokens, 2 * HEAD_DIM)
        labels = lax.dynamic_slice_in_dim(key_groups, step * block_owners, block_owners, 0).reshape(
            -1
        )
        matches = (segments[:, None] == labels[None, :])[:, :, None]
        allowed = jnp.broadcast_to(matches, (total_rows, labels.shape[0], sub_tokens)).reshape(
            total_rows, labels.shape[0] * sub_tokens
        )
        scores = block_scores(stacked, local_heads, keys, allowed)
        updated = jnp.maximum(peak, jnp.max(scores, axis=2))
        rescale = jnp.exp(peak - updated)
        weights = jnp.where(allowed[None], jnp.exp(scores - updated[:, :, None]), 0.0)
        total = total * rescale + jnp.sum(weights, axis=2)
        flat_weights = weights.astype(jnp.bfloat16).reshape(local_heads * total_rows, keys.shape[0])
        mixed = mixed * rescale.reshape(-1)[:, None] + jnp.dot(
            flat_weights, keys[:, HEAD_DIM:], preferred_element_type=jnp.float32
        )
        return (updated, total, mixed)

    running, denominator, numerator = lax.fori_loop(
        0, blocks, absorb, (running, denominator, numerator)
    )
    attention = (numerator / denominator.reshape(-1)[:, None]).astype(jnp.bfloat16)
    attention = (
        attention.reshape(local_heads, total_rows, HEAD_DIM)
        .transpose(1, 0, 2)
        .reshape(total_rows, query_width)
    )
    summed = lax.psum_scatter(
        jnp.dot(attention, w_out, preferred_element_type=jnp.float32).astype(jnp.bfloat16),
        "tensor",
        scatter_dimension=0,
        tiled=True,
    ).astype(jnp.float32)
    layer_out = (tokens.astype(jnp.float32) + summed).astype(jnp.bfloat16)
    new_count = total_rows // PAGE
    fresh = (
        keyvalue.reshape(new_count, PAGE, KV_HEADS, 2 * HEAD_DIM)
        .transpose(0, 2, 1, 3)
        .reshape(new_count, KV_HEADS * PAGE * 2 * HEAD_DIM)
    )
    local_pages = kv_pool.shape[0]
    targets = position * local_pages + jnp.arange(local_pages, dtype=jnp.int32)
    match_table = new_slot[0][None, :] == targets[:, None]
    placed = jnp.dot(
        match_table.astype(jnp.bfloat16), fresh, preferred_element_type=jnp.float32
    ).astype(jnp.bfloat16)
    placed = placed.reshape(kv_pool.shape)
    landed = jnp.any(match_table, axis=1)
    pool_out = jnp.where(landed[:, None, None, None], placed, kv_pool)
    return (layer_out, pool_out)


def prepare(place, tokens, gain, kv_pool):
    rows, width = tokens.shape
    half = width // 2
    step = 32
    pages, heads = kv_pool.shape[:2]
    blocks = rows // step

    def kernel(place_ref, x, g, pool, mine_ref, other_ref, *refs):
        held, (x_buf, g_buf, pool_buf, sems) = refs[:heads], refs[heads:]
        me, core = place_ref[0], place_ref[1]
        pool_copy = pltpu.make_async_copy(pool, pool_buf, sems.at[blocks + 1])

        def row_copy(b):
            at = pl.ds(b * step, step)
            return pltpu.make_async_copy(x.at[at], x_buf.at[at], sems.at[b])

        gain_copy = pltpu.make_async_copy(g, g_buf, sems.at[blocks])
        row_copy(0).start()
        gain_copy.start()
        for b in range(1, blocks):
            row_copy(b).start()
        pool_copy.start()
        near = pl.multiple_of(core * half, half)
        far = pl.multiple_of((1 - core) * half, half)
        for b in range(blocks):
            row_copy(b).wait()
            if b == 0:
                gain_copy.wait()

            def block(i, carry):
                at = pl.ds(pl.multiple_of(b * step + i * 16, 16), 16)
                total = jnp.zeros((16, 1), F32)
                for part in range(2):
                    values = x_buf[at, part * half : (part + 1) * half].astype(F32)
                    total += jnp.sum(values * values, axis=1, keepdims=True)
                inverse = lax.rsqrt(total * (1.0 / width) + EPSILON)
                for start, out in ((near, mine_ref), (far, other_ref)):
                    cols = pl.ds(start, half)
                    values = x_buf[at, cols].astype(F32)
                    out[at, :] = (values * inverse * g_buf[cols].astype(F32)[None, :]).astype(BF16)
                return carry

            lax.fori_loop(0, step // 16, block, 0)
        pool_copy.wait()
        for i in range(heads):
            for p in range(pages):
                held[i][p] = pool_buf[p, jnp.bitwise_xor(me, i)]

    return pl.pallas_call(
        kernel,
        in_specs=[SMEM] + [HBM] * 3,
        out_specs=[VMEM] * (2 + heads),
        out_shape=[shape((rows, half))] * 2 + [shape((pages,) + kv_pool.shape[2:])] * heads,
        scratch_shapes=[
            pltpu.VMEM((rows, width), BF16),
            pltpu.VMEM((width,), BF16),
            pltpu.VMEM(kv_pool.shape, BF16),
            pltpu.SemaphoreType.DMA((blocks + 2,)),
        ],
        compiler_params=params(16),
        cost_estimate=SMALL,
        name="prepare",
    )(place, tokens, gain, kv_pool)


def project_local(place, near, far, w_query, w_keyvalue, after):
    rows, half = near[0].shape
    q_width, kv_width = w_query.shape[1], w_keyvalue.shape[1]
    steps = 8
    depth = 2 * half // steps
    waits = len(after)

    def kernel(place_ref, near_own, near_peer, far_own, far_peer, wq, wkv, *refs):
        q_ref, kv_ref, wq_buf, wkv_buf, q_acc, kv_acc, sems = refs[waits:]
        core = place_ref[1]
        stream = weight_stream(core, half, steps, (wq, wkv), (wq_buf, wkv_buf), sems)
        for j in range(steps):
            for copy in stream(j):
                copy.start()
        for j in range(steps):
            for copy in stream(j):
                copy.wait()
            group = (near_own, near_peer) if j < steps // 2 else (far_own, far_peer)
            cols = slice((j % (steps // 2)) * depth, (j % (steps // 2) + 1) * depth)
            x = jnp.concatenate([ref[:, cols] for ref in group], axis=0)
            q_part = jnp.dot(x, wq_buf[j], preferred_element_type=F32)
            kv_part = jnp.dot(x, wkv_buf[j], preferred_element_type=F32)
            if j == 0:
                q_acc[...] = q_part
                kv_acc[...] = kv_part
            elif j < steps - 1:
                q_acc[...] += q_part
                kv_acc[...] += kv_part
            else:
                q_last = (q_acc[...] + q_part).astype(BF16)
                kv_last = (kv_acc[...] + kv_part).astype(BF16)
        for b in range(2):
            at = pl.ds(pl.multiple_of((core if b == 0 else 1 - core) * rows, rows), rows)
            q_ref[at, :] = q_last[b * rows : (b + 1) * rows]
            kv_ref[at, :] = kv_last[b * rows : (b + 1) * rows]

    total = 2 * rows
    return pl.pallas_call(
        kernel,
        in_specs=[SMEM] + [VMEM] * 4 + [HBM] * 2 + [ANY] * waits,
        out_specs=[VMEM] * 4,
        out_shape=[
            shape((total, q_width)),
            shape((total, kv_width)),
            pltpu.VMEM((steps, depth, q_width), BF16),
            pltpu.VMEM((steps, depth, kv_width), BF16),
        ],
        scratch_shapes=[
            pltpu.VMEM((total, q_width), F32),
            pltpu.VMEM((total, kv_width), F32),
            pltpu.SemaphoreType.DMA((2 * steps,)),
        ],
        compiler_params=params(10),
        cost_estimate=LARGE,
        name="project_local",
    )(place, *near, *far, w_query, w_keyvalue, *after)


def weight_stream(core, half, steps, sources, buffers, sems):
    depth = 2 * half // steps

    def copies(j):
        base = core if j < steps // 2 else 1 - core
        start = pl.multiple_of(base * half + (j % (steps // 2)) * depth, depth)
        count = len(sources)
        return [
            pltpu.make_async_copy(w.at[pl.ds(start, depth)], buf.at[j], sems.at[count * j + i])
            for i, (w, buf) in enumerate(zip(sources, buffers))
        ]

    return copies


PAGES_STEP = 8
REQUESTS = 4
SIZES_AT = 4
REQUESTS_AT = 8


def attention_scratch(block_rows, heads, fresh_rows, slots):
    stacked = heads * block_rows
    return [
        pltpu.VMEM((stacked, fresh_rows + slots * PAGE), F32),
        pltpu.VMEM((stacked, HEAD_DIM), F32),
        pltpu.VMEM((stacked, HEAD_DIM), F32),
        pltpu.VMEM((slots * PAGE, 2 * HEAD_DIM), BF16),
        pltpu.SMEM((slots,), jnp.int32),
    ]


def attend_block(place_ref, q, first_row, fresh, pulled, scratch):
    scores, total_ref, mixed_ref, cache, labels = scratch
    me = place_ref[0]
    block_rows, width = q.shape
    heads = width // HEAD_DIM
    stacked = heads * block_rows
    groups, per = pulled.shape[:2]
    tensors = 4
    slots = per // tensors
    wide = PAGES_STEP * PAGE
    factor = math.log2(math.e) / math.sqrt(HEAD_DIM)
    bound = []
    running = jnp.int32(0)
    for k in range(REQUESTS):
        running = running + place_ref[SIZES_AT + k] * UNIT
        bound.append(running)

    def segment_of(position):
        return sum((position >= b).astype(jnp.int32) for b in bound)

    lowest = segment_of(first_row)
    highest = segment_of(first_row + block_rows - 1)
    count = jnp.int32(0)
    for g in range(groups):
        for p in range(per):
            owner = g * tensors + jnp.bitwise_xor(me, p // slots)
            label = place_ref[REQUESTS_AT + p % slots * groups * tensors + owner]
            wanted = (label >= lowest) & (label <= highest)

            @pl.when(wanted)
            def _():
                cache[pl.ds(pl.multiple_of(count * PAGE, PAGE), PAGE), :] = pulled[g, p]
                labels[count] = label

            count = count + wanted.astype(jnp.int32)
    steps = (count + PAGES_STEP - 1) // PAGES_STEP
    for k in range(PAGES_STEP - 1):

        @pl.when(count + k < steps * PAGES_STEP)
        def _():
            cache[pl.ds(pl.multiple_of((count + k) * PAGE, PAGE), PAGE), :] = jnp.zeros(
                (PAGE, 2 * HEAD_DIM), BF16
            )
            labels[count + k] = jnp.int32(-1)

    q_rows = jnp.concatenate([q[:, h * HEAD_DIM : (h + 1) * HEAD_DIM] for h in range(heads)], axis=0)
    row_position = first_row + lax.broadcasted_iota(jnp.int32, (block_rows, 1), 0)
    row_segment = segment_of(row_position)

    def masked_scores(keys, allowed):
        raw = lax.dot_general(q_rows, keys, (((1,), (1,)), ((), ())), preferred_element_type=F32)
        n = keys.shape[0]
        return jnp.where(allowed[None], raw.reshape(heads, block_rows, n), NEG_FILL).reshape(
            stacked, n
        )

    def fold(values, combine):
        pieces = [values[:, i : i + HEAD_DIM] for i in range(0, values.shape[1], HEAD_DIM)]
        result = pieces[0]
        for piece in pieces[1:]:
            result = combine(result, piece)
        return result

    new = jnp.concatenate([rows for rows, _ in fresh], axis=0)
    fresh_rows = new.shape[0]
    key_position = jnp.concatenate(
        [
            base + lax.broadcasted_iota(jnp.int32, (1, rows.shape[0]), 1)
            for rows, base in fresh
        ],
        axis=1,
    )
    allowed = (row_segment == segment_of(key_position)) & (key_position <= row_position)
    masked = masked_scores(new[:, :HEAD_DIM], allowed)
    scores[:, :fresh_rows] = masked
    total_ref[...] = fold(masked, jnp.maximum)
    lanes = lax.broadcasted_iota(jnp.int32, (1, wide), 1) // PAGE

    def add_scores(g, carry):
        label = jnp.full((1, wide), -1, jnp.int32)
        for j in range(PAGES_STEP):
            label = jnp.where(lanes == j, labels[g * PAGES_STEP + j], label)
        keys = cache[pl.ds(pl.multiple_of(g * wide, wide), wide), :HEAD_DIM]
        masked = masked_scores(keys, row_segment == label)
        scores[:, pl.ds(pl.multiple_of(fresh_rows + g * wide, PAGE), wide)] = masked
        total_ref[...] = jnp.maximum(total_ref[...], fold(masked, jnp.maximum))
        return carry

    lax.fori_loop(0, steps, add_scores, 0)
    top = jnp.max(total_ref[...], axis=1, keepdims=True) * factor
    probs = jnp.exp2(scores[:, :fresh_rows] * factor - top)
    total_ref[...] = fold(probs, jnp.add)
    mixed_ref[...] = jnp.dot(probs.astype(BF16), new[:, HEAD_DIM:], preferred_element_type=F32)

    def add_values(g, carry):
        part = scores[:, pl.ds(pl.multiple_of(fresh_rows + g * wide, PAGE), wide)]
        probs = jnp.exp2(part * factor - top)
        values = cache[pl.ds(pl.multiple_of(g * wide, wide), wide), HEAD_DIM:]
        total_ref[...] += fold(probs, jnp.add)
        mixed_ref[...] += jnp.dot(probs.astype(BF16), values, preferred_element_type=F32)
        return carry

    lax.fori_loop(0, steps, add_values, 0)
    denominator = jnp.sum(total_ref[...], axis=1, keepdims=True)
    result = (mixed_ref[...] / denominator).astype(BF16)
    return jnp.concatenate(
        [result[h * block_rows : (h + 1) * block_rows] for h in range(heads)], axis=1
    )


def project_held(near, far, w_query, w_keyvalue, after):
    rows, half = near.shape
    pieces = len(far)
    steps, depth, q_width = w_query.shape
    kv_width = w_keyvalue.shape[2]

    def kernel(near_ref, *refs):
        far_refs = refs[:pieces]
        wq, wkv = refs[pieces : pieces + 2]
        q_ref, kv_ref = refs[pieces + 2 + len(after) :]
        for w, out in ((wq, q_ref), (wkv, kv_ref)):
            total = None
            for j in range(steps):
                at = j * depth
                if at < half:
                    x = near_ref[:, at : at + depth]
                else:
                    wide = half // pieces
                    x = far_refs[(at - half) // wide][:, at % wide : at % wide + depth]
                part = jnp.dot(x, w[j], preferred_element_type=F32)
                total = part if j == 0 else total + part
            out[...] = total.astype(BF16)

    return pl.pallas_call(
        kernel,
        in_specs=[VMEM] * (3 + pieces) + [ANY] * len(after),
        out_specs=[VMEM] * 2,
        out_shape=[shape((rows, q_width)), shape((rows, kv_width))],
        compiler_params=params(6),
        cost_estimate=SMALL,
        name="project_held",
    )(near, *far, w_query, w_keyvalue, *after)


def project_far(place, near, far, w_query, w_keyvalue, after):
    rows, half = near.shape
    q_width, kv_width = w_query.shape[1], w_keyvalue.shape[1]
    steps = 8
    depth = 2 * half // steps

    def kernel(place_ref, near_ref, far_ref, wq, wkv, *refs):
        q_ref, kv_ref, wq_buf, wkv_buf, x_buf, sems = refs[len(after) :]
        rows_in = [
            pltpu.make_async_copy(ref, x_buf.at[i], sems.at[2 * steps + i])
            for i, ref in enumerate((near_ref, far_ref))
        ]
        stream = weight_stream(place_ref[1], half, steps, (wq, wkv), (wq_buf, wkv_buf), sems)
        for j in range(steps):
            for copy in stream(j):
                copy.start()
            if j < 2:
                rows_in[j].start()
        q_sum = kv_sum = None
        for j in range(steps):
            for copy in stream(j):
                copy.wait()
            group, inner = divmod(j, steps // 2)
            if inner == 0:
                rows_in[group].wait()
            x = x_buf[group, :, inner * depth : (inner + 1) * depth]
            q_part = jnp.dot(x, wq_buf[j], preferred_element_type=F32)
            kv_part = jnp.dot(x, wkv_buf[j], preferred_element_type=F32)
            q_sum = q_part if j == 0 else q_sum + q_part
            kv_sum = kv_part if j == 0 else kv_sum + kv_part
        q_ref[...] = q_sum.astype(BF16)
        kv_ref[...] = kv_sum.astype(BF16)

    return pl.pallas_call(
        kernel,
        in_specs=[SMEM] + [ANY] * 2 + [HBM] * 2 + [ANY] * len(after),
        out_specs=[VMEM] * 2,
        out_shape=[shape((rows, q_width)), shape((rows, kv_width))],
        scratch_shapes=[
            pltpu.VMEM((steps, depth, q_width), BF16),
            pltpu.VMEM((steps, depth, kv_width), BF16),
            pltpu.VMEM((2, rows, half), BF16),
            pltpu.SemaphoreType.DMA((2 * steps + 2,)),
        ],
        compiler_params=params(32),
        cost_estimate=SMALL,
        name="project_far",
    )(place, near, far, w_query, w_keyvalue, *after)


def attend_out(place, query, fresh, bases, base, pulled, w_out):
    rows, depth = query.shape
    width = w_out.shape[1]
    half = width // 2
    heads = depth // HEAD_DIM
    out_steps = 4
    wide = half // out_steps
    known = len(fresh)
    count = sum(f.shape[0] for f in fresh)
    fresh_rows = -(-count // HEAD_DIM) * HEAD_DIM
    pad = fresh_rows - count

    def kernel(place_ref, q_ref, pulled_ref, *refs):
        fresh_refs = refs[:known]
        wo = refs[known]
        there_refs, refs_after = refs[known + 1 : known + 1 + out_steps], refs[known + 1 + out_steps :]
        stay_ref, wo_buf, sems = refs_after[:3]
        core, side = place_ref[1], place_ref[2]

        def copy(j):
            first = 1 - core if j < out_steps else core
            start = pl.multiple_of(first * half + (j % out_steps) * wide, wide)
            return pltpu.make_async_copy(wo.at[:, pl.ds(start, wide)], wo_buf.at[j], sems.at[j])

        for j in range(2 * out_steps):
            copy(j).start()
        pairs = [(ref[...], at(side)) for ref, at in zip(fresh_refs, bases)]
        if pad:
            pairs.append((jnp.zeros((pad, 2 * HEAD_DIM), BF16), jnp.int32(1 << 20)))
        mixed = attend_block(
            place_ref, q_ref[...], base(side), pairs, pulled_ref, refs_after[3:]
        )
        for j in range(2 * out_steps):
            copy(j).wait()
            part = jnp.dot(mixed, wo_buf[j], preferred_element_type=F32).astype(BF16)
            if j < out_steps:
                there_refs[j][...] = part
            else:
                at = (j - out_steps) * wide
                stay_ref[:, at : at + wide] = part

    return pl.pallas_call(
        kernel,
        in_specs=[SMEM] + [VMEM] * (2 + known) + [HBM],
        out_specs=[VMEM] * (out_steps + 1),
        out_shape=[shape((rows, wide))] * out_steps + [shape((rows, half))],
        scratch_shapes=[
            pltpu.VMEM((2 * out_steps, depth, wide), BF16),
            pltpu.SemaphoreType.DMA((2 * out_steps,)),
        ]
        + attention_scratch(rows, heads, fresh_rows, pulled.shape[0] * pulled.shape[1]),
        compiler_params=params(30),
        cost_estimate=MEDIUM,
        name="attend_out",
    )(place, query, pulled, *fresh, w_out)


def local_rows(place, query, fresh, bases, base, pulled, w_out, after):
    both, depth = query.shape
    rows = both // 2
    width = w_out.shape[1]
    heads = depth // HEAD_DIM
    steps = 8
    wide = width // steps
    known = len(fresh)
    fresh_rows = sum(f.shape[0] for f in fresh)

    def kernel(place_ref, q_ref, pulled_ref, *refs):
        fresh_refs = refs[:known]
        wo = refs[known]
        rest = refs[known + 1 + len(after) :]
        own_ref, peer_ref, wo_buf, a_buf, sems = rest[:5]
        core, side = place_ref[1], place_ref[2]

        def out_copy(j):
            return pltpu.make_async_copy(
                wo.at[:, j * wide : (j + 1) * wide], wo_buf.at[j], sems.at[j]
            )

        for j in range(steps):
            out_copy(j).start()

        def block(b, carry):
            at = pl.ds(pl.multiple_of(b * rows, rows), rows)
            a_buf[at, :] = attend_block(
                place_ref,
                q_ref[at, :],
                base(side) + b * rows,
                [(ref[...], first(side)) for ref, first in zip(fresh_refs, bases)],
                pulled_ref,
                rest[5:],
            )
            return carry

        lax.fori_loop(0, 2, block, 0)
        own_at = pl.ds(pl.multiple_of(core * rows, rows), rows)
        peer_at = pl.ds(pl.multiple_of((1 - core) * rows, rows), rows)
        a = jnp.concatenate([a_buf[own_at, :], a_buf[peer_at, :]], axis=0)
        for j in range(steps):
            out_copy(j).wait()
            part = jnp.dot(a, wo_buf[j], preferred_element_type=F32).astype(BF16)
            own_ref[:, j * wide : (j + 1) * wide] = part[:rows]
            peer_ref[:, j * wide : (j + 1) * wide] = part[rows:]

    return pl.pallas_call(
        kernel,
        in_specs=[SMEM] + [VMEM] * (2 + known) + [HBM] + [ANY] * len(after),
        out_specs=[VMEM, VMEM],
        out_shape=[shape((rows, width)), shape((rows, width))],
        scratch_shapes=[
            pltpu.VMEM((steps, depth, wide), BF16),
            pltpu.VMEM((both, depth), BF16),
            pltpu.SemaphoreType.DMA((steps,)),
        ]
        + attention_scratch(rows, heads, fresh_rows, pulled.shape[0] * pulled.shape[1]),
        compiler_params=params(40),
        cost_estimate=SMALL,
        name="local_rows",
    )(place, query, pulled, *fresh, w_out, *after)


def add_pair(left, pieces):
    rows, width = left.shape
    count = len(pieces)
    wide = width // count

    def kernel(left_ref, *refs):
        out_ref = refs[count]
        for i in range(count):
            cols = slice(i * wide, (i + 1) * wide)
            out_ref[:, cols] = (left_ref[:, cols].astype(F32) + refs[i][...].astype(F32)).astype(
                BF16
            )

    return pl.pallas_call(
        kernel,
        in_specs=[VMEM] * (1 + count),
        out_specs=VMEM,
        out_shape=shape((rows, width)),
        compiler_params=params(8),
        cost_estimate=SMALL,
        name="add_pair",
    )(left, *pieces)


def finish_near(place, tokens, own, peer, near):
    rows, width = tokens.shape
    half = width // 2
    step = 16

    def kernel(place_ref, x_ref, own_ref, peer_ref, near_ref, done_ref, local_ref):
        core = place_ref[1]
        near_cols = pl.ds(pl.multiple_of(core * half, half), half)
        far_cols = pl.ds(pl.multiple_of((1 - core) * half, half), half)

        def block(i, carry):
            at = pl.ds(pl.multiple_of(i * step, step), step)
            local = own_ref[at, near_cols].astype(F32) + peer_ref[at, near_cols].astype(F32)
            total = local + near_ref[at, :].astype(F32)
            done_ref[at, :] = (x_ref[at, near_cols].astype(F32) + total).astype(BF16)
            local_ref[at, :] = own_ref[at, far_cols].astype(F32) + peer_ref[at, far_cols].astype(F32)
            return carry

        lax.fori_loop(0, rows // step, block, 0)

    return pl.pallas_call(
        kernel,
        in_specs=[SMEM] + [VMEM] * 4,
        out_specs=[VMEM] * 2,
        out_shape=[shape((rows, half)), shape((rows, half), F32)],
        compiler_params=params(16),
        cost_estimate=SMALL,
        name="finish_near",
    )(place, tokens, own, peer, near)


def finish(place, tokens, done, local, far):
    rows, width = tokens.shape
    half = width // 2
    step = 32
    blocks = rows // step

    def kernel(place_ref, x_ref, done_ref, local_ref, far_ref, out_ref, buf, sems):
        core = place_ref[1]
        near_cols = pl.ds(pl.multiple_of(core * half, half), half)
        far_cols = pl.ds(pl.multiple_of((1 - core) * half, half), half)

        def near_copy():
            return pltpu.make_async_copy(done_ref, out_ref.at[:, near_cols], sems.at[blocks])

        def far_copy(b):
            at = pl.ds(b * step, step)
            return pltpu.make_async_copy(buf.at[at], out_ref.at[at, far_cols], sems.at[b])

        near_copy().start()
        for b in range(blocks):
            for i in range(0, step, 16):
                at = slice(b * step + i, b * step + i + 16)
                total = local_ref[at, :] + far_ref[at, :].astype(F32)
                buf[at, :] = (x_ref[at, far_cols].astype(F32) + total).astype(BF16)
            far_copy(b).start()
        near_copy().wait()
        for b in range(blocks):
            far_copy(b).wait()

    return pl.pallas_call(
        kernel,
        in_specs=[SMEM] + [VMEM] * 4,
        out_specs=ANY,
        out_shape=shape((rows, width)),
        scratch_shapes=[
            pltpu.VMEM((rows, half), BF16),
            pltpu.SemaphoreType.DMA((blocks + 1,)),
        ],
        compiler_params=params(16),
        cost_estimate=SMALL,
        name="finish",
    )(place, tokens, done, local, far)


def pick_pages(place, wanted, held, after):
    replicas = len(wanted)
    slots = wanted[0].shape[1]
    tensors = len(held)
    _, page, width = held[0].shape
    total = tensors * slots

    def kernel(place_ref, *refs):
        wants, sources = refs[:replicas], refs[replicas : replicas + tensors]
        out_ref = refs[replicas + tensors + len(after)]
        me, rep = place_ref[0], place_ref[3]
        for k in range(replicas):
            asker = lax.rem(rep + k, replicas)
            for i in range(tensors):
                owner = rep * tensors + jnp.bitwise_xor(me, i)
                for s in range(slots):
                    out_ref[asker, i * slots + s] = sources[i][wants[k][0, s, owner]]

    return pl.pallas_call(
        kernel,
        in_specs=[SMEM] * (1 + replicas) + [VMEM] * tensors + [ANY] * len(after),
        out_specs=VMEM,
        out_shape=shape((replicas, total, page, width)),
        compiler_params=params(8),
        cost_estimate=SMALL,
        name="pick_pages",
    )(place, *wanted, *held, *after)


def write_pool(place, slots, kv_pool, early, late):
    pages, heads = kv_pool.shape[:2]
    new_count = slots.shape[1]
    early_rows, late_rows = early[0].shape[0], late[0].shape[0]
    side_rows = (early_rows + late_rows) // 2
    total_rows = early_rows + late_rows

    def kernel(place_ref, slot_ref, pool_ref, *refs):
        early_refs, late_refs, (out_ref, rows_ref) = refs[:3], refs[3:6], refs[6:]
        me, side = place_ref[0], place_ref[2]

        def source(group, i):
            own, y, core = group
            return (own, core.at[0], y, core.at[1])[i]

        for i in range(heads):
            rows_ref[i, :early_rows] = source(early_refs, i)[...]
            rows_ref[i, early_rows:] = source(late_refs, i)[...]
        for p in range(pages):
            found = jnp.int32(-1)
            for j in range(new_count):
                found = jnp.where(slot_ref[0, j] == me * pages + p, j, found)
            first = jnp.maximum(found, 0) * PAGE
            far = (first >= side_rows).astype(jnp.int32)
            inner = first - far * side_rows
            for i in range(heads):
                origin = side if i < 2 else 1 - side
                start = jnp.bitwise_xor(far, origin) * side_rows + inner
                at = jnp.bitwise_xor(me, i)

                @pl.when(found >= 0)
                def _():
                    out_ref[p, at] = rows_ref[i, pl.ds(pl.multiple_of(start, PAGE), PAGE), :]

                @pl.when(found < 0)
                def _():
                    out_ref[p, at] = pool_ref[p, at]

    return pl.pallas_call(
        kernel,
        in_specs=[SMEM, SMEM] + [VMEM] * 7,
        out_specs=VMEM,
        out_shape=shape(kv_pool.shape),
        scratch_shapes=[pltpu.VMEM((heads, total_rows, kv_pool.shape[3]), BF16)],
        compiler_params=params(12),
        cost_estimate=SMALL,
        name="write_pool",
    )(place, slots, kv_pool, *early, *late)


def chip_pair_body(
    tokens,
    gain,
    w_query,
    w_keyvalue,
    w_out,
    kv_pool,
    suffix_pages,
    page_index,
    page_request,
    new_slot,
):
    replicas = lax.axis_size("replica")
    me = lax.axis_index("tensor")
    core = me % 2
    side = me // 2
    rows = tokens.shape[0]
    rep = lax.axis_index("replica")
    place = jnp.stack([me, core, side, rep]).astype(jnp.int32)
    def over_core(x):
        return lax.ppermute(x, "tensor", [(0, 1), (1, 0), (2, 3), (3, 2)])

    def over_y(x):
        return lax.ppermute(x, "tensor", [(0, 2), (2, 0), (1, 3), (3, 1)])

    def tie(x, *others):
        return lax.optimization_barrier((x, *others))[0]

    w_query, w_keyvalue, w_out = in_hbm(w_query), in_hbm(w_keyvalue), in_hbm(w_out)

    wanted = [jnp.swapaxes(page_index, 1, 2)]
    for k in range(1, replicas):
        back = [(i, (i - k) % replicas) for i in range(replicas)]
        wanted.append(lax.ppermute(wanted[0], "replica", back))

    mine, other, *held = prepare(place, in_hbm(tokens), in_hbm(gain), in_hbm(kv_pool))
    for i in range(1, 4):
        held[i] = lax.ppermute(held[i], "tensor", [(t, t ^ i) for t in range(4)])

    peer_near = over_core(other)
    peer_far = over_core(mine)
    is_first = core == 0
    near_tied = tie(peer_near, held[2], held[3])
    first_half = jnp.where(is_first, mine, near_tied)
    second_half = jnp.where(is_first, near_tied, mine)
    first = over_y(first_half)
    second = over_y(second_half)

    picked = pick_pages(place, wanted, held, [first_half, second_half])
    sizes, requests = lax.optimization_barrier((suffix_pages, page_request, picked))[:2]
    requests = jnp.swapaxes(requests, 1, 2).reshape(-1)
    scalars = jnp.concatenate([place, sizes[0], requests])
    pulled = lax.all_to_all(picked, "replica", split_axis=0, concat_axis=0, tiled=True)

    q_local, kv_local, wq, wkv = project_local(
        place, [mine, peer_near], [other, peer_far], w_query, w_keyvalue, [picked, scalars]
    )


    def local_base(s):
        return s * (2 * rows)

    def first_base(s):
        return (1 - s) * (2 * rows)

    def second_base(s):
        return (1 - s) * (2 * rows) + rows

    first = tie(first, q_local)
    wide = first.shape[1] // 4
    pieces = [over_core(first[:, i * wide : (i + 1) * wide]) for i in range(4)]
    q_first, kv_first = project_held(first, pieces, wq, wkv, [])
    early_own = jnp.concatenate([kv_local, kv_first], axis=0)
    early_y = over_y(early_own)
    *there, stay = attend_out(
        scalars, q_first, [kv_local, kv_first], [local_base, first_base], first_base, pulled, w_out
    )
    first_mix = add_pair(stay, [over_core(tie(part, early_y)) for part in there])
    first_sum = over_y(first_mix)

    second = tie(second, first_mix)
    q_second, kv_second = project_far(place, second, over_core(second), w_query, w_keyvalue, [])
    fresh = [kv_local, kv_first, kv_second]
    bases = [local_base, first_base, second_base]
    *there, stay = attend_out(scalars, q_second, fresh, bases, second_base, pulled, w_out)
    late_y = over_y(kv_second)
    there[-1] = tie(there[-1], late_y)
    second_mix = add_pair(stay, [over_core(part) for part in there])
    second_sum = over_y(tie(second_mix, first_sum))

    own_part, peer_part = local_rows(
        scalars, q_local, fresh, bases, local_base, pulled, w_out, [second_mix]
    )
    peer_part = over_core(peer_part)

    early = over_core(jnp.stack([early_own, early_y]))
    late = over_core(jnp.stack([kv_second, late_y]))
    pool_out = write_pool(
        place, new_slot, kv_pool, [early_own, early_y, early], [kv_second, late_y, late]
    )

    second_sum = tie(second_sum, pool_out)
    near = jnp.where(is_first, first_sum, second_sum)
    far = over_core(jnp.where(is_first, second_sum, first_sum))
    done, local = finish_near(place, tokens, own_part, peer_part, near)
    layer_out = finish(place, tokens, done, local, far)
    return (layer_out, pool_out)


def solution(mesh):
    pair = mesh.shape["tensor"] == KV_HEADS
    return jax.shard_map(
        chip_pair_body if pair else gathered_body,
        mesh=mesh,
        in_specs=(
            P(("groups", "replica", "tensor"), None),
            P(),
            P(None, "tensor"),
            P(None, "tensor"),
            P("tensor", None),
            P(("groups", "replica", "tensor"), None, None, None),
            P(("groups", "replica"), None),
            P(("groups", "replica"), None, None),
            P(("groups", "replica"), None, None),
            P(("groups", "replica"), None),
        ),
        out_specs=(
            P(("groups", "replica", "tensor"), None),
            P(("groups", "replica", "tensor"), None, None, None),
        ),
        check_vma=False,
    )
```
